32 devices in a mesh: grp: 1, row: 16 (over z, y, core), col: 2 (over x).
Axes of the slice: x: 2, y: 2, z: 4, core: 2. Of those that a mesh axis runs over, the one named last changes fastest.
Arguments:
- pair: bfloat16 [256, 256, 128], P(('grp', 'row'), 'col'), may hold values from -6 to 6
- mask: int32 [256], P('grp'), may hold values 0 or 1
- gain_in: float32 [128], replicated, may hold values from 0.1 to 1.9
- bias_in: float32 [128], replicated, may hold values from -3 to 3
- proj_weight: bfloat16 [128, 512], replicated, may hold values from -0.5 to 0.5
- gate_weight: bfloat16 [128, 128], replicated, may hold values from -0.5 to 0.5
- product_norm_gain: float32 [128], replicated, may hold values from 0.1 to 1.9
- product_norm_bias: float32 [128], replicated, may hold values from -3 to 3
- out_weight: bfloat16 [128, 128], replicated, may hold values from -0.5 to 0.5
- cotangent: bfloat16 [256, 256, 128], P(('grp', 'row'), 'col'), may hold values from -6 to 6
Outputs:
- update: bfloat16 [256, 256, 128], P(('grp', 'row'), 'col')
- grad_pair: bfloat16 [256, 256, 128], P(('grp', 'row'), 'col')
The draws below stay inside these ranges and needn't reach their ends.
All inputs are finite; a program needn't handle non-finite values.
Results may differ from the reference program's by a relative error of at most 0.0076.
Values may be sent and summed in bfloat16 or wider, within the bound.
No kernel may reach another device: no remote copies, remote signals or barrier semaphores. Data moves between devices by JAX's collectives and lax.ppermute only.
A program may use at most 64 MiB of HBM per device.

```python
import math
import jax
import jax.numpy as jnp
from jax import lax

C = 128
H = 128
N = 256


def plant(array, stream_key, low, largest):
    shape = array.shape
    spot = [jax.random.randint(jax.random.fold_in(stream_key, axis), (), 0, shape[axis]) for axis in range(len(shape))]
    array = array.at[tuple(spot)].set(low)
    longest = shape.index(max(shape))
    spot[longest] = (spot[longest] + 1) % shape[longest]
    return array.at[tuple(spot)].set(largest)


def level_of(rng, extent, shards, least, top_value):
    level = 1.0
    for axis_at, shards_of in shards:
        draws = jax.random.uniform(jax.random.fold_in(jax.random.fold_in(rng, 6), axis_at), (shards_of,), jnp.float32, least / len(shards), top_value / len(shards))
        level = level * jnp.repeat(jnp.exp(draws), extent[axis_at] // shards_of).reshape((-1,) + (1,) * (len(extent) - 1 - axis_at))
    return level


def gaussian(key, extent, deviation, reach, split=(), held_as=jnp.bfloat16):
    drawn = jax.random.normal(key, extent, jnp.float32) * deviation
    if len(split) > 0:
        drawn = level_of(key, extent, split, -0.22, 0.18) * drawn
    return jnp.clip(drawn, min=-reach, max=reach).astype(held_as)


def setup_inputs(seed: int = 0, part: int = 0) -> dict:
    splits = jax.random.split(jax.random.key(seed), 11)
    own_keys = jax.random.split(jax.random.fold_in(splits[10], part), 11)
    pair = gaussian(own_keys[0], (N, N, C), 1.0, 6.0, ((0, 16), (1, 2)))
    mask = plant((jax.random.randint(own_keys[1], (N,), 0, 8) < 7).astype(jnp.int32), jax.random.fold_in(own_keys[1], 1), 0, 1)
    gain_in = jnp.clip(1.0 + 0.18 * jax.random.normal(splits[2], (C,), jnp.float32), 0.1, 1.9)
    bias_in = gaussian(splits[3], (C,), 0.5, 3.0, (), jnp.float32)
    proj_weight = gaussian(splits[4], (C, 4 * H), C ** -0.5, 0.5)
    gate_weight = gaussian(splits[5], (C, C), C ** -0.5, 0.5)
    product_norm_gain = jnp.clip(1.0 + 0.18 * jax.random.normal(splits[6], (H,), jnp.float32), 0.1, 1.9)
    product_norm_bias = gaussian(splits[7], (H,), 0.5, 3.0, (), jnp.float32)
    out_weight = gaussian(splits[8], (H, C), H ** -0.5, 0.5)
    cotangent = gaussian(own_keys[9], (N, N, C), 1.0, 6.0, ((0, 16), (1, 2)))
    return dict(pair=pair, mask=mask, gain_in=gain_in, bias_in=bias_in, proj_weight=proj_weight, gate_weight=gate_weight, product_norm_gain=product_norm_gain, product_norm_bias=product_norm_bias, out_weight=out_weight, cotangent=cotangent)


EPS = 1e-05

def layer_normalize(values, reduce_dimension):
    feature_average = lax.optimization_barrier(jnp.mean(values, axis=reduce_dimension, keepdims=True))
    centred = values - feature_average
    var = lax.optimization_barrier(jnp.mean(centred * centred, axis=reduce_dimension, keepdims=True))
    inverse_deviation = lax.rsqrt(var + EPS)
    return (centred * inverse_deviation, inverse_deviation)

def front(z_rows, row_mask, mask_f, gain_in, bias_in, proj_weight, gate_weight):
    zhat, inverse_deviation = layer_normalize(z_rows.astype(jnp.float32), 2)
    zbar = (zhat * gain_in + bias_in).astype(jnp.bfloat16)
    proj = jnp.einsum('ikc,ch->hik', zbar.astype(jnp.float32), proj_weight.astype(jnp.float32))
    pa, qa, pb, qb = (proj[:H], proj[H:2 * H], proj[2 * H:3 * H], proj[3 * H:])
    pair_mask = (row_mask[:, None] * mask_f[None, :])[None]
    sig_a = jax.nn.sigmoid(pa)
    sig_b = jax.nn.sigmoid(pb)
    left = (sig_a * qa * pair_mask).astype(jnp.bfloat16)
    right = (sig_b * qb * pair_mask).astype(jnp.bfloat16)
    gate = jax.nn.sigmoid(jnp.einsum('ikc,cd->ikd', zbar.astype(jnp.float32), gate_weight.astype(jnp.float32)))
    return (zhat, inverse_deviation, qa, qb, sig_a, sig_b, pair_mask, left, right, gate)

def reference(pair, mask, gain_in, bias_in, proj_weight, gate_weight, product_norm_gain, product_norm_bias, out_weight, cotangent):
    block = math.gcd(N, 64)
    count = N // block
    mask_f = mask.astype(jnp.float32)
    pair_blocks = pair.reshape(count, block, N, C)
    mask_blocks = mask_f.reshape(count, block)
    cot_blocks = cotangent.reshape(count, block, N, C)

    def apply_front(z_rows, m_rows):
        return front(z_rows, m_rows, mask_f, gain_in, bias_in, proj_weight, gate_weight)

    def first(items):
        parts = apply_front(items[0], items[1])
        return (parts[7], parts[8])
    left_b, right_b = lax.map(first, (pair_blocks, mask_blocks))
    left = jnp.moveaxis(left_b, 0, 1).reshape(H, N, N)
    right = jnp.moveaxis(right_b, 0, 1).reshape(H, N, N)

    def contract(items):
        return jnp.dot(items[0], items[1].T, preferred_element_type=jnp.float32).astype(jnp.bfloat16)
    product = lax.map(contract, (left, right))
    prod_blocks = jnp.moveaxis(product.reshape(H, count, block, N), 1, 0)

    def second(items):
        z_rows, m_rows, c_rows, input_rows = items
        gate = apply_front(z_rows, m_rows)[9]
        normalized_input, inverse_deviation = layer_normalize(input_rows.astype(jnp.float32), 0)
        scaled_normalized = (normalized_input * product_norm_gain[:, None, None] + product_norm_bias[:, None, None]).astype(jnp.bfloat16)
        proj_out = jnp.einsum('hik,hc->ikc', scaled_normalized.astype(jnp.float32), out_weight.astype(jnp.float32))
        update = (gate * proj_out).astype(jnp.bfloat16)
        cot_f = c_rows.astype(jnp.float32)
        grad_u = (cot_f * gate).astype(jnp.bfloat16)
        grad_gate = (cot_f * proj_out * gate * (1.0 - gate)).astype(jnp.bfloat16)
        grad_y = jnp.einsum('ikc,hc->hik', grad_u.astype(jnp.float32), out_weight.astype(jnp.float32))
        normalized_gradient = grad_y * product_norm_gain[:, None, None]
        input_gradient = (normalized_gradient - lax.optimization_barrier(jnp.mean(normalized_gradient, axis=0, keepdims=True)) - normalized_input * lax.optimization_barrier(jnp.mean(normalized_gradient * normalized_input, axis=0, keepdims=True))) * inverse_deviation
        return (update, input_gradient.astype(jnp.bfloat16), grad_gate)
    update_b, grad_x_b, grad_gate_b = lax.map(second, (pair_blocks, mask_blocks, cot_blocks, prod_blocks))
    update = update_b.reshape(N, N, C)
    input_gradient = jnp.moveaxis(grad_x_b, 0, 1).reshape(H, N, N)

    def back_contract(items):
        grad_h, left_h, right_h = items
        grad_l = jnp.dot(grad_h, right_h, preferred_element_type=jnp.float32).astype(jnp.bfloat16)
        grad_r = jnp.dot(grad_h.T, left_h, preferred_element_type=jnp.float32).astype(jnp.bfloat16)
        return (grad_l, grad_r)
    grad_left, grad_right = lax.map(back_contract, (input_gradient, left, right))
    gl_blocks = jnp.moveaxis(grad_left.reshape(H, count, block, N), 1, 0)
    gr_blocks = jnp.moveaxis(grad_right.reshape(H, count, block, N), 1, 0)

    def third(items):
        z_rows, m_rows, gg_rows, gl_rows, gr_rows = items
        zhat, inverse_deviation, qa, qb, sig_a, sig_b, pair_mask, left_r, right_r, gate = apply_front(z_rows, m_rows)
        gl_f = gl_rows.astype(jnp.float32) * pair_mask
        gr_f = gr_rows.astype(jnp.float32) * pair_mask
        dproj = jnp.concatenate([gl_f * qa * sig_a * (1.0 - sig_a), gl_f * sig_a, gr_f * qb * sig_b * (1.0 - sig_b), gr_f * sig_b], axis=0).astype(jnp.bfloat16)
        grad_zbar = jnp.einsum('hik,ch->ikc', dproj.astype(jnp.float32), proj_weight.astype(jnp.float32))
        grad_zbar = grad_zbar + jnp.einsum('ikd,cd->ikc', gg_rows.astype(jnp.float32), gate_weight.astype(jnp.float32))
        grad_zh = grad_zbar * gain_in
        grad = (grad_zh - lax.optimization_barrier(jnp.mean(grad_zh, axis=2, keepdims=True)) - zhat * lax.optimization_barrier(jnp.mean(grad_zh * zhat, axis=2, keepdims=True))) * inverse_deviation
        return grad.astype(jnp.bfloat16)
    grad_pair = lax.map(third, (pair_blocks, mask_blocks, grad_gate_b, gl_blocks, gr_blocks)).reshape(N, N, C)
    return (update, grad_pair)
```

```python
import jax
import jax.numpy as jnp
from jax import lax
from jax.sharding import PartitionSpec as P

EPS = 1e-05


def layer_normalize(values, reduce_dimension):
    feature_average = jnp.mean(values, axis=reduce_dimension, keepdims=True)
    centred = values - feature_average
    var = jnp.mean(centred * centred, axis=reduce_dimension, keepdims=True)
    inverse_deviation = lax.rsqrt(var + EPS)
    return (centred * inverse_deviation, inverse_deviation)


def regroup_in(values, n_row, n_col):
    depth, total, cols = values.shape
    rows = total // (n_row * n_col)
    shaped = values.reshape(depth, n_row, n_col, rows, cols).transpose(0, 1, 3, 2, 4)
    return shaped.reshape(depth, n_row * rows, n_col * cols)


def regroup_out(values, n_row, n_col):
    depth, full_rows, full_cols = values.shape
    rows = full_rows // n_row
    cols = full_cols // n_col
    shaped = values.reshape(depth, n_row, rows, n_col, cols).transpose(0, 1, 3, 2, 4)
    return shaped.reshape(depth, n_row * n_col * rows, cols)


def body(
    pair,
    mask,
    gain_in,
    bias_in,
    proj_weight,
    gate_weight,
    product_norm_gain,
    product_norm_bias,
    out_weight,
    cotangent,
):
    rows, cols, width = pair.shape
    hidden = out_weight.shape[0]
    n_row = lax.axis_size("row")
    n_col = lax.axis_size("col")
    mask_f = mask.astype(jnp.float32)
    row_mask = lax.dynamic_slice_in_dim(mask_f, lax.axis_index("row") * rows, rows)
    col_mask = lax.dynamic_slice_in_dim(mask_f, lax.axis_index("col") * cols, cols)
    pair_mask = (row_mask[:, None] * col_mask[None, :])[None]
    zhat, inv_in = layer_normalize(pair.astype(jnp.float32), 2)
    zbar = (zhat * gain_in + bias_in).astype(jnp.bfloat16)
    proj = jnp.einsum("ikc,ch->hik", zbar, proj_weight, preferred_element_type=jnp.float32)
    pa, qa = (proj[:hidden], proj[hidden : 2 * hidden])
    pb, qb = (proj[2 * hidden : 3 * hidden], proj[3 * hidden :])
    sig_a = jax.nn.sigmoid(pa)
    sig_b = jax.nn.sigmoid(pb)
    left = (sig_a * qa * pair_mask).astype(jnp.bfloat16)
    right = (sig_b * qb * pair_mask).astype(jnp.bfloat16)
    gate = jax.nn.sigmoid(
        jnp.einsum("ikc,cd->ikd", zbar, gate_weight, preferred_element_type=jnp.float32)
    )
    n_dev = n_row * n_col
    share = hidden // n_dev
    both = jnp.concatenate(
        [
            left.reshape(n_dev, share, rows, cols),
            right.reshape(n_dev, share, rows, cols),
        ],
        axis=1,
    )
    both = lax.all_to_all(both, ("row", "col"), split_axis=0, concat_axis=0, tiled=True)
    both = both.reshape(n_row, n_col, 2 * share, rows, cols).transpose(2, 0, 3, 1, 4)
    both = both.reshape(2 * share, n_row * rows, n_col * cols)
    left_ch, right_ch = both[:share], both[share:]
    product = jnp.einsum(
        "hik,hjk->hij", left_ch, right_ch, preferred_element_type=jnp.float32
    ).astype(jnp.bfloat16)
    product_piece = lax.all_to_all(
        regroup_out(product, n_row, n_col), ("row", "col"), split_axis=1, concat_axis=0, tiled=True
    )
    normalized_input, product_inverse_deviation = layer_normalize(
        product_piece.astype(jnp.float32), 0
    )
    scaled_normalized = (
        normalized_input * product_norm_gain[:, None, None] + product_norm_bias[:, None, None]
    ).astype(jnp.bfloat16)
    proj_out = jnp.einsum(
        "hik,hc->ikc", scaled_normalized, out_weight, preferred_element_type=jnp.float32
    )
    update = (gate * proj_out).astype(jnp.bfloat16)
    cot_f = cotangent.astype(jnp.float32)
    grad_u = (cot_f * gate).astype(jnp.bfloat16)
    grad_gate = (cot_f * proj_out * gate * (1.0 - gate)).astype(jnp.bfloat16)
    grad_y = jnp.einsum("ikc,hc->hik", grad_u, out_weight, preferred_element_type=jnp.float32)
    normalized_gradient = grad_y * product_norm_gain[:, None, None]
    input_gradient = (
        (
            normalized_gradient
            - jnp.mean(normalized_gradient, axis=0, keepdims=True)
            - normalized_input
            * jnp.mean(normalized_gradient * normalized_input, axis=0, keepdims=True)
        )
        * product_inverse_deviation
    ).astype(jnp.bfloat16)
    grad_ch = regroup_in(
        lax.all_to_all(input_gradient, ("row", "col"), split_axis=0, concat_axis=1, tiled=True),
        n_row,
        n_col,
    )
    grad_left = jnp.einsum(
        "hij,hjk->hik", grad_ch, right_ch, preferred_element_type=jnp.float32
    ).astype(jnp.bfloat16)
    grad_right = jnp.einsum(
        "hij,hik->hjk", grad_ch, left_ch, preferred_element_type=jnp.float32
    ).astype(jnp.bfloat16)
    grads = jnp.concatenate([grad_left, grad_right], axis=0)
    grads = grads.reshape(2 * share, n_row, rows, n_col, cols).transpose(1, 3, 0, 2, 4)
    grads = grads.reshape(n_dev, 2 * share, rows, cols)
    grads = lax.all_to_all(grads, ("row", "col"), split_axis=0, concat_axis=0, tiled=True)
    gl_tile = grads[:, :share].reshape(hidden, rows, cols)
    gr_tile = grads[:, share:].reshape(hidden, rows, cols)
    gl_f = gl_tile.astype(jnp.float32) * pair_mask
    gr_f = gr_tile.astype(jnp.float32) * pair_mask
    dproj = jnp.concatenate(
        [
            gl_f * qa * sig_a * (1.0 - sig_a),
            gl_f * sig_a,
            gr_f * qb * sig_b * (1.0 - sig_b),
            gr_f * sig_b,
        ],
        axis=0,
    ).astype(jnp.bfloat16)
    grad_zbar = jnp.einsum("hik,ch->ikc", dproj, proj_weight, preferred_element_type=jnp.float32)
    grad_zbar = grad_zbar + jnp.einsum(
        "ikd,cd->ikc", grad_gate, gate_weight, preferred_element_type=jnp.float32
    )
    grad_zh = grad_zbar * gain_in
    grad_pair = (
        (
            grad_zh
            - jnp.mean(grad_zh, axis=2, keepdims=True)
            - zhat * jnp.mean(grad_zh * zhat, axis=2, keepdims=True)
        )
        * inv_in
    ).astype(jnp.bfloat16)
    return (update, grad_pair)


def solution(mesh):
    placed = (
        P(("grp", "row"), "col", None),
        P("grp"),
        P(),
        P(),
        P(),
        P(),
        P(),
        P(),
        P(),
        P(("grp", "row"), "col", None),
    )
    return jax.shard_map(
        body,
        mesh=mesh,
        in_specs=placed,
        out_specs=(P(("grp", "row"), "col", None), P(("grp", "row"), "col", None)),
        check_vma=False,
    )
```

```python
import jax
import jax.numpy as jnp
from jax import lax
from jax.experimental import pallas as pl
from jax.experimental.pallas import tpu as pltpu
from jax.sharding import PartitionSpec as P

EPS = 1e-05
F32 = jnp.float32
BF16 = jnp.bfloat16
MIB = 1 << 20


def dot(a, b, over=((1,), (0,))):
    return lax.dot_general(a, b, (over, ((), ())), preferred_element_type=F32)


def eye(size):
    down = lax.broadcasted_iota(jnp.int32, (size, size), 0)
    across = lax.broadcasted_iota(jnp.int32, (size, size), 1)
    return (down == across).astype(BF16)


def turned(values):
    return dot(eye(values.shape[1]), values, ((1,), (1,)))


def down_lanes(vector, lanes):
    return jnp.broadcast_to(vector[None, :], (lanes, vector.shape[0])).T


def turned_weight(weight):
    c, m = weight.shape
    return jnp.concatenate(
        [turned(weight[:, at : at + c]) for at in range(0, m, c)], axis=0
    ).astype(BF16)


def normalized(values):
    mean = jnp.mean(values, axis=0, keepdims=True)
    centred = values - mean
    var = jnp.mean(centred * centred, axis=0, keepdims=True)
    inverse = lax.rsqrt(var + EPS)
    return centred * inverse, inverse


def masks_of(mask_s, mask_v, rows, cols):
    first_row = lax.axis_index("row") * rows
    first_col = pl.multiple_of(lax.axis_index("col") * cols, cols)
    col_mask = mask_v[:, pl.ds(first_col, cols)].astype(F32)
    return first_row, col_mask


def front_kernel(pair, mask_s, mask_v, gain, bias, proj_weight, out, gain_b, bias_b, left, right):
    rows, cols, width = pair.shape
    n_dev, share2 = out.shape[0], out.shape[1]
    share = share2 // 2
    hidden = n_dev * share
    first_row, col_mask = masks_of(mask_s, mask_v, rows, cols)
    gain_b[...] = down_lanes(gain[...], cols)
    bias_b[...] = down_lanes(bias[...], cols)
    weight = turned_weight(proj_weight[...])

    def row(i, carry):
        zhat, _ = normalized(turned(pair[i]))
        zbar = (zhat * gain_b[...] + bias_b[...]).astype(BF16)
        proj = dot(weight, zbar)
        pm = col_mask * mask_s[first_row + i].astype(F32)
        pa, qa = proj[:hidden], proj[hidden : 2 * hidden]
        pb, qb = proj[2 * hidden : 3 * hidden], proj[3 * hidden :]
        left[pl.ds(i, hidden, stride=rows), :] = jax.nn.sigmoid(pa) * qa * pm
        right[pl.ds(i, hidden, stride=rows), :] = jax.nn.sigmoid(pb) * qb * pm
        return carry

    lax.fori_loop(0, rows, row, 0, unroll=2)
    shape = (n_dev, share, rows, cols)
    out[:, :share] = left[...].reshape(shape).astype(BF16)
    out[:, share:] = right[...].reshape(shape).astype(BF16)


def side_kernel(
    pair, cot, mask_s, mask_v, gain, bias, proj_weight, gate_weight, norm_gain, out_weight,
    coef, zhat_out, inv_out, gate_out, dxh_out, gain_b, bias_b, norm_gain_b,
):
    rows, cols, width = pair.shape
    hidden = out_weight.shape[0]
    first_row, col_mask = masks_of(mask_s, mask_v, rows, cols)
    gain_b[...] = down_lanes(gain[...], cols)
    bias_b[...] = down_lanes(bias[...], cols)
    norm_gain_b[...] = down_lanes(norm_gain[...], cols)
    weight = turned_weight(proj_weight[...])
    gate_t = turned_weight(gate_weight[...])

    def row(i, carry):
        zhat, inverse = normalized(turned(pair[i]))
        zhat_out[i] = zhat
        inv_out[pl.ds(i, 1), :] = inverse
        zbar = (zhat * gain_b[...] + bias_b[...]).astype(BF16)
        proj = dot(weight, zbar)
        pm = col_mask * mask_s[first_row + i].astype(F32)
        pa, qa = proj[:hidden], proj[hidden : 2 * hidden]
        pb, qb = proj[2 * hidden : 3 * hidden], proj[3 * hidden :]
        sa, sb = jax.nn.sigmoid(pa), jax.nn.sigmoid(pb)
        coef[i, :hidden] = pm * qa * sa * (1.0 - sa)
        coef[i, hidden : 2 * hidden] = pm * sa
        coef[i, 2 * hidden : 3 * hidden] = pm * qb * sb * (1.0 - sb)
        coef[i, 3 * hidden :] = pm * sb
        gate = jax.nn.sigmoid(dot(turned(zbar).astype(BF16), gate_t, ((1,), (1,))))
        gate_out[i] = gate
        du = (cot[i].astype(F32) * gate).astype(BF16)
        dy = dot(out_weight[...], du, ((1,), (1,)))
        dxh_out[pl.ds(i, hidden, stride=rows), :] = dy * norm_gain_b[...]
        return carry

    lax.fori_loop(0, rows, row, 0)


def channel_matrix(ref, at):
    n_row, n_col, _, rows, cols = ref.shape
    return jnp.concatenate(
        [ref[:, c, at].reshape(n_row * rows, cols) for c in range(n_col)], axis=1
    )


def put_channel(ref, at, values):
    n_row, n_col, _, rows, cols = ref.shape
    values = values.astype(BF16)
    for c in range(n_col):
        ref[:, c, at] = values[:, c * cols : (c + 1) * cols].reshape(n_row, rows, cols)


def product_kernel(both, out):
    share = out.shape[2]
    for h in range(share):
        put_channel(
            out, h,
            dot(channel_matrix(both, h), channel_matrix(both, share + h), ((1,), (1,))),
        )


def middle_kernel(product, dxh, out, xhat):
    hidden = product.shape[0]
    values = product[...].astype(F32)
    mean = jnp.sum(values, axis=0) * (1.0 / hidden)
    centred = values - mean[None]
    var = jnp.sum(centred * centred, axis=0) * (1.0 / hidden)
    inverse = lax.rsqrt(var + EPS)
    xhat[...] = centred * inverse[None]
    m1 = jnp.sum(dxh[...], axis=0) * (1.0 / hidden)
    m2 = jnp.sum(dxh[...] * xhat[...], axis=0) * (1.0 / hidden)
    out[...] = ((dxh[...] - m1[None] - xhat[...] * m2[None]) * inverse[None]).astype(BF16)


def update_kernel(
    product, gate, cot, norm_gain, norm_bias, out_weight, gate_weight,
    update, dzg, spread, norm_gain_b, norm_bias_b,
):
    hidden, rows, cols = product.shape
    norm_gain_b[...] = down_lanes(norm_gain[...], cols)
    norm_bias_b[...] = down_lanes(norm_bias[...], cols)
    spread[...] = product[...].astype(F32).reshape(hidden * rows, cols)

    def row(i, carry):
        xhat, _ = normalized(spread[pl.ds(i, hidden, stride=rows), :])
        ybar = (xhat * norm_gain_b[...] + norm_bias_b[...]).astype(BF16)
        u = dot(turned(ybar).astype(BF16), out_weight[...])
        g = gate[i]
        update[i] = (g * u).astype(BF16)
        dgp = (cot[i].astype(F32) * u * g * (1.0 - g)).astype(BF16)
        dzg[i] = dot(gate_weight[...], dgp, ((1,), (1,)))
        return carry

    lax.fori_loop(0, rows, row, 0)


def grads_kernel(both, grad, out):
    share = grad.shape[2]
    for h in range(share):
        g = channel_matrix(grad, h)
        put_channel(out, h, dot(g, channel_matrix(both, share + h)))
        put_channel(out, share + h, dot(g, channel_matrix(both, h), ((0,), (0,))))


def back_kernel(grads, coef, zhat, inv, dzg, gain, proj_weight, out, gain_b, left, right):
    rows, cols, width = out.shape
    n_dev, share2 = grads.shape[0], grads.shape[1]
    share = share2 // 2
    hidden = n_dev * share
    gain_b[...] = down_lanes(gain[...], cols)
    left[...] = grads[:, :share].astype(F32).reshape(hidden * rows, cols)
    right[...] = grads[:, share:].astype(F32).reshape(hidden * rows, cols)

    def row(i, carry):
        gl = left[pl.ds(i, hidden, stride=rows), :]
        gr = right[pl.ds(i, hidden, stride=rows), :]
        dproj = jnp.concatenate(
            [
                (gl * coef[i, :hidden]).astype(BF16),
                (gl * coef[i, hidden : 2 * hidden]).astype(BF16),
                (gr * coef[i, 2 * hidden : 3 * hidden]).astype(BF16),
                (gr * coef[i, 3 * hidden :]).astype(BF16),
            ],
            axis=0,
        )
        dzh = (dot(proj_weight[...], dproj) + dzg[i]) * gain_b[...]
        z = zhat[i]
        m1 = jnp.mean(dzh, axis=0, keepdims=True)
        m2 = jnp.mean(dzh * z, axis=0, keepdims=True)
        grad = ((dzh - m1 - z * m2) * inv[pl.ds(i, 1), :]).astype(BF16)
        out[i] = turned(grad).astype(BF16)
        return carry

    lax.fori_loop(0, rows, row, 0, unroll=2)


VMEM = pl.BlockSpec(memory_space=pltpu.VMEM)
SMEM = pl.BlockSpec(memory_space=pltpu.SMEM)


def call(kernel, outs, scratch, args, smem=(), flops=0, moved=0, limit=32):
    return pl.pallas_call(
        kernel,
        out_shape=outs,
        in_specs=[SMEM if at in smem else VMEM for at in range(len(args))],
        out_specs=jax.tree.map(lambda _: VMEM, outs),
        scratch_shapes=[pltpu.VMEM(shape, dtype) for shape, dtype in scratch],
        compiler_params=pltpu.CompilerParams(vmem_limit_bytes=limit * MIB),
        cost_estimate=pl.CostEstimate(flops=flops, bytes_accessed=moved, transcendentals=0),
    )(*args)


def body(
    pair, mask, gain_in, bias_in, proj_weight, gate_weight,
    product_norm_gain, product_norm_bias, out_weight, cotangent,
):
    rows, cols, width = pair.shape
    hidden = out_weight.shape[0]
    n_row = lax.axis_size("row")
    n_col = lax.axis_size("col")
    n_dev = n_row * n_col
    share = hidden // n_dev
    cells = rows * cols
    mask_v = mask.reshape(1, -1)

    def shape(*dims, dtype=BF16):
        return jax.ShapeDtypeStruct(dims, dtype)

    def exchange(values):
        return lax.all_to_all(values, ("row", "col"), split_axis=0, concat_axis=0, tiled=True)

    square = ((width, cols), F32)
    plane = ((hidden * rows, cols), F32)
    send = call(
        front_kernel,
        shape(n_dev, 2 * share, rows, cols),
        [square, square, plane, plane],
        (pair, mask, mask_v, gain_in, bias_in, proj_weight),
        smem=(1,),
        flops=2 * cells * width * 5 * hidden,
        moved=6 * cells * width,
    )
    both = exchange(send).reshape(n_row, n_col, 2 * share, rows, cols)
    coef, zhat, inv, gate, dxh = call(
        side_kernel,
        (
            shape(rows, 4 * hidden, cols, dtype=F32),
            shape(rows, width, cols, dtype=F32),
            shape(rows, cols, dtype=F32),
            shape(rows, cols, width, dtype=F32),
            shape(hidden * rows, cols, dtype=F32),
        ),
        [square, square, square],
        (
            pair, cotangent, mask, mask_v, gain_in, bias_in, proj_weight, gate_weight,
            product_norm_gain, out_weight,
        ),
        smem=(2,),
        flops=2 * cells * width * 8 * hidden,
        moved=32 * cells * width,
    )
    product = call(
        product_kernel,
        shape(n_row, n_col, share, rows, cols),
        [],
        (both,),
        flops=2 * share * (n_row * rows) ** 3,
        moved=6 * cells * hidden,
    )
    product = exchange(product.reshape(n_dev, share, rows, cols)).reshape(hidden, rows, cols)
    grad = call(
        middle_kernel,
        shape(hidden, rows, cols),
        [((hidden, rows, cols), F32)],
        (product, dxh.reshape(hidden, rows, cols)),
        flops=20 * cells * hidden,
        moved=8 * cells * hidden,
    )
    grad = exchange(grad.reshape(n_dev, share, rows, cols))
    update, dzg = call(
        update_kernel,
        (shape(rows, cols, width), shape(rows, width, cols, dtype=F32)),
        [plane, square, square],
        (
            product, gate, cotangent, product_norm_gain, product_norm_bias, out_weight,
            gate_weight,
        ),
        flops=2 * cells * width * 3 * hidden,
        moved=14 * cells * hidden,
    )
    grads = call(
        grads_kernel,
        shape(n_row, n_col, 2 * share, rows, cols),
        [],
        (both, grad.reshape(n_row, n_col, share, rows, cols)),
        flops=4 * share * (n_row * rows) ** 3,
        moved=10 * cells * hidden,
    )
    grads = exchange(grads.reshape(n_dev, 2 * share, rows, cols))
    grad_pair = call(
        back_kernel,
        shape(rows, cols, width),
        [square, plane, plane],
        (grads, coef, zhat, inv, dzg, gain_in, proj_weight),
        flops=2 * cells * width * 5 * hidden,
        moved=30 * cells * width,
    )
    return (update, grad_pair)


def solution(mesh):
    placed = (
        P(("grp", "row"), "col", None),
        P("grp"),
        P(),
        P(),
        P(),
        P(),
        P(),
        P(),
        P(),
        P(("grp", "row"), "col", None),
    )
    return jax.shard_map(
        body,
        mesh=mesh,
        in_specs=placed,
        out_specs=(P(("grp", "row"), "col", None), P(("grp", "row"), "col", None)),
        check_vma=False,
    )
```

```python
import math

import jax
import jax.numpy as jnp
from jax import lax
from jax.experimental import pallas as pl
from jax.experimental.pallas import tpu as pltpu
from jax.sharding import PartitionSpec as P

EPS = 1e-05
F32 = jnp.float32
BF16 = jnp.bfloat16
MIB = 1 << 20


def dot(a, b, over=((1,), (0,))):
    return lax.dot_general(a, b, (over, ((), ())), preferred_element_type=F32)


def eye(size):
    down = lax.broadcasted_iota(jnp.int32, (size, size), 0)
    across = lax.broadcasted_iota(jnp.int32, (size, size), 1)
    return (down == across).astype(F32).astype(BF16)


def turned(values):
    return dot(eye(values.shape[1]), values, ((1,), (1,)))


def down_lanes(vector, lanes):
    return jnp.broadcast_to(vector, (lanes, vector.shape[1])).T


def turned_weight(weight):
    c, m = weight.shape
    return jnp.concatenate(
        [turned(weight[:, at : at + c]) for at in range(0, m, c)], axis=0
    ).astype(BF16)


def sigmoid(values):
    return 0.5 + 0.5 * jnp.tanh(0.5 * values)


def normalized(values):
    mean = jnp.mean(values, axis=0, keepdims=True)
    centred = values - mean
    var = jnp.mean(centred * centred, axis=0, keepdims=True)
    inverse = lax.rsqrt(var + EPS)
    return centred * inverse, inverse


def start(sems, copies):
    running = [
        pltpu.make_async_copy(source, target, sems.at[at])
        for at, (source, target) in enumerate(copies)
    ]
    for copy in running:
        copy.start()
    return running


def wait(copies):
    for copy in copies:
        copy.wait()


def groups_of(rows):
    size = math.gcd(rows, 4)
    return [(at, size) for at in range(0, rows, size)]


def side_by_side(ref, at, size):
    return jnp.concatenate([ref[at + r] for r in range(size)], axis=1)


def pair_mask(mask_s, mask_v, at, size, rows, cols):
    first_row = lax.axis_index("row") * rows + at
    first_col = pl.multiple_of(lax.axis_index("col") * cols, cols)
    col_mask = mask_v[:, pl.ds(first_col, cols)].astype(F32)
    return jnp.concatenate(
        [col_mask * mask_s[first_row + r].astype(F32) for r in range(size)], axis=1
    )


def front_kernel(
    pair_h, mask_h, mask_row_h, gain_h, bias_h, proj_h, out,
    pair, mask_s, mask_v, gain, bias, proj_weight, left, right, sems, row_sems,
):
    rows, cols, width = pair.shape
    n_dev, share2 = out.shape[0], out.shape[1]
    share = share2 // 2
    hidden = n_dev * share
    groups = groups_of(rows)
    small = start(
        sems,
        [(gain_h, gain), (bias_h, bias), (proj_h, proj_weight), (mask_h, mask_s), (mask_row_h, mask_v)],
    )
    blocks = start(
        row_sems,
        [(pair_h.at[pl.ds(at, size)], pair.at[pl.ds(at, size)]) for at, size in groups],
    )
    wait(small)
    gain_b = jnp.concatenate([down_lanes(gain[...], cols)] * groups[0][1], axis=1)
    bias_b = jnp.concatenate([down_lanes(bias[...], cols)] * groups[0][1], axis=1)
    weight = turned_weight(proj_weight[...])
    for (at, size), block in zip(groups, blocks):
        block.wait()
        zhat, _ = normalized(turned(pair[at : at + size].reshape(size * cols, width)))
        zbar = (zhat * gain_b + bias_b).astype(BF16)
        pm = pair_mask(mask_s, mask_v, at, size, rows, cols)
        for part, target in ((0, left), (2, right)):
            p = dot(weight[part * hidden : (part + 1) * hidden], zbar)
            q = dot(weight[(part + 1) * hidden : (part + 2) * hidden], zbar)
            values = sigmoid(p) * q * pm
            for r in range(size):
                target[pl.ds(at + r, hidden, stride=rows), :] = values[:, r * cols : (r + 1) * cols]
    shape = (n_dev, share, rows, cols)
    out[:, :share] = left[...].reshape(shape).astype(BF16)
    out[:, share:] = right[...].reshape(shape).astype(BF16)


def side_kernel(
    pair_h, cot_h, mask_h, mask_row_h, gain_h, bias_h, proj_h, gate_h, norm_gain_h, out_w_h,
    coef_h, zhat_h, inv_h, gate_out_h, dxh_h,
    pair, cot, mask_s, mask_v, gain, bias, proj_weight, gate_weight, norm_gain, out_weight,
    coef, zhat_out, inv_out, gate_out, dxh_out, in_sems, out_sems,
):
    rows, cols, width = pair.shape
    hidden = out_weight.shape[0]
    wait(
        start(
            in_sems,
            [
                (pair_h, pair), (cot_h, cot), (mask_h, mask_s), (mask_row_h, mask_v),
                (gain_h, gain), (bias_h, bias), (proj_h, proj_weight), (gate_h, gate_weight),
                (norm_gain_h, norm_gain), (out_w_h, out_weight),
            ],
        )
    )
    groups = groups_of(rows)
    gain_b = jnp.concatenate([down_lanes(gain[...], cols)] * groups[0][1], axis=1)
    bias_b = jnp.concatenate([down_lanes(bias[...], cols)] * groups[0][1], axis=1)
    norm_gain_b = jnp.concatenate([down_lanes(norm_gain[...], cols)] * groups[0][1], axis=1)
    weight = turned_weight(proj_weight[...])
    gate_t = turned_weight(gate_weight[...])
    for at, size in groups:
        zhat, inverse = normalized(turned(pair[at : at + size].reshape(size * cols, width)))
        zbar = (zhat * gain_b + bias_b).astype(BF16)
        pm = pair_mask(mask_s, mask_v, at, size, rows, cols)
        gate = sigmoid(dot(gate_t, zbar))
        cot_t = turned(cot[at : at + size].reshape(size * cols, width))
        dxh = dot(out_weight[...], (cot_t * gate).astype(BF16)) * norm_gain_b
        dxh = dxh - jnp.mean(dxh, axis=0, keepdims=True)
        for r in range(size):
            lanes = slice(r * cols, (r + 1) * cols)
            zhat_out[at + r] = zhat[:, lanes]
            inv_out[at + r : at + r + 1] = inverse[:, lanes]
            gate_out[at + r] = gate[:, lanes]
            dxh_out[pl.ds(at + r, hidden, stride=rows), :] = dxh[:, lanes]
        for part in (0, 2):
            s = sigmoid(dot(weight[part * hidden : (part + 1) * hidden], zbar))
            q = dot(weight[(part + 1) * hidden : (part + 2) * hidden], zbar)
            first = pm * q * s * (1.0 - s)
            second = pm * s
            for r in range(size):
                lanes = slice(r * cols, (r + 1) * cols)
                coef[at + r, part * hidden : (part + 1) * hidden] = first[:, lanes]
                coef[at + r, (part + 1) * hidden : (part + 2) * hidden] = second[:, lanes]
    wait(
        start(
            out_sems,
            [
                (coef, coef_h), (zhat_out, zhat_h), (inv_out, inv_h), (gate_out, gate_out_h),
                (dxh_out, dxh_h),
            ],
        )
    )


def channel_matrix(ref, at):
    n_row, n_col, _, rows, cols = ref.shape
    return jnp.concatenate(
        [ref[:, c, at].reshape(n_row * rows, cols) for c in range(n_col)], axis=1
    )


def put_channel(ref, at, values):
    n_row, n_col, _, rows, cols = ref.shape
    values = values.astype(BF16)
    for c in range(n_col):
        ref[:, c, at] = values[:, c * cols : (c + 1) * cols].reshape(n_row, rows, cols)


def product_kernel(both, after, out):
    share = out.shape[2]
    for h in range(share):
        put_channel(
            out, h,
            dot(channel_matrix(both, h), channel_matrix(both, share + h), ((1,), (1,))),
        )


def middle_kernel(product, dxh_h, out, dxh, xhat, sems):
    hidden = product.shape[0]
    (copy,) = start(sems, [(dxh_h, dxh)])
    values = product[...].astype(F32)
    mean = jnp.sum(values, axis=0) * (1.0 / hidden)
    centred = values - mean[None]
    var = jnp.sum(centred * centred, axis=0) * (1.0 / hidden)
    inverse = lax.rsqrt(var + EPS)
    xhat[...] = centred * inverse[None]
    copy.wait()
    m2 = jnp.sum(dxh[...] * xhat[...], axis=0) * (1.0 / hidden)
    out[...] = ((dxh[...] - xhat[...] * m2[None]) * inverse[None]).astype(BF16)


def update_kernel(
    product, gate_h, cot_h, norm_gain_h, norm_bias_h, out_w_h, gate_w_h, update_h, dzg_h,
    gate, cot, norm_gain, norm_bias, out_weight, gate_weight, update, dzg, spread,
    in_sems, out_sems,
):
    hidden, rows, cols = product.shape
    width = cot.shape[2]
    copies = start(
        in_sems,
        [
            (gate_h, gate), (cot_h, cot), (norm_gain_h, norm_gain), (norm_bias_h, norm_bias),
            (out_w_h, out_weight), (gate_w_h, gate_weight),
        ],
    )
    spread[...] = product[...].astype(F32).reshape(hidden * rows, cols)
    wait(copies)
    groups = groups_of(rows)
    norm_gain_b = jnp.concatenate([down_lanes(norm_gain[...], cols)] * groups[0][1], axis=1)
    norm_bias_b = jnp.concatenate([down_lanes(norm_bias[...], cols)] * groups[0][1], axis=1)
    out_t = turned_weight(out_weight[...])
    for at, size in groups:
        xhat, _ = normalized(
            jnp.concatenate(
                [spread[pl.ds(at + r, hidden, stride=rows), :] for r in range(size)], axis=1
            )
        )
        ybar = (xhat * norm_gain_b + norm_bias_b).astype(BF16)
        u = dot(out_t, ybar)
        g = side_by_side(gate, at, size)
        done = (g * u).astype(BF16)
        cot_t = turned(cot[at : at + size].reshape(size * cols, width))
        back = dot(gate_weight[...], (cot_t * u * g * (1.0 - g)).astype(BF16))
        for r in range(size):
            lanes = slice(r * cols, (r + 1) * cols)
            update[at + r] = turned(done[:, lanes]).astype(BF16)
            dzg[at + r] = back[:, lanes]
    wait(start(out_sems, [(update, update_h), (dzg, dzg_h)]))


def grads_kernel(both, grad, out):
    share = grad.shape[2]
    for h in range(share):
        g = channel_matrix(grad, h)
        put_channel(out, h, dot(g, channel_matrix(both, share + h)))
        put_channel(out, share + h, dot(g, channel_matrix(both, h), ((0,), (0,))))


def back_kernel(
    grads, coef_h, zhat_h, inv_h, dzg_h, gain_h, proj_h, out_h,
    coef, zhat, inv, dzg, gain, proj_weight, out, left, right,
    sems, coef_sems, zhat_sems, dzg_sems, out_sems,
):
    rows, cols, width = out.shape
    n_dev, share2 = grads.shape[0], grads.shape[1]
    share = share2 // 2
    hidden = n_dev * share
    groups = groups_of(rows)

    def blocks_of(source, target):
        return [(source.at[pl.ds(at, size)], target.at[pl.ds(at, size)]) for at, size in groups]

    small = start(sems, [(gain_h, gain), (proj_h, proj_weight), (inv_h, inv)])
    blocks = [
        start(coef_sems, blocks_of(coef_h, coef)),
        start(zhat_sems, blocks_of(zhat_h, zhat)),
        start(dzg_sems, blocks_of(dzg_h, dzg)),
    ]
    left[...] = grads[:, :share].astype(F32).reshape(hidden * rows, cols)
    right[...] = grads[:, share:].astype(F32).reshape(hidden * rows, cols)
    wait(small)
    gain_b = jnp.concatenate([down_lanes(gain[...], cols)] * groups[0][1], axis=1)
    leaving = []
    for n, (at, size) in enumerate(groups):
        wait([copies[n] for copies in blocks])
        columns = []
        for r in range(size):
            gl = left[pl.ds(at + r, hidden, stride=rows), :]
            gr = right[pl.ds(at + r, hidden, stride=rows), :]
            columns.append(
                jnp.concatenate(
                    [
                        (g * coef[at + r, part * hidden : (part + 1) * hidden]).astype(BF16)
                        for part, g in enumerate((gl, gl, gr, gr))
                    ],
                    axis=0,
                )
            )
        dproj = jnp.concatenate(columns, axis=1)
        dzh = (dot(proj_weight[...], dproj) + side_by_side(dzg, at, size)) * gain_b
        z = side_by_side(zhat, at, size)
        inverse = jnp.concatenate([inv[at + r : at + r + 1] for r in range(size)], axis=1)
        m1 = jnp.mean(dzh, axis=0, keepdims=True)
        m2 = jnp.mean(dzh * z, axis=0, keepdims=True)
        grad = ((dzh - m1 - z * m2) * inverse).astype(BF16)
        for r in range(size):
            out[at + r] = turned(grad[:, r * cols : (r + 1) * cols]).astype(BF16)
        copy = pltpu.make_async_copy(
            out.at[pl.ds(at, size)], out_h.at[pl.ds(at, size)], out_sems.at[n]
        )
        copy.start()
        leaving.append(copy)
    wait(leaving)


def call(kernel, outs, scratch, args, near=(), outs_near=False, flops=0, moved=0, limit=24):
    here = pl.BlockSpec(memory_space=pltpu.VMEM)
    far = pl.BlockSpec(memory_space=pltpu.HBM)
    return pl.pallas_call(
        kernel,
        out_shape=outs if outs_near else jax.tree.map(lambda out: pltpu.HBM(out.shape, out.dtype), outs),
        in_specs=[here if at in near else far for at in range(len(args))],
        out_specs=jax.tree.map(lambda _: here if outs_near else far, outs),
        scratch_shapes=scratch,
        compiler_params=pltpu.CompilerParams(vmem_limit_bytes=limit * MIB),
        cost_estimate=pl.CostEstimate(flops=flops, bytes_accessed=moved, transcendentals=0),
    )(
        *[
            arg if at in near else pltpu.with_memory_space_constraint(arg, pltpu.HBM)
            for at, arg in enumerate(args)
        ]
    )


def body(
    pair, mask, gain_in, bias_in, proj_weight, gate_weight,
    product_norm_gain, product_norm_bias, out_weight, cotangent,
):
    rows, cols, width = pair.shape
    hidden = out_weight.shape[0]
    n_row = lax.axis_size("row")
    n_col = lax.axis_size("col")
    n_dev = n_row * n_col
    share = hidden // n_dev
    cells = rows * cols
    n_groups = len(groups_of(rows))
    mask_row = mask.reshape(1, -1)
    gain_in, bias_in = gain_in.reshape(1, -1), bias_in.reshape(1, -1)
    norm_gain, norm_bias = product_norm_gain.reshape(1, -1), product_norm_bias.reshape(1, -1)

    def shape(*dims, dtype=BF16):
        return jax.ShapeDtypeStruct(dims, dtype)

    def vmem(*dims, dtype=BF16):
        return pltpu.VMEM(dims, dtype)

    def sems(count):
        return pltpu.SemaphoreType.DMA((count,))

    def exchange(values):
        return lax.all_to_all(values, ("row", "col"), split_axis=0, concat_axis=0, tiled=True)

    mask_s = pltpu.SMEM(mask.shape, jnp.int32)
    mask_v = vmem(*mask_row.shape, dtype=jnp.int32)
    vector = vmem(1, width, dtype=F32)
    plane = vmem(hidden * rows, cols, dtype=F32)
    block = vmem(rows, cols, width)
    wide = vmem(rows, width, cols, dtype=F32)
    square = vmem(width, hidden)
    send = call(
        front_kernel,
        shape(n_dev, 2 * share, rows, cols),
        [
            block, mask_s, mask_v, vector, vector, vmem(width, 4 * hidden), plane, plane,
            sems(5), sems(n_groups),
        ],
        (pair, mask, mask_row, gain_in, bias_in, proj_weight),
        outs_near=True,
        flops=2 * cells * width * 5 * hidden,
        moved=6 * cells * width,
    )
    both = exchange(send).reshape(n_row, n_col, 2 * share, rows, cols)
    coef, zhat, inv, gate, dxh = call(
        side_kernel,
        (
            shape(rows, 4 * hidden, cols, dtype=F32),
            shape(rows, width, cols, dtype=F32),
            shape(rows, cols, dtype=F32),
            shape(rows, width, cols, dtype=F32),
            shape(hidden * rows, cols, dtype=F32),
        ),
        [
            block, block, mask_s, mask_v, vector, vector, vmem(width, 4 * hidden), square, vector,
            square, vmem(rows, 4 * hidden, cols, dtype=F32), wide, vmem(rows, cols, dtype=F32),
            wide, plane, sems(10), sems(5),
        ],
        (
            pair, cotangent, mask, mask_row, gain_in, bias_in, proj_weight, gate_weight,
            norm_gain, out_weight,
        ),
        flops=2 * cells * width * 8 * hidden,
        moved=32 * cells * width,
    )
    product = call(
        product_kernel,
        shape(n_row, n_col, share, rows, cols),
        [],
        (both, inv),
        near=(0,),
        outs_near=True,
        flops=2 * share * (n_row * rows) ** 3,
        moved=6 * cells * hidden,
    )
    product = exchange(product.reshape(n_dev, share, rows, cols)).reshape(hidden, rows, cols)
    spread = vmem(hidden, rows, cols, dtype=F32)
    grad = call(
        middle_kernel,
        shape(hidden, rows, cols),
        [spread, spread, sems(1)],
        (product, dxh.reshape(hidden, rows, cols)),
        near=(0,),
        outs_near=True,
        flops=20 * cells * hidden,
        moved=8 * cells * hidden,
    )
    grad = exchange(grad.reshape(n_dev, share, rows, cols))
    update, dzg = call(
        update_kernel,
        (shape(rows, cols, width), shape(rows, width, cols, dtype=F32)),
        [wide, block, vector, vector, square, square, block, wide, plane, sems(6), sems(2)],
        (product, gate, cotangent, norm_gain, norm_bias, out_weight, gate_weight),
        near=(0,),
        flops=2 * cells * width * 3 * hidden,
        moved=14 * cells * hidden,
    )
    grads = call(
        grads_kernel,
        shape(n_row, n_col, 2 * share, rows, cols),
        [],
        (both, grad.reshape(n_row, n_col, share, rows, cols)),
        near=(0, 1),
        outs_near=True,
        flops=4 * share * (n_row * rows) ** 3,
        moved=10 * cells * hidden,
    )
    grads = exchange(grads.reshape(n_dev, 2 * share, rows, cols))
    grad_pair = call(
        back_kernel,
        shape(rows, cols, width),
        [
            vmem(rows, 4 * hidden, cols, dtype=F32), wide, vmem(rows, cols, dtype=F32), wide,
            vector, vmem(width, 4 * hidden), block, plane, plane,
            sems(3), sems(n_groups), sems(n_groups), sems(n_groups), sems(n_groups),
        ],
        (grads, coef, zhat, inv, dzg, gain_in, proj_weight),
        near=(0,),
        flops=2 * cells * width * 5 * hidden,
        moved=30 * cells * width,
    )
    return (update, grad_pair)


def solution(mesh):
    placed = (
        P(("grp", "row"), "col", None),
        P("grp"),
        P(),
        P(),
        P(),
        P(),
        P(),
        P(),
        P(),
        P(("grp", "row"), "col", None),
    )
    return jax.shard_map(
        body,
        mesh=mesh,
        in_specs=placed,
        out_specs=(P(("grp", "row"), "col", None), P(("grp", "row"), "col", None)),
        check_vma=False,
    )
```

```python
import functools
import math

import jax
import jax.numpy as jnp
from jax import lax
from jax.experimental import pallas as pl
from jax.experimental.pallas import tpu as pltpu
from jax.sharding import PartitionSpec as P

EPS = 1e-05
F32 = jnp.float32
BF16 = jnp.bfloat16
MIB = 1 << 20


def dot(a, b, over=((1,), (0,))):
    return lax.dot_general(a, b, (over, ((), ())), preferred_element_type=F32)


def eye(size):
    down = lax.broadcasted_iota(jnp.int32, (size, size), 0)
    across = lax.broadcasted_iota(jnp.int32, (size, size), 1)
    return (down == across).astype(F32).astype(BF16)


def turned(values):
    return dot(eye(values.shape[1]), values, ((1,), (1,)))


def down_lanes(vector, lanes):
    return jnp.broadcast_to(vector, (lanes, vector.shape[1])).T


def turned_weight(weight):
    c, m = weight.shape
    return jnp.concatenate(
        [turned(weight[:, at : at + c]) for at in range(0, m, c)], axis=0
    ).astype(BF16)


def sigmoid(values):
    return 0.5 + 0.5 * jnp.tanh(0.5 * values)


def normalized(values):
    mean = jnp.mean(values, axis=0, keepdims=True)
    centred = values - mean
    var = jnp.mean(centred * centred, axis=0, keepdims=True)
    inverse = lax.rsqrt(var + EPS)
    return centred * inverse, inverse


def start(sems, copies):
    running = [
        pltpu.make_async_copy(source, target, sems.at[at])
        for at, (source, target) in enumerate(copies)
    ]
    for copy in running:
        copy.start()
    return running


def wait(copies):
    for copy in copies:
        copy.wait()


def groups_of(rows):
    size = math.gcd(rows, 4)
    return [(at, size) for at in range(0, rows, size)]


def side_by_side(ref, at, size):
    return jnp.concatenate([ref[at + r] for r in range(size)], axis=1)


def pair_mask(mask_s, mask_v, at, size, rows, cols):
    first_row = (lax.axis_index("half") * lax.axis_size("row") + lax.axis_index("row")) * rows + at
    first_col = pl.multiple_of(lax.axis_index("col") * cols, cols)
    col_mask = mask_v[:, pl.ds(first_col, cols)].astype(F32)
    return jnp.concatenate(
        [col_mask * mask_s[first_row + r].astype(F32) for r in range(size)], axis=1
    )


def place():
    return lax.axis_index("row") * lax.axis_size("col") + lax.axis_index("col")


def front_kernel(
    part, n_out, pair_h, mask_h, mask_row_h, gain_h, bias_h, proj_h, *refs
):
    outs = refs[:n_out]
    pair, mask_s, mask_v, gain, bias, proj_weight, plane, sems, row_sems = refs[n_out:]
    rows, cols, width = pair.shape
    hidden = plane.shape[0] // rows
    groups = groups_of(rows)
    small = start(
        sems,
        [(gain_h, gain), (bias_h, bias), (proj_h, proj_weight), (mask_h, mask_s), (mask_row_h, mask_v)],
    )
    blocks = start(
        row_sems,
        [(pair_h.at[pl.ds(at, size)], pair.at[pl.ds(at, size)]) for at, size in groups],
    )
    wait(small)
    gain_b = jnp.concatenate([down_lanes(gain[...], cols)] * groups[0][1], axis=1)
    bias_b = jnp.concatenate([down_lanes(bias[...], cols)] * groups[0][1], axis=1)
    weight = turned_weight(proj_weight[:, part * hidden : (part + 2) * hidden])
    for (at, size), block in zip(groups, blocks):
        block.wait()
        zhat, _ = normalized(turned(pair[at : at + size].reshape(size * cols, width)))
        zbar = (zhat * gain_b + bias_b).astype(BF16)
        pm = pair_mask(mask_s, mask_v, at, size, rows, cols)
        values = sigmoid(dot(weight[:hidden], zbar)) * dot(weight[hidden:], zbar) * pm
        for r in range(size):
            plane[pl.ds(at + r, hidden, stride=rows), :] = values[:, r * cols : (r + 1) * cols]
    if n_out == 1:
        values = plane[...].reshape(outs[0].shape[1:]).astype(BF16)
        for half in range(outs[0].shape[0]):
            outs[0][half] = values
    else:
        give_pieces(plane, outs)


def give_pieces(plane, outs):
    here = place()
    length = plane.shape[0] // len(outs)
    for m, out in enumerate(outs):
        first = pl.multiple_of((here ^ m) * length, length)
        out[...] = plane[pl.ds(first, length), :].reshape(out.shape).astype(BF16)


def side_kernel(
    pair_h, cot_h, mask_h, mask_row_h, gain_h, bias_h, proj_h, gate_h, norm_gain_h, out_w_h,
    coef_h, zhat_h, inv_h, gate_out_h, dxh_h,
    pair, cot, mask_s, mask_v, gain, bias, proj_weight, gate_weight, norm_gain, out_weight,
    coef, zhat_out, inv_out, gate_out, dxh_out, in_sems, out_sems,
):
    rows, cols, width = pair.shape
    hidden = out_weight.shape[0]
    wait(
        start(
            in_sems,
            [
                (pair_h, pair), (cot_h, cot), (mask_h, mask_s), (mask_row_h, mask_v),
                (gain_h, gain), (bias_h, bias), (proj_h, proj_weight), (gate_h, gate_weight),
                (norm_gain_h, norm_gain), (out_w_h, out_weight),
            ],
        )
    )
    groups = groups_of(rows)
    gain_b = jnp.concatenate([down_lanes(gain[...], cols)] * groups[0][1], axis=1)
    bias_b = jnp.concatenate([down_lanes(bias[...], cols)] * groups[0][1], axis=1)
    norm_gain_b = jnp.concatenate([down_lanes(norm_gain[...], cols)] * groups[0][1], axis=1)
    weight = turned_weight(proj_weight[...])
    gate_t = turned_weight(gate_weight[...])
    for at, size in groups:
        zhat, inverse = normalized(turned(pair[at : at + size].reshape(size * cols, width)))
        zbar = (zhat * gain_b + bias_b).astype(BF16)
        pm = pair_mask(mask_s, mask_v, at, size, rows, cols)
        gate = sigmoid(dot(gate_t, zbar))
        cot_t = turned(cot[at : at + size].reshape(size * cols, width))
        dxh = dot(out_weight[...], (cot_t * gate).astype(BF16)) * norm_gain_b
        dxh = dxh - jnp.mean(dxh, axis=0, keepdims=True)
        for r in range(size):
            lanes = slice(r * cols, (r + 1) * cols)
            zhat_out[at + r] = zhat[:, lanes]
            inv_out[at + r : at + r + 1] = inverse[:, lanes]
            gate_out[at + r] = gate[:, lanes]
            dxh_out[pl.ds(at + r, hidden, stride=rows), :] = dxh[:, lanes]
        for part in (0, 2):
            s = sigmoid(dot(weight[part * hidden : (part + 1) * hidden], zbar))
            q = dot(weight[(part + 1) * hidden : (part + 2) * hidden], zbar)
            first = pm * q * s * (1.0 - s)
            second = pm * s
            for r in range(size):
                lanes = slice(r * cols, (r + 1) * cols)
                coef[at + r, part] = first[:, lanes]
                coef[at + r, part + 1] = second[:, lanes]
    wait(
        start(
            out_sems,
            [
                (coef, coef_h), (zhat_out, zhat_h), (inv_out, inv_h), (gate_out, gate_out_h),
                (dxh_out, dxh_h),
            ],
        )
    )


def channel_matrix(ref, at):
    *_, n_col, _, rows, cols = ref.shape
    lead = (slice(None),) * (len(ref.shape) - 4)
    return jnp.concatenate(
        [ref[(*lead, c, at)].reshape(-1, cols) for c in range(n_col)], axis=1
    )


def put_channel(ref, at, values):
    *shape, n_col, _, rows, cols = ref.shape
    lead = (slice(None),) * len(shape)
    values = values.astype(BF16)
    for c in range(n_col):
        ref[(*lead, c, at)] = values[:, c * cols : (c + 1) * cols].reshape(*shape, rows, cols)


def product_kernel(right, after, *refs):
    pieces, (out, left) = refs[:-2], refs[-2:]
    here = place()
    n_col, share = left.shape[1:3]
    for m, piece in enumerate(pieces):
        source = here ^ m
        left[source // n_col, source % n_col] = piece[...]
    for h in range(share):
        put_channel(out, h, dot(channel_matrix(left, h), channel_matrix(right, h), ((1,), (1,))))


def middle_kernel(product, dxh_h, out, dxh, xhat, sems):
    hidden = product.shape[0]
    (copy,) = start(sems, [(dxh_h, dxh)])
    values = product[...].astype(F32)
    mean = jnp.sum(values, axis=0) * (1.0 / hidden)
    centred = values - mean[None]
    var = jnp.sum(centred * centred, axis=0) * (1.0 / hidden)
    inverse = lax.rsqrt(var + EPS)
    xhat[...] = centred * inverse[None]
    copy.wait()
    m2 = jnp.sum(dxh[...] * xhat[...], axis=0) * (1.0 / hidden)
    out[...] = ((dxh[...] - xhat[...] * m2[None]) * inverse[None]).astype(BF16)


def update_kernel(
    product, gate_h, cot_h, norm_gain_h, norm_bias_h, out_w_h, gate_w_h, update_h, dzg_h,
    gate, cot, norm_gain, norm_bias, out_weight, gate_weight, update, dzg, spread,
    in_sems, out_sems,
):
    hidden, rows, cols = product.shape
    width = cot.shape[2]
    copies = start(
        in_sems,
        [
            (gate_h, gate), (cot_h, cot), (norm_gain_h, norm_gain), (norm_bias_h, norm_bias),
            (out_w_h, out_weight), (gate_w_h, gate_weight),
        ],
    )
    spread[...] = product[...].astype(F32).reshape(hidden * rows, cols)
    wait(copies)
    groups = groups_of(rows)
    norm_gain_b = jnp.concatenate([down_lanes(norm_gain[...], cols)] * groups[0][1], axis=1)
    norm_bias_b = jnp.concatenate([down_lanes(norm_bias[...], cols)] * groups[0][1], axis=1)
    out_t = turned_weight(out_weight[...])
    for at, size in groups:
        xhat, _ = normalized(
            jnp.concatenate(
                [spread[pl.ds(at + r, hidden, stride=rows), :] for r in range(size)], axis=1
            )
        )
        ybar = (xhat * norm_gain_b + norm_bias_b).astype(BF16)
        u = dot(out_t, ybar)
        g = side_by_side(gate, at, size)
        done = (g * u).astype(BF16)
        cot_t = turned(cot[at : at + size].reshape(size * cols, width))
        back = dot(gate_weight[...], (cot_t * u * g * (1.0 - g)).astype(BF16))
        for r in range(size):
            lanes = slice(r * cols, (r + 1) * cols)
            update[at + r] = turned(done[:, lanes]).astype(BF16)
            dzg[at + r] = back[:, lanes]
    wait(start(out_sems, [(update, update_h), (dzg, dzg_h)]))


def grad_right_kernel(grad, left, out):
    for h in range(out.shape[-3]):
        put_channel(out, h, dot(channel_matrix(grad, h), channel_matrix(left, h), ((0,), (0,))))


def grad_left_kernel(grad, right, *refs):
    outs, ready = refs[:-1], refs[-1]
    here = place()
    n_col, share = ready.shape[1:3]
    for h in range(share):
        put_channel(ready, h, dot(channel_matrix(grad, h), channel_matrix(right, h)))
    for m, out in enumerate(outs):
        target = here ^ m
        out[...] = ready[target // n_col, target % n_col]


def through_projection(plane, coef, weight, at, size, rows):
    hidden = plane.shape[0] // rows
    columns = []
    for r in range(size):
        g = plane[pl.ds(at + r, hidden, stride=rows), :]
        columns.append(
            jnp.concatenate(
                [(g * coef[at + r, part]).astype(BF16) for part in range(2)], axis=0
            )
        )
    return dot(weight, jnp.concatenate(columns, axis=1))


def back_left_kernel(coef_h, dzg_h, proj_h, *refs):
    pieces, out_h = refs[:-9], refs[-9]
    coef, dzg, proj_weight, out, plane, sems, coef_sems, dzg_sems = refs[-8:]
    rows, width, cols = out.shape
    hidden = plane.shape[0] // rows
    groups = groups_of(rows)
    small = start(sems, [(proj_h, proj_weight)])
    blocks = [
        start(
            coef_sems,
            [
                (coef_h.at[pl.ds(at, size), pl.ds(0, 2)], coef.at[pl.ds(at, size)])
                for at, size in groups
            ],
        ),
        start(
            dzg_sems,
            [(dzg_h.at[pl.ds(at, size)], dzg.at[pl.ds(at, size)]) for at, size in groups],
        ),
    ]
    here = place()
    length = plane.shape[0] // len(pieces)
    for m, piece in enumerate(pieces):
        first = pl.multiple_of((here ^ m) * length, length)
        plane[pl.ds(first, length), :] = piece[...].astype(F32).reshape(length, cols)
    wait(small)
    weight = proj_weight[:, : 2 * hidden]
    for n, (at, size) in enumerate(groups):
        wait([copies[n] for copies in blocks])
        back = through_projection(plane, coef, weight, at, size, rows)
        for r in range(size):
            out[at + r] = back[:, r * cols : (r + 1) * cols] + dzg[at + r]
    wait(start(sems, [(out, out_h)]))


def back_kernel(
    grads, coef_h, zhat_h, inv_h, dzg_h, gain_h, proj_h, out_h,
    coef, zhat, inv, dzg, gain, proj_weight, out, plane,
    sems, coef_sems, zhat_sems, dzg_sems, out_sems,
):
    rows, cols, width = out.shape
    hidden = plane.shape[0] // rows
    groups = groups_of(rows)

    def blocks_of(source, target):
        return [(source.at[pl.ds(at, size)], target.at[pl.ds(at, size)]) for at, size in groups]

    small = start(sems, [(gain_h, gain), (proj_h, proj_weight), (inv_h, inv)])
    blocks = [
        start(
            coef_sems,
            [
                (coef_h.at[pl.ds(at, size), pl.ds(2, 2)], coef.at[pl.ds(at, size)])
                for at, size in groups
            ],
        ),
        start(zhat_sems, blocks_of(zhat_h, zhat)),
        start(dzg_sems, blocks_of(dzg_h, dzg)),
    ]
    total = grads[0].astype(F32)
    for half in range(1, grads.shape[0]):
        total = total + grads[half].astype(F32)
    plane[...] = total.reshape(plane.shape)
    wait(small)
    gain_b = jnp.concatenate([down_lanes(gain[...], cols)] * groups[0][1], axis=1)
    weight = proj_weight[:, 2 * hidden :]
    leaving = []
    for n, (at, size) in enumerate(groups):
        wait([copies[n] for copies in blocks])
        back = through_projection(plane, coef, weight, at, size, rows)
        dzh = (back + side_by_side(dzg, at, size)) * gain_b
        z = side_by_side(zhat, at, size)
        inverse = jnp.concatenate([inv[at + r : at + r + 1] for r in range(size)], axis=1)
        m1 = jnp.mean(dzh, axis=0, keepdims=True)
        m2 = jnp.mean(dzh * z, axis=0, keepdims=True)
        grad = ((dzh - m1 - z * m2) * inverse).astype(BF16)
        for r in range(size):
            out[at + r] = turned(grad[:, r * cols : (r + 1) * cols]).astype(BF16)
        copy = pltpu.make_async_copy(
            out.at[pl.ds(at, size)], out_h.at[pl.ds(at, size)], out_sems.at[n]
        )
        copy.start()
        leaving.append(copy)
    wait(leaving)


def call(kernel, outs, scratch, args, near=(), outs_near=False, flops=0, moved=0, limit=24):
    here = pl.BlockSpec(memory_space=pltpu.VMEM)
    far = pl.BlockSpec(memory_space=pltpu.HBM)
    return pl.pallas_call(
        kernel,
        out_shape=outs if outs_near else jax.tree.map(lambda out: pltpu.HBM(out.shape, out.dtype), outs),
        in_specs=[here if at in near else far for at in range(len(args))],
        out_specs=jax.tree.map(lambda _: here if outs_near else far, outs),
        scratch_shapes=scratch,
        compiler_params=pltpu.CompilerParams(vmem_limit_bytes=limit * MIB),
        cost_estimate=pl.CostEstimate(flops=flops, bytes_accessed=moved, transcendentals=0),
    )(
        *[
            arg if at in near else pltpu.with_memory_space_constraint(arg, pltpu.HBM)
            for at, arg in enumerate(args)
        ]
    )


def body(
    pair, mask, gain_in, bias_in, proj_weight, gate_weight,
    product_norm_gain, product_norm_bias, out_weight, cotangent,
):
    rows, cols, width = pair.shape
    hidden = out_weight.shape[0]
    n_half = lax.axis_size("half")
    n_row = lax.axis_size("row")
    n_col = lax.axis_size("col")
    n_place = n_row * n_col
    share = hidden // n_place
    cells = rows * cols
    n_groups = len(groups_of(rows))
    mask_row = mask.reshape(1, -1)
    gain_in, bias_in = gain_in.reshape(1, -1), bias_in.reshape(1, -1)
    norm_gain, norm_bias = product_norm_gain.reshape(1, -1), product_norm_bias.reshape(1, -1)

    def shape(*dims, dtype=BF16):
        return jax.ShapeDtypeStruct(dims, dtype)

    def vmem(*dims, dtype=BF16):
        return pltpu.VMEM(dims, dtype)

    def sems(count):
        return pltpu.SemaphoreType.DMA((count,))

    def exchange(values):
        return lax.all_to_all(values, ("row", "col"), split_axis=0, concat_axis=0, tiled=True)

    def exchange_all(values):
        flat = values.reshape(n_half * n_place, share, rows, cols)
        return lax.all_to_all(
            flat, ("half", "row", "col"), split_axis=0, concat_axis=0, tiled=True
        )

    def exchange_pieces(pieces):
        return pieces[:1] + tuple(
            lax.ppermute(piece, ("row", "col"), [(at, at ^ m) for at in range(n_place)])
            for m, piece in enumerate(pieces[1:], 1)
        )

    mask_s = pltpu.SMEM(mask.shape, jnp.int32)
    mask_v = vmem(*mask_row.shape, dtype=jnp.int32)
    vector = vmem(1, width, dtype=F32)
    plane = vmem(hidden * rows, cols, dtype=F32)
    block = vmem(rows, cols, width)
    wide = vmem(rows, width, cols, dtype=F32)
    square = vmem(width, hidden)
    proj_v = vmem(width, 4 * hidden)
    coef_v = vmem(rows, 2, hidden, cols, dtype=F32)
    pieces_shape = (shape(share, rows, cols),) * n_place

    def front(part, outs):
        return call(
            functools.partial(front_kernel, part, len(outs)),
            outs,
            [block, mask_s, mask_v, vector, vector, proj_v, plane, sems(5), sems(n_groups)],
            (pair, mask, mask_row, gain_in, bias_in, proj_weight),
            outs_near=True,
            flops=2 * cells * width * 3 * hidden,
            moved=5 * cells * width,
        )

    (right,) = front(2, (shape(n_half, n_place, share, rows, cols),))
    right = exchange_all(right).reshape(n_half, n_row, n_col, share, rows, cols)
    left = exchange_pieces(tuple(front(0, pieces_shape)))
    coef, zhat, inv, gate, dxh = call(
        side_kernel,
        (
            shape(rows, 4, hidden, cols, dtype=F32),
            shape(rows, width, cols, dtype=F32),
            shape(rows, cols, dtype=F32),
            shape(rows, width, cols, dtype=F32),
            shape(hidden * rows, cols, dtype=F32),
        ),
        [
            block, block, mask_s, mask_v, vector, vector, proj_v, square, vector,
            square, vmem(rows, 4, hidden, cols, dtype=F32), wide, vmem(rows, cols, dtype=F32),
            wide, plane, sems(10), sems(5),
        ],
        (
            pair, cotangent, mask, mask_row, gain_in, bias_in, proj_weight, gate_weight,
            norm_gain, out_weight,
        ),
        flops=2 * cells * width * 8 * hidden,
        moved=32 * cells * width,
    )
    product, left = call(
        product_kernel,
        (shape(n_row, n_col, share, rows, cols), shape(n_row, n_col, share, rows, cols)),
        [],
        (right, inv, *left),
        near=(0, *range(2, 2 + n_place)),
        outs_near=True,
        flops=2 * share * n_half * (n_row * rows) ** 2 * n_col * cols,
        moved=8 * cells * hidden,
    )
    product = exchange(product.reshape(n_place, share, rows, cols)).reshape(hidden, rows, cols)
    spread = vmem(hidden, rows, cols, dtype=F32)
    grad = call(
        middle_kernel,
        shape(hidden, rows, cols),
        [spread, spread, sems(1)],
        (product, dxh.reshape(hidden, rows, cols)),
        near=(0,),
        outs_near=True,
        flops=20 * cells * hidden,
        moved=8 * cells * hidden,
    )
    grad = exchange(grad.reshape(n_place, share, rows, cols))
    grad = grad.reshape(n_row, n_col, share, rows, cols)
    update, dzg = call(
        update_kernel,
        (shape(rows, cols, width), shape(rows, width, cols, dtype=F32)),
        [wide, block, vector, vector, square, square, block, wide, plane, sems(6), sems(2)],
        (product, gate, cotangent, norm_gain, norm_bias, out_weight, gate_weight),
        near=(0,),
        flops=2 * cells * width * 3 * hidden,
        moved=14 * cells * hidden,
    )
    grad_right = call(
        grad_right_kernel,
        shape(n_half, n_row, n_col, share, rows, cols),
        [],
        (grad, left),
        near=(0, 1),
        outs_near=True,
        flops=2 * share * n_half * (n_row * rows) ** 2 * n_col * cols,
        moved=8 * cells * hidden,
    )
    grad_right = exchange_all(grad_right).reshape(n_half, n_place, share, rows, cols)
    grad_left = call(
        grad_left_kernel,
        pieces_shape,
        [vmem(n_row, n_col, share, rows, cols)],
        (grad, right),
        near=(0, 1),
        outs_near=True,
        flops=2 * share * n_half * (n_row * rows) ** 2 * n_col * cols,
        moved=8 * cells * hidden,
    )
    grad_left = exchange_pieces(tuple(grad_left))
    dzg = call(
        back_left_kernel,
        shape(rows, width, cols, dtype=F32),
        [coef_v, wide, proj_v, wide, plane, sems(1), sems(n_groups), sems(n_groups)],
        (coef, dzg, proj_weight, *grad_left),
        near=tuple(range(3, 3 + n_place)),
        flops=2 * cells * width * 2 * hidden,
        moved=18 * cells * width,
    )
    grad_pair = call(
        back_kernel,
        shape(rows, cols, width),
        [
            coef_v, wide, vmem(rows, cols, dtype=F32), wide, vector, proj_v, block, plane,
            sems(3), sems(n_groups), sems(n_groups), sems(n_groups), sems(n_groups),
        ],
        (grad_right, coef, zhat, inv, dzg, gain_in, proj_weight),
        near=(0,),
        flops=2 * cells * width * 3 * hidden,
        moved=22 * cells * width,
    )
    return (update, grad_pair)


def solution(mesh):
    n_grp, n_row, n_col = (mesh.shape[name] for name in ("grp", "row", "col"))
    n_half = math.gcd(n_row, 2)
    split = jax.sharding.Mesh(
        mesh.devices.reshape(n_grp, n_half, n_row // n_half, n_col), ("grp", "half", "row", "col")
    )
    cells = P(("grp", "half", "row"), "col", None)
    return jax.shard_map(
        body,
        mesh=split,
        in_specs=(cells, P("grp"), P(), P(), P(), P(), P(), P(), P(), cells),
        out_specs=(cells, cells),
        check_vma=False,
    )
```

```python
import functools
import math

import jax
import jax.numpy as jnp
from jax import lax
from jax.experimental import pallas as pl
from jax.experimental.pallas import tpu as pltpu
from jax.sharding import PartitionSpec as P

EPS = 1e-05
F32 = jnp.float32
BF16 = jnp.bfloat16
MIB = 1 << 20


def dot(a, b, over=((1,), (0,))):
    return lax.dot_general(a, b, (over, ((), ())), preferred_element_type=F32)


def eye(size):
    down = lax.broadcasted_iota(jnp.int32, (size, size), 0)
    across = lax.broadcasted_iota(jnp.int32, (size, size), 1)
    return (down == across).astype(F32).astype(BF16)


def turned(values):
    return dot(eye(values.shape[1]), values, ((1,), (1,)))


def down_lanes(vector, lanes):
    return jnp.broadcast_to(vector, (lanes, vector.shape[1])).T


def turned_weight(weight):
    c, m = weight.shape
    return jnp.concatenate(
        [turned(weight[:, at : at + c]) for at in range(0, m, c)], axis=0
    ).astype(BF16)


def sigmoid(values):
    return 0.5 + 0.5 * jnp.tanh(0.5 * values)


def normalized(values):
    mean = jnp.mean(values, axis=0, keepdims=True)
    centred = values - mean
    var = jnp.mean(centred * centred, axis=0, keepdims=True)
    inverse = lax.rsqrt(var + EPS)
    return centred * inverse, inverse


def start(sems, copies):
    running = [
        pltpu.make_async_copy(source, target, sems.at[at])
        for at, (source, target) in enumerate(copies)
    ]
    for copy in running:
        copy.start()
    return running


def wait(copies):
    for copy in copies:
        copy.wait()


def groups_of(rows):
    size = math.gcd(rows, 4)
    return [(at, size) for at in range(0, rows, size)]


def side_by_side(ref, at, size):
    return jnp.concatenate([ref[at + r] for r in range(size)], axis=1)


def pair_mask(mask_s, mask_v, at, size, rows, cols):
    here = lax.axis_index("half")
    for name in ("row", "core"):
        here = here * lax.axis_size(name) + lax.axis_index(name)
    first_row = here * rows + at
    first_col = pl.multiple_of(lax.axis_index("col") * cols, cols)
    col_mask = mask_v[:, pl.ds(first_col, cols)].astype(F32)
    return jnp.concatenate(
        [col_mask * mask_s[first_row + r].astype(F32) for r in range(size)], axis=1
    )


def sources(n_row, n_quad):
    row = lax.axis_index("row")
    quad = lax.axis_index("core") * lax.axis_size("col") + lax.axis_index("col")
    return [(m, n, (row ^ n) * n_quad + (quad ^ m)) for m in range(n_quad) for n in range(n_row)]


def received(refs, n_row):
    n_quad = len(refs) - n_row + 1
    return [
        (number, refs[m][0] if n == 0 else refs[n_quad + n - 1][m])
        for m, n, number in sources(n_row, n_quad)
    ]


def front_kernel(
    part, n_out, pair_h, mask_h, mask_row_h, gain_h, bias_h, proj_h, *refs
):
    outs = refs[:n_out]
    pair, mask_s, mask_v, gain, bias, proj_weight, plane, sems, row_sems = refs[n_out:]
    rows, cols, width = pair.shape
    hidden = plane.shape[0] // rows
    groups = groups_of(rows)
    small = start(
        sems,
        [(gain_h, gain), (bias_h, bias), (proj_h, proj_weight), (mask_h, mask_s), (mask_row_h, mask_v)],
    )
    blocks = start(
        row_sems,
        [(pair_h.at[pl.ds(at, size)], pair.at[pl.ds(at, size)]) for at, size in groups],
    )
    wait(small)
    gain_b = jnp.concatenate([down_lanes(gain[...], cols)] * groups[0][1], axis=1)
    bias_b = jnp.concatenate([down_lanes(bias[...], cols)] * groups[0][1], axis=1)
    weight = turned_weight(proj_weight[:, part * hidden : (part + 2) * hidden])
    for (at, size), block in zip(groups, blocks):
        block.wait()
        zhat, _ = normalized(turned(pair[at : at + size].reshape(size * cols, width)))
        zbar = (zhat * gain_b + bias_b).astype(BF16)
        pm = pair_mask(mask_s, mask_v, at, size, rows, cols)
        values = sigmoid(dot(weight[:hidden], zbar)) * dot(weight[hidden:], zbar) * pm
        for r in range(size):
            plane[pl.ds(at + r, hidden, stride=rows), :] = values[:, r * cols : (r + 1) * cols]
    if n_out == 1:
        values = plane[...].reshape(outs[0].shape[1:]).astype(BF16)
        for half in range(outs[0].shape[0]):
            outs[0][half] = values
    else:
        give_pieces(plane, outs)


def give_pieces(plane, outs):
    n_row = outs[0].shape[0]
    length = plane.shape[0] // (len(outs) * n_row)
    for m, n, number in sources(n_row, len(outs)):
        first = pl.multiple_of(number * length, length)
        values = plane[pl.ds(first, length), :]
        outs[m][n] = values.reshape(outs[m].shape[1:]).astype(BF16)


def side_kernel(
    pair_h, cot_h, gain_h, bias_h, gate_h, norm_gain_h, out_w_h,
    zhat_h, inv_h, gate_out_h, dxh_h,
    pair, cot, gain, bias, gate_weight, norm_gain, out_weight,
    zhat_out, inv_out, gate_out, dxh_out, in_sems, out_sems,
):
    rows, cols, width = pair.shape
    hidden = out_weight.shape[0]
    wait(
        start(
            in_sems,
            [
                (pair_h, pair), (cot_h, cot), (gain_h, gain), (bias_h, bias),
                (gate_h, gate_weight), (norm_gain_h, norm_gain), (out_w_h, out_weight),
            ],
        )
    )
    groups = groups_of(rows)
    gain_b = jnp.concatenate([down_lanes(gain[...], cols)] * groups[0][1], axis=1)
    bias_b = jnp.concatenate([down_lanes(bias[...], cols)] * groups[0][1], axis=1)
    norm_gain_b = jnp.concatenate([down_lanes(norm_gain[...], cols)] * groups[0][1], axis=1)
    gate_t = turned_weight(gate_weight[...])
    for at, size in groups:
        zhat, inverse = normalized(turned(pair[at : at + size].reshape(size * cols, width)))
        zbar = (zhat * gain_b + bias_b).astype(BF16)
        gate = sigmoid(dot(gate_t, zbar))
        cot_t = turned(cot[at : at + size].reshape(size * cols, width))
        dxh = dot(out_weight[...], (cot_t * gate).astype(BF16)) * norm_gain_b
        dxh = dxh - jnp.mean(dxh, axis=0, keepdims=True)
        for r in range(size):
            lanes = slice(r * cols, (r + 1) * cols)
            zhat_out[at + r] = zhat[:, lanes]
            inv_out[at + r : at + r + 1] = inverse[:, lanes]
            gate_out[at + r] = gate[:, lanes]
            dxh_out[pl.ds(at + r, hidden, stride=rows), :] = dxh[:, lanes]
    wait(
        start(
            out_sems,
            [(zhat_out, zhat_h), (inv_out, inv_h), (gate_out, gate_out_h), (dxh_out, dxh_h)],
        )
    )


def factors_kernel(
    zhat_h, mask_h, mask_row_h, gain_h, bias_h, proj_h, after, coef_h,
    zhat, mask_s, mask_v, gain, bias, proj_weight, coef, in_sems, out_sems,
):
    rows, width, cols = zhat.shape
    hidden = coef.shape[2]
    wait(
        start(
            in_sems,
            [
                (zhat_h, zhat), (mask_h, mask_s), (mask_row_h, mask_v), (gain_h, gain),
                (bias_h, bias), (proj_h, proj_weight),
            ],
        )
    )
    groups = groups_of(rows)
    gain_b = jnp.concatenate([down_lanes(gain[...], cols)] * groups[0][1], axis=1)
    bias_b = jnp.concatenate([down_lanes(bias[...], cols)] * groups[0][1], axis=1)
    weight = turned_weight(proj_weight[...])
    leaving = []
    for n, (at, size) in enumerate(groups):
        zbar = (side_by_side(zhat, at, size) * gain_b + bias_b).astype(BF16)
        pm = pair_mask(mask_s, mask_v, at, size, rows, cols)
        for part in (0, 2):
            s = sigmoid(dot(weight[part * hidden : (part + 1) * hidden], zbar))
            q = dot(weight[(part + 1) * hidden : (part + 2) * hidden], zbar)
            second = pm * s
            first = second * q * (1.0 - s)
            for r in range(size):
                lanes = slice(r * cols, (r + 1) * cols)
                coef[at + r, part] = first[:, lanes]
                coef[at + r, part + 1] = second[:, lanes]
        copy = pltpu.make_async_copy(
            coef.at[pl.ds(at, size)], coef_h.at[pl.ds(at, size)], out_sems.at[n]
        )
        copy.start()
        leaving.append(copy)
    wait(leaving)


def channel_matrix(ref, at):
    *_, n_col, _, rows, cols = ref.shape
    lead = (slice(None),) * (len(ref.shape) - 4)
    return jnp.concatenate(
        [ref[(*lead, c, at)].reshape(-1, cols) for c in range(n_col)], axis=1
    )


def put_channel(ref, at, values):
    *shape, n_col, _, rows, cols = ref.shape
    lead = (slice(None),) * len(shape)
    values = values.astype(BF16)
    for c in range(n_col):
        ref[(*lead, c, at)] = values[:, c * cols : (c + 1) * cols].reshape(*shape, rows, cols)


def product_kernel(n_row, right, after, *refs):
    pieces, (out, left) = refs[:-2], refs[-2:]
    n_col, share = left.shape[1:3]
    for number, piece in received(pieces, n_row):
        left[number // n_col, number % n_col] = piece
    for h in range(share):
        put_channel(out, h, dot(channel_matrix(left, h), channel_matrix(right, h), ((1,), (1,))))


def middle_kernel(product, dxh_h, after, out, dxh, xhat, sems):
    hidden = product.shape[0]
    (copy,) = start(sems, [(dxh_h, dxh)])
    values = product[...].astype(F32)
    mean = jnp.sum(values, axis=0) * (1.0 / hidden)
    centred = values - mean[None]
    var = jnp.sum(centred * centred, axis=0) * (1.0 / hidden)
    inverse = lax.rsqrt(var + EPS)
    xhat[...] = centred * inverse[None]
    copy.wait()
    m2 = jnp.sum(dxh[...] * xhat[...], axis=0) * (1.0 / hidden)
    out[...] = ((dxh[...] - xhat[...] * m2[None]) * inverse[None]).astype(BF16)


def update_kernel(
    product, gate_h, cot_h, norm_gain_h, norm_bias_h, out_w_h, gate_w_h, after, update_h, dzg_h,
    gate, cot, norm_gain, norm_bias, out_weight, gate_weight, update, dzg, spread,
    in_sems, out_sems,
):
    hidden, rows, cols = product.shape
    width = cot.shape[2]
    copies = start(
        in_sems,
        [
            (gate_h, gate), (cot_h, cot), (norm_gain_h, norm_gain), (norm_bias_h, norm_bias),
            (out_w_h, out_weight), (gate_w_h, gate_weight),
        ],
    )
    spread[...] = product[...].astype(F32).reshape(hidden * rows, cols)
    wait(copies)
    groups = groups_of(rows)
    norm_gain_b = jnp.concatenate([down_lanes(norm_gain[...], cols)] * groups[0][1], axis=1)
    norm_bias_b = jnp.concatenate([down_lanes(norm_bias[...], cols)] * groups[0][1], axis=1)
    out_t = turned_weight(out_weight[...])
    for at, size in groups:
        xhat, _ = normalized(
            jnp.concatenate(
                [spread[pl.ds(at + r, hidden, stride=rows), :] for r in range(size)], axis=1
            )
        )
        ybar = (xhat * norm_gain_b + norm_bias_b).astype(BF16)
        u = dot(out_t, ybar)
        g = side_by_side(gate, at, size)
        done = (g * u).astype(BF16)
        cot_t = turned(cot[at : at + size].reshape(size * cols, width))
        back = dot(gate_weight[...], (cot_t * u * g * (1.0 - g)).astype(BF16))
        for r in range(size):
            lanes = slice(r * cols, (r + 1) * cols)
            update[at + r] = turned(done[:, lanes]).astype(BF16)
            dzg[at + r] = back[:, lanes]
    wait(start(out_sems, [(update, update_h), (dzg, dzg_h)]))


def grad_right_kernel(grad, left, after, out):
    for h in range(out.shape[-3]):
        put_channel(out, h, dot(channel_matrix(grad, h), channel_matrix(left, h), ((0,), (0,))))


def grad_left_kernel(grad, right, *refs):
    outs, ready = refs[:-1], refs[-1]
    n_col, share = ready.shape[1:3]
    for h in range(share):
        put_channel(ready, h, dot(channel_matrix(grad, h), channel_matrix(right, h)))
    for m, n, number in sources(outs[0].shape[0], len(outs)):
        outs[m][n] = ready[number // n_col, number % n_col]


def through_projection(plane, coef, weight, at, size, rows):
    hidden = plane.shape[0] // rows
    columns = []
    for r in range(size):
        g = plane[pl.ds(at + r, hidden, stride=rows), :]
        columns.append(
            jnp.concatenate(
                [(g * coef[at + r, part]).astype(BF16) for part in range(2)], axis=0
            )
        )
    return dot(weight, jnp.concatenate(columns, axis=1))


def back_left_kernel(n_row, coef_h, dzg_h, proj_h, *refs):
    pieces, out_h = refs[:-9], refs[-9]
    coef, dzg, proj_weight, out, plane, sems, coef_sems, dzg_sems = refs[-8:]
    rows, width, cols = out.shape
    hidden = plane.shape[0] // rows
    groups = groups_of(rows)
    small = start(sems, [(proj_h, proj_weight)])
    blocks = [
        start(
            coef_sems,
            [
                (coef_h.at[pl.ds(at, size), pl.ds(0, 2)], coef.at[pl.ds(at, size)])
                for at, size in groups
            ],
        ),
        start(
            dzg_sems,
            [(dzg_h.at[pl.ds(at, size)], dzg.at[pl.ds(at, size)]) for at, size in groups],
        ),
    ]
    arrived = received(pieces, n_row)
    length = plane.shape[0] // len(arrived)
    for number, piece in arrived:
        first = pl.multiple_of(number * length, length)
        plane[pl.ds(first, length), :] = piece.astype(F32).reshape(length, cols)
    wait(small)
    weight = proj_weight[:, : 2 * hidden]
    for n, (at, size) in enumerate(groups):
        wait([copies[n] for copies in blocks])
        back = through_projection(plane, coef, weight, at, size, rows)
        for r in range(size):
            out[at + r] = back[:, r * cols : (r + 1) * cols] + dzg[at + r]
    wait(start(sems, [(out, out_h)]))


def back_kernel(
    grads, coef_h, zhat_h, inv_h, dzg_h, gain_h, proj_h, out_h,
    coef, zhat, inv, dzg, gain, proj_weight, out, plane,
    sems, coef_sems, zhat_sems, dzg_sems, out_sems,
):
    rows, cols, width = out.shape
    hidden = plane.shape[0] // rows
    groups = groups_of(rows)

    def blocks_of(source, target):
        return [(source.at[pl.ds(at, size)], target.at[pl.ds(at, size)]) for at, size in groups]

    small = start(sems, [(gain_h, gain), (proj_h, proj_weight), (inv_h, inv)])
    blocks = [
        start(
            coef_sems,
            [
                (coef_h.at[pl.ds(at, size), pl.ds(2, 2)], coef.at[pl.ds(at, size)])
                for at, size in groups
            ],
        ),
        start(zhat_sems, blocks_of(zhat_h, zhat)),
        start(dzg_sems, blocks_of(dzg_h, dzg)),
    ]
    total = grads[0].astype(F32)
    for half in range(1, grads.shape[0]):
        total = total + grads[half].astype(F32)
    plane[...] = total.reshape(plane.shape)
    wait(small)
    gain_b = jnp.concatenate([down_lanes(gain[...], cols)] * groups[0][1], axis=1)
    weight = proj_weight[:, 2 * hidden :]
    leaving = []
    for n, (at, size) in enumerate(groups):
        wait([copies[n] for copies in blocks])
        back = through_projection(plane, coef, weight, at, size, rows)
        dzh = (back + side_by_side(dzg, at, size)) * gain_b
        z = side_by_side(zhat, at, size)
        inverse = jnp.concatenate([inv[at + r : at + r + 1] for r in range(size)], axis=1)
        m1 = jnp.mean(dzh, axis=0, keepdims=True)
        m2 = jnp.mean(dzh * z, axis=0, keepdims=True)
        grad = ((dzh - m1 - z * m2) * inverse).astype(BF16)
        for r in range(size):
            out[at + r] = turned(grad[:, r * cols : (r + 1) * cols]).astype(BF16)
        copy = pltpu.make_async_copy(
            out.at[pl.ds(at, size)], out_h.at[pl.ds(at, size)], out_sems.at[n]
        )
        copy.start()
        leaving.append(copy)
    wait(leaving)


def call(kernel, outs, scratch, args, near=(), order=(), outs_near=False, flops=0, moved=0):
    here, far = (pl.BlockSpec(memory_space=space) for space in (pltpu.VMEM, pltpu.HBM))
    anywhere = pl.BlockSpec(memory_space=pl.ANY)
    specs = [here if at in near else anywhere if at in order else far for at in range(len(args))]
    return pl.pallas_call(
        kernel,
        out_shape=outs if outs_near else jax.tree.map(lambda o: pltpu.HBM(o.shape, o.dtype), outs),
        in_specs=specs,
        out_specs=jax.tree.map(lambda _: here if outs_near else far, outs),
        scratch_shapes=scratch,
        compiler_params=pltpu.CompilerParams(vmem_limit_bytes=24 * MIB),
        cost_estimate=pl.CostEstimate(flops=flops, bytes_accessed=moved, transcendentals=0),
    )(
        *[
            pltpu.with_memory_space_constraint(arg, pltpu.HBM) if spec is far else arg
            for arg, spec in zip(args, specs)
        ]
    )


def body(
    pair, mask, gain_in, bias_in, proj_weight, gate_weight,
    product_norm_gain, product_norm_bias, out_weight, cotangent,
):
    rows, cols, width = pair.shape
    hidden = out_weight.shape[0]
    n_half = lax.axis_size("half")
    n_row = lax.axis_size("row")
    n_core = lax.axis_size("core")
    n_col = lax.axis_size("col")
    n_quad = n_core * n_col
    n_line = n_row * n_core
    n_place = n_line * n_col
    within = ("row", "core", "col")
    share = hidden // n_place
    cells = rows * cols
    n_groups = len(groups_of(rows))
    mask_row = mask.reshape(1, -1)
    gain_in, bias_in = gain_in.reshape(1, -1), bias_in.reshape(1, -1)
    norm_gain, norm_bias = product_norm_gain.reshape(1, -1), product_norm_bias.reshape(1, -1)

    def shape(*dims, dtype=BF16):
        return jax.ShapeDtypeStruct(dims, dtype)

    def vmem(*dims, dtype=BF16):
        return pltpu.VMEM(dims, dtype)

    def sems(count):
        return pltpu.SemaphoreType.DMA((count,))

    def exchange(values):
        return lax.all_to_all(values, within, split_axis=0, concat_axis=0, tiled=True)

    def exchange_all(values):
        flat = values.reshape(n_half * n_place, share, rows, cols)
        return lax.all_to_all(
            flat, ("half", *within), split_axis=0, concat_axis=0, tiled=True
        )

    def permute(values, axes, size, distance):
        return lax.ppermute(values, axes, [(at, at ^ distance) for at in range(size)])

    def exchange_pieces(pieces):
        first = [pieces[0]]
        first += [permute(pieces[m], ("core", "col"), n_quad, m) for m in range(1, n_quad)]
        second = [
            permute(jnp.stack([piece[n] for piece in first]), ("row",), n_row, n)
            for n in range(1, n_row)
        ]
        return tuple(first + second)

    mask_s = pltpu.SMEM(mask.shape, jnp.int32)
    mask_v = vmem(*mask_row.shape, dtype=jnp.int32)
    vector = vmem(1, width, dtype=F32)
    plane = vmem(hidden * rows, cols, dtype=F32)
    block = vmem(rows, cols, width)
    wide = vmem(rows, width, cols, dtype=F32)
    square = vmem(width, hidden)
    proj_v = vmem(width, 4 * hidden)
    coef_v = vmem(rows, 2, hidden, cols, dtype=F32)
    pieces_shape = (shape(n_row, share, rows, cols),) * n_quad
    n_pieces = n_quad + n_row - 1

    def front(part, outs):
        return call(
            functools.partial(front_kernel, part, len(outs)),
            outs,
            [block, mask_s, mask_v, vector, vector, proj_v, plane, sems(5), sems(n_groups)],
            (pair, mask, mask_row, gain_in, bias_in, proj_weight),
            outs_near=True,
            flops=2 * cells * width * 3 * hidden,
            moved=5 * cells * width,
        )

    (right,) = front(2, (shape(n_half, n_place, share, rows, cols),))
    right = exchange_all(right).reshape(n_half, n_line, n_col, share, rows, cols)
    left = exchange_pieces(tuple(front(0, pieces_shape)))
    zhat, inv, gate, dxh = call(
        side_kernel,
        (
            shape(rows, width, cols, dtype=F32),
            shape(rows, cols, dtype=F32),
            shape(rows, width, cols, dtype=F32),
            shape(hidden * rows, cols, dtype=F32),
        ),
        [
            block, block, vector, vector, square, vector, square,
            wide, vmem(rows, cols, dtype=F32), wide, plane, sems(7), sems(4),
        ],
        (pair, cotangent, gain_in, bias_in, gate_weight, norm_gain, out_weight),
        flops=2 * cells * width * 4 * hidden,
        moved=16 * cells * width,
    )
    product, left = call(
        functools.partial(product_kernel, n_row),
        (shape(n_line, n_col, share, rows, cols), shape(n_line, n_col, share, rows, cols)),
        [],
        (right, inv, *left),
        near=(0, *range(2, 2 + n_pieces)),
        outs_near=True,
        flops=2 * share * n_half * (n_line * rows) ** 2 * n_col * cols,
        moved=8 * cells * hidden,
    )
    coef = call(
        factors_kernel,
        shape(rows, 4, hidden, cols, dtype=F32),
        [
            wide, mask_s, mask_v, vector, vector, proj_v, vmem(rows, 4, hidden, cols, dtype=F32),
            sems(6), sems(n_groups),
        ],
        (zhat, mask, mask_row, gain_in, bias_in, proj_weight, product),
        order=(6,),
        flops=2 * cells * width * 5 * hidden,
        moved=20 * cells * width,
    )
    product = exchange(product.reshape(n_place, share, rows, cols)).reshape(hidden, rows, cols)
    spread = vmem(hidden, rows, cols, dtype=F32)
    grad = call(
        middle_kernel,
        shape(hidden, rows, cols),
        [spread, spread, sems(1)],
        (product, dxh.reshape(hidden, rows, cols), coef),
        near=(0,),
        outs_near=True,
        flops=20 * cells * hidden,
        moved=8 * cells * hidden,
    )
    sent = grad
    grad = exchange(grad.reshape(n_place, share, rows, cols))
    grad = grad.reshape(n_line, n_col, share, rows, cols)
    update, dzg = call(
        update_kernel,
        (shape(rows, cols, width), shape(rows, width, cols, dtype=F32)),
        [wide, block, vector, vector, square, square, block, wide, plane, sems(6), sems(2)],
        (product, gate, cotangent, norm_gain, norm_bias, out_weight, gate_weight, sent),
        near=(0,),
        order=(7,),
        flops=2 * cells * width * 3 * hidden,
        moved=14 * cells * hidden,
    )
    grad_right = call(
        grad_right_kernel,
        shape(n_half, n_line, n_col, share, rows, cols),
        [],
        (grad, left, dzg),
        near=(0, 1),
        outs_near=True,
        flops=2 * share * n_half * (n_line * rows) ** 2 * n_col * cols,
        moved=8 * cells * hidden,
    )
    grad_right = exchange_all(grad_right).reshape(n_half, n_place, share, rows, cols)
    grad_left = call(
        grad_left_kernel,
        pieces_shape,
        [vmem(n_line, n_col, share, rows, cols)],
        (grad, right),
        near=(0, 1),
        outs_near=True,
        flops=2 * share * n_half * (n_line * rows) ** 2 * n_col * cols,
        moved=8 * cells * hidden,
    )
    grad_left = exchange_pieces(tuple(grad_left))
    dzg = call(
        functools.partial(back_left_kernel, n_row),
        shape(rows, width, cols, dtype=F32),
        [coef_v, wide, proj_v, wide, plane, sems(1), sems(n_groups), sems(n_groups)],
        (coef, dzg, proj_weight, *grad_left),
        near=tuple(range(3, 3 + n_pieces)),
        flops=2 * cells * width * 2 * hidden,
        moved=18 * cells * width,
    )
    grad_pair = call(
        back_kernel,
        shape(rows, cols, width),
        [
            coef_v, wide, vmem(rows, cols, dtype=F32), wide, vector, proj_v, block, plane,
            sems(3), sems(n_groups), sems(n_groups), sems(n_groups), sems(n_groups),
        ],
        (grad_right, coef, zhat, inv, dzg, gain_in, proj_weight),
        near=(0,),
        flops=2 * cells * width * 3 * hidden,
        moved=22 * cells * width,
    )
    return (update, grad_pair)


def solution(mesh):
    n_grp, n_row, n_col = (mesh.shape[name] for name in ("grp", "row", "col"))
    n_half = math.gcd(n_row, 2)
    n_core = math.gcd(n_row // n_half, 2)
    split = jax.sharding.Mesh(
        mesh.devices.reshape(n_grp, n_half, n_row // (n_half * n_core), n_core, n_col),
        ("grp", "half", "row", "core", "col"),
    )
    cells = P(("grp", "half", "row", "core"), "col", None)
    return jax.shard_map(
        body,
        mesh=split,
        in_specs=(cells, P("grp"), P(), P(), P(), P(), P(), P(), P(), cells),
        out_specs=(cells, cells),
        check_vma=False,
    )
```

```python
import functools
import math

import jax
import jax.numpy as jnp
from jax import lax
from jax.experimental import pallas as pl
from jax.experimental.pallas import tpu as pltpu
from jax.sharding import PartitionSpec as P

EPS = 1e-05
F32 = jnp.float32
BF16 = jnp.bfloat16
MIB = 1 << 20


def dot(a, b, over=((1,), (0,))):
    return lax.dot_general(a, b, (over, ((), ())), preferred_element_type=F32)


def eye(size):
    down = lax.broadcasted_iota(jnp.int32, (size, size), 0)
    across = lax.broadcasted_iota(jnp.int32, (size, size), 1)
    return (down == across).astype(F32).astype(BF16)


def turned(values):
    return dot(eye(values.shape[1]), values, ((1,), (1,)))


def down_lanes(vector, lanes):
    return jnp.broadcast_to(vector, (lanes, vector.shape[1])).T


def turned_weight(weight):
    c, m = weight.shape
    return jnp.concatenate(
        [turned(weight[:, at : at + c]) for at in range(0, m, c)], axis=0
    ).astype(BF16)


def sigmoid(values):
    return 0.5 + 0.5 * jnp.tanh(0.5 * values)


def normalized(values):
    mean = jnp.mean(values, axis=0, keepdims=True)
    centred = values - mean
    var = jnp.mean(centred * centred, axis=0, keepdims=True)
    inverse = lax.rsqrt(var + EPS)
    return centred * inverse, inverse


def start(sems, copies):
    running = [
        pltpu.make_async_copy(source, target, sems.at[at])
        for at, (source, target) in enumerate(copies)
    ]
    for copy in running:
        copy.start()
    return running


def wait(copies):
    for copy in copies:
        copy.wait()


def groups_of(rows):
    size = math.gcd(rows, 4)
    return [(at, size) for at in range(0, rows, size)]


def side_by_side(ref, at, size):
    return jnp.concatenate([ref[at + r] for r in range(size)], axis=1)


def pair_mask(mask_s, mask_v, at, size, rows, cols):
    here = lax.axis_index("half")
    for name in ("row", "core"):
        here = here * lax.axis_size(name) + lax.axis_index(name)
    first_row = here * rows + at
    first_col = pl.multiple_of(lax.axis_index("col") * cols, cols)
    col_mask = mask_v[:, pl.ds(first_col, cols)].astype(F32)
    return jnp.concatenate(
        [col_mask * mask_s[first_row + r].astype(F32) for r in range(size)], axis=1
    )


def sources(n_chip, n_core):
    n_col = lax.axis_size("col")
    core = lax.axis_index("core")
    chip = lax.axis_index("row") * n_col + lax.axis_index("col")
    found = []
    for n in range(n_chip):
        other = chip ^ n
        for m in range(n_core):
            line = other // n_col * n_core + (core ^ m)
            found.append((m, n, line * n_col + other % n_col))
    return found


def received(refs, n_chip):
    n_core = len(refs) - n_chip + 1
    return [
        (number, refs[m][0] if n == 0 else refs[n_core + n - 1][m])
        for m, n, number in sources(n_chip, n_core)
    ]


def front_kernel(
    part, n_out, pair_h, mask_h, mask_row_h, gain_h, bias_h, proj_h, *refs
):
    outs = refs[:n_out]
    pair, mask_s, mask_v, gain, bias, proj_weight, plane, sems, row_sems = refs[n_out:]
    rows, cols, width = pair.shape
    hidden = plane.shape[0] // rows
    groups = groups_of(rows)
    small = start(
        sems,
        [(gain_h, gain), (bias_h, bias), (proj_h, proj_weight), (mask_h, mask_s), (mask_row_h, mask_v)],
    )
    blocks = start(
        row_sems,
        [(pair_h.at[pl.ds(at, size)], pair.at[pl.ds(at, size)]) for at, size in groups],
    )
    wait(small)
    gain_b = jnp.concatenate([down_lanes(gain[...], cols)] * groups[0][1], axis=1)
    bias_b = jnp.concatenate([down_lanes(bias[...], cols)] * groups[0][1], axis=1)
    weight = turned_weight(proj_weight[:, part * hidden : (part + 2) * hidden])
    for (at, size), block in zip(groups, blocks):
        block.wait()
        zhat, _ = normalized(turned(pair[at : at + size].reshape(size * cols, width)))
        zbar = (zhat * gain_b + bias_b).astype(BF16)
        pm = pair_mask(mask_s, mask_v, at, size, rows, cols)
        values = sigmoid(dot(weight[:hidden], zbar)) * dot(weight[hidden:], zbar) * pm
        for r in range(size):
            plane[pl.ds(at + r, hidden, stride=rows), :] = values[:, r * cols : (r + 1) * cols]
    if n_out == 1:
        values = plane[...].reshape(outs[0].shape[1:]).astype(BF16)
        for half in range(outs[0].shape[0]):
            outs[0][half] = values
    else:
        give_pieces(plane, outs)


def give_pieces(plane, outs):
    n_chip = outs[0].shape[0]
    length = plane.shape[0] // (len(outs) * n_chip)
    for m, n, number in sources(n_chip, len(outs)):
        first = pl.multiple_of(number * length, length)
        values = plane[pl.ds(first, length), :]
        outs[m][n] = values.reshape(outs[m].shape[1:]).astype(BF16)


def side_kernel(
    pair_h, cot_h, gain_h, bias_h, gate_h, norm_gain_h, out_w_h,
    zhat_h, inv_h, gate_out_h, dxh_h,
    pair, cot, gain, bias, gate_weight, norm_gain, out_weight,
    zhat_out, inv_out, gate_out, dxh_out, in_sems, out_sems,
):
    rows, cols, width = pair.shape
    hidden = out_weight.shape[0]
    wait(
        start(
            in_sems,
            [
                (pair_h, pair), (cot_h, cot), (gain_h, gain), (bias_h, bias),
                (gate_h, gate_weight), (norm_gain_h, norm_gain), (out_w_h, out_weight),
            ],
        )
    )
    groups = groups_of(rows)
    gain_b = jnp.concatenate([down_lanes(gain[...], cols)] * groups[0][1], axis=1)
    bias_b = jnp.concatenate([down_lanes(bias[...], cols)] * groups[0][1], axis=1)
    norm_gain_b = jnp.concatenate([down_lanes(norm_gain[...], cols)] * groups[0][1], axis=1)
    gate_t = turned_weight(gate_weight[...])
    for at, size in groups:
        zhat, inverse = normalized(turned(pair[at : at + size].reshape(size * cols, width)))
        zbar = (zhat * gain_b + bias_b).astype(BF16)
        gate = sigmoid(dot(gate_t, zbar))
        cot_t = turned(cot[at : at + size].reshape(size * cols, width))
        dxh = dot(out_weight[...], (cot_t * gate).astype(BF16)) * norm_gain_b
        dxh = dxh - jnp.mean(dxh, axis=0, keepdims=True)
        for r in range(size):
            lanes = slice(r * cols, (r + 1) * cols)
            zhat_out[at + r] = zhat[:, lanes]
            inv_out[at + r : at + r + 1] = inverse[:, lanes]
            gate_out[at + r] = gate[:, lanes]
            dxh_out[pl.ds(at + r, hidden, stride=rows), :] = dxh[:, lanes]
    wait(
        start(
            out_sems,
            [(zhat_out, zhat_h), (inv_out, inv_h), (gate_out, gate_out_h), (dxh_out, dxh_h)],
        )
    )


def factors_kernel(
    zhat_h, mask_h, mask_row_h, gain_h, bias_h, proj_h, after, coef_h,
    zhat, mask_s, mask_v, gain, bias, proj_weight, coef, in_sems, out_sems,
):
    rows, width, cols = zhat.shape
    hidden = coef.shape[2]
    wait(
        start(
            in_sems,
            [
                (zhat_h, zhat), (mask_h, mask_s), (mask_row_h, mask_v), (gain_h, gain),
                (bias_h, bias), (proj_h, proj_weight),
            ],
        )
    )
    groups = groups_of(rows)
    gain_b = jnp.concatenate([down_lanes(gain[...], cols)] * groups[0][1], axis=1)
    bias_b = jnp.concatenate([down_lanes(bias[...], cols)] * groups[0][1], axis=1)
    weight = turned_weight(proj_weight[...])
    leaving = []
    for n, (at, size) in enumerate(groups):
        zbar = (side_by_side(zhat, at, size) * gain_b + bias_b).astype(BF16)
        pm = pair_mask(mask_s, mask_v, at, size, rows, cols)
        for part in (0, 2):
            s = sigmoid(dot(weight[part * hidden : (part + 1) * hidden], zbar))
            q = dot(weight[(part + 1) * hidden : (part + 2) * hidden], zbar)
            second = pm * s
            first = second * q * (1.0 - s)
            for r in range(size):
                lanes = slice(r * cols, (r + 1) * cols)
                coef[at + r, part] = first[:, lanes]
                coef[at + r, part + 1] = second[:, lanes]
        copy = pltpu.make_async_copy(
            coef.at[pl.ds(at, size)], coef_h.at[pl.ds(at, size)], out_sems.at[n]
        )
        copy.start()
        leaving.append(copy)
    wait(leaving)


def channel_matrix(ref, at):
    *_, n_col, _, rows, cols = ref.shape
    lead = (slice(None),) * (len(ref.shape) - 4)
    return jnp.concatenate(
        [ref[(*lead, c, at)].reshape(-1, cols) for c in range(n_col)], axis=1
    )


def put_channel(ref, at, values):
    *shape, n_col, _, rows, cols = ref.shape
    lead = (slice(None),) * len(shape)
    values = values.astype(BF16)
    for c in range(n_col):
        ref[(*lead, c, at)] = values[:, c * cols : (c + 1) * cols].reshape(*shape, rows, cols)


def product_kernel(n_chip, right, after, *refs):
    pieces, (out, left) = refs[:-2], refs[-2:]
    n_col, share = left.shape[1:3]
    for number, piece in received(pieces, n_chip):
        left[number // n_col, number % n_col] = piece
    for h in range(share):
        put_channel(out, h, dot(channel_matrix(left, h), channel_matrix(right, h), ((1,), (1,))))


def middle_kernel(product, dxh_h, after, out, dxh, xhat, sems):
    hidden = product.shape[0]
    (copy,) = start(sems, [(dxh_h, dxh)])
    values = product[...].astype(F32)
    mean = jnp.sum(values, axis=0) * (1.0 / hidden)
    centred = values - mean[None]
    var = jnp.sum(centred * centred, axis=0) * (1.0 / hidden)
    inverse = lax.rsqrt(var + EPS)
    xhat[...] = centred * inverse[None]
    copy.wait()
    m2 = jnp.sum(dxh[...] * xhat[...], axis=0) * (1.0 / hidden)
    out[...] = ((dxh[...] - xhat[...] * m2[None]) * inverse[None]).astype(BF16)


def update_kernel(
    product, gate_h, cot_h, norm_gain_h, norm_bias_h, out_w_h, gate_w_h, after, update_h, dzg_h,
    gate, cot, norm_gain, norm_bias, out_weight, gate_weight, update, dzg, spread,
    in_sems, out_sems,
):
    hidden, rows, cols = product.shape
    width = cot.shape[2]
    copies = start(
        in_sems,
        [
            (gate_h, gate), (cot_h, cot), (norm_gain_h, norm_gain), (norm_bias_h, norm_bias),
            (out_w_h, out_weight), (gate_w_h, gate_weight),
        ],
    )
    spread[...] = product[...].astype(F32).reshape(hidden * rows, cols)
    wait(copies)
    groups = groups_of(rows)
    norm_gain_b = jnp.concatenate([down_lanes(norm_gain[...], cols)] * groups[0][1], axis=1)
    norm_bias_b = jnp.concatenate([down_lanes(norm_bias[...], cols)] * groups[0][1], axis=1)
    out_t = turned_weight(out_weight[...])
    for at, size in groups:
        xhat, _ = normalized(
            jnp.concatenate(
                [spread[pl.ds(at + r, hidden, stride=rows), :] for r in range(size)], axis=1
            )
        )
        ybar = (xhat * norm_gain_b + norm_bias_b).astype(BF16)
        u = dot(out_t, ybar)
        g = side_by_side(gate, at, size)
        done = (g * u).astype(BF16)
        cot_t = turned(cot[at : at + size].reshape(size * cols, width))
        back = dot(gate_weight[...], (cot_t * u * g * (1.0 - g)).astype(BF16))
        for r in range(size):
            lanes = slice(r * cols, (r + 1) * cols)
            update[at + r] = turned(done[:, lanes]).astype(BF16)
            dzg[at + r] = back[:, lanes]
    wait(start(out_sems, [(update, update_h), (dzg, dzg_h)]))


def grad_right_kernel(grad, left, after, out):
    for h in range(out.shape[-3]):
        put_channel(out, h, dot(channel_matrix(grad, h), channel_matrix(left, h), ((0,), (0,))))


def grad_left_kernel(grad, right, *refs):
    outs, ready = refs[:-1], refs[-1]
    n_col, share = ready.shape[1:3]
    for h in range(share):
        put_channel(ready, h, dot(channel_matrix(grad, h), channel_matrix(right, h)))
    for m, n, number in sources(outs[0].shape[0], len(outs)):
        outs[m][n] = ready[number // n_col, number % n_col]


def through_projection(plane, coef, weight, at, size, rows):
    hidden = plane.shape[0] // rows
    columns = []
    for r in range(size):
        g = plane[pl.ds(at + r, hidden, stride=rows), :]
        columns.append(
            jnp.concatenate(
                [(g * coef[at + r, part]).astype(BF16) for part in range(2)], axis=0
            )
        )
    return dot(weight, jnp.concatenate(columns, axis=1))


def back_left_kernel(n_chip, coef_h, dzg_h, proj_h, *refs):
    pieces, out_h = refs[:-9], refs[-9]
    coef, dzg, proj_weight, out, plane, sems, coef_sems, dzg_sems = refs[-8:]
    rows, width, cols = out.shape
    hidden = plane.shape[0] // rows
    groups = groups_of(rows)
    small = start(sems, [(proj_h, proj_weight)])
    blocks = [
        start(
            coef_sems,
            [
                (coef_h.at[pl.ds(at, size), pl.ds(0, 2)], coef.at[pl.ds(at, size)])
                for at, size in groups
            ],
        ),
        start(
            dzg_sems,
            [(dzg_h.at[pl.ds(at, size)], dzg.at[pl.ds(at, size)]) for at, size in groups],
        ),
    ]
    arrived = received(pieces, n_chip)
    length = plane.shape[0] // len(arrived)
    for number, piece in arrived:
        first = pl.multiple_of(number * length, length)
        plane[pl.ds(first, length), :] = piece.astype(F32).reshape(length, cols)
    wait(small)
    weight = proj_weight[:, : 2 * hidden]
    for n, (at, size) in enumerate(groups):
        wait([copies[n] for copies in blocks])
        back = through_projection(plane, coef, weight, at, size, rows)
        for r in range(size):
            out[at + r] = back[:, r * cols : (r + 1) * cols] + dzg[at + r]
    wait(start(sems, [(out, out_h)]))


def back_kernel(
    grads, coef_h, zhat_h, inv_h, dzg_h, gain_h, proj_h, out_h,
    coef, zhat, inv, dzg, gain, proj_weight, out, plane,
    sems, coef_sems, zhat_sems, dzg_sems, out_sems,
):
    rows, cols, width = out.shape
    hidden = plane.shape[0] // rows
    groups = groups_of(rows)

    def blocks_of(source, target):
        return [(source.at[pl.ds(at, size)], target.at[pl.ds(at, size)]) for at, size in groups]

    small = start(sems, [(gain_h, gain), (proj_h, proj_weight), (inv_h, inv)])
    blocks = [
        start(
            coef_sems,
            [
                (coef_h.at[pl.ds(at, size), pl.ds(2, 2)], coef.at[pl.ds(at, size)])
                for at, size in groups
            ],
        ),
        start(zhat_sems, blocks_of(zhat_h, zhat)),
        start(dzg_sems, blocks_of(dzg_h, dzg)),
    ]
    total = grads[0].astype(F32)
    for half in range(1, grads.shape[0]):
        total = total + grads[half].astype(F32)
    plane[...] = total.reshape(plane.shape)
    wait(small)
    gain_b = jnp.concatenate([down_lanes(gain[...], cols)] * groups[0][1], axis=1)
    weight = proj_weight[:, 2 * hidden :]
    leaving = []
    for n, (at, size) in enumerate(groups):
        wait([copies[n] for copies in blocks])
        back = through_projection(plane, coef, weight, at, size, rows)
        dzh = (back + side_by_side(dzg, at, size)) * gain_b
        z = side_by_side(zhat, at, size)
        inverse = jnp.concatenate([inv[at + r : at + r + 1] for r in range(size)], axis=1)
        m1 = jnp.mean(dzh, axis=0, keepdims=True)
        m2 = jnp.mean(dzh * z, axis=0, keepdims=True)
        grad = ((dzh - m1 - z * m2) * inverse).astype(BF16)
        for r in range(size):
            out[at + r] = turned(grad[:, r * cols : (r + 1) * cols]).astype(BF16)
        copy = pltpu.make_async_copy(
            out.at[pl.ds(at, size)], out_h.at[pl.ds(at, size)], out_sems.at[n]
        )
        copy.start()
        leaving.append(copy)
    wait(leaving)


def call(kernel, outs, scratch, args, near=(), order=(), outs_near=False, flops=0, moved=0):
    here, far = (pl.BlockSpec(memory_space=space) for space in (pltpu.VMEM, pltpu.HBM))
    anywhere = pl.BlockSpec(memory_space=pl.ANY)
    specs = [here if at in near else anywhere if at in order else far for at in range(len(args))]
    return pl.pallas_call(
        kernel,
        out_shape=outs if outs_near else jax.tree.map(lambda o: pltpu.HBM(o.shape, o.dtype), outs),
        in_specs=specs,
        out_specs=jax.tree.map(lambda _: here if outs_near else far, outs),
        scratch_shapes=scratch,
        compiler_params=pltpu.CompilerParams(vmem_limit_bytes=24 * MIB),
        cost_estimate=pl.CostEstimate(flops=flops, bytes_accessed=moved, transcendentals=0),
    )(
        *[
            pltpu.with_memory_space_constraint(arg, pltpu.HBM) if spec is far else arg
            for arg, spec in zip(args, specs)
        ]
    )


def body(
    pair, mask, gain_in, bias_in, proj_weight, gate_weight,
    product_norm_gain, product_norm_bias, out_weight, cotangent,
):
    rows, cols, width = pair.shape
    hidden = out_weight.shape[0]
    n_half = lax.axis_size("half")
    n_row = lax.axis_size("row")
    n_core = lax.axis_size("core")
    n_col = lax.axis_size("col")
    n_chip = n_row * n_col
    n_line = n_row * n_core
    n_place = n_line * n_col
    within = ("row", "core", "col")
    share = hidden // n_place
    cells = rows * cols
    n_groups = len(groups_of(rows))
    mask_row = mask.reshape(1, -1)
    gain_in, bias_in = gain_in.reshape(1, -1), bias_in.reshape(1, -1)
    norm_gain, norm_bias = product_norm_gain.reshape(1, -1), product_norm_bias.reshape(1, -1)

    def shape(*dims, dtype=BF16):
        return jax.ShapeDtypeStruct(dims, dtype)

    def vmem(*dims, dtype=BF16):
        return pltpu.VMEM(dims, dtype)

    def sems(count):
        return pltpu.SemaphoreType.DMA((count,))

    def exchange(values):
        return lax.all_to_all(values, within, split_axis=0, concat_axis=0, tiled=True)

    def exchange_all(values):
        flat = values.reshape(n_half * n_place, share, rows, cols)
        return lax.all_to_all(
            flat, ("half", *within), split_axis=0, concat_axis=0, tiled=True
        )

    def permute(values, axes, size, distance):
        return lax.ppermute(values, axes, [(at, at ^ distance) for at in range(size)])

    def exchange_pieces(pieces):
        first = [pieces[0]]
        first += [permute(pieces[m], ("core",), n_core, m) for m in range(1, n_core)]
        second = [
            permute(jnp.stack([piece[n] for piece in first]), ("row", "col"), n_chip, n)
            for n in range(1, n_chip)
        ]
        return tuple(first + second)

    mask_s = pltpu.SMEM(mask.shape, jnp.int32)
    mask_v = vmem(*mask_row.shape, dtype=jnp.int32)
    vector = vmem(1, width, dtype=F32)
    plane = vmem(hidden * rows, cols, dtype=F32)
    block = vmem(rows, cols, width)
    wide = vmem(rows, width, cols, dtype=F32)
    square = vmem(width, hidden)
    proj_v = vmem(width, 4 * hidden)
    coef_v = vmem(rows, 2, hidden, cols, dtype=F32)
    pieces_shape = (shape(n_chip, share, rows, cols),) * n_core
    n_pieces = n_core + n_chip - 1

    def front(part, outs):
        return call(
            functools.partial(front_kernel, part, len(outs)),
            outs,
            [block, mask_s, mask_v, vector, vector, proj_v, plane, sems(5), sems(n_groups)],
            (pair, mask, mask_row, gain_in, bias_in, proj_weight),
            outs_near=True,
            flops=2 * cells * width * 3 * hidden,
            moved=5 * cells * width,
        )

    (right,) = front(2, (shape(n_half, n_place, share, rows, cols),))
    right = exchange_all(right).reshape(n_half, n_line, n_col, share, rows, cols)
    left = exchange_pieces(tuple(front(0, pieces_shape)))
    zhat, inv, gate, dxh = call(
        side_kernel,
        (
            shape(rows, width, cols, dtype=F32),
            shape(rows, cols, dtype=F32),
            shape(rows, width, cols, dtype=F32),
            shape(hidden * rows, cols, dtype=F32),
        ),
        [
            block, block, vector, vector, square, vector, square,
            wide, vmem(rows, cols, dtype=F32), wide, plane, sems(7), sems(4),
        ],
        (pair, cotangent, gain_in, bias_in, gate_weight, norm_gain, out_weight),
        flops=2 * cells * width * 4 * hidden,
        moved=16 * cells * width,
    )
    product, left = call(
        functools.partial(product_kernel, n_chip),
        (shape(n_line, n_col, share, rows, cols), shape(n_line, n_col, share, rows, cols)),
        [],
        (right, inv, *left),
        near=(0, *range(2, 2 + n_pieces)),
        outs_near=True,
        flops=2 * share * n_half * (n_line * rows) ** 2 * n_col * cols,
        moved=8 * cells * hidden,
    )
    coef = call(
        factors_kernel,
        shape(rows, 4, hidden, cols, dtype=F32),
        [
            wide, mask_s, mask_v, vector, vector, proj_v, vmem(rows, 4, hidden, cols, dtype=F32),
            sems(6), sems(n_groups),
        ],
        (zhat, mask, mask_row, gain_in, bias_in, proj_weight, product),
        order=(6,),
        flops=2 * cells * width * 5 * hidden,
        moved=20 * cells * width,
    )
    product = exchange(product.reshape(n_place, share, rows, cols)).reshape(hidden, rows, cols)
    spread = vmem(hidden, rows, cols, dtype=F32)
    grad = call(
        middle_kernel,
        shape(hidden, rows, cols),
        [spread, spread, sems(1)],
        (product, dxh.reshape(hidden, rows, cols), coef),
        near=(0,),
        outs_near=True,
        flops=20 * cells * hidden,
        moved=8 * cells * hidden,
    )
    sent = grad
    grad = exchange(grad.reshape(n_place, share, rows, cols))
    grad = grad.reshape(n_line, n_col, share, rows, cols)
    update, dzg = call(
        update_kernel,
        (shape(rows, cols, width), shape(rows, width, cols, dtype=F32)),
        [wide, block, vector, vector, square, square, block, wide, plane, sems(6), sems(2)],
        (product, gate, cotangent, norm_gain, norm_bias, out_weight, gate_weight, sent),
        near=(0,),
        order=(7,),
        flops=2 * cells * width * 3 * hidden,
        moved=14 * cells * hidden,
    )
    grad_right = call(
        grad_right_kernel,
        shape(n_half, n_line, n_col, share, rows, cols),
        [],
        (grad, left, dzg),
        near=(0, 1),
        outs_near=True,
        flops=2 * share * n_half * (n_line * rows) ** 2 * n_col * cols,
        moved=8 * cells * hidden,
    )
    grad_right = exchange_all(grad_right).reshape(n_half, n_place, share, rows, cols)
    grad_left = call(
        grad_left_kernel,
        pieces_shape,
        [vmem(n_line, n_col, share, rows, cols)],
        (grad, right),
        near=(0, 1),
        outs_near=True,
        flops=2 * share * n_half * (n_line * rows) ** 2 * n_col * cols,
        moved=8 * cells * hidden,
    )
    grad_left = exchange_pieces(tuple(grad_left))
    dzg = call(
        functools.partial(back_left_kernel, n_chip),
        shape(rows, width, cols, dtype=F32),
        [coef_v, wide, proj_v, wide, plane, sems(1), sems(n_groups), sems(n_groups)],
        (coef, dzg, proj_weight, *grad_left),
        near=tuple(range(3, 3 + n_pieces)),
        flops=2 * cells * width * 2 * hidden,
        moved=18 * cells * width,
    )
    grad_pair = call(
        back_kernel,
        shape(rows, cols, width),
        [
            coef_v, wide, vmem(rows, cols, dtype=F32), wide, vector, proj_v, block, plane,
            sems(3), sems(n_groups), sems(n_groups), sems(n_groups), sems(n_groups),
        ],
        (grad_right, coef, zhat, inv, dzg, gain_in, proj_weight),
        near=(0,),
        flops=2 * cells * width * 3 * hidden,
        moved=22 * cells * width,
    )
    return (update, grad_pair)


def solution(mesh):
    n_grp, n_row, n_col = (mesh.shape[name] for name in ("grp", "row", "col"))
    n_half = math.gcd(n_row, 2)
    n_core = math.gcd(n_row // n_half, 2)
    split = jax.sharding.Mesh(
        mesh.devices.reshape(n_grp, n_half, n_row // (n_half * n_core), n_core, n_col),
        ("grp", "half", "row", "core", "col"),
    )
    cells = P(("grp", "half", "row", "core"), "col", None)
    return jax.shard_map(
        body,
        mesh=split,
        in_specs=(cells, P("grp"), P(), P(), P(), P(), P(), P(), P(), cells),
        out_specs=(cells, cells),
        check_vma=False,
    )
```

```python
import functools
import math

import jax
import jax.numpy as jnp
from jax import lax
from jax.experimental import pallas as pl
from jax.experimental.pallas import tpu as pltpu
from jax.sharding import PartitionSpec as P

EPS = 1e-05
F32 = jnp.float32
BF16 = jnp.bfloat16
MIB = 1 << 20


def dot(a, b, over=((1,), (0,))):
    return lax.dot_general(a, b, (over, ((), ())), preferred_element_type=F32)


def eye(size):
    down = lax.broadcasted_iota(jnp.int32, (size, size), 0)
    across = lax.broadcasted_iota(jnp.int32, (size, size), 1)
    return (down == across).astype(F32).astype(BF16)


def turned(values):
    return dot(eye(values.shape[1]), values, ((1,), (1,)))


def down_lanes(vector, lanes):
    return jnp.broadcast_to(vector, (lanes, vector.shape[1])).T


def turned_weight(weight):
    c, m = weight.shape
    return jnp.concatenate(
        [turned(weight[:, at : at + c]) for at in range(0, m, c)], axis=0
    ).astype(BF16)


def sigmoid(values):
    return 0.5 + 0.5 * jnp.tanh(0.5 * values)


def normalized(values):
    mean = jnp.mean(values, axis=0, keepdims=True)
    centred = values - mean
    var = jnp.mean(centred * centred, axis=0, keepdims=True)
    inverse = lax.rsqrt(var + EPS)
    return centred * inverse, inverse


def start(sems, copies):
    running = [
        pltpu.make_async_copy(source, target, sems.at[at])
        for at, (source, target) in enumerate(copies)
    ]
    for copy in running:
        copy.start()
    return running


def wait(copies):
    for copy in copies:
        copy.wait()


def groups_of(rows):
    size = math.gcd(rows, 4)
    return [(at, size) for at in range(0, rows, size)]


def side_by_side(ref, at, size):
    return jnp.concatenate([ref[at + r] for r in range(size)], axis=1)


def pair_mask(mask_s, mask_v, at, size, rows, cols):
    here = lax.axis_index("half")
    for name in ("row", "core"):
        here = here * lax.axis_size(name) + lax.axis_index(name)
    first_row = here * rows + at
    first_col = pl.multiple_of(lax.axis_index("col") * cols, cols)
    col_mask = mask_v[:, pl.ds(first_col, cols)].astype(F32)
    return jnp.concatenate(
        [col_mask * mask_s[first_row + r].astype(F32) for r in range(size)], axis=1
    )


def sources(n_chip, n_core):
    n_col = lax.axis_size("col")
    core = lax.axis_index("core")
    chip = lax.axis_index("row") * n_col + lax.axis_index("col")
    found = []
    for n in range(n_chip):
        other = chip ^ n
        for m in range(n_core):
            line = other // n_col * n_core + (core ^ m)
            found.append((m, n, line * n_col + other % n_col))
    return found


def received(refs, n_chip):
    n_core = len(refs) - n_chip + 1
    return [
        (number, refs[m][0] if n == 0 else refs[n_core + n - 1][m])
        for m, n, number in sources(n_chip, n_core)
    ]


def front_kernel(
    part, n_out, pair_h, mask_h, mask_row_h, gain_h, bias_h, proj_h, *refs
):
    outs = refs[:n_out]
    pair, mask_s, mask_v, gain, bias, proj_weight, plane, sems, row_sems, *more = refs[n_out:]
    rows, cols, width = pair.shape
    hidden = plane.shape[0] // rows
    groups = groups_of(rows)
    blocks = start(
        row_sems,
        [(pair_h.at[pl.ds(at, size)], pair.at[pl.ds(at, size)]) for at, size in groups],
    )
    small = start(
        sems,
        [
            (gain_h, gain), (bias_h, bias),
            (proj_h.at[:, pl.ds(part * hidden, 2 * hidden)], proj_weight),
            (mask_h, mask_s), (mask_row_h, mask_v),
        ],
    )
    wait(small)
    gain_b = jnp.concatenate([down_lanes(gain[...], cols)] * groups[0][1], axis=1)
    bias_b = jnp.concatenate([down_lanes(bias[...], cols)] * groups[0][1], axis=1)
    weight = turned_weight(proj_weight[...])
    for (at, size), block in zip(groups, blocks):
        block.wait()
        zhat, _ = normalized(turned(pair[at : at + size].reshape(size * cols, width)))
        zbar = (zhat * gain_b + bias_b).astype(BF16)
        pm = pair_mask(mask_s, mask_v, at, size, rows, cols)
        values = sigmoid(dot(weight[:hidden], zbar)) * dot(weight[hidden:], zbar) * pm
        for r in range(size):
            plane[pl.ds(at + r, hidden, stride=rows), :] = values[:, r * cols : (r + 1) * cols]
    if n_out > 1:
        give_pieces(plane, outs)
    else:
        give_all(plane, outs[0], *more)


def give_all(plane, out_h, ready, sems):
    n_place = ready.shape[0]
    size = math.gcd(n_place, 4)
    length = plane.shape[0] // n_place * size
    leaving = []
    for n, at in enumerate(range(0, n_place, size)):
        values = plane[n * length : (n + 1) * length]
        ready[at : at + size] = values.reshape(size, *ready.shape[1:]).astype(BF16)
        for half in range(out_h.shape[0]):
            copy = pltpu.make_async_copy(
                ready.at[pl.ds(at, size)], out_h.at[half, pl.ds(at, size)], sems.at[half, n]
            )
            copy.start()
            leaving.append(copy)
    wait(leaving)


def give_pieces(plane, outs):
    n_chip = outs[0].shape[0]
    length = plane.shape[0] // (len(outs) * n_chip)
    for m, n, number in sources(n_chip, len(outs)):
        first = pl.multiple_of(number * length, length)
        values = plane[pl.ds(first, length), :]
        outs[m][n] = values.reshape(outs[m].shape[1:]).astype(BF16)


def side_kernel(
    pair_h, cot_h, gain_h, bias_h, gate_h, norm_gain_h, out_w_h,
    zhat_h, inv_h, gate_out_h, dxh_h,
    pair, cot, gain, bias, gate_weight, norm_gain, out_weight,
    zhat_out, inv_out, gate_out, dxh_out, in_sems, out_sems,
):
    rows, cols, width = pair.shape
    hidden = out_weight.shape[0]
    wait(
        start(
            in_sems,
            [
                (pair_h, pair), (cot_h, cot), (gain_h, gain), (bias_h, bias),
                (gate_h, gate_weight), (norm_gain_h, norm_gain), (out_w_h, out_weight),
            ],
        )
    )
    groups = groups_of(rows)
    gain_b = jnp.concatenate([down_lanes(gain[...], cols)] * groups[0][1], axis=1)
    bias_b = jnp.concatenate([down_lanes(bias[...], cols)] * groups[0][1], axis=1)
    norm_gain_b = jnp.concatenate([down_lanes(norm_gain[...], cols)] * groups[0][1], axis=1)
    gate_t = turned_weight(gate_weight[...])
    for at, size in groups:
        zhat, inverse = normalized(turned(pair[at : at + size].reshape(size * cols, width)))
        zbar = (zhat * gain_b + bias_b).astype(BF16)
        gate = sigmoid(dot(gate_t, zbar))
        cot_t = turned(cot[at : at + size].reshape(size * cols, width))
        dxh = dot(out_weight[...], (cot_t * gate).astype(BF16)) * norm_gain_b
        dxh = dxh - jnp.mean(dxh, axis=0, keepdims=True)
        for r in range(size):
            lanes = slice(r * cols, (r + 1) * cols)
            zhat_out[at + r] = zhat[:, lanes]
            inv_out[at + r : at + r + 1] = inverse[:, lanes]
            gate_out[at + r] = gate[:, lanes]
            dxh_out[pl.ds(at + r, hidden, stride=rows), :] = dxh[:, lanes]
    wait(
        start(
            out_sems,
            [(zhat_out, zhat_h), (inv_out, inv_h), (gate_out, gate_out_h), (dxh_out, dxh_h)],
        )
    )


def factors_kernel(
    zhat_h, mask_h, mask_row_h, gain_h, bias_h, proj_h, dxh_h, after, coef_h, dxh,
    zhat, mask_s, mask_v, gain, bias, proj_weight, coef, in_sems, out_sems, fetch_sems,
):
    rows, width, cols = zhat.shape
    hidden = coef.shape[2]
    fetched = start(fetch_sems, [(dxh_h, dxh)])
    wait(
        start(
            in_sems,
            [
                (zhat_h, zhat), (mask_h, mask_s), (mask_row_h, mask_v), (gain_h, gain),
                (bias_h, bias), (proj_h, proj_weight),
            ],
        )
    )
    groups = groups_of(rows)
    gain_b = jnp.concatenate([down_lanes(gain[...], cols)] * groups[0][1], axis=1)
    bias_b = jnp.concatenate([down_lanes(bias[...], cols)] * groups[0][1], axis=1)
    weight = turned_weight(proj_weight[...])
    leaving = []
    for n, (at, size) in enumerate(groups):
        zbar = (side_by_side(zhat, at, size) * gain_b + bias_b).astype(BF16)
        pm = pair_mask(mask_s, mask_v, at, size, rows, cols)
        for part in (0, 2):
            s = sigmoid(dot(weight[part * hidden : (part + 1) * hidden], zbar))
            q = dot(weight[(part + 1) * hidden : (part + 2) * hidden], zbar)
            second = pm * s
            first = second * q * (1.0 - s)
            for r in range(size):
                lanes = slice(r * cols, (r + 1) * cols)
                coef[at + r, part] = first[:, lanes]
                coef[at + r, part + 1] = second[:, lanes]
        copy = pltpu.make_async_copy(
            coef.at[pl.ds(at, size)], coef_h.at[pl.ds(at, size)], out_sems.at[n]
        )
        copy.start()
        leaving.append(copy)
    wait(leaving + fetched)


def channel_matrix(ref, at):
    *_, n_col, _, rows, cols = ref.shape
    lead = (slice(None),) * (len(ref.shape) - 4)
    return jnp.concatenate(
        [ref[(*lead, c, at)].reshape(-1, cols) for c in range(n_col)], axis=1
    )


def put_channel(ref, at, values):
    *shape, n_col, _, rows, cols = ref.shape
    lead = (slice(None),) * len(shape)
    values = values.astype(BF16)
    for c in range(n_col):
        ref[(*lead, c, at)] = values[:, c * cols : (c + 1) * cols].reshape(*shape, rows, cols)


def leave(ready, out_h, at, sem):
    lead = (slice(None),) * (len(ready.shape) - 3)
    copy = pltpu.make_async_copy(
        ready.at[(*lead, pl.ds(at, 1))], out_h.at[(*lead, pl.ds(at, 1))], sem
    )
    copy.start()
    return copy


def product_kernel(n_chip, right, after, *refs):
    pieces, (out_h, left, ready, sems) = refs[:-4], refs[-4:]
    n_col, share = left.shape[1:3]
    for number, piece in received(pieces, n_chip):
        left[number // n_col, number % n_col] = piece
    leaving = []
    for h in range(share):
        values = dot(channel_matrix(left, h), channel_matrix(right, h), ((1,), (1,)))
        put_channel(ready, h, values)
        leaving.append(leave(ready, out_h, h, sems.at[h]))
    wait(leaving)


def middle_kernel(product, dxh, out_h, xhat, ready, sems):
    hidden = product.shape[0]
    values = product[...].astype(F32)
    mean = jnp.sum(values, axis=0) * (1.0 / hidden)
    centred = values - mean[None]
    var = jnp.sum(centred * centred, axis=0) * (1.0 / hidden)
    inverse = lax.rsqrt(var + EPS)
    xhat[...] = centred * inverse[None]
    m2 = jnp.sum(dxh[...] * xhat[...], axis=0) * (1.0 / hidden)
    leaving = []
    size = math.gcd(hidden, 32)
    for n, at in enumerate(range(0, hidden, size)):
        part = slice(at, at + size)
        ready[part] = ((dxh[part] - xhat[part] * m2[None]) * inverse[None]).astype(BF16)
        copy = pltpu.make_async_copy(
            ready.at[pl.ds(at, size)], out_h.at[pl.ds(at, size)], sems.at[n]
        )
        copy.start()
        leaving.append(copy)
    wait(leaving)


def update_kernel(
    product, gate_h, cot_h, norm_gain_h, norm_bias_h, out_w_h, gate_w_h, after, update_h, dzg_h,
    gate, cot, norm_gain, norm_bias, out_weight, gate_weight, update, dzg, spread,
    in_sems, out_sems,
):
    hidden, rows, cols = product.shape
    width = cot.shape[2]
    copies = start(
        in_sems,
        [
            (gate_h, gate), (cot_h, cot), (norm_gain_h, norm_gain), (norm_bias_h, norm_bias),
            (out_w_h, out_weight), (gate_w_h, gate_weight),
        ],
    )
    spread[...] = product[...].astype(F32).reshape(hidden * rows, cols)
    wait(copies)
    groups = groups_of(rows)
    norm_gain_b = jnp.concatenate([down_lanes(norm_gain[...], cols)] * groups[0][1], axis=1)
    norm_bias_b = jnp.concatenate([down_lanes(norm_bias[...], cols)] * groups[0][1], axis=1)
    out_t = turned_weight(out_weight[...])
    for at, size in groups:
        xhat, _ = normalized(
            jnp.concatenate(
                [spread[pl.ds(at + r, hidden, stride=rows), :] for r in range(size)], axis=1
            )
        )
        ybar = (xhat * norm_gain_b + norm_bias_b).astype(BF16)
        u = dot(out_t, ybar)
        g = side_by_side(gate, at, size)
        done = (g * u).astype(BF16)
        cot_t = turned(cot[at : at + size].reshape(size * cols, width))
        back = dot(gate_weight[...], (cot_t * u * g * (1.0 - g)).astype(BF16))
        for r in range(size):
            lanes = slice(r * cols, (r + 1) * cols)
            update[at + r] = turned(done[:, lanes]).astype(BF16)
            dzg[at + r] = back[:, lanes]
    wait(start(out_sems, [(update, update_h), (dzg, dzg_h)]))


def grad_right_kernel(grad, left, after, out_h, ready, sems):
    leaving = []
    for h in range(ready.shape[-3]):
        values = dot(channel_matrix(grad, h), channel_matrix(left, h), ((0,), (0,)))
        put_channel(ready, h, values)
        leaving.append(leave(ready, out_h, h, sems.at[h]))
    wait(leaving)


def grad_left_kernel(grad, right, *refs):
    outs, ready = refs[:-1], refs[-1]
    n_col, share = ready.shape[1:3]
    for h in range(share):
        put_channel(ready, h, dot(channel_matrix(grad, h), channel_matrix(right, h)))
    for m, n, number in sources(outs[0].shape[0], len(outs)):
        outs[m][n] = ready[number // n_col, number % n_col]


def through_projection(plane, coef, weight, at, size, rows):
    hidden = plane.shape[0] // rows
    columns = []
    for r in range(size):
        g = plane[pl.ds(at + r, hidden, stride=rows), :]
        columns.append(
            jnp.concatenate(
                [(g * coef[at + r, part]).astype(BF16) for part in range(2)], axis=0
            )
        )
    return dot(weight, jnp.concatenate(columns, axis=1))


def back_left_kernel(n_chip, coef_h, dzg_h, zhat_h, inv_h, proj_h, *refs):
    pieces, (out, coef_right, zhat, inv) = refs[:-11], refs[-11:-7]
    coef, dzg, proj_weight, plane, sems, coef_sems, dzg_sems = refs[-7:]
    rows, width, cols = out.shape
    hidden = plane.shape[0] // rows
    groups = groups_of(rows)
    (small, *fetched) = start(
        sems,
        [
            (proj_h, proj_weight), (coef_h.at[:, pl.ds(2, 2)], coef_right), (zhat_h, zhat),
            (inv_h, inv),
        ],
    )
    blocks = [
        start(
            coef_sems,
            [
                (coef_h.at[pl.ds(at, size), pl.ds(0, 2)], coef.at[pl.ds(at, size)])
                for at, size in groups
            ],
        ),
        start(
            dzg_sems,
            [(dzg_h.at[pl.ds(at, size)], dzg.at[pl.ds(at, size)]) for at, size in groups],
        ),
    ]
    arrived = received(pieces, n_chip)
    length = plane.shape[0] // len(arrived)
    for number, piece in arrived:
        first = pl.multiple_of(number * length, length)
        plane[pl.ds(first, length), :] = piece.astype(F32).reshape(length, cols)
    small.wait()
    weight = proj_weight[:, : 2 * hidden]
    for n, (at, size) in enumerate(groups):
        wait([copies[n] for copies in blocks])
        back = through_projection(plane, coef, weight, at, size, rows)
        for r in range(size):
            out[at + r] = back[:, r * cols : (r + 1) * cols] + dzg[at + r]
    wait(fetched)


def back_kernel(
    grads, coef, zhat, inv, dzg, gain_h, proj_h, out_h,
    gain, proj_weight, out, plane, sems, out_sems,
):
    rows, cols, width = out.shape
    hidden = plane.shape[0] // rows
    groups = groups_of(rows)
    small = start(sems, [(gain_h, gain), (proj_h.at[:, pl.ds(2 * hidden, 2 * hidden)], proj_weight)])
    total = grads[0].astype(F32)
    for half in range(1, grads.shape[0]):
        total = total + grads[half].astype(F32)
    plane[...] = total.reshape(plane.shape)
    wait(small)
    gain_b = jnp.concatenate([down_lanes(gain[...], cols)] * groups[0][1], axis=1)
    weight = proj_weight[...]
    leaving = []
    for n, (at, size) in enumerate(groups):
        back = through_projection(plane, coef, weight, at, size, rows)
        dzh = (back + side_by_side(dzg, at, size)) * gain_b
        z = side_by_side(zhat, at, size)
        inverse = jnp.concatenate([inv[at + r : at + r + 1] for r in range(size)], axis=1)
        m1 = jnp.mean(dzh, axis=0, keepdims=True)
        m2 = jnp.mean(dzh * z, axis=0, keepdims=True)
        grad = ((dzh - m1 - z * m2) * inverse).astype(BF16)
        for r in range(size):
            out[at + r] = turned(grad[:, r * cols : (r + 1) * cols]).astype(BF16)
        copy = pltpu.make_async_copy(
            out.at[pl.ds(at, size)], out_h.at[pl.ds(at, size)], out_sems.at[n]
        )
        copy.start()
        leaving.append(copy)
    wait(leaving)


def call(kernel, outs, scratch, args, near=(), outs_near=(), flops=0, moved=0):
    here, far = (pl.BlockSpec(memory_space=space) for space in (pltpu.VMEM, pltpu.HBM))
    specs = [here if at in near else far for at in range(len(args))]
    return pl.pallas_call(
        kernel,
        out_shape=[
            out if at in outs_near else pltpu.HBM(out.shape, out.dtype)
            for at, out in enumerate(outs)
        ],
        in_specs=specs,
        out_specs=[here if at in outs_near else far for at in range(len(outs))],
        scratch_shapes=scratch,
        compiler_params=pltpu.CompilerParams(vmem_limit_bytes=24 * MIB),
        cost_estimate=pl.CostEstimate(flops=flops, bytes_accessed=moved, transcendentals=0),
    )(
        *[
            pltpu.with_memory_space_constraint(arg, pltpu.HBM) if spec is far else arg
            for arg, spec in zip(args, specs)
        ]
    )


def body(
    pair, mask, gain_in, bias_in, proj_weight, gate_weight,
    product_norm_gain, product_norm_bias, out_weight, cotangent,
):
    rows, cols, width = pair.shape
    hidden = out_weight.shape[0]
    n_half = lax.axis_size("half")
    n_row = lax.axis_size("row")
    n_core = lax.axis_size("core")
    n_col = lax.axis_size("col")
    n_chip = n_row * n_col
    n_line = n_row * n_core
    n_place = n_line * n_col
    within = ("row", "core", "col")
    share = hidden // n_place
    cells = rows * cols
    n_groups = len(groups_of(rows))
    mask_row = mask.reshape(1, -1)
    gain_in, bias_in = gain_in.reshape(1, -1), bias_in.reshape(1, -1)
    norm_gain, norm_bias = product_norm_gain.reshape(1, -1), product_norm_bias.reshape(1, -1)

    def shape(*dims, dtype=BF16):
        return jax.ShapeDtypeStruct(dims, dtype)

    def vmem(*dims, dtype=BF16):
        return pltpu.VMEM(dims, dtype)

    def sems(count):
        return pltpu.SemaphoreType.DMA((count,))

    def exchange(values):
        return lax.all_to_all(values, within, split_axis=0, concat_axis=0, tiled=True)

    def exchange_all(values):
        flat = values.reshape(n_half * n_place, share, rows, cols)
        return lax.all_to_all(
            flat, ("half", *within), split_axis=0, concat_axis=0, tiled=True
        )

    def permute(values, axes, size, distance):
        return lax.ppermute(values, axes, [(at, at ^ distance) for at in range(size)])

    def exchange_pieces(pieces):
        first = [pieces[0]]
        first += [permute(pieces[m], ("core",), n_core, m) for m in range(1, n_core)]
        second = [
            permute(jnp.stack([piece[n] for piece in first]), ("row", "col"), n_chip, n)
            for n in range(n_chip - 1, 0, -1)
        ]
        return tuple(first + second[::-1])

    mask_s = pltpu.SMEM(mask.shape, jnp.int32)
    mask_v = vmem(*mask_row.shape, dtype=jnp.int32)
    vector = vmem(1, width, dtype=F32)
    plane = vmem(hidden * rows, cols, dtype=F32)
    block = vmem(rows, cols, width)
    wide = vmem(rows, width, cols, dtype=F32)
    square = vmem(width, hidden)
    proj_v = vmem(width, 4 * hidden)
    coef_v = vmem(rows, 2, hidden, cols, dtype=F32)
    pieces_shape = (shape(n_chip, share, rows, cols),) * n_core
    n_pieces = n_core + n_chip - 1

    def front(part, outs, scratch, near):
        return call(
            functools.partial(front_kernel, part, len(outs)),
            outs,
            [
                block, mask_s, mask_v, vector, vector, vmem(width, 2 * hidden), plane,
                sems(5), sems(n_groups), *scratch,
            ],
            (pair, mask, mask_row, gain_in, bias_in, proj_weight),
            outs_near=near,
            flops=2 * cells * width * 3 * hidden,
            moved=5 * cells * width,
        )

    everywhere = vmem(n_place, share, rows, cols)
    (right,) = front(
        2,
        (shape(n_half, n_place, share, rows, cols),),
        [everywhere, pltpu.SemaphoreType.DMA((n_half, n_place // math.gcd(n_place, 4)))],
        (),
    )
    right = exchange_all(right).reshape(n_half, n_line, n_col, share, rows, cols)
    left = exchange_pieces(tuple(front(0, pieces_shape, [], range(n_core))))
    zhat, inv, gate, dxh = call(
        side_kernel,
        (
            shape(rows, width, cols, dtype=F32),
            shape(rows, cols, dtype=F32),
            shape(rows, width, cols, dtype=F32),
            shape(hidden * rows, cols, dtype=F32),
        ),
        [
            block, block, vector, vector, square, vector, square,
            wide, vmem(rows, cols, dtype=F32), wide, plane, sems(7), sems(4),
        ],
        (pair, cotangent, gain_in, bias_in, gate_weight, norm_gain, out_weight),
        flops=2 * cells * width * 4 * hidden,
        moved=16 * cells * width,
    )
    product, left = call(
        functools.partial(product_kernel, n_chip),
        (shape(n_line, n_col, share, rows, cols), shape(n_line, n_col, share, rows, cols)),
        [vmem(n_line, n_col, share, rows, cols), sems(share)],
        (right, inv, *left),
        near=(0, *range(2, 2 + n_pieces)),
        outs_near=(1,),
        flops=2 * share * n_half * (n_line * rows) ** 2 * n_col * cols,
        moved=8 * cells * hidden,
    )
    spread = vmem(hidden, rows, cols, dtype=F32)
    coef, dxh = call(
        factors_kernel,
        (shape(rows, 4, hidden, cols, dtype=F32), shape(hidden, rows, cols, dtype=F32)),
        [
            wide, mask_s, mask_v, vector, vector, proj_v, vmem(rows, 4, hidden, cols, dtype=F32),
            sems(6), sems(n_groups), sems(1),
        ],
        (
            zhat, mask, mask_row, gain_in, bias_in, proj_weight,
            dxh.reshape(hidden, rows, cols), product,
        ),
        outs_near=(1,),
        flops=2 * cells * width * 5 * hidden,
        moved=20 * cells * width,
    )
    product = exchange(product.reshape(n_place, share, rows, cols)).reshape(hidden, rows, cols)
    (sent,) = call(
        middle_kernel,
        (shape(hidden, rows, cols),),
        [spread, vmem(hidden, rows, cols), sems(hidden // math.gcd(hidden, 32))],
        (product, dxh),
        near=(0, 1),
        flops=20 * cells * hidden,
        moved=8 * cells * hidden,
    )
    grad = exchange(sent.reshape(n_place, share, rows, cols))
    grad = grad.reshape(n_line, n_col, share, rows, cols)
    update, dzg = call(
        update_kernel,
        (shape(rows, cols, width), shape(rows, width, cols, dtype=F32)),
        [wide, block, vector, vector, square, square, block, wide, plane, sems(6), sems(2)],
        (product, gate, cotangent, norm_gain, norm_bias, out_weight, gate_weight, sent),
        near=(0,),
        flops=2 * cells * width * 3 * hidden,
        moved=14 * cells * hidden,
    )
    (grad_right,) = call(
        grad_right_kernel,
        (shape(n_half, n_line, n_col, share, rows, cols),),
        [vmem(n_half, n_line, n_col, share, rows, cols), sems(share)],
        (grad, left, dzg),
        near=(0, 1),
        flops=2 * share * n_half * (n_line * rows) ** 2 * n_col * cols,
        moved=8 * cells * hidden,
    )
    grad_right = exchange_all(grad_right).reshape(n_half, n_place, share, rows, cols)
    grad_left = call(
        grad_left_kernel,
        pieces_shape,
        [vmem(n_line, n_col, share, rows, cols)],
        (grad, right),
        near=(0, 1),
        outs_near=range(n_core),
        flops=2 * share * n_half * (n_line * rows) ** 2 * n_col * cols,
        moved=8 * cells * hidden,
    )
    grad_left = exchange_pieces(tuple(grad_left))
    dzg, coef, zhat, inv = call(
        functools.partial(back_left_kernel, n_chip),
        (
            shape(rows, width, cols, dtype=F32),
            shape(rows, 2, hidden, cols, dtype=F32),
            shape(rows, width, cols, dtype=F32),
            shape(rows, cols, dtype=F32),
        ),
        [coef_v, wide, proj_v, plane, sems(4), sems(n_groups), sems(n_groups)],
        (coef, dzg, zhat, inv, proj_weight, *grad_left),
        near=tuple(range(5, 5 + n_pieces)),
        outs_near=range(4),
        flops=2 * cells * width * 2 * hidden,
        moved=18 * cells * width,
    )
    (grad_pair,) = call(
        back_kernel,
        (shape(rows, cols, width),),
        [vector, vmem(width, 2 * hidden), block, plane, sems(2), sems(n_groups)],
        (grad_right, coef, zhat, inv, dzg, gain_in, proj_weight),
        near=range(5),
        flops=2 * cells * width * 3 * hidden,
        moved=22 * cells * width,
    )
    return (update, grad_pair)


def solution(mesh):
    n_grp, n_row, n_col = (mesh.shape[name] for name in ("grp", "row", "col"))
    n_half = math.gcd(n_row, 2)
    n_core = math.gcd(n_row // n_half, 2)
    split = jax.sharding.Mesh(
        mesh.devices.reshape(n_grp, n_half, n_row // (n_half * n_core), n_core, n_col),
        ("grp", "half", "row", "core", "col"),
    )
    cells = P(("grp", "half", "row", "core"), "col", None)
    return jax.shard_map(
        body,
        mesh=split,
        in_specs=(cells, P("grp"), P(), P(), P(), P(), P(), P(), P(), cells),
        out_specs=(cells, cells),
        check_vma=False,
    )
```

```python
import functools
import math

import jax
import jax.numpy as jnp
from jax import lax
from jax.experimental import pallas as pl
from jax.experimental.pallas import tpu as pltpu
from jax.sharding import PartitionSpec as P

EPS = 1e-05
F32 = jnp.float32
BF16 = jnp.bfloat16
MIB = 1 << 20


def dot(a, b, over=((1,), (0,))):
    return lax.dot_general(a, b, (over, ((), ())), preferred_element_type=F32)


def eye(size):
    down = lax.broadcasted_iota(jnp.int32, (size, size), 0)
    across = lax.broadcasted_iota(jnp.int32, (size, size), 1)
    return (down == across).astype(F32).astype(BF16)


def turned(values):
    return dot(eye(values.shape[1]), values, ((1,), (1,)))


def down_lanes(vector, lanes):
    return jnp.broadcast_to(vector, (lanes, vector.shape[1])).T


def turned_weight(weight):
    c, m = weight.shape
    return jnp.concatenate(
        [turned(weight[:, at : at + c]) for at in range(0, m, c)], axis=0
    ).astype(BF16)


def sigmoid(values):
    return 0.5 + 0.5 * jnp.tanh(0.5 * values)


def normalized(values):
    mean = jnp.mean(values, axis=0, keepdims=True)
    centred = values - mean
    var = jnp.mean(centred * centred, axis=0, keepdims=True)
    inverse = lax.rsqrt(var + EPS)
    return centred * inverse, inverse


def start(sems, copies):
    running = [
        pltpu.make_async_copy(source, target, sems.at[at])
        for at, (source, target) in enumerate(copies)
    ]
    for copy in running:
        copy.start()
    return running


def wait(copies):
    for copy in copies:
        copy.wait()


def groups_of(rows):
    size = math.gcd(rows, 4)
    return [(at, size) for at in range(0, rows, size)]


def side_by_side(ref, at, size):
    return jnp.concatenate([ref[at + r] for r in range(size)], axis=1)


def pair_mask(mask_s, mask_v, at, size, rows, cols):
    here = lax.axis_index("half")
    for name in ("row", "core"):
        here = here * lax.axis_size(name) + lax.axis_index(name)
    first_row = here * rows + at
    first_col = pl.multiple_of(lax.axis_index("col") * cols, cols)
    col_mask = mask_v[:, pl.ds(first_col, cols)].astype(F32)
    return jnp.concatenate(
        [col_mask * mask_s[first_row + r].astype(F32) for r in range(size)], axis=1
    )


def sources(n_chip, n_core):
    n_col = lax.axis_size("col")
    core = lax.axis_index("core")
    chip = lax.axis_index("row") * n_col + lax.axis_index("col")
    found = []
    for n in range(n_chip):
        other = chip ^ n
        for m in range(n_core):
            line = other // n_col * n_core + (core ^ m)
            found.append((m, n, line * n_col + other % n_col))
    return found


def received(refs, n_chip):
    n_core = len(refs) - n_chip + 1
    return [
        (number, refs[m][0] if n == 0 else refs[n_core + n - 1][m])
        for m, n, number in sources(n_chip, n_core)
    ]


def front_kernel(
    part, n_out, pair_h, mask_h, mask_row_h, gain_h, bias_h, proj_h, *refs
):
    outs = refs[:n_out]
    pair, mask_s, mask_v, gain, bias, proj_weight, plane, sems, row_sems, *more = refs[n_out:]
    rows, cols, width = pair.shape
    hidden = plane.shape[0] // rows
    groups = groups_of(rows)
    blocks = start(
        row_sems,
        [(pair_h.at[pl.ds(at, size)], pair.at[pl.ds(at, size)]) for at, size in groups],
    )
    small = start(
        sems,
        [
            (gain_h, gain), (bias_h, bias),
            (proj_h.at[:, pl.ds(part * hidden, 2 * hidden)], proj_weight),
            (mask_h, mask_s), (mask_row_h, mask_v),
        ],
    )
    wait(small)
    gain_b = jnp.concatenate([down_lanes(gain[...], cols)] * groups[0][1], axis=1)
    bias_b = jnp.concatenate([down_lanes(bias[...], cols)] * groups[0][1], axis=1)
    weight = turned_weight(proj_weight[...])
    for (at, size), block in zip(groups, blocks):
        block.wait()
        zhat, _ = normalized(turned(pair[at : at + size].reshape(size * cols, width)))
        zbar = (zhat * gain_b + bias_b).astype(BF16)
        pm = pair_mask(mask_s, mask_v, at, size, rows, cols)
        values = sigmoid(dot(weight[:hidden], zbar)) * dot(weight[hidden:], zbar) * pm
        for r in range(size):
            plane[pl.ds(at + r, hidden, stride=rows), :] = values[:, r * cols : (r + 1) * cols]
    if n_out > 1:
        give_pieces(plane, outs)
    else:
        give_all(plane, outs[0], *more)


def give_all(plane, out_h, ready, sems):
    n_place = ready.shape[0]
    size = math.gcd(n_place, 4)
    length = plane.shape[0] // n_place * size
    leaving = []
    for n, at in enumerate(range(0, n_place, size)):
        values = plane[n * length : (n + 1) * length]
        ready[at : at + size] = values.reshape(size, *ready.shape[1:]).astype(BF16)
        for half in range(out_h.shape[0]):
            copy = pltpu.make_async_copy(
                ready.at[pl.ds(at, size)], out_h.at[half, pl.ds(at, size)], sems.at[half, n]
            )
            copy.start()
            leaving.append(copy)
    wait(leaving)


def give_pieces(plane, outs):
    n_chip = outs[0].shape[0]
    length = plane.shape[0] // (len(outs) * n_chip)
    for m, n, number in sources(n_chip, len(outs)):
        first = pl.multiple_of(number * length, length)
        values = plane[pl.ds(first, length), :]
        outs[m][n] = values.reshape(outs[m].shape[1:]).astype(BF16)


def side_kernel(
    pair_h, cot_h, gain_h, bias_h, gate_h, norm_gain_h, out_w_h,
    zhat_h, inv_h, gate_out_h, dxh_h,
    pair, cot, gain, bias, gate_weight, norm_gain, out_weight,
    zhat_out, inv_out, gate_out, dxh_out, in_sems, out_sems,
):
    rows, cols, width = pair.shape
    hidden = out_weight.shape[0]
    wait(
        start(
            in_sems,
            [
                (pair_h, pair), (cot_h, cot), (gain_h, gain), (bias_h, bias),
                (gate_h, gate_weight), (norm_gain_h, norm_gain), (out_w_h, out_weight),
            ],
        )
    )
    groups = groups_of(rows)
    gain_b = jnp.concatenate([down_lanes(gain[...], cols)] * groups[0][1], axis=1)
    bias_b = jnp.concatenate([down_lanes(bias[...], cols)] * groups[0][1], axis=1)
    norm_gain_b = jnp.concatenate([down_lanes(norm_gain[...], cols)] * groups[0][1], axis=1)
    gate_t = turned_weight(gate_weight[...])
    for at, size in groups:
        zhat, inverse = normalized(turned(pair[at : at + size].reshape(size * cols, width)))
        zbar = (zhat * gain_b + bias_b).astype(BF16)
        gate = sigmoid(dot(gate_t, zbar))
        cot_t = turned(cot[at : at + size].reshape(size * cols, width))
        dxh = dot(out_weight[...], (cot_t * gate).astype(BF16)) * norm_gain_b
        dxh = dxh - jnp.mean(dxh, axis=0, keepdims=True)
        for r in range(size):
            lanes = slice(r * cols, (r + 1) * cols)
            zhat_out[at + r] = zhat[:, lanes]
            inv_out[at + r : at + r + 1] = inverse[:, lanes]
            gate_out[at + r] = gate[:, lanes]
            dxh_out[pl.ds(at + r, hidden, stride=rows), :] = dxh[:, lanes]
    wait(
        start(
            out_sems,
            [(zhat_out, zhat_h), (inv_out, inv_h), (gate_out, gate_out_h), (dxh_out, dxh_h)],
        )
    )


def factors_kernel(
    zhat_h, mask_h, mask_row_h, gain_h, bias_h, proj_h, dxh_h, after, coef_h, dxh,
    zhat, mask_s, mask_v, gain, bias, proj_weight, coef, in_sems, out_sems, fetch_sems,
):
    rows, width, cols = zhat.shape
    hidden = coef.shape[2]
    fetched = start(fetch_sems, [(dxh_h, dxh)])
    wait(
        start(
            in_sems,
            [
                (zhat_h, zhat), (mask_h, mask_s), (mask_row_h, mask_v), (gain_h, gain),
                (bias_h, bias), (proj_h, proj_weight),
            ],
        )
    )
    groups = groups_of(rows)
    gain_b = jnp.concatenate([down_lanes(gain[...], cols)] * groups[0][1], axis=1)
    bias_b = jnp.concatenate([down_lanes(bias[...], cols)] * groups[0][1], axis=1)
    weight = turned_weight(proj_weight[...])
    leaving = []
    for n, (at, size) in enumerate(groups):
        zbar = (side_by_side(zhat, at, size) * gain_b + bias_b).astype(BF16)
        pm = pair_mask(mask_s, mask_v, at, size, rows, cols)
        for part in (0, 2):
            s = sigmoid(dot(weight[part * hidden : (part + 1) * hidden], zbar))
            q = dot(weight[(part + 1) * hidden : (part + 2) * hidden], zbar)
            second = pm * s
            first = second * q * (1.0 - s)
            for r in range(size):
                lanes = slice(r * cols, (r + 1) * cols)
                coef[at + r, part] = first[:, lanes]
                coef[at + r, part + 1] = second[:, lanes]
        copy = pltpu.make_async_copy(
            coef.at[pl.ds(at, size)], coef_h.at[pl.ds(at, size)], out_sems.at[n]
        )
        copy.start()
        leaving.append(copy)
    wait(leaving + fetched)


def channel_matrix(ref, at):
    *_, n_col, _, rows, cols = ref.shape
    lead = (slice(None),) * (len(ref.shape) - 4)
    return jnp.concatenate(
        [ref[(*lead, c, at)].reshape(-1, cols) for c in range(n_col)], axis=1
    )


def put_channel(ref, at, values):
    *shape, n_col, _, rows, cols = ref.shape
    lead = (slice(None),) * len(shape)
    values = values.astype(BF16)
    for c in range(n_col):
        ref[(*lead, c, at)] = values[:, c * cols : (c + 1) * cols].reshape(*shape, rows, cols)


def leave(ready, out_h, at, sem):
    lead = (slice(None),) * (len(ready.shape) - 3)
    copy = pltpu.make_async_copy(
        ready.at[(*lead, pl.ds(at, 1))], out_h.at[(*lead, pl.ds(at, 1))], sem
    )
    copy.start()
    return copy


def product_kernel(n_chip, right, after, *refs):
    pieces, (out_h, left_h, left, ready, sems, left_sem) = refs[:-6], refs[-6:]
    n_col, share = left.shape[1:3]
    for number, piece in received(pieces, n_chip):
        left[number // n_col, number % n_col] = piece
    leaving = start(left_sem, [(left, left_h)])
    for h in range(share):
        values = dot(channel_matrix(left, h), channel_matrix(right, h), ((1,), (1,)))
        put_channel(ready, h, values)
        leaving.append(leave(ready, out_h, h, sems.at[h]))
    wait(leaving)


def middle_kernel(product, dxh, out_h, xhat, ready, sems):
    hidden = product.shape[0]
    values = product[...].astype(F32)
    mean = jnp.sum(values, axis=0) * (1.0 / hidden)
    centred = values - mean[None]
    var = jnp.sum(centred * centred, axis=0) * (1.0 / hidden)
    inverse = lax.rsqrt(var + EPS)
    xhat[...] = centred * inverse[None]
    m2 = jnp.sum(dxh[...] * xhat[...], axis=0) * (1.0 / hidden)
    leaving = []
    size = math.gcd(hidden, 32)
    for n, at in enumerate(range(0, hidden, size)):
        part = slice(at, at + size)
        ready[part] = ((dxh[part] - xhat[part] * m2[None]) * inverse[None]).astype(BF16)
        copy = pltpu.make_async_copy(
            ready.at[pl.ds(at, size)], out_h.at[pl.ds(at, size)], sems.at[n]
        )
        copy.start()
        leaving.append(copy)
    wait(leaving)


def update_kernel(
    product, gate_h, cot_h, norm_gain_h, norm_bias_h, out_w_h, gate_w_h, left_h, after, update_h, dzg_h,
    left,
    gate, cot, norm_gain, norm_bias, out_weight, gate_weight, update, dzg, spread,
    in_sems, out_sems, fetch_sems,
):
    hidden, rows, cols = product.shape
    width = cot.shape[2]
    fetched = start(fetch_sems, [(left_h, left)])
    copies = start(
        in_sems,
        [
            (gate_h, gate), (cot_h, cot), (norm_gain_h, norm_gain), (norm_bias_h, norm_bias),
            (out_w_h, out_weight), (gate_w_h, gate_weight),
        ],
    )
    spread[...] = product[...].astype(F32).reshape(hidden * rows, cols)
    wait(copies)
    groups = groups_of(rows)
    norm_gain_b = jnp.concatenate([down_lanes(norm_gain[...], cols)] * groups[0][1], axis=1)
    norm_bias_b = jnp.concatenate([down_lanes(norm_bias[...], cols)] * groups[0][1], axis=1)
    out_t = turned_weight(out_weight[...])
    for at, size in groups:
        xhat, _ = normalized(
            jnp.concatenate(
                [spread[pl.ds(at + r, hidden, stride=rows), :] for r in range(size)], axis=1
            )
        )
        ybar = (xhat * norm_gain_b + norm_bias_b).astype(BF16)
        u = dot(out_t, ybar)
        g = side_by_side(gate, at, size)
        done = (g * u).astype(BF16)
        cot_t = turned(cot[at : at + size].reshape(size * cols, width))
        back = dot(gate_weight[...], (cot_t * u * g * (1.0 - g)).astype(BF16))
        for r in range(size):
            lanes = slice(r * cols, (r + 1) * cols)
            update[at + r] = turned(done[:, lanes]).astype(BF16)
            dzg[at + r] = back[:, lanes]
    wait(fetched + start(out_sems, [(update, update_h), (dzg, dzg_h)]))


def grad_right_kernel(grad, left, after, out_h, ready, sems):
    leaving = []
    for h in range(ready.shape[-3]):
        values = dot(channel_matrix(grad, h), channel_matrix(left, h), ((0,), (0,)))
        put_channel(ready, h, values)
        leaving.append(leave(ready, out_h, h, sems.at[h]))
    wait(leaving)


def grad_left_kernel(grad, right, *refs):
    outs, ready = refs[:-1], refs[-1]
    n_col, share = ready.shape[1:3]
    for h in range(share):
        put_channel(ready, h, dot(channel_matrix(grad, h), channel_matrix(right, h)))
    for m, n, number in sources(outs[0].shape[0], len(outs)):
        outs[m][n] = ready[number // n_col, number % n_col]


def back_kernel(n_chip, grads, coef_h, zhat_h, inv_h, dzg_h, gain_h, proj_h, *refs):
    pieces, out_h = refs[:-15], refs[-15]
    (
        coef, zhat, inv, dzg, gain, proj_weight, out, left, right,
        sems, coef_sems, zhat_sems, dzg_sems, out_sems,
    ) = refs[-14:]
    rows, cols, width = out.shape
    hidden = left.shape[0] // rows
    groups = groups_of(rows)
    small = start(sems, [(gain_h, gain), (proj_h, proj_weight), (inv_h, inv)])
    blocks = []
    for n, (at, size) in enumerate(groups):
        part = pl.ds(at, size)
        blocks.append(
            [
                pltpu.make_async_copy(source.at[part], target.at[part], sem.at[n])
                for source, target, sem in (
                    (coef_h, coef, coef_sems), (zhat_h, zhat, zhat_sems), (dzg_h, dzg, dzg_sems)
                )
            ]
        )
        for copy in blocks[-1]:
            copy.start()
    arrived = received(pieces, n_chip)
    length = left.shape[0] // len(arrived)
    for number, piece in arrived:
        first = pl.multiple_of(number * length, length)
        left[pl.ds(first, length), :] = piece.astype(F32).reshape(length, cols)
    total = grads[0].astype(F32)
    for half in range(1, grads.shape[0]):
        total = total + grads[half].astype(F32)
    right[...] = total.reshape(right.shape)
    wait(small)
    gain_b = jnp.concatenate([down_lanes(gain[...], cols)] * groups[0][1], axis=1)
    leaving = []
    for n, (at, size) in enumerate(groups):
        wait(blocks[n])
        columns = []
        for r in range(size):
            gl = left[pl.ds(at + r, hidden, stride=rows), :]
            gr = right[pl.ds(at + r, hidden, stride=rows), :]
            columns.append(
                jnp.concatenate(
                    [
                        (g * coef[at + r, part]).astype(BF16)
                        for part, g in enumerate((gl, gl, gr, gr))
                    ],
                    axis=0,
                )
            )
        back = dot(proj_weight[...], jnp.concatenate(columns, axis=1))
        dzh = (back + side_by_side(dzg, at, size)) * gain_b
        z = side_by_side(zhat, at, size)
        inverse = jnp.concatenate([inv[at + r : at + r + 1] for r in range(size)], axis=1)
        m1 = jnp.mean(dzh, axis=0, keepdims=True)
        m2 = jnp.mean(dzh * z, axis=0, keepdims=True)
        grad = ((dzh - m1 - z * m2) * inverse).astype(BF16)
        for r in range(size):
            out[at + r] = turned(grad[:, r * cols : (r + 1) * cols]).astype(BF16)
        copy = pltpu.make_async_copy(
            out.at[pl.ds(at, size)], out_h.at[pl.ds(at, size)], out_sems.at[n]
        )
        copy.start()
        leaving.append(copy)
    wait(leaving)


def call(kernel, outs, scratch, args, near=(), outs_near=(), flops=0, moved=0):
    here, far = (pl.BlockSpec(memory_space=space) for space in (pltpu.VMEM, pltpu.HBM))
    specs = [here if at in near else far for at in range(len(args))]
    return pl.pallas_call(
        kernel,
        out_shape=[
            out if at in outs_near else pltpu.HBM(out.shape, out.dtype)
            for at, out in enumerate(outs)
        ],
        in_specs=specs,
        out_specs=[here if at in outs_near else far for at in range(len(outs))],
        scratch_shapes=scratch,
        compiler_params=pltpu.CompilerParams(vmem_limit_bytes=16 * MIB),
        cost_estimate=pl.CostEstimate(flops=flops, bytes_accessed=moved, transcendentals=0),
    )(
        *[
            pltpu.with_memory_space_constraint(arg, pltpu.HBM) if spec is far else arg
            for arg, spec in zip(args, specs)
        ]
    )


def body(
    pair, mask, gain_in, bias_in, proj_weight, gate_weight,
    product_norm_gain, product_norm_bias, out_weight, cotangent,
):
    rows, cols, width = pair.shape
    hidden = out_weight.shape[0]
    n_half = lax.axis_size("half")
    n_row = lax.axis_size("row")
    n_core = lax.axis_size("core")
    n_col = lax.axis_size("col")
    n_chip = n_row * n_col
    n_line = n_row * n_core
    n_place = n_line * n_col
    within = ("row", "core", "col")
    share = hidden // n_place
    cells = rows * cols
    n_groups = len(groups_of(rows))
    mask_row = mask.reshape(1, -1)
    gain_in, bias_in = gain_in.reshape(1, -1), bias_in.reshape(1, -1)
    norm_gain, norm_bias = product_norm_gain.reshape(1, -1), product_norm_bias.reshape(1, -1)

    def shape(*dims, dtype=BF16):
        return jax.ShapeDtypeStruct(dims, dtype)

    def vmem(*dims, dtype=BF16):
        return pltpu.VMEM(dims, dtype)

    def sems(count):
        return pltpu.SemaphoreType.DMA((count,))

    def exchange(values):
        return lax.all_to_all(values, within, split_axis=0, concat_axis=0, tiled=True)

    def exchange_all(values):
        flat = values.reshape(n_half * n_place, share, rows, cols)
        return lax.all_to_all(
            flat, ("half", *within), split_axis=0, concat_axis=0, tiled=True
        )

    def permute(values, axes, size, distance):
        return lax.ppermute(values, axes, [(at, at ^ distance) for at in range(size)])

    def exchange_pieces(pieces):
        first = [pieces[0]]
        first += [permute(pieces[m], ("core",), n_core, m) for m in range(1, n_core)]
        second = [
            permute(jnp.stack([piece[n] for piece in first]), ("row", "col"), n_chip, n)
            for n in range(n_chip - 1, 0, -1)
        ]
        return tuple(first + second[::-1])

    mask_s = pltpu.SMEM(mask.shape, jnp.int32)
    mask_v = vmem(*mask_row.shape, dtype=jnp.int32)
    vector = vmem(1, width, dtype=F32)
    plane = vmem(hidden * rows, cols, dtype=F32)
    block = vmem(rows, cols, width)
    wide = vmem(rows, width, cols, dtype=F32)
    square = vmem(width, hidden)
    proj_v = vmem(width, 4 * hidden)
    pieces_shape = (shape(n_chip, share, rows, cols),) * n_core
    n_pieces = n_core + n_chip - 1

    def front(part, outs, scratch, near):
        return call(
            functools.partial(front_kernel, part, len(outs)),
            outs,
            [
                block, mask_s, mask_v, vector, vector, vmem(width, 2 * hidden), plane,
                sems(5), sems(n_groups), *scratch,
            ],
            (pair, mask, mask_row, gain_in, bias_in, proj_weight),
            outs_near=near,
            flops=2 * cells * width * 3 * hidden,
            moved=5 * cells * width,
        )

    everywhere = vmem(n_place, share, rows, cols)
    (right,) = front(
        2,
        (shape(n_half, n_place, share, rows, cols),),
        [everywhere, pltpu.SemaphoreType.DMA((n_half, n_place // math.gcd(n_place, 4)))],
        (),
    )
    right = exchange_all(right).reshape(n_half, n_line, n_col, share, rows, cols)
    left = exchange_pieces(tuple(front(0, pieces_shape, [], range(n_core))))
    zhat, inv, gate, dxh = call(
        side_kernel,
        (
            shape(rows, width, cols, dtype=F32),
            shape(rows, cols, dtype=F32),
            shape(rows, width, cols, dtype=F32),
            shape(hidden * rows, cols, dtype=F32),
        ),
        [
            block, block, vector, vector, square, vector, square,
            wide, vmem(rows, cols, dtype=F32), wide, plane, sems(7), sems(4),
        ],
        (pair, cotangent, gain_in, bias_in, gate_weight, norm_gain, out_weight),
        flops=2 * cells * width * 4 * hidden,
        moved=16 * cells * width,
    )
    product, left = call(
        functools.partial(product_kernel, n_chip),
        (shape(n_line, n_col, share, rows, cols), shape(n_line, n_col, share, rows, cols)),
        [
            vmem(n_line, n_col, share, rows, cols), vmem(n_line, n_col, share, rows, cols),
            sems(share), sems(1),
        ],
        (right, inv, *left),
        near=(0, *range(2, 2 + n_pieces)),
        flops=2 * share * n_half * (n_line * rows) ** 2 * n_col * cols,
        moved=8 * cells * hidden,
    )
    spread = vmem(hidden, rows, cols, dtype=F32)
    coef, dxh = call(
        factors_kernel,
        (shape(rows, 4, hidden, cols, dtype=F32), shape(hidden, rows, cols, dtype=F32)),
        [
            wide, mask_s, mask_v, vector, vector, proj_v, vmem(rows, 4, hidden, cols, dtype=F32),
            sems(6), sems(n_groups), sems(1),
        ],
        (
            zhat, mask, mask_row, gain_in, bias_in, proj_weight,
            dxh.reshape(hidden, rows, cols), product,
        ),
        outs_near=(1,),
        flops=2 * cells * width * 5 * hidden,
        moved=20 * cells * width,
    )
    product = exchange(product.reshape(n_place, share, rows, cols)).reshape(hidden, rows, cols)
    (sent,) = call(
        middle_kernel,
        (shape(hidden, rows, cols),),
        [spread, vmem(hidden, rows, cols), sems(hidden // math.gcd(hidden, 32))],
        (product, dxh),
        near=(0, 1),
        flops=20 * cells * hidden,
        moved=8 * cells * hidden,
    )
    grad = exchange(sent.reshape(n_place, share, rows, cols))
    grad = grad.reshape(n_line, n_col, share, rows, cols)
    update, dzg, left = call(
        update_kernel,
        (
            shape(rows, cols, width),
            shape(rows, width, cols, dtype=F32),
            shape(n_line, n_col, share, rows, cols),
        ),
        [
            wide, block, vector, vector, square, square, block, wide, plane,
            sems(6), sems(2), sems(1),
        ],
        (product, gate, cotangent, norm_gain, norm_bias, out_weight, gate_weight, left, sent),
        near=(0,),
        outs_near=(2,),
        flops=2 * cells * width * 3 * hidden,
        moved=14 * cells * hidden,
    )
    (grad_right,) = call(
        grad_right_kernel,
        (shape(n_half, n_line, n_col, share, rows, cols),),
        [vmem(n_half, n_line, n_col, share, rows, cols), sems(share)],
        (grad, left, dzg),
        near=(0, 1),
        flops=2 * share * n_half * (n_line * rows) ** 2 * n_col * cols,
        moved=8 * cells * hidden,
    )
    grad_right = exchange_all(grad_right).reshape(n_half, n_place, share, rows, cols)
    grad_left = call(
        grad_left_kernel,
        pieces_shape,
        [vmem(n_line, n_col, share, rows, cols)],
        (grad, right),
        near=(0, 1),
        outs_near=range(n_core),
        flops=2 * share * n_half * (n_line * rows) ** 2 * n_col * cols,
        moved=8 * cells * hidden,
    )
    grad_left = exchange_pieces(tuple(grad_left))
    (grad_pair,) = call(
        functools.partial(back_kernel, n_chip),
        (shape(rows, cols, width),),
        [
            vmem(rows, 4, hidden, cols, dtype=F32), wide, vmem(rows, cols, dtype=F32), wide,
            vector, proj_v, block, plane, plane,
            sems(3), sems(n_groups), sems(n_groups), sems(n_groups), sems(n_groups),
        ],
        (grad_right, coef, zhat, inv, dzg, gain_in, proj_weight, *grad_left),
        near=(0, *range(7, 7 + n_pieces)),
        flops=2 * cells * width * 5 * hidden,
        moved=30 * cells * width,
    )
    return (update, grad_pair)


def solution(mesh):
    n_grp, n_row, n_col = (mesh.shape[name] for name in ("grp", "row", "col"))
    n_half = math.gcd(n_row, 2)
    n_core = math.gcd(n_row // n_half, 2)
    split = jax.sharding.Mesh(
        mesh.devices.reshape(n_grp, n_half, n_row // (n_half * n_core), n_core, n_col),
        ("grp", "half", "row", "core", "col"),
    )
    cells = P(("grp", "half", "row", "core"), "col", None)
    return jax.shard_map(
        body,
        mesh=split,
        in_specs=(cells, P("grp"), P(), P(), P(), P(), P(), P(), P(), cells),
        out_specs=(cells, cells),
        check_vma=False,
    )
```

```python
import functools
import math

import jax
import jax.numpy as jnp
from jax import lax
from jax.experimental import pallas as pl
from jax.experimental.pallas import tpu as pltpu
from jax.sharding import PartitionSpec as P

EPS = 1e-05
F32 = jnp.float32
BF16 = jnp.bfloat16
MIB = 1 << 20


def dot(a, b, over=((1,), (0,))):
    return lax.dot_general(a, b, (over, ((), ())), preferred_element_type=F32)


def eye(size):
    down = lax.broadcasted_iota(jnp.int32, (size, size), 0)
    across = lax.broadcasted_iota(jnp.int32, (size, size), 1)
    return (down == across).astype(F32).astype(BF16)


def turned(values):
    return dot(eye(values.shape[1]), values, ((1,), (1,)))


def down_lanes(vector, lanes):
    return jnp.broadcast_to(vector, (lanes, vector.shape[1])).T


def turned_weight(weight):
    c, m = weight.shape
    return jnp.concatenate(
        [turned(weight[:, at : at + c]) for at in range(0, m, c)], axis=0
    ).astype(BF16)


def sigmoid(values):
    return 0.5 + 0.5 * jnp.tanh(0.5 * values)


def normalized(values):
    mean = jnp.mean(values, axis=0, keepdims=True)
    centred = values - mean
    var = jnp.mean(centred * centred, axis=0, keepdims=True)
    inverse = lax.rsqrt(var + EPS)
    return centred * inverse, inverse


def start(sems, copies):
    running = [
        pltpu.make_async_copy(source, target, sems.at[at])
        for at, (source, target) in enumerate(copies)
    ]
    for copy in running:
        copy.start()
    return running


def wait(copies):
    for copy in copies:
        copy.wait()


def groups_of(rows):
    size = math.gcd(rows, 4)
    return [(at, size) for at in range(0, rows, size)]


def side_by_side(ref, at, size):
    return jnp.concatenate([ref[at + r] for r in range(size)], axis=1)


def pair_mask(mask_s, mask_v, at, size, rows, cols):
    here = lax.axis_index("half")
    for name in ("row", "core"):
        here = here * lax.axis_size(name) + lax.axis_index(name)
    first_row = here * rows + at
    first_col = pl.multiple_of(lax.axis_index("col") * cols, cols)
    col_mask = mask_v[:, pl.ds(first_col, cols)].astype(F32)
    return jnp.concatenate(
        [col_mask * mask_s[first_row + r].astype(F32) for r in range(size)], axis=1
    )


def sources(n_chip, n_core):
    n_col = lax.axis_size("col")
    core = lax.axis_index("core")
    chip = lax.axis_index("row") * n_col + lax.axis_index("col")
    found = []
    for n in range(n_chip):
        other = chip ^ n
        for m in range(n_core):
            line = other // n_col * n_core + (core ^ m)
            found.append((m, n, line * n_col + other % n_col))
    return found


def received(refs, n_chip):
    n_core = len(refs) - n_chip + 1
    return [
        (number, refs[m][0] if n == 0 else refs[n_core + n - 1][m])
        for m, n, number in sources(n_chip, n_core)
    ]


def front_kernel(
    part, n_out, pair_h, mask_h, mask_row_h, gain_h, bias_h, proj_h, *refs
):
    outs = refs[:n_out]
    pair, mask_s, mask_v, gain, bias, proj_weight, zbar, plane, sems, *more = refs[n_out:]
    rows, cols, width = pair.shape
    hidden = plane.shape[0] // rows
    groups = groups_of(rows)
    wait(
        start(
            sems,
            [
                (gain_h, gain), (bias_h, bias),
                (proj_h.at[:, pl.ds(part * hidden, 2 * hidden)], proj_weight),
                (mask_h, mask_s), (mask_row_h, mask_v), (pair_h, pair),
            ],
        )
    )
    gain_b = jnp.concatenate([down_lanes(gain[...], cols)] * groups[0][1], axis=1)
    bias_b = jnp.concatenate([down_lanes(bias[...], cols)] * groups[0][1], axis=1)
    for at, size in groups:
        zhat, _ = normalized(turned(pair[at : at + size].reshape(size * cols, width)))
        zbar[:, at * cols : (at + size) * cols] = (zhat * gain_b + bias_b).astype(BF16)
    weight = turned_weight(proj_weight[...])

    def channels(first, count):
        for at, size in groups:
            z = zbar[:, at * cols : (at + size) * cols]
            p = dot(weight[first : first + count], z)
            q = dot(weight[hidden + first : hidden + first + count], z)
            values = sigmoid(p) * q * pair_mask(mask_s, mask_v, at, size, rows, cols)
            for r in range(size):
                plane[pl.ds(first * rows + at + r, count, stride=rows), :] = values[
                    :, r * cols : (r + 1) * cols
                ]

    if n_out > 1:
        channels(0, hidden)
        give_pieces(plane, outs)
        return
    (out_h,), (ready, out_sems) = outs, more
    n_place, share = ready.shape[:2]
    size = n_place // math.gcd(n_place, 4)
    leaving = []
    for n, at in enumerate(range(0, n_place, size)):
        channels(at * share, size * share)
        values = plane[at * share * rows : (at + size) * share * rows]
        ready[at : at + size] = values.reshape(size, *ready.shape[1:]).astype(BF16)
        for half in range(out_h.shape[0]):
            copy = pltpu.make_async_copy(
                ready.at[pl.ds(at, size)], out_h.at[half, pl.ds(at, size)], out_sems.at[half, n]
            )
            copy.start()
            leaving.append(copy)
    wait(leaving)


def give_pieces(plane, outs):
    n_chip = outs[0].shape[0]
    length = plane.shape[0] // (len(outs) * n_chip)
    for m, n, number in sources(n_chip, len(outs)):
        first = pl.multiple_of(number * length, length)
        values = plane[pl.ds(first, length), :]
        outs[m][n] = values.reshape(outs[m].shape[1:]).astype(BF16)


def side_kernel(
    pair_h, cot_h, gain_h, bias_h, gate_h, norm_gain_h, out_w_h,
    zhat_h, inv_h, gate_out_h, dxh_out,
    pair, cot, gain, bias, gate_weight, norm_gain, out_weight,
    zhat_out, inv_out, gate_out, in_sems, out_sems,
):
    rows, cols, width = pair.shape
    hidden = out_weight.shape[0]
    wait(
        start(
            in_sems,
            [
                (pair_h, pair), (cot_h, cot), (gain_h, gain), (bias_h, bias),
                (gate_h, gate_weight), (norm_gain_h, norm_gain), (out_w_h, out_weight),
            ],
        )
    )
    groups = groups_of(rows)
    gain_b = jnp.concatenate([down_lanes(gain[...], cols)] * groups[0][1], axis=1)
    bias_b = jnp.concatenate([down_lanes(bias[...], cols)] * groups[0][1], axis=1)
    norm_gain_b = jnp.concatenate([down_lanes(norm_gain[...], cols)] * groups[0][1], axis=1)
    gate_t = turned_weight(gate_weight[...])
    for at, size in groups:
        zhat, inverse = normalized(turned(pair[at : at + size].reshape(size * cols, width)))
        zbar = (zhat * gain_b + bias_b).astype(BF16)
        gate = sigmoid(dot(gate_t, zbar))
        cot_t = turned(cot[at : at + size].reshape(size * cols, width))
        dxh = dot(out_weight[...], (cot_t * gate).astype(BF16)) * norm_gain_b
        dxh = dxh - jnp.mean(dxh, axis=0, keepdims=True)
        for r in range(size):
            lanes = slice(r * cols, (r + 1) * cols)
            zhat_out[at + r] = zhat[:, lanes]
            inv_out[at + r : at + r + 1] = inverse[:, lanes]
            gate_out[at + r] = gate[:, lanes]
            dxh_out[pl.ds(at + r, hidden, stride=rows), :] = dxh[:, lanes]
    wait(
        start(
            out_sems,
            [(zhat_out, zhat_h), (inv_out, inv_h), (gate_out, gate_out_h)],
        )
    )


def factors_kernel(
    zhat_h, mask_h, mask_row_h, gain_h, bias_h, proj_h, after, coef_h,
    zhat, mask_s, mask_v, gain, bias, proj_weight, coef, in_sems, out_sems,
):
    rows, width, cols = zhat.shape
    hidden = coef.shape[2]
    wait(
        start(
            in_sems,
            [
                (zhat_h, zhat), (mask_h, mask_s), (mask_row_h, mask_v), (gain_h, gain),
                (bias_h, bias), (proj_h, proj_weight),
            ],
        )
    )
    groups = groups_of(rows)
    gain_b = jnp.concatenate([down_lanes(gain[...], cols)] * groups[0][1], axis=1)
    bias_b = jnp.concatenate([down_lanes(bias[...], cols)] * groups[0][1], axis=1)
    weight = turned_weight(proj_weight[...])
    leaving = []
    for n, (at, size) in enumerate(groups):
        zbar = (side_by_side(zhat, at, size) * gain_b + bias_b).astype(BF16)
        pm = pair_mask(mask_s, mask_v, at, size, rows, cols)
        for part in (0, 2):
            s = sigmoid(dot(weight[part * hidden : (part + 1) * hidden], zbar))
            q = dot(weight[(part + 1) * hidden : (part + 2) * hidden], zbar)
            second = pm * s
            first = second * q * (1.0 - s)
            for r in range(size):
                lanes = slice(r * cols, (r + 1) * cols)
                coef[at + r, part] = first[:, lanes]
                coef[at + r, part + 1] = second[:, lanes]
        copy = pltpu.make_async_copy(
            coef.at[pl.ds(at, size)], coef_h.at[pl.ds(at, size)], out_sems.at[n]
        )
        copy.start()
        leaving.append(copy)
    wait(leaving)


def channel_matrix(ref, at):
    *_, n_col, _, rows, cols = ref.shape
    lead = (slice(None),) * (len(ref.shape) - 4)
    return jnp.concatenate(
        [ref[(*lead, c, at)].reshape(-1, cols) for c in range(n_col)], axis=1
    )


def put_channel(ref, at, values):
    *shape, n_col, _, rows, cols = ref.shape
    lead = (slice(None),) * len(shape)
    values = values.astype(BF16)
    for c in range(n_col):
        ref[(*lead, c, at)] = values[:, c * cols : (c + 1) * cols].reshape(*shape, rows, cols)


def product_kernel(n_chip, right, after, *refs):
    pieces, (out, left) = refs[:-2], refs[-2:]
    n_col, share = left.shape[1:3]
    for number, piece in received(pieces, n_chip):
        left[number // n_col, number % n_col] = piece
    for h in range(share):
        values = dot(channel_matrix(left, h), channel_matrix(right, h), ((1,), (1,)))
        put_channel(out, h, values)


def middle_kernel(product, dxh, out, xhat):
    hidden = product.shape[0]
    values = product[...].astype(F32)
    mean = jnp.sum(values, axis=0) * (1.0 / hidden)
    centred = values - mean
    var = jnp.sum(centred * centred, axis=0) * (1.0 / hidden)
    inverse = lax.rsqrt(var + EPS)
    xhat[...] = centred * inverse
    m2 = jnp.sum(dxh[...] * xhat[...], axis=0) * (1.0 / hidden)
    out[...] = ((dxh[...] - xhat[...] * m2) * inverse).astype(BF16)


def update_kernel(
    product, gate_h, cot_h, norm_gain_h, norm_bias_h, out_w_h, gate_w_h, after, update_h, dzg_h,
    gate, cot, norm_gain, norm_bias, out_weight, gate_weight, update, dzg, spread,
    in_sems, out_sems,
):
    hidden, rows, cols = product.shape
    width = cot.shape[2]
    copies = start(
        in_sems,
        [
            (gate_h, gate), (cot_h, cot), (norm_gain_h, norm_gain), (norm_bias_h, norm_bias),
            (out_w_h, out_weight), (gate_w_h, gate_weight),
        ],
    )
    spread[...] = product[...].astype(F32).reshape(hidden * rows, cols)
    wait(copies)
    groups = groups_of(rows)
    norm_gain_b = jnp.concatenate([down_lanes(norm_gain[...], cols)] * groups[0][1], axis=1)
    norm_bias_b = jnp.concatenate([down_lanes(norm_bias[...], cols)] * groups[0][1], axis=1)
    out_t = turned_weight(out_weight[...])
    for at, size in groups:
        xhat, _ = normalized(
            jnp.concatenate(
                [spread[pl.ds(at + r, hidden, stride=rows), :] for r in range(size)], axis=1
            )
        )
        ybar = (xhat * norm_gain_b + norm_bias_b).astype(BF16)
        u = dot(out_t, ybar)
        g = side_by_side(gate, at, size)
        done = (g * u).astype(BF16)
        cot_t = turned(cot[at : at + size].reshape(size * cols, width))
        back = dot(gate_weight[...], (cot_t * u * g * (1.0 - g)).astype(BF16))
        for r in range(size):
            lanes = slice(r * cols, (r + 1) * cols)
            update[at + r] = turned(done[:, lanes]).astype(BF16)
            dzg[at + r] = back[:, lanes]
    wait(start(out_sems, [(update, update_h), (dzg, dzg_h)]))


def grad_right_kernel(grad, left, out_h, ready, sems):
    lead = (slice(None),) * (len(ready.shape) - 3)
    leaving = []
    for h in range(ready.shape[-3]):
        values = dot(channel_matrix(grad, h), channel_matrix(left, h), ((0,), (0,)))
        put_channel(ready, h, values)
        part = (*lead, pl.ds(h, 1))
        copy = pltpu.make_async_copy(ready.at[part], out_h.at[part], sems.at[h])
        copy.start()
        leaving.append(copy)
    wait(leaving)


def grad_left_kernel(grad, right, *refs):
    outs, ready = refs[:-1], refs[-1]
    n_col, share = ready.shape[1:3]
    for h in range(share):
        put_channel(ready, h, dot(channel_matrix(grad, h), channel_matrix(right, h)))
    for m, n, number in sources(outs[0].shape[0], len(outs)):
        outs[m][n] = ready[number // n_col, number % n_col]


def back_kernel(n_chip, grads, coef_h, zhat_h, inv_h, dzg_h, gain_h, proj_h, *refs):
    pieces, out_h = refs[:-15], refs[-15]
    (
        coef, zhat, inv, dzg, gain, proj_weight, out, left, right,
        sems, coef_sems, zhat_sems, dzg_sems, out_sems,
    ) = refs[-14:]
    rows, cols, width = out.shape
    hidden = left.shape[0] // rows
    groups = groups_of(rows)
    small = start(sems, [(gain_h, gain), (proj_h, proj_weight), (inv_h, inv)])
    ahead = rows // math.gcd(rows, 2)
    blocks = {}
    for n, at in enumerate(range(0, rows, ahead)):
        part = pl.ds(at, ahead)
        blocks[at] = [
            pltpu.make_async_copy(source.at[part], target.at[part], sem.at[n])
            for source, target, sem in (
                (coef_h, coef, coef_sems), (zhat_h, zhat, zhat_sems), (dzg_h, dzg, dzg_sems)
            )
        ]
        for copy in blocks[at]:
            copy.start()
    arrived = received(pieces, n_chip)
    length = left.shape[0] // len(arrived)
    for number, piece in arrived:
        first = pl.multiple_of(number * length, length)
        left[pl.ds(first, length), :] = piece.astype(F32).reshape(length, cols)
    total = grads[0].astype(F32)
    for half in range(1, grads.shape[0]):
        total = total + grads[half].astype(F32)
    right[...] = total.reshape(right.shape)
    wait(small)
    gain_b = jnp.concatenate([down_lanes(gain[...], cols)] * groups[0][1], axis=1)
    leaving = []
    for at, size in groups:
        wait(blocks.get(at, []))
        columns = []
        for r in range(size):
            gl = left[pl.ds(at + r, hidden, stride=rows), :]
            gr = right[pl.ds(at + r, hidden, stride=rows), :]
            columns.append(
                jnp.concatenate(
                    [
                        (g * coef[at + r, part]).astype(BF16)
                        for part, g in enumerate((gl, gl, gr, gr))
                    ],
                    axis=0,
                )
            )
        back = dot(proj_weight[...], jnp.concatenate(columns, axis=1))
        dzh = (back + side_by_side(dzg, at, size)) * gain_b
        z = side_by_side(zhat, at, size)
        inverse = jnp.concatenate([inv[at + r : at + r + 1] for r in range(size)], axis=1)
        m1 = jnp.mean(dzh, axis=0, keepdims=True)
        m2 = jnp.mean(dzh * z, axis=0, keepdims=True)
        grad = ((dzh - m1 - z * m2) * inverse).astype(BF16)
        for r in range(size):
            out[at + r] = turned(grad[:, r * cols : (r + 1) * cols]).astype(BF16)
        done = at + size
        if done % ahead == 0:
            part = pl.ds(done - ahead, ahead)
            copy = pltpu.make_async_copy(
                out.at[part], out_h.at[part], out_sems.at[done // ahead - 1]
            )
            copy.start()
            leaving.append(copy)
    wait(leaving)


def call(kernel, outs, scratch, args, near=(), outs_near=(), flops=0, moved=0):
    here, far = (pl.BlockSpec(memory_space=space) for space in (pltpu.VMEM, pltpu.HBM))
    specs = [here if at in near else far for at in range(len(args))]
    return pl.pallas_call(
        kernel,
        out_shape=[
            out if at in outs_near else pltpu.HBM(out.shape, out.dtype)
            for at, out in enumerate(outs)
        ],
        in_specs=specs,
        out_specs=[here if at in outs_near else far for at in range(len(outs))],
        scratch_shapes=scratch,
        compiler_params=pltpu.CompilerParams(vmem_limit_bytes=16 * MIB),
        cost_estimate=pl.CostEstimate(flops=flops, bytes_accessed=moved, transcendentals=0),
    )(
        *[
            pltpu.with_memory_space_constraint(arg, pltpu.HBM) if spec is far else arg
            for arg, spec in zip(args, specs)
        ]
    )


def body(
    pair, mask, gain_in, bias_in, proj_weight, gate_weight,
    product_norm_gain, product_norm_bias, out_weight, cotangent,
):
    rows, cols, width = pair.shape
    hidden = out_weight.shape[0]
    n_half = lax.axis_size("half")
    n_row = lax.axis_size("row")
    n_core = lax.axis_size("core")
    n_col = lax.axis_size("col")
    n_chip = n_row * n_col
    n_line = n_row * n_core
    n_place = n_line * n_col
    within = ("row", "core", "col")
    share = hidden // n_place
    cells = rows * cols
    n_groups = len(groups_of(rows))
    mask_row = mask.reshape(1, -1)
    gain_in, bias_in = gain_in.reshape(1, -1), bias_in.reshape(1, -1)
    norm_gain, norm_bias = product_norm_gain.reshape(1, -1), product_norm_bias.reshape(1, -1)

    def shape(*dims, dtype=BF16):
        return jax.ShapeDtypeStruct(dims, dtype)

    def vmem(*dims, dtype=BF16):
        return pltpu.VMEM(dims, dtype)

    def sems(count):
        return pltpu.SemaphoreType.DMA((count,))

    def exchange(values):
        return lax.all_to_all(values, within, split_axis=0, concat_axis=0, tiled=True)

    def exchange_all(values):
        flat = values.reshape(n_half * n_place, share, rows, cols)
        return lax.all_to_all(
            flat, ("half", *within), split_axis=0, concat_axis=0, tiled=True
        )

    def permute(values, axes, size, distance):
        return lax.ppermute(values, axes, [(at, at ^ distance) for at in range(size)])

    def exchange_pieces(pieces):
        first = [pieces[0]]
        first += [permute(pieces[m], ("core",), n_core, m) for m in range(1, n_core)]
        second = [
            permute(jnp.stack([piece[n] for piece in first]), ("row", "col"), n_chip, n)
            for n in range(n_chip - 1, 0, -1)
        ]
        return tuple(first + second[::-1])

    mask_s = pltpu.SMEM(mask.shape, jnp.int32)
    mask_v = vmem(*mask_row.shape, dtype=jnp.int32)
    vector = vmem(1, width, dtype=F32)
    plane = vmem(hidden * rows, cols, dtype=F32)
    block = vmem(rows, cols, width)
    wide = vmem(rows, width, cols, dtype=F32)
    square = vmem(width, hidden)
    proj_v = vmem(width, 4 * hidden)
    pieces_shape = (shape(n_chip, share, rows, cols),) * n_core
    n_pieces = n_core + n_chip - 1

    def front(part, outs, scratch, near):
        return call(
            functools.partial(front_kernel, part, len(outs)),
            outs,
            [
                block, mask_s, mask_v, vector, vector, vmem(width, 2 * hidden),
                vmem(width, cells), plane, sems(6), *scratch,
            ],
            (pair, mask, mask_row, gain_in, bias_in, proj_weight),
            outs_near=near,
            flops=2 * cells * width * 3 * hidden,
            moved=5 * cells * width,
        )

    everywhere = vmem(n_place, share, rows, cols)
    (right,) = front(
        2,
        (shape(n_half, n_place, share, rows, cols),),
        [everywhere, pltpu.SemaphoreType.DMA((n_half, math.gcd(n_place, 4)))],
        (),
    )
    right = exchange_all(right).reshape(n_half, n_line, n_col, share, rows, cols)
    left = exchange_pieces(tuple(front(0, pieces_shape, [], range(n_core))))
    zhat, inv, gate, dxh = call(
        side_kernel,
        (
            shape(rows, width, cols, dtype=F32),
            shape(rows, cols, dtype=F32),
            shape(rows, width, cols, dtype=F32),
            shape(hidden * rows, cols, dtype=F32),
        ),
        [
            block, block, vector, vector, square, vector, square,
            wide, vmem(rows, cols, dtype=F32), wide, sems(7), sems(3),
        ],
        (pair, cotangent, gain_in, bias_in, gate_weight, norm_gain, out_weight),
        outs_near=(3,),
        flops=2 * cells * width * 4 * hidden,
        moved=16 * cells * width,
    )
    product, left = call(
        functools.partial(product_kernel, n_chip),
        (shape(n_line, n_col, share, rows, cols), shape(n_line, n_col, share, rows, cols)),
        [],
        (right, inv, *left),
        near=(0, *range(2, 2 + n_pieces)),
        outs_near=(0, 1),
        flops=2 * share * n_half * (n_line * rows) ** 2 * n_col * cols,
        moved=8 * cells * hidden,
    )
    product = exchange(product.reshape(n_place, share, rows, cols)).reshape(hidden, rows, cols)
    (grad,) = call(
        middle_kernel,
        (shape(hidden, rows, cols),),
        [vmem(hidden, rows, cols, dtype=F32)],
        (product, dxh.reshape(hidden, rows, cols)),
        near=(0, 1),
        outs_near=(0,),
        flops=20 * cells * hidden,
        moved=8 * cells * hidden,
    )
    grad = exchange(grad.reshape(n_place, share, rows, cols))
    grad = grad.reshape(n_line, n_col, share, rows, cols)
    (grad_right,) = call(
        grad_right_kernel,
        (shape(n_half, n_line, n_col, share, rows, cols),),
        [vmem(n_half, n_line, n_col, share, rows, cols), sems(share)],
        (grad, left),
        near=(0, 1),
        flops=2 * share * n_half * (n_line * rows) ** 2 * n_col * cols,
        moved=8 * cells * hidden,
    )
    grad_right = exchange_all(grad_right).reshape(n_half, n_place, share, rows, cols)
    grad_left = call(
        grad_left_kernel,
        pieces_shape,
        [vmem(n_line, n_col, share, rows, cols)],
        (grad, right),
        near=(0, 1),
        outs_near=range(n_core),
        flops=2 * share * n_half * (n_line * rows) ** 2 * n_col * cols,
        moved=8 * cells * hidden,
    )
    grad_left = exchange_pieces(tuple(grad_left))
    arrived = grad_left[-min(3, n_chip - 1)]
    (coef,) = call(
        factors_kernel,
        (shape(rows, 4, hidden, cols, dtype=F32),),
        [
            wide, mask_s, mask_v, vector, vector, proj_v, vmem(rows, 4, hidden, cols, dtype=F32),
            sems(6), sems(n_groups),
        ],
        (zhat, mask, mask_row, gain_in, bias_in, proj_weight, arrived),
        near=(6,),
        flops=2 * cells * width * 5 * hidden,
        moved=20 * cells * width,
    )
    update, dzg = call(
        update_kernel,
        (shape(rows, cols, width), shape(rows, width, cols, dtype=F32)),
        [wide, block, vector, vector, square, square, block, wide, plane, sems(6), sems(2)],
        (product, gate, cotangent, norm_gain, norm_bias, out_weight, gate_weight, arrived),
        near=(0, 7),
        flops=2 * cells * width * 3 * hidden,
        moved=14 * cells * hidden,
    )
    (grad_pair,) = call(
        functools.partial(back_kernel, n_chip),
        (shape(rows, cols, width),),
        [
            vmem(rows, 4, hidden, cols, dtype=F32), wide, vmem(rows, cols, dtype=F32), wide,
            vector, proj_v, block, plane, plane,
            sems(3), sems(2), sems(2), sems(2), sems(2),
        ],
        (grad_right, coef, zhat, inv, dzg, gain_in, proj_weight, *grad_left),
        near=(0, *range(7, 7 + n_pieces)),
        flops=2 * cells * width * 5 * hidden,
        moved=30 * cells * width,
    )
    return (update, grad_pair)


def solution(mesh):
    n_grp, n_row, n_col = (mesh.shape[name] for name in ("grp", "row", "col"))
    n_half = math.gcd(n_row, 2)
    n_core = math.gcd(n_row // n_half, 2)
    split = jax.sharding.Mesh(
        mesh.devices.reshape(n_grp, n_half, n_row // (n_half * n_core), n_core, n_col),
        ("grp", "half", "row", "core", "col"),
    )
    cells = P(("grp", "half", "row", "core"), "col", None)
    return jax.shard_map(
        body,
        mesh=split,
        in_specs=(cells, P("grp"), P(), P(), P(), P(), P(), P(), P(), cells),
        out_specs=(cells, cells),
        check_vma=False,
    )
```

```python
import functools
import math

import jax
import jax.numpy as jnp
from jax import lax
from jax.experimental import pallas as pl
from jax.experimental.pallas import tpu as pltpu
from jax.sharding import PartitionSpec as P

EPS = 1e-05
F32 = jnp.float32
BF16 = jnp.bfloat16
MIB = 1 << 20


def dot(a, b, over=((1,), (0,))):
    return lax.dot_general(a, b, (over, ((), ())), preferred_element_type=F32)


def eye(size):
    down = lax.broadcasted_iota(jnp.int32, (size, size), 0)
    across = lax.broadcasted_iota(jnp.int32, (size, size), 1)
    return (down == across).astype(F32).astype(BF16)


def turned(values):
    return dot(eye(values.shape[1]), values, ((1,), (1,)))


def down_lanes(vector, lanes):
    return jnp.broadcast_to(vector, (lanes, vector.shape[1])).T


def turned_weight(weight):
    c, m = weight.shape
    return jnp.concatenate(
        [turned(weight[:, at : at + c]) for at in range(0, m, c)], axis=0
    ).astype(BF16)


def sigmoid(values):
    return 0.5 + 0.5 * jnp.tanh(0.5 * values)


def normalized(values):
    mean = jnp.mean(values, axis=0, keepdims=True)
    centred = values - mean
    var = jnp.mean(centred * centred, axis=0, keepdims=True)
    inverse = lax.rsqrt(var + EPS)
    return centred * inverse, inverse


def start(sems, copies):
    running = [
        pltpu.make_async_copy(source, target, sems.at[at])
        for at, (source, target) in enumerate(copies)
    ]
    for copy in running:
        copy.start()
    return running


def wait(copies):
    for copy in copies:
        copy.wait()


def groups_of(rows):
    size = math.gcd(rows, 4)
    return [(at, size) for at in range(0, rows, size)]


def side_by_side(ref, at, size):
    return jnp.concatenate([ref[at + r] for r in range(size)], axis=1)


def pair_mask(mask_s, mask_v, at, size, rows, cols):
    here = lax.axis_index("half")
    for name in ("row", "core"):
        here = here * lax.axis_size(name) + lax.axis_index(name)
    first_row = here * rows + at
    first_col = pl.multiple_of(lax.axis_index("col") * cols, cols)
    col_mask = mask_v[:, pl.ds(first_col, cols)].astype(F32)
    return jnp.concatenate(
        [col_mask * mask_s[first_row + r].astype(F32) for r in range(size)], axis=1
    )


def sources(n_chip, n_core):
    n_col = lax.axis_size("col")
    core = lax.axis_index("core")
    chip = lax.axis_index("row") * n_col + lax.axis_index("col")
    found = []
    for n in range(n_chip):
        other = chip ^ n
        for m in range(n_core):
            line = other // n_col * n_core + (core ^ m)
            found.append((m, n, line * n_col + other % n_col))
    return found


def received(refs, n_chip):
    n_core = len(refs) - n_chip + 1
    return [
        (number, refs[m][0] if n == 0 else refs[n_core + n - 1][m])
        for m, n, number in sources(n_chip, n_core)
    ]


def front_kernel(
    part, n_out, pair_h, mask_h, mask_row_h, gain_h, bias_h, proj_h, *refs
):
    outs = refs[:n_out]
    pair, mask_s, mask_v, gain, bias, proj_weight, zbar, plane, sems, *more = refs[n_out:]
    rows, cols, width = pair.shape
    hidden = plane.shape[0] // rows
    groups = groups_of(rows)
    wait(
        start(
            sems,
            [
                (gain_h, gain), (bias_h, bias),
                (proj_h.at[:, pl.ds(part * hidden, 2 * hidden)], proj_weight),
                (mask_h, mask_s), (mask_row_h, mask_v), (pair_h, pair),
            ],
        )
    )
    gain_b = jnp.concatenate([down_lanes(gain[...], cols)] * groups[0][1], axis=1)
    bias_b = jnp.concatenate([down_lanes(bias[...], cols)] * groups[0][1], axis=1)
    for at, size in groups:
        zhat, _ = normalized(turned(pair[at : at + size].reshape(size * cols, width)))
        zbar[:, at * cols : (at + size) * cols] = (zhat * gain_b + bias_b).astype(BF16)
    weight = turned_weight(proj_weight[...])

    def channels(first, count):
        for at, size in groups:
            z = zbar[:, at * cols : (at + size) * cols]
            p = dot(weight[first : first + count], z)
            q = dot(weight[hidden + first : hidden + first + count], z)
            values = sigmoid(p) * q * pair_mask(mask_s, mask_v, at, size, rows, cols)
            for r in range(size):
                plane[pl.ds(first * rows + at + r, count, stride=rows), :] = values[
                    :, r * cols : (r + 1) * cols
                ]

    if n_out > 1:
        channels(0, hidden)
        give_pieces(plane, outs)
        return
    (out_h,), (ready, out_sems) = outs, more
    n_place, share = ready.shape[:2]
    size = n_place // math.gcd(n_place, 4)
    leaving = []
    for n, at in enumerate(range(0, n_place, size)):
        channels(at * share, size * share)
        values = plane[at * share * rows : (at + size) * share * rows]
        ready[at : at + size] = values.reshape(size, *ready.shape[1:]).astype(BF16)
        for half in range(out_h.shape[0]):
            copy = pltpu.make_async_copy(
                ready.at[pl.ds(at, size)], out_h.at[half, pl.ds(at, size)], out_sems.at[half, n]
            )
            copy.start()
            leaving.append(copy)
    wait(leaving)


def give_pieces(plane, outs):
    n_chip = outs[0].shape[0]
    length = plane.shape[0] // (len(outs) * n_chip)
    for m, n, number in sources(n_chip, len(outs)):
        first = pl.multiple_of(number * length, length)
        values = plane[pl.ds(first, length), :]
        outs[m][n] = values.reshape(outs[m].shape[1:]).astype(BF16)


def side_kernel(
    pair_h, cot_h, gain_h, bias_h, gate_h, norm_gain_h, out_w_h,
    zhat_h, inv_h, gate_out_h, dxh_out,
    pair, cot, gain, bias, gate_weight, norm_gain, out_weight,
    zhat_out, inv_out, gate_out, in_sems, out_sems,
):
    rows, cols, width = pair.shape
    hidden = out_weight.shape[0]
    wait(
        start(
            in_sems,
            [
                (pair_h, pair), (cot_h, cot), (gain_h, gain), (bias_h, bias),
                (gate_h, gate_weight), (norm_gain_h, norm_gain), (out_w_h, out_weight),
            ],
        )
    )
    groups = groups_of(rows)
    gain_b = jnp.concatenate([down_lanes(gain[...], cols)] * groups[0][1], axis=1)
    bias_b = jnp.concatenate([down_lanes(bias[...], cols)] * groups[0][1], axis=1)
    norm_gain_b = jnp.concatenate([down_lanes(norm_gain[...], cols)] * groups[0][1], axis=1)
    gate_t = turned_weight(gate_weight[...])
    for at, size in groups:
        zhat, inverse = normalized(turned(pair[at : at + size].reshape(size * cols, width)))
        zbar = (zhat * gain_b + bias_b).astype(BF16)
        gate = sigmoid(dot(gate_t, zbar))
        cot_t = turned(cot[at : at + size].reshape(size * cols, width))
        dxh = dot(out_weight[...], (cot_t * gate).astype(BF16)) * norm_gain_b
        dxh = dxh - jnp.mean(dxh, axis=0, keepdims=True)
        for r in range(size):
            lanes = slice(r * cols, (r + 1) * cols)
            zhat_out[at + r] = zhat[:, lanes]
            inv_out[at + r : at + r + 1] = inverse[:, lanes]
            gate_out[at + r] = gate[:, lanes]
            dxh_out[pl.ds(at + r, hidden, stride=rows), :] = dxh[:, lanes]
    wait(
        start(
            out_sems,
            [(zhat_out, zhat_h), (inv_out, inv_h), (gate_out, gate_out_h)],
        )
    )


def factors_kernel(
    zhat_h, mask_h, mask_row_h, gain_h, bias_h, proj_h, coef_h,
    zhat, mask_s, mask_v, gain, bias, proj_weight, coef, in_sems, out_sems,
):
    rows, width, cols = zhat.shape
    hidden = coef.shape[2]
    wait(
        start(
            in_sems,
            [
                (zhat_h, zhat), (mask_h, mask_s), (mask_row_h, mask_v), (gain_h, gain),
                (bias_h, bias), (proj_h, proj_weight),
            ],
        )
    )
    groups = groups_of(rows)
    gain_b = jnp.concatenate([down_lanes(gain[...], cols)] * groups[0][1], axis=1)
    bias_b = jnp.concatenate([down_lanes(bias[...], cols)] * groups[0][1], axis=1)
    weight = turned_weight(proj_weight[...])
    leaving = []
    for n, (at, size) in enumerate(groups):
        zbar = (side_by_side(zhat, at, size) * gain_b + bias_b).astype(BF16)
        pm = pair_mask(mask_s, mask_v, at, size, rows, cols)
        for part in (0, 2):
            s = sigmoid(dot(weight[part * hidden : (part + 1) * hidden], zbar))
            q = dot(weight[(part + 1) * hidden : (part + 2) * hidden], zbar)
            second = pm * s
            first = second * q * (1.0 - s)
            for r in range(size):
                lanes = slice(r * cols, (r + 1) * cols)
                coef[at + r, part] = first[:, lanes].astype(BF16)
                coef[at + r, part + 1] = second[:, lanes].astype(BF16)
        copy = pltpu.make_async_copy(
            coef.at[pl.ds(at, size)], coef_h.at[pl.ds(at, size)], out_sems.at[n]
        )
        copy.start()
        leaving.append(copy)
    wait(leaving)


def channel_matrix(ref, at):
    *_, n_col, _, rows, cols = ref.shape
    lead = (slice(None),) * (len(ref.shape) - 4)
    return jnp.concatenate(
        [ref[(*lead, c, at)].reshape(-1, cols) for c in range(n_col)], axis=1
    )


def put_channel(ref, at, values):
    *shape, n_col, _, rows, cols = ref.shape
    lead = (slice(None),) * len(shape)
    values = values.astype(BF16)
    for c in range(n_col):
        ref[(*lead, c, at)] = values[:, c * cols : (c + 1) * cols].reshape(*shape, rows, cols)


def product_kernel(n_chip, right, after, *refs):
    pieces, (out, left) = refs[:-2], refs[-2:]
    n_col, share = left.shape[1:3]
    for number, piece in received(pieces, n_chip):
        left[number // n_col, number % n_col] = piece
    for h in range(share):
        values = dot(channel_matrix(left, h), channel_matrix(right, h), ((1,), (1,)))
        put_channel(out, h, values)


def middle_kernel(product, dxh, out, xhat):
    hidden = product.shape[0]
    values = product[...].astype(F32)
    mean = jnp.sum(values, axis=0) * (1.0 / hidden)
    centred = values - mean
    var = jnp.sum(centred * centred, axis=0) * (1.0 / hidden)
    inverse = lax.rsqrt(var + EPS)
    xhat[...] = centred * inverse
    m2 = jnp.sum(dxh[...] * xhat[...], axis=0) * (1.0 / hidden)
    out[...] = ((dxh[...] - xhat[...] * m2) * inverse).astype(BF16)


def update_kernel(
    product, gate_h, cot_h, norm_gain_h, norm_bias_h, out_w_h, gate_w_h, after, update_h, dzg_h,
    gate, cot, norm_gain, norm_bias, out_weight, gate_weight, update, dzg, spread,
    in_sems, out_sems,
):
    hidden, rows, cols = product.shape
    width = cot.shape[2]
    copies = start(
        in_sems,
        [
            (gate_h, gate), (cot_h, cot), (norm_gain_h, norm_gain), (norm_bias_h, norm_bias),
            (out_w_h, out_weight), (gate_w_h, gate_weight),
        ],
    )
    spread[...] = product[...].astype(F32).reshape(hidden * rows, cols)
    wait(copies)
    groups = groups_of(rows)
    norm_gain_b = jnp.concatenate([down_lanes(norm_gain[...], cols)] * groups[0][1], axis=1)
    norm_bias_b = jnp.concatenate([down_lanes(norm_bias[...], cols)] * groups[0][1], axis=1)
    out_t = turned_weight(out_weight[...])
    for at, size in groups:
        xhat, _ = normalized(
            jnp.concatenate(
                [spread[pl.ds(at + r, hidden, stride=rows), :] for r in range(size)], axis=1
            )
        )
        ybar = (xhat * norm_gain_b + norm_bias_b).astype(BF16)
        u = dot(out_t, ybar)
        g = side_by_side(gate, at, size)
        done = (g * u).astype(BF16)
        cot_t = turned(cot[at : at + size].reshape(size * cols, width))
        back = dot(gate_weight[...], (cot_t * u * g * (1.0 - g)).astype(BF16))
        for r in range(size):
            lanes = slice(r * cols, (r + 1) * cols)
            update[at + r] = turned(done[:, lanes]).astype(BF16)
            dzg[at + r] = back[:, lanes]
    wait(start(out_sems, [(update, update_h), (dzg, dzg_h)]))


def grad_right_kernel(grad, left, out_h, ready, sems):
    lead = (slice(None),) * (len(ready.shape) - 3)
    leaving = []
    for h in range(ready.shape[-3]):
        values = dot(channel_matrix(grad, h), channel_matrix(left, h), ((0,), (0,)))
        put_channel(ready, h, values)
        part = (*lead, pl.ds(h, 1))
        copy = pltpu.make_async_copy(ready.at[part], out_h.at[part], sems.at[h])
        copy.start()
        leaving.append(copy)
    wait(leaving)


def grad_left_kernel(grad, right, *refs):
    outs, ready = refs[:-1], refs[-1]
    n_col, share = ready.shape[1:3]
    for h in range(share):
        put_channel(ready, h, dot(channel_matrix(grad, h), channel_matrix(right, h)))
    for m, n, number in sources(outs[0].shape[0], len(outs)):
        outs[m][n] = ready[number // n_col, number % n_col]


def back_kernel(n_chip, grads, coef_h, zhat_h, inv_h, dzg_h, gain_h, proj_h, *refs):
    pieces, out_h = refs[:-15], refs[-15]
    (
        coef, zhat, inv, dzg, gain, proj_weight, out, left, right,
        sems, coef_sems, zhat_sems, dzg_sems, out_sems,
    ) = refs[-14:]
    rows, cols, width = out.shape
    hidden = left.shape[0] // rows
    groups = groups_of(rows)
    small = start(sems, [(gain_h, gain), (proj_h, proj_weight), (inv_h, inv)])
    ahead = rows // math.gcd(rows, 2)
    blocks = {}
    for n, at in enumerate(range(0, rows, ahead)):
        part = pl.ds(at, ahead)
        blocks[at] = [
            pltpu.make_async_copy(source.at[part], target.at[part], sem.at[n])
            for source, target, sem in (
                (coef_h, coef, coef_sems), (zhat_h, zhat, zhat_sems), (dzg_h, dzg, dzg_sems)
            )
        ]
        for copy in blocks[at]:
            copy.start()
    arrived = received(pieces, n_chip)
    length = left.shape[0] // len(arrived)
    for number, piece in arrived:
        first = pl.multiple_of(number * length, length)
        left[pl.ds(first, length), :] = piece.astype(F32).reshape(length, cols)
    total = grads[0].astype(F32)
    for half in range(1, grads.shape[0]):
        total = total + grads[half].astype(F32)
    right[...] = total.reshape(right.shape)
    wait(small)
    gain_b = jnp.concatenate([down_lanes(gain[...], cols)] * groups[0][1], axis=1)
    leaving = []
    for at, size in groups:
        wait(blocks.get(at, []))
        columns = []
        for r in range(size):
            gl = left[pl.ds(at + r, hidden, stride=rows), :].astype(BF16)
            gr = right[pl.ds(at + r, hidden, stride=rows), :].astype(BF16)
            columns.append(
                jnp.concatenate(
                    [g * coef[at + r, part] for part, g in enumerate((gl, gl, gr, gr))], axis=0
                )
            )
        back = dot(proj_weight[...], jnp.concatenate(columns, axis=1))
        dzh = (back + side_by_side(dzg, at, size)) * gain_b
        z = side_by_side(zhat, at, size)
        inverse = jnp.concatenate([inv[at + r : at + r + 1] for r in range(size)], axis=1)
        m1 = jnp.mean(dzh, axis=0, keepdims=True)
        m2 = jnp.mean(dzh * z, axis=0, keepdims=True)
        grad = ((dzh - m1 - z * m2) * inverse).astype(BF16)
        for r in range(size):
            out[at + r] = turned(grad[:, r * cols : (r + 1) * cols]).astype(BF16)
        done = at + size
        if done % ahead == 0:
            part = pl.ds(done - ahead, ahead)
            copy = pltpu.make_async_copy(
                out.at[part], out_h.at[part], out_sems.at[done // ahead - 1]
            )
            copy.start()
            leaving.append(copy)
    wait(leaving)


def call(kernel, outs, scratch, args, near=(), outs_near=(), flops=0, moved=0):
    here, far = (pl.BlockSpec(memory_space=space) for space in (pltpu.VMEM, pltpu.HBM))
    specs = [here if at in near else far for at in range(len(args))]
    return pl.pallas_call(
        kernel,
        out_shape=[
            out if at in outs_near else pltpu.HBM(out.shape, out.dtype)
            for at, out in enumerate(outs)
        ],
        in_specs=specs,
        out_specs=[here if at in outs_near else far for at in range(len(outs))],
        scratch_shapes=scratch,
        compiler_params=pltpu.CompilerParams(vmem_limit_bytes=16 * MIB),
        cost_estimate=pl.CostEstimate(flops=flops, bytes_accessed=moved, transcendentals=0),
    )(
        *[
            pltpu.with_memory_space_constraint(arg, pltpu.HBM) if spec is far else arg
            for arg, spec in zip(args, specs)
        ]
    )


def body(
    pair, mask, gain_in, bias_in, proj_weight, gate_weight,
    product_norm_gain, product_norm_bias, out_weight, cotangent,
):
    rows, cols, width = pair.shape
    hidden = out_weight.shape[0]
    n_half = lax.axis_size("half")
    n_row = lax.axis_size("row")
    n_core = lax.axis_size("core")
    n_col = lax.axis_size("col")
    n_chip = n_row * n_col
    n_line = n_row * n_core
    n_place = n_line * n_col
    within = ("row", "core", "col")
    share = hidden // n_place
    cells = rows * cols
    n_groups = len(groups_of(rows))
    mask_row = mask.reshape(1, -1)
    gain_in, bias_in = gain_in.reshape(1, -1), bias_in.reshape(1, -1)
    norm_gain, norm_bias = product_norm_gain.reshape(1, -1), product_norm_bias.reshape(1, -1)

    def shape(*dims, dtype=BF16):
        return jax.ShapeDtypeStruct(dims, dtype)

    def vmem(*dims, dtype=BF16):
        return pltpu.VMEM(dims, dtype)

    def sems(count):
        return pltpu.SemaphoreType.DMA((count,))

    def exchange(values):
        return lax.all_to_all(values, within, split_axis=0, concat_axis=0, tiled=True)

    def exchange_all(values):
        flat = values.reshape(n_half * n_place, share, rows, cols)
        return lax.all_to_all(
            flat, ("half", *within), split_axis=0, concat_axis=0, tiled=True
        )

    def permute(values, axes, size, distance):
        return lax.ppermute(values, axes, [(at, at ^ distance) for at in range(size)])

    def exchange_pieces(pieces):
        first = [pieces[0]]
        first += [permute(pieces[m], ("core",), n_core, m) for m in range(1, n_core)]
        second = [
            permute(jnp.stack([piece[n] for piece in first]), ("row", "col"), n_chip, n)
            for n in range(n_chip - 1, 0, -1)
        ]
        return tuple(first + second[::-1])

    mask_s = pltpu.SMEM(mask.shape, jnp.int32)
    mask_v = vmem(*mask_row.shape, dtype=jnp.int32)
    vector = vmem(1, width, dtype=F32)
    plane = vmem(hidden * rows, cols, dtype=F32)
    block = vmem(rows, cols, width)
    wide = vmem(rows, width, cols, dtype=F32)
    square = vmem(width, hidden)
    proj_v = vmem(width, 4 * hidden)
    pieces_shape = (shape(n_chip, share, rows, cols),) * n_core
    n_pieces = n_core + n_chip - 1

    def front(part, outs, scratch, near):
        return call(
            functools.partial(front_kernel, part, len(outs)),
            outs,
            [
                block, mask_s, mask_v, vector, vector, vmem(width, 2 * hidden),
                vmem(width, cells), plane, sems(6), *scratch,
            ],
            (pair, mask, mask_row, gain_in, bias_in, proj_weight),
            outs_near=near,
            flops=2 * cells * width * 3 * hidden,
            moved=5 * cells * width,
        )

    everywhere = vmem(n_place, share, rows, cols)
    (right,) = front(
        2,
        (shape(n_half, n_place, share, rows, cols),),
        [everywhere, pltpu.SemaphoreType.DMA((n_half, math.gcd(n_place, 4)))],
        (),
    )
    right = exchange_all(right).reshape(n_half, n_line, n_col, share, rows, cols)
    left = exchange_pieces(tuple(front(0, pieces_shape, [], range(n_core))))
    zhat, inv, gate, dxh = call(
        side_kernel,
        (
            shape(rows, width, cols, dtype=F32),
            shape(rows, cols, dtype=F32),
            shape(rows, width, cols, dtype=F32),
            shape(hidden * rows, cols, dtype=F32),
        ),
        [
            block, block, vector, vector, square, vector, square,
            wide, vmem(rows, cols, dtype=F32), wide, sems(7), sems(3),
        ],
        (pair, cotangent, gain_in, bias_in, gate_weight, norm_gain, out_weight),
        outs_near=(3,),
        flops=2 * cells * width * 4 * hidden,
        moved=16 * cells * width,
    )
    (coef,) = call(
        factors_kernel,
        (shape(rows, 4, hidden, cols),),
        [
            wide, mask_s, mask_v, vector, vector, proj_v, vmem(rows, 4, hidden, cols),
            sems(6), sems(n_groups),
        ],
        (zhat, mask, mask_row, gain_in, bias_in, proj_weight),
        flops=2 * cells * width * 5 * hidden,
        moved=16 * cells * width,
    )
    product, left = call(
        functools.partial(product_kernel, n_chip),
        (shape(n_line, n_col, share, rows, cols), shape(n_line, n_col, share, rows, cols)),
        [],
        (right, coef, *left),
        near=(0, *range(2, 2 + n_pieces)),
        outs_near=(0, 1),
        flops=2 * share * n_half * (n_line * rows) ** 2 * n_col * cols,
        moved=8 * cells * hidden,
    )
    product = exchange(product.reshape(n_place, share, rows, cols)).reshape(hidden, rows, cols)
    (grad,) = call(
        middle_kernel,
        (shape(hidden, rows, cols),),
        [vmem(hidden, rows, cols, dtype=F32)],
        (product, dxh.reshape(hidden, rows, cols)),
        near=(0, 1),
        outs_near=(0,),
        flops=20 * cells * hidden,
        moved=8 * cells * hidden,
    )
    grad = exchange(grad.reshape(n_place, share, rows, cols))
    grad = grad.reshape(n_line, n_col, share, rows, cols)
    (sent,) = call(
        grad_right_kernel,
        (shape(n_half, n_line, n_col, share, rows, cols),),
        [vmem(n_half, n_line, n_col, share, rows, cols), sems(share)],
        (grad, left),
        near=(0, 1),
        flops=2 * share * n_half * (n_line * rows) ** 2 * n_col * cols,
        moved=8 * cells * hidden,
    )
    grad_right = exchange_all(sent).reshape(n_half, n_place, share, rows, cols)
    grad_left = call(
        grad_left_kernel,
        pieces_shape,
        [vmem(n_line, n_col, share, rows, cols)],
        (grad, right),
        near=(0, 1),
        outs_near=range(n_core),
        flops=2 * share * n_half * (n_line * rows) ** 2 * n_col * cols,
        moved=8 * cells * hidden,
    )
    grad_left = exchange_pieces(tuple(grad_left))
    update, dzg = call(
        update_kernel,
        (shape(rows, cols, width), shape(rows, width, cols, dtype=F32)),
        [wide, block, vector, vector, square, square, block, wide, plane, sems(6), sems(2)],
        (product, gate, cotangent, norm_gain, norm_bias, out_weight, gate_weight, sent),
        near=(0,),
        flops=2 * cells * width * 3 * hidden,
        moved=14 * cells * hidden,
    )
    (grad_pair,) = call(
        functools.partial(back_kernel, n_chip),
        (shape(rows, cols, width),),
        [
            vmem(rows, 4, hidden, cols), wide, vmem(rows, cols, dtype=F32), wide,
            vector, proj_v, block, plane, plane,
            sems(3), sems(2), sems(2), sems(2), sems(2),
        ],
        (grad_right, coef, zhat, inv, dzg, gain_in, proj_weight, *grad_left),
        near=(0, *range(7, 7 + n_pieces)),
        flops=2 * cells * width * 5 * hidden,
        moved=30 * cells * width,
    )
    return (update, grad_pair)


def solution(mesh):
    n_grp, n_row, n_col = (mesh.shape[name] for name in ("grp", "row", "col"))
    n_half = math.gcd(n_row, 2)
    n_core = math.gcd(n_row // n_half, 2)
    split = jax.sharding.Mesh(
        mesh.devices.reshape(n_grp, n_half, n_row // (n_half * n_core), n_core, n_col),
        ("grp", "half", "row", "core", "col"),
    )
    cells = P(("grp", "half", "row", "core"), "col", None)
    return jax.shard_map(
        body,
        mesh=split,
        in_specs=(cells, P("grp"), P(), P(), P(), P(), P(), P(), P(), cells),
        out_specs=(cells, cells),
        check_vma=False,
    )
```

```python
import functools
import math

import jax
import jax.numpy as jnp
from jax import lax
from jax.experimental import pallas as pl
from jax.experimental.pallas import tpu as pltpu
from jax.sharding import PartitionSpec as P

EPS = 1e-05
F32 = jnp.float32
BF16 = jnp.bfloat16
MIB = 1 << 20


def dot(a, b, over=((1,), (0,))):
    return lax.dot_general(a, b, (over, ((), ())), preferred_element_type=F32)


def eye(size):
    down = lax.broadcasted_iota(jnp.int32, (size, size), 0)
    across = lax.broadcasted_iota(jnp.int32, (size, size), 1)
    return (down == across).astype(F32).astype(BF16)


def turned(values):
    return dot(eye(values.shape[1]), values, ((1,), (1,)))


def down_lanes(vector, lanes):
    return jnp.broadcast_to(vector, (lanes, vector.shape[1])).T


def turned_weight(weight):
    c, m = weight.shape
    return jnp.concatenate(
        [turned(weight[:, at : at + c]) for at in range(0, m, c)], axis=0
    ).astype(BF16)


def sigmoid(values):
    return 0.5 + 0.5 * jnp.tanh(0.5 * values)


def normalized(values):
    mean = jnp.mean(values, axis=0, keepdims=True)
    centred = values - mean
    var = jnp.mean(centred * centred, axis=0, keepdims=True)
    inverse = lax.rsqrt(var + EPS)
    return centred * inverse, inverse


def start(sems, copies):
    running = [
        pltpu.make_async_copy(source, target, sems.at[at])
        for at, (source, target) in enumerate(copies)
    ]
    for copy in running:
        copy.start()
    return running


def wait(copies):
    for copy in copies:
        copy.wait()


def groups_of(rows):
    size = math.gcd(rows, 4)
    return [(at, size) for at in range(0, rows, size)]


def side_by_side(ref, at, size):
    return jnp.concatenate([ref[at + r] for r in range(size)], axis=1)


def pair_mask(mask_s, mask_v, at, size, rows, cols):
    here = lax.axis_index("half")
    for name in ("row", "core"):
        here = here * lax.axis_size(name) + lax.axis_index(name)
    first_row = here * rows + at
    first_col = pl.multiple_of(lax.axis_index("col") * cols, cols)
    col_mask = mask_v[:, pl.ds(first_col, cols)].astype(F32)
    return jnp.concatenate(
        [col_mask * mask_s[first_row + r].astype(F32) for r in range(size)], axis=1
    )


def sources(n_chip, n_core):
    n_col = lax.axis_size("col")
    core = lax.axis_index("core")
    chip = lax.axis_index("row") * n_col + lax.axis_index("col")
    found = []
    for n in range(n_chip):
        other = chip ^ n
        for m in range(n_core):
            line = other // n_col * n_core + (core ^ m)
            found.append((m, n, line * n_col + other % n_col))
    return found


def received(refs, n_chip):
    n_core = len(refs) - n_chip + 1
    return [
        (number, refs[m][0] if n == 0 else refs[n_core + n - 1][m])
        for m, n, number in sources(n_chip, n_core)
    ]


def front_kernel(
    n_out, pair_h, mask_h, mask_row_h, gain_h, bias_h, proj_h, *refs
):
    outs = refs[:n_out]
    pair, mask_s, mask_v, gain, bias, proj_weight, left, right, sems = refs[n_out:]
    rows, cols, width = pair.shape
    hidden = left.shape[0] // rows
    groups = groups_of(rows)
    wait(
        start(
            sems,
            [
                (gain_h, gain), (bias_h, bias), (proj_h, proj_weight),
                (mask_h, mask_s), (mask_row_h, mask_v), (pair_h, pair),
            ],
        )
    )
    gain_b = jnp.concatenate([down_lanes(gain[...], cols)] * groups[0][1], axis=1)
    bias_b = jnp.concatenate([down_lanes(bias[...], cols)] * groups[0][1], axis=1)
    weight = turned_weight(proj_weight[...])
    for at, size in groups:
        zhat, _ = normalized(turned(pair[at : at + size].reshape(size * cols, width)))
        zbar = (zhat * gain_b + bias_b).astype(BF16)
        pm = pair_mask(mask_s, mask_v, at, size, rows, cols)
        for part, plane in ((0, left), (2, right)):
            p = dot(weight[part * hidden : (part + 1) * hidden], zbar)
            q = dot(weight[(part + 1) * hidden : (part + 2) * hidden], zbar)
            values = sigmoid(p) * q * pm
            for r in range(size):
                plane[pl.ds(at + r, hidden, stride=rows), :] = values[:, r * cols : (r + 1) * cols]
    n_chip, share2 = outs[0].shape[:2]
    share = share2 // 2
    length = share * rows
    for m, n, number in sources(n_chip, n_out):
        first = pl.multiple_of(number * length, length)
        for part, plane in enumerate((left, right)):
            values = plane[pl.ds(first, length), :].reshape(share, rows, cols)
            outs[m][n, part * share : (part + 1) * share] = values.astype(BF16)


def side_kernel(
    pair_h, cot_h, gain_h, bias_h, gate_h, norm_gain_h, out_w_h,
    zhat_h, inv_h, gate_out_h, dxh_out,
    pair, cot, gain, bias, gate_weight, norm_gain, out_weight,
    zhat_out, inv_out, gate_out, in_sems, out_sems,
):
    rows, cols, width = pair.shape
    hidden = out_weight.shape[0]
    wait(
        start(
            in_sems,
            [
                (pair_h, pair), (cot_h, cot), (gain_h, gain), (bias_h, bias),
                (gate_h, gate_weight), (norm_gain_h, norm_gain), (out_w_h, out_weight),
            ],
        )
    )
    groups = groups_of(rows)
    gain_b = jnp.concatenate([down_lanes(gain[...], cols)] * groups[0][1], axis=1)
    bias_b = jnp.concatenate([down_lanes(bias[...], cols)] * groups[0][1], axis=1)
    norm_gain_b = jnp.concatenate([down_lanes(norm_gain[...], cols)] * groups[0][1], axis=1)
    gate_t = turned_weight(gate_weight[...])
    for at, size in groups:
        zhat, inverse = normalized(turned(pair[at : at + size].reshape(size * cols, width)))
        zbar = (zhat * gain_b + bias_b).astype(BF16)
        gate = sigmoid(dot(gate_t, zbar))
        cot_t = turned(cot[at : at + size].reshape(size * cols, width))
        dxh = dot(out_weight[...], (cot_t * gate).astype(BF16)) * norm_gain_b
        dxh = dxh - jnp.mean(dxh, axis=0, keepdims=True)
        for r in range(size):
            lanes = slice(r * cols, (r + 1) * cols)
            zhat_out[at + r] = zhat[:, lanes]
            inv_out[at + r : at + r + 1] = inverse[:, lanes]
            gate_out[at + r] = gate[:, lanes]
            dxh_out[pl.ds(at + r, hidden, stride=rows), :] = dxh[:, lanes]
    wait(
        start(
            out_sems,
            [(zhat_out, zhat_h), (inv_out, inv_h), (gate_out, gate_out_h)],
        )
    )


def factors_kernel(
    zhat_h, mask_h, mask_row_h, gain_h, bias_h, proj_h, coef_h,
    zhat, mask_s, mask_v, gain, bias, proj_weight, coef, in_sems, out_sems,
):
    rows, width, cols = zhat.shape
    hidden = coef.shape[2]
    wait(
        start(
            in_sems,
            [
                (zhat_h, zhat), (mask_h, mask_s), (mask_row_h, mask_v), (gain_h, gain),
                (bias_h, bias), (proj_h, proj_weight),
            ],
        )
    )
    groups = groups_of(rows)
    gain_b = jnp.concatenate([down_lanes(gain[...], cols)] * groups[0][1], axis=1)
    bias_b = jnp.concatenate([down_lanes(bias[...], cols)] * groups[0][1], axis=1)
    weight = turned_weight(proj_weight[...])
    leaving = []
    for n, (at, size) in enumerate(groups):
        zbar = (side_by_side(zhat, at, size) * gain_b + bias_b).astype(BF16)
        pm = pair_mask(mask_s, mask_v, at, size, rows, cols)
        for part in (0, 2):
            s = sigmoid(dot(weight[part * hidden : (part + 1) * hidden], zbar))
            q = dot(weight[(part + 1) * hidden : (part + 2) * hidden], zbar)
            second = pm * s
            first = second * q * (1.0 - s)
            for r in range(size):
                lanes = slice(r * cols, (r + 1) * cols)
                coef[at + r, part] = first[:, lanes].astype(BF16)
                coef[at + r, part + 1] = second[:, lanes].astype(BF16)
        copy = pltpu.make_async_copy(
            coef.at[pl.ds(at, size)], coef_h.at[pl.ds(at, size)], out_sems.at[n]
        )
        copy.start()
        leaving.append(copy)
    wait(leaving)


def channel_matrix(ref, at):
    *_, n_col, _, rows, cols = ref.shape
    lead = (slice(None),) * (len(ref.shape) - 4)
    return jnp.concatenate(
        [ref[(*lead, c, at)].reshape(-1, cols) for c in range(n_col)], axis=1
    )


def half_columns(ref, which):
    count = ref.shape[1] // lax.axis_size("half")
    first = (lax.axis_index("half") ^ which) * count
    return [first + c for c in range(count)]


def half_matrix(ref, at, which):
    cols = ref.shape[-1]
    return jnp.concatenate(
        [ref[:, c, at].reshape(-1, cols) for c in half_columns(ref, which)], axis=1
    )


def put_channel(ref, at, values, columns):
    n_line, _, _, rows, cols = ref.shape
    values = values.astype(BF16)
    for n, c in enumerate(columns):
        ref[:, c, at] = values[:, n * cols : (n + 1) * cols].reshape(n_line, rows, cols)


def product_kernel(n_chip, n_core, after, *refs):
    pieces, crossed, (out, own, other) = refs[: n_core + n_chip - 1], refs[-3 - n_chip : -3], refs[-3:]
    n_col, share = other.shape[1:3]
    for number, piece in received(pieces, n_chip):
        own[number // n_col, number % n_col] = piece
    for m, n, number in sources(n_chip, n_core):
        other[number // n_col, number % n_col] = crossed[n][m]
    for h in range(share):
        left = channel_matrix(own, h)
        for which, right in enumerate((channel_matrix(own, share + h), channel_matrix(other, h))):
            put_channel(out, h, dot(left, right, ((1,), (1,))), half_columns(out, which))


def middle_kernel(product, dxh, out, xhat):
    hidden = product.shape[0]
    values = product[...].astype(F32)
    mean = jnp.sum(values, axis=0) * (1.0 / hidden)
    centred = values - mean
    var = jnp.sum(centred * centred, axis=0) * (1.0 / hidden)
    inverse = lax.rsqrt(var + EPS)
    xhat[...] = centred * inverse
    m2 = jnp.sum(dxh[...] * xhat[...], axis=0) * (1.0 / hidden)
    out[...] = ((dxh[...] - xhat[...] * m2) * inverse).astype(BF16)


def update_kernel(
    product, gate_h, cot_h, norm_gain_h, norm_bias_h, out_w_h, gate_w_h, after, update_h, dzg_h,
    gate, cot, norm_gain, norm_bias, out_weight, gate_weight, update, dzg, spread,
    in_sems, out_sems,
):
    hidden, rows, cols = product.shape
    width = cot.shape[2]
    copies = start(
        in_sems,
        [
            (gate_h, gate), (cot_h, cot), (norm_gain_h, norm_gain), (norm_bias_h, norm_bias),
            (out_w_h, out_weight), (gate_w_h, gate_weight),
        ],
    )
    spread[...] = product[...].astype(F32).reshape(hidden * rows, cols)
    wait(copies)
    groups = groups_of(rows)
    norm_gain_b = jnp.concatenate([down_lanes(norm_gain[...], cols)] * groups[0][1], axis=1)
    norm_bias_b = jnp.concatenate([down_lanes(norm_bias[...], cols)] * groups[0][1], axis=1)
    out_t = turned_weight(out_weight[...])
    for at, size in groups:
        xhat, _ = normalized(
            jnp.concatenate(
                [spread[pl.ds(at + r, hidden, stride=rows), :] for r in range(size)], axis=1
            )
        )
        ybar = (xhat * norm_gain_b + norm_bias_b).astype(BF16)
        u = dot(out_t, ybar)
        g = side_by_side(gate, at, size)
        done = (g * u).astype(BF16)
        cot_t = turned(cot[at : at + size].reshape(size * cols, width))
        back = dot(gate_weight[...], (cot_t * u * g * (1.0 - g)).astype(BF16))
        for r in range(size):
            lanes = slice(r * cols, (r + 1) * cols)
            update[at + r] = turned(done[:, lanes]).astype(BF16)
            dzg[at + r] = back[:, lanes]
    wait(start(out_sems, [(update, update_h), (dzg, dzg_h)]))


def grads_kernel(n_out, grad, own, other, *refs):
    outs, ready = refs[:n_out], refs[n_out]
    n_col, share = other.shape[1:3]
    everywhere = range(n_col)
    for h in range(share):
        left, right = channel_matrix(own, h), channel_matrix(own, share + h)
        here, there = half_matrix(grad, h, 0), half_matrix(grad, h, 1)
        back = dot(here, right) + dot(there, channel_matrix(other, h))
        put_channel(ready, h, back, everywhere)
        put_channel(ready, share + h, dot(here, left, ((0,), (0,))), everywhere)
        put_channel(ready, 2 * share + h, dot(there, left, ((0,), (0,))), everywhere)
    for m, n, number in sources(outs[0].shape[0], n_out):
        outs[m][n] = ready[number // n_col, number % n_col]


def back_kernel(n_chip, n_core, coef_h, zhat_h, inv_h, dzg_h, gain_h, proj_h, *refs):
    pieces, crossed, out_h = refs[: n_core + n_chip - 1], refs[-15 - n_chip : -15], refs[-15]
    (
        coef, zhat, inv, dzg, gain, proj_weight, out, left, right,
        sems, coef_sems, zhat_sems, dzg_sems, out_sems,
    ) = refs[-14:]
    rows, cols, width = out.shape
    hidden = left.shape[0] // rows
    groups = groups_of(rows)
    small = start(sems, [(gain_h, gain), (proj_h, proj_weight), (inv_h, inv)])
    ahead = rows // math.gcd(rows, 2)
    blocks = {}
    for n, at in enumerate(range(0, rows, ahead)):
        part = pl.ds(at, ahead)
        blocks[at] = [
            pltpu.make_async_copy(source.at[part], target.at[part], sem.at[n])
            for source, target, sem in (
                (coef_h, coef, coef_sems), (zhat_h, zhat, zhat_sems), (dzg_h, dzg, dzg_sems)
            )
        ]
        for copy in blocks[at]:
            copy.start()
    share = crossed[0].shape[1]
    length = share * rows
    got = {(m, n): ref[m] for n, ref in enumerate(crossed) for m in range(n_core)}
    places = sources(n_chip, n_core)
    for (number, piece), (m, n, _) in zip(received(pieces, n_chip), places):
        part = pl.ds(pl.multiple_of(number * length, length), length)
        left[part, :] = piece[:share].astype(F32).reshape(length, cols)
        total = piece[share : 2 * share].astype(F32) + got[m, n].astype(F32)
        right[part, :] = total.reshape(length, cols)
    wait(small)
    gain_b = jnp.concatenate([down_lanes(gain[...], cols)] * groups[0][1], axis=1)
    leaving = []
    for at, size in groups:
        wait(blocks.get(at, []))
        columns = []
        for r in range(size):
            gl = left[pl.ds(at + r, hidden, stride=rows), :].astype(BF16)
            gr = right[pl.ds(at + r, hidden, stride=rows), :].astype(BF16)
            columns.append(
                jnp.concatenate(
                    [g * coef[at + r, part] for part, g in enumerate((gl, gl, gr, gr))], axis=0
                )
            )
        back = dot(proj_weight[...], jnp.concatenate(columns, axis=1))
        dzh = (back + side_by_side(dzg, at, size)) * gain_b
        z = side_by_side(zhat, at, size)
        inverse = jnp.concatenate([inv[at + r : at + r + 1] for r in range(size)], axis=1)
        m1 = jnp.mean(dzh, axis=0, keepdims=True)
        m2 = jnp.mean(dzh * z, axis=0, keepdims=True)
        grad = ((dzh - m1 - z * m2) * inverse).astype(BF16)
        for r in range(size):
            out[at + r] = turned(grad[:, r * cols : (r + 1) * cols]).astype(BF16)
        done = at + size
        if done % ahead == 0:
            part = pl.ds(done - ahead, ahead)
            copy = pltpu.make_async_copy(
                out.at[part], out_h.at[part], out_sems.at[done // ahead - 1]
            )
            copy.start()
            leaving.append(copy)
    wait(leaving)


def call(kernel, outs, scratch, args, near=(), outs_near=(), flops=0, moved=0):
    here, far = (pl.BlockSpec(memory_space=space) for space in (pltpu.VMEM, pltpu.HBM))
    specs = [here if at in near else far for at in range(len(args))]
    return pl.pallas_call(
        kernel,
        out_shape=[
            out if at in outs_near else pltpu.HBM(out.shape, out.dtype)
            for at, out in enumerate(outs)
        ],
        in_specs=specs,
        out_specs=[here if at in outs_near else far for at in range(len(outs))],
        scratch_shapes=scratch,
        compiler_params=pltpu.CompilerParams(vmem_limit_bytes=16 * MIB),
        cost_estimate=pl.CostEstimate(flops=flops, bytes_accessed=moved, transcendentals=0),
    )(
        *[
            pltpu.with_memory_space_constraint(arg, pltpu.HBM) if spec is far else arg
            for arg, spec in zip(args, specs)
        ]
    )


def body(
    pair, mask, gain_in, bias_in, proj_weight, gate_weight,
    product_norm_gain, product_norm_bias, out_weight, cotangent,
):
    rows, cols, width = pair.shape
    hidden = out_weight.shape[0]
    n_half = lax.axis_size("half")
    n_row = lax.axis_size("row")
    n_core = lax.axis_size("core")
    n_col = lax.axis_size("col")
    n_chip = n_row * n_col
    n_line = n_row * n_core
    n_place = n_line * n_col
    within = ("row", "core", "col")
    share = hidden // n_place
    cells = rows * cols
    n_groups = len(groups_of(rows))
    mask_row = mask.reshape(1, -1)
    gain_in, bias_in = gain_in.reshape(1, -1), bias_in.reshape(1, -1)
    norm_gain, norm_bias = product_norm_gain.reshape(1, -1), product_norm_bias.reshape(1, -1)

    def shape(*dims, dtype=BF16):
        return jax.ShapeDtypeStruct(dims, dtype)

    def vmem(*dims, dtype=BF16):
        return pltpu.VMEM(dims, dtype)

    def sems(count):
        return pltpu.SemaphoreType.DMA((count,))

    def exchange(values):
        return lax.all_to_all(values, within, split_axis=0, concat_axis=0, tiled=True)

    def permute(values, axes, size, distance):
        return lax.ppermute(values, axes, [(at, at ^ distance) for at in range(size)])

    def exchange_pieces(pieces, crossing):
        first = [pieces[0]]
        first += [permute(pieces[m], ("core",), n_core, m) for m in range(1, n_core)]
        inside, crossed = {}, {}
        for n in range(n_chip - 1, -1, -1):
            values = jnp.stack([piece[n, crossing : crossing + share] for piece in first])
            crossed[n] = permute(values, ("half", "row", "col"), n_half * n_chip, n_chip + n)
            if n > 0:
                values = jnp.stack([piece[n, : 2 * share] for piece in first])
                inside[n] = permute(values, ("row", "col"), n_chip, n)
        return (
            *first,
            *[inside[n] for n in range(1, n_chip)],
            *[crossed[n] for n in range(n_chip)],
        )

    mask_s = pltpu.SMEM(mask.shape, jnp.int32)
    mask_v = vmem(*mask_row.shape, dtype=jnp.int32)
    vector = vmem(1, width, dtype=F32)
    plane = vmem(hidden * rows, cols, dtype=F32)
    block = vmem(rows, cols, width)
    wide = vmem(rows, width, cols, dtype=F32)
    square = vmem(width, hidden)
    proj_v = vmem(width, 4 * hidden)
    n_pieces = n_core + 2 * n_chip - 1
    pieces = call(
        functools.partial(front_kernel, n_core),
        (shape(n_chip, 2 * share, rows, cols),) * n_core,
        [block, mask_s, mask_v, vector, vector, proj_v, plane, plane, sems(6)],
        (pair, mask, mask_row, gain_in, bias_in, proj_weight),
        outs_near=range(n_core),
        flops=2 * cells * width * 5 * hidden,
        moved=6 * cells * width,
    )
    arrived = exchange_pieces(pieces, share)
    zhat, inv, gate, dxh = call(
        side_kernel,
        (
            shape(rows, width, cols, dtype=F32),
            shape(rows, cols, dtype=F32),
            shape(rows, width, cols, dtype=F32),
            shape(hidden * rows, cols, dtype=F32),
        ),
        [
            block, block, vector, vector, square, vector, square,
            wide, vmem(rows, cols, dtype=F32), wide, sems(7), sems(3),
        ],
        (pair, cotangent, gain_in, bias_in, gate_weight, norm_gain, out_weight),
        outs_near=(3,),
        flops=2 * cells * width * 4 * hidden,
        moved=16 * cells * width,
    )
    (coef,) = call(
        factors_kernel,
        (shape(rows, 4, hidden, cols),),
        [
            wide, mask_s, mask_v, vector, vector, proj_v, vmem(rows, 4, hidden, cols),
            sems(6), sems(n_groups),
        ],
        (zhat, mask, mask_row, gain_in, bias_in, proj_weight),
        flops=2 * cells * width * 5 * hidden,
        moved=16 * cells * width,
    )
    product, own, other = call(
        functools.partial(product_kernel, n_chip, n_core),
        (
            shape(n_line, n_col, share, rows, cols),
            shape(n_line, n_col, 2 * share, rows, cols),
            shape(n_line, n_col, share, rows, cols),
        ),
        [],
        (coef, *arrived),
        near=range(1, 1 + n_pieces),
        outs_near=range(3),
        flops=2 * share * n_half * (n_line * rows) ** 2 * n_col * cols,
        moved=8 * cells * hidden,
    )
    product = exchange(product.reshape(n_place, share, rows, cols)).reshape(hidden, rows, cols)
    (grad,) = call(
        middle_kernel,
        (shape(hidden, rows, cols),),
        [vmem(hidden, rows, cols, dtype=F32)],
        (product, dxh.reshape(hidden, rows, cols)),
        near=(0, 1),
        outs_near=(0,),
        flops=20 * cells * hidden,
        moved=8 * cells * hidden,
    )
    grad = exchange(grad.reshape(n_place, share, rows, cols))
    grad = grad.reshape(n_line, n_col, share, rows, cols)
    pieces = call(
        functools.partial(grads_kernel, n_core),
        (shape(n_chip, 3 * share, rows, cols),) * n_core,
        [vmem(n_line, n_col, 3 * share, rows, cols)],
        (grad, own, other),
        near=range(3),
        outs_near=range(n_core),
        flops=4 * share * n_half * (n_line * rows) ** 2 * n_col * cols,
        moved=12 * cells * hidden,
    )
    arrived = exchange_pieces(pieces, 2 * share)
    update, dzg = call(
        update_kernel,
        (shape(rows, cols, width), shape(rows, width, cols, dtype=F32)),
        [wide, block, vector, vector, square, square, block, wide, plane, sems(6), sems(2)],
        (product, gate, cotangent, norm_gain, norm_bias, out_weight, gate_weight, pieces[0]),
        near=(0, 7),
        flops=2 * cells * width * 3 * hidden,
        moved=14 * cells * hidden,
    )
    (grad_pair,) = call(
        functools.partial(back_kernel, n_chip, n_core),
        (shape(rows, cols, width),),
        [
            vmem(rows, 4, hidden, cols), wide, vmem(rows, cols, dtype=F32), wide,
            vector, proj_v, block, plane, plane,
            sems(3), sems(2), sems(2), sems(2), sems(2),
        ],
        (coef, zhat, inv, dzg, gain_in, proj_weight, *arrived),
        near=range(6, 6 + n_pieces),
        flops=2 * cells * width * 5 * hidden,
        moved=30 * cells * width,
    )
    return (update, grad_pair)


def solution(mesh):
    n_grp, n_row, n_col = (mesh.shape[name] for name in ("grp", "row", "col"))
    n_half = math.gcd(n_row, 2)
    n_core = math.gcd(n_row // n_half, 2)
    split = jax.sharding.Mesh(
        mesh.devices.reshape(n_grp, n_half, n_row // (n_half * n_core), n_core, n_col),
        ("grp", "half", "row", "core", "col"),
    )
    cells = P(("grp", "half", "row", "core"), "col", None)
    return jax.shard_map(
        body,
        mesh=split,
        in_specs=(cells, P("grp"), P(), P(), P(), P(), P(), P(), P(), cells),
        out_specs=(cells, cells),
        check_vma=False,
    )
```

```python
import functools
import math

import jax
import jax.numpy as jnp
from jax import lax
from jax.experimental import pallas as pl
from jax.experimental.pallas import tpu as pltpu
from jax.sharding import PartitionSpec as P

EPS = 1e-05
F32 = jnp.float32
BF16 = jnp.bfloat16
MIB = 1 << 20


def dot(a, b, over=((1,), (0,))):
    return lax.dot_general(a, b, (over, ((), ())), preferred_element_type=F32)


def eye(size):
    down = lax.broadcasted_iota(jnp.int32, (size, size), 0)
    across = lax.broadcasted_iota(jnp.int32, (size, size), 1)
    return (down == across).astype(F32).astype(BF16)


def turned(values):
    return dot(eye(values.shape[1]), values, ((1,), (1,)))


def down_lanes(vector, lanes):
    return jnp.broadcast_to(vector, (lanes, vector.shape[1])).T


def turned_weight(weight):
    c, m = weight.shape
    return jnp.concatenate(
        [turned(weight[:, at : at + c]) for at in range(0, m, c)], axis=0
    ).astype(BF16)


def sigmoid(values):
    return 0.5 + 0.5 * jnp.tanh(0.5 * values)


def normalized(values):
    mean = jnp.mean(values, axis=0, keepdims=True)
    centred = values - mean
    var = jnp.mean(centred * centred, axis=0, keepdims=True)
    inverse = lax.rsqrt(var + EPS)
    return centred * inverse, inverse


def start(sems, copies):
    running = [
        pltpu.make_async_copy(source, target, sems.at[at])
        for at, (source, target) in enumerate(copies)
    ]
    for copy in running:
        copy.start()
    return running


def wait(copies):
    for copy in copies:
        copy.wait()


def groups_of(rows):
    size = math.gcd(rows, 4)
    return [(at, size) for at in range(0, rows, size)]


def side_by_side(ref, at, size):
    return jnp.concatenate([ref[at + r] for r in range(size)], axis=1)


def pair_mask(mask_s, mask_v, at, size, rows, cols):
    here = lax.axis_index("half")
    for name in ("row", "core"):
        here = here * lax.axis_size(name) + lax.axis_index(name)
    first_row = here * rows + at
    first_col = pl.multiple_of(lax.axis_index("col") * cols, cols)
    col_mask = mask_v[:, pl.ds(first_col, cols)].astype(F32)
    return jnp.concatenate(
        [col_mask * mask_s[first_row + r].astype(F32) for r in range(size)], axis=1
    )


def sources(n_chip, n_core):
    n_col = lax.axis_size("col")
    core = lax.axis_index("core")
    chip = lax.axis_index("row") * n_col + lax.axis_index("col")
    found = []
    for n in range(n_chip):
        other = chip ^ n
        for m in range(n_core):
            line = other // n_col * n_core + (core ^ m)
            found.append((m, n, line * n_col + other % n_col))
    return found


def received(refs, n_chip):
    n_core = len(refs) - n_chip + 1
    return [
        (number, refs[m][0] if n == 0 else refs[n_core + n - 1][m])
        for m, n, number in sources(n_chip, n_core)
    ]


def front_kernel(
    part, n_out, pair_h, mask_h, mask_row_h, gain_h, bias_h, proj_h, *refs
):
    outs = refs[:n_out]
    pair, mask_s, mask_v, gain, bias, proj_weight, zbar, plane, sems, *more = refs[n_out:]
    rows, cols, width = pair.shape
    hidden = plane.shape[0] // rows
    groups = groups_of(rows)
    wait(
        start(
            sems,
            [
                (gain_h, gain), (bias_h, bias),
                (proj_h.at[:, pl.ds(part * hidden, 2 * hidden)], proj_weight),
                (mask_h, mask_s), (mask_row_h, mask_v), (pair_h, pair),
            ],
        )
    )
    gain_b = jnp.concatenate([down_lanes(gain[...], cols)] * groups[0][1], axis=1)
    bias_b = jnp.concatenate([down_lanes(bias[...], cols)] * groups[0][1], axis=1)
    for at, size in groups:
        zhat, _ = normalized(turned(pair[at : at + size].reshape(size * cols, width)))
        zbar[:, at * cols : (at + size) * cols] = (zhat * gain_b + bias_b).astype(BF16)
    weight = turned_weight(proj_weight[...])

    def channels(first, count):
        for at, size in groups:
            z = zbar[:, at * cols : (at + size) * cols]
            p = dot(weight[first : first + count], z)
            q = dot(weight[hidden + first : hidden + first + count], z)
            values = sigmoid(p) * q * pair_mask(mask_s, mask_v, at, size, rows, cols)
            for r in range(size):
                plane[pl.ds(first * rows + at + r, count, stride=rows), :] = values[
                    :, r * cols : (r + 1) * cols
                ]

    if n_out > 1:
        channels(0, hidden)
        give_pieces(plane, outs)
        return
    (out_h,), (ready, out_sems) = outs, more
    n_place, share = ready.shape[:2]
    size = n_place // math.gcd(n_place, 4)
    leaving = []
    for n, at in enumerate(range(0, n_place, size)):
        channels(at * share, size * share)
        values = plane[at * share * rows : (at + size) * share * rows]
        ready[at : at + size] = values.reshape(size, *ready.shape[1:]).astype(BF16)
        for half in range(out_h.shape[0]):
            copy = pltpu.make_async_copy(
                ready.at[pl.ds(at, size)], out_h.at[half, pl.ds(at, size)], out_sems.at[half, n]
            )
            copy.start()
            leaving.append(copy)
    wait(leaving)


def give_pieces(plane, outs):
    n_chip = outs[0].shape[0]
    length = plane.shape[0] // (len(outs) * n_chip)
    for m, n, number in sources(n_chip, len(outs)):
        first = pl.multiple_of(number * length, length)
        values = plane[pl.ds(first, length), :]
        outs[m][n] = values.reshape(outs[m].shape[1:]).astype(BF16)


def side_kernel(
    pair_h, cot_h, gain_h, bias_h, gate_h, norm_gain_h, out_w_h,
    zhat_h, inv_h, gate_out_h, dxh_out,
    pair, cot, gain, bias, gate_weight, norm_gain, out_weight,
    zhat_out, inv_out, gate_out, in_sems, out_sems,
):
    rows, cols, width = pair.shape
    hidden = out_weight.shape[0]
    wait(
        start(
            in_sems,
            [
                (pair_h, pair), (cot_h, cot), (gain_h, gain), (bias_h, bias),
                (gate_h, gate_weight), (norm_gain_h, norm_gain), (out_w_h, out_weight),
            ],
        )
    )
    groups = groups_of(rows)
    gain_b = jnp.concatenate([down_lanes(gain[...], cols)] * groups[0][1], axis=1)
    bias_b = jnp.concatenate([down_lanes(bias[...], cols)] * groups[0][1], axis=1)
    norm_gain_b = jnp.concatenate([down_lanes(norm_gain[...], cols)] * groups[0][1], axis=1)
    gate_t = turned_weight(gate_weight[...])
    for at, size in groups:
        zhat, inverse = normalized(turned(pair[at : at + size].reshape(size * cols, width)))
        zbar = (zhat * gain_b + bias_b).astype(BF16)
        gate = sigmoid(dot(gate_t, zbar))
        cot_t = turned(cot[at : at + size].reshape(size * cols, width))
        dxh = dot(out_weight[...], (cot_t * gate).astype(BF16)) * norm_gain_b
        dxh = dxh - jnp.mean(dxh, axis=0, keepdims=True)
        for r in range(size):
            lanes = slice(r * cols, (r + 1) * cols)
            zhat_out[at + r] = zhat[:, lanes]
            inv_out[at + r : at + r + 1] = inverse[:, lanes]
            gate_out[at + r] = gate[:, lanes]
            dxh_out[pl.ds(at + r, hidden, stride=rows), :] = dxh[:, lanes]
    wait(
        start(
            out_sems,
            [(zhat_out, zhat_h), (inv_out, inv_h), (gate_out, gate_out_h)],
        )
    )


def factors_kernel(
    zhat_h, mask_h, mask_row_h, gain_h, bias_h, proj_h, coef_h,
    zhat, mask_s, mask_v, gain, bias, proj_weight, coef, in_sems, out_sems,
):
    rows, width, cols = zhat.shape
    hidden = coef.shape[2]
    wait(
        start(
            in_sems,
            [
                (zhat_h, zhat), (mask_h, mask_s), (mask_row_h, mask_v), (gain_h, gain),
                (bias_h, bias), (proj_h, proj_weight),
            ],
        )
    )
    groups = groups_of(rows)
    gain_b = jnp.concatenate([down_lanes(gain[...], cols)] * groups[0][1], axis=1)
    bias_b = jnp.concatenate([down_lanes(bias[...], cols)] * groups[0][1], axis=1)
    weight = turned_weight(proj_weight[...])
    leaving = []
    for n, (at, size) in enumerate(groups):
        zbar = (side_by_side(zhat, at, size) * gain_b + bias_b).astype(BF16)
        pm = pair_mask(mask_s, mask_v, at, size, rows, cols)
        for part in (0, 2):
            s = sigmoid(dot(weight[part * hidden : (part + 1) * hidden], zbar))
            q = dot(weight[(part + 1) * hidden : (part + 2) * hidden], zbar)
            second = pm * s
            first = second * q * (1.0 - s)
            for r in range(size):
                lanes = slice(r * cols, (r + 1) * cols)
                coef[at + r, part] = first[:, lanes].astype(BF16)
                coef[at + r, part + 1] = second[:, lanes].astype(BF16)
        copy = pltpu.make_async_copy(
            coef.at[pl.ds(at, size)], coef_h.at[pl.ds(at, size)], out_sems.at[n]
        )
        copy.start()
        leaving.append(copy)
    wait(leaving)


def channel_matrix(ref, at):
    *_, n_col, _, rows, cols = ref.shape
    lead = (slice(None),) * (len(ref.shape) - 4)
    return jnp.concatenate(
        [ref[(*lead, c, at)].reshape(-1, cols) for c in range(n_col)], axis=1
    )


def put_channel(ref, at, values):
    *shape, n_col, _, rows, cols = ref.shape
    lead = (slice(None),) * len(shape)
    values = values.astype(BF16)
    for c in range(n_col):
        ref[(*lead, c, at)] = values[:, c * cols : (c + 1) * cols].reshape(*shape, rows, cols)


def product_kernel(n_chip, right, after, *refs):
    pieces, (out, left) = refs[:-2], refs[-2:]
    n_col, share = left.shape[1:3]
    for number, piece in received(pieces, n_chip):
        left[number // n_col, number % n_col] = piece
    for h in range(share):
        values = dot(channel_matrix(left, h), channel_matrix(right, h), ((1,), (1,)))
        put_channel(out, h, values)


def middle_kernel(product, dxh, out, xhat):
    hidden = product.shape[0]
    values = product[...].astype(F32)
    mean = jnp.sum(values, axis=0) * (1.0 / hidden)
    centred = values - mean
    var = jnp.sum(centred * centred, axis=0) * (1.0 / hidden)
    inverse = lax.rsqrt(var + EPS)
    xhat[...] = centred * inverse
    m2 = jnp.sum(dxh[...] * xhat[...], axis=0) * (1.0 / hidden)
    out[...] = ((dxh[...] - xhat[...] * m2) * inverse).astype(BF16)


def update_kernel(
    product, gate_h, cot_h, norm_gain_h, norm_bias_h, out_w_h, gate_w_h, after, coef_h, zhat_h,
    inv_h, update_h, dzg, coef, zhat, inv,
    gate, cot, norm_gain, norm_bias, out_weight, gate_weight, update, spread,
    in_sems, out_sems, fetch_sems,
):
    hidden, rows, cols = product.shape
    width = cot.shape[2]
    copies = start(
        in_sems,
        [
            (gate_h, gate), (cot_h, cot), (norm_gain_h, norm_gain), (norm_bias_h, norm_bias),
            (out_w_h, out_weight), (gate_w_h, gate_weight),
        ],
    )
    fetched = start(fetch_sems, [(coef_h, coef), (zhat_h, zhat), (inv_h, inv)])
    spread[...] = product[...].astype(F32).reshape(hidden * rows, cols)
    wait(copies)
    groups = groups_of(rows)
    norm_gain_b = jnp.concatenate([down_lanes(norm_gain[...], cols)] * groups[0][1], axis=1)
    norm_bias_b = jnp.concatenate([down_lanes(norm_bias[...], cols)] * groups[0][1], axis=1)
    out_t = turned_weight(out_weight[...])
    for at, size in groups:
        xhat, _ = normalized(
            jnp.concatenate(
                [spread[pl.ds(at + r, hidden, stride=rows), :] for r in range(size)], axis=1
            )
        )
        ybar = (xhat * norm_gain_b + norm_bias_b).astype(BF16)
        u = dot(out_t, ybar)
        g = side_by_side(gate, at, size)
        done = (g * u).astype(BF16)
        cot_t = turned(cot[at : at + size].reshape(size * cols, width))
        back = dot(gate_weight[...], (cot_t * u * g * (1.0 - g)).astype(BF16))
        for r in range(size):
            lanes = slice(r * cols, (r + 1) * cols)
            update[at + r] = turned(done[:, lanes]).astype(BF16)
            dzg[at + r] = back[:, lanes]
    wait(fetched + start(out_sems, [(update, update_h)]))


def grad_right_kernel(grad, left, out_h, ready, sems):
    share = ready.shape[-3]
    columns = ready.shape[1] * ready.shape[-2]
    factors = [(channel_matrix(grad, h), channel_matrix(left, h)) for h in range(share)]
    leaving = []
    for half in range(ready.shape[0]):
        for h, (g, other) in enumerate(factors):
            part = g[:, half * columns : (half + 1) * columns]
            put_channel(ready.at[half], h, dot(part, other, ((0,), (0,))))
        copy = pltpu.make_async_copy(ready.at[half], out_h.at[half], sems.at[half])
        copy.start()
        leaving.append(copy)
    wait(leaving)


def grad_left_kernel(grad, right, *refs):
    outs, ready = refs[:-1], refs[-1]
    n_col, share = ready.shape[1:3]
    for h in range(share):
        put_channel(ready, h, dot(channel_matrix(grad, h), channel_matrix(right, h)))
    for m, n, number in sources(outs[0].shape[0], len(outs)):
        outs[m][n] = ready[number // n_col, number % n_col]


def back_kernel(n_chip, grads, coef, zhat, inv, dzg, gain_h, proj_h, *refs):
    pieces, out_h = refs[:-8], refs[-8]
    gain, proj_weight, out, left, right, sems, out_sems = refs[-7:]
    rows, cols, width = out.shape
    hidden = left.shape[0] // rows
    groups = groups_of(rows)
    ahead = rows // math.gcd(rows, 2)
    small = start(sems, [(gain_h, gain), (proj_h, proj_weight)])
    arrived = received(pieces, n_chip)
    length = left.shape[0] // len(arrived)
    for number, piece in arrived:
        first = pl.multiple_of(number * length, length)
        left[pl.ds(first, length), :] = piece.astype(F32).reshape(length, cols)
    total = grads[0].astype(F32)
    for half in range(1, grads.shape[0]):
        total = total + grads[half].astype(F32)
    right[...] = total.reshape(right.shape)
    wait(small)
    gain_b = jnp.concatenate([down_lanes(gain[...], cols)] * groups[0][1], axis=1)
    leaving = []
    for at, size in groups:
        columns = []
        for r in range(size):
            gl = left[pl.ds(at + r, hidden, stride=rows), :].astype(BF16)
            gr = right[pl.ds(at + r, hidden, stride=rows), :].astype(BF16)
            columns.append(
                jnp.concatenate(
                    [g * coef[at + r, part] for part, g in enumerate((gl, gl, gr, gr))], axis=0
                )
            )
        back = dot(proj_weight[...], jnp.concatenate(columns, axis=1))
        dzh = (back + side_by_side(dzg, at, size)) * gain_b
        z = side_by_side(zhat, at, size)
        inverse = jnp.concatenate([inv[at + r : at + r + 1] for r in range(size)], axis=1)
        m1 = jnp.mean(dzh, axis=0, keepdims=True)
        m2 = jnp.mean(dzh * z, axis=0, keepdims=True)
        grad = ((dzh - m1 - z * m2) * inverse).astype(BF16)
        for r in range(size):
            out[at + r] = turned(grad[:, r * cols : (r + 1) * cols]).astype(BF16)
        done = at + size
        if done % ahead == 0:
            part = pl.ds(done - ahead, ahead)
            copy = pltpu.make_async_copy(
                out.at[part], out_h.at[part], out_sems.at[done // ahead - 1]
            )
            copy.start()
            leaving.append(copy)
    wait(leaving)


def call(kernel, outs, scratch, args, near=(), outs_near=(), flops=0, moved=0):
    here, far = (pl.BlockSpec(memory_space=space) for space in (pltpu.VMEM, pltpu.HBM))
    specs = [here if at in near else far for at in range(len(args))]
    return pl.pallas_call(
        kernel,
        out_shape=[
            out if at in outs_near else pltpu.HBM(out.shape, out.dtype)
            for at, out in enumerate(outs)
        ],
        in_specs=specs,
        out_specs=[here if at in outs_near else far for at in range(len(outs))],
        scratch_shapes=scratch,
        compiler_params=pltpu.CompilerParams(vmem_limit_bytes=16 * MIB),
        cost_estimate=pl.CostEstimate(flops=flops, bytes_accessed=moved, transcendentals=0),
    )(
        *[
            pltpu.with_memory_space_constraint(arg, pltpu.HBM) if spec is far else arg
            for arg, spec in zip(args, specs)
        ]
    )


def body(
    pair, mask, gain_in, bias_in, proj_weight, gate_weight,
    product_norm_gain, product_norm_bias, out_weight, cotangent,
):
    rows, cols, width = pair.shape
    hidden = out_weight.shape[0]
    n_half = lax.axis_size("half")
    n_row = lax.axis_size("row")
    n_core = lax.axis_size("core")
    n_col = lax.axis_size("col")
    n_chip = n_row * n_col
    n_line = n_row * n_core
    n_place = n_line * n_col
    within = ("row", "core", "col")
    share = hidden // n_place
    cells = rows * cols
    n_groups = len(groups_of(rows))
    mask_row = mask.reshape(1, -1)
    gain_in, bias_in = gain_in.reshape(1, -1), bias_in.reshape(1, -1)
    norm_gain, norm_bias = product_norm_gain.reshape(1, -1), product_norm_bias.reshape(1, -1)

    def shape(*dims, dtype=BF16):
        return jax.ShapeDtypeStruct(dims, dtype)

    def vmem(*dims, dtype=BF16):
        return pltpu.VMEM(dims, dtype)

    def sems(count):
        return pltpu.SemaphoreType.DMA((count,))

    def exchange(values):
        return lax.all_to_all(values, within, split_axis=0, concat_axis=0, tiled=True)

    def exchange_all(values):
        flat = values.reshape(n_half * n_place, share, rows, cols)
        return lax.all_to_all(
            flat, ("half", *within), split_axis=0, concat_axis=0, tiled=True
        )

    def permute(values, axes, size, distance):
        return lax.ppermute(values, axes, [(at, at ^ distance) for at in range(size)])

    def exchange_pieces(pieces):
        first = [pieces[0]]
        first += [permute(pieces[m], ("core",), n_core, m) for m in range(1, n_core)]
        second = [
            permute(jnp.stack([piece[n] for piece in first]), ("row", "col"), n_chip, n)
            for n in range(n_chip - 1, 0, -1)
        ]
        return tuple(first + second[::-1])

    mask_s = pltpu.SMEM(mask.shape, jnp.int32)
    mask_v = vmem(*mask_row.shape, dtype=jnp.int32)
    vector = vmem(1, width, dtype=F32)
    plane = vmem(hidden * rows, cols, dtype=F32)
    block = vmem(rows, cols, width)
    wide = vmem(rows, width, cols, dtype=F32)
    square = vmem(width, hidden)
    proj_v = vmem(width, 4 * hidden)
    pieces_shape = (shape(n_chip, share, rows, cols),) * n_core
    n_pieces = n_core + n_chip - 1

    def front(part, outs, scratch, near):
        return call(
            functools.partial(front_kernel, part, len(outs)),
            outs,
            [
                block, mask_s, mask_v, vector, vector, vmem(width, 2 * hidden),
                vmem(width, cells), plane, sems(6), *scratch,
            ],
            (pair, mask, mask_row, gain_in, bias_in, proj_weight),
            outs_near=near,
            flops=2 * cells * width * 3 * hidden,
            moved=5 * cells * width,
        )

    everywhere = vmem(n_place, share, rows, cols)
    (right,) = front(
        2,
        (shape(n_half, n_place, share, rows, cols),),
        [everywhere, pltpu.SemaphoreType.DMA((n_half, math.gcd(n_place, 4)))],
        (),
    )
    right = exchange_all(right).reshape(n_half, n_line, n_col, share, rows, cols)
    left = exchange_pieces(tuple(front(0, pieces_shape, [], range(n_core))))
    zhat, inv, gate, dxh = call(
        side_kernel,
        (
            shape(rows, width, cols, dtype=F32),
            shape(rows, cols, dtype=F32),
            shape(rows, width, cols, dtype=F32),
            shape(hidden * rows, cols, dtype=F32),
        ),
        [
            block, block, vector, vector, square, vector, square,
            wide, vmem(rows, cols, dtype=F32), wide, sems(7), sems(3),
        ],
        (pair, cotangent, gain_in, bias_in, gate_weight, norm_gain, out_weight),
        outs_near=(3,),
        flops=2 * cells * width * 4 * hidden,
        moved=16 * cells * width,
    )
    (coef,) = call(
        factors_kernel,
        (shape(rows, 4, hidden, cols),),
        [
            wide, mask_s, mask_v, vector, vector, proj_v, vmem(rows, 4, hidden, cols),
            sems(6), sems(n_groups),
        ],
        (zhat, mask, mask_row, gain_in, bias_in, proj_weight),
        flops=2 * cells * width * 5 * hidden,
        moved=16 * cells * width,
    )
    product, left = call(
        functools.partial(product_kernel, n_chip),
        (shape(n_line, n_col, share, rows, cols), shape(n_line, n_col, share, rows, cols)),
        [],
        (right, coef, *left),
        near=(0, *range(2, 2 + n_pieces)),
        outs_near=(0, 1),
        flops=2 * share * n_half * (n_line * rows) ** 2 * n_col * cols,
        moved=8 * cells * hidden,
    )
    product = exchange(product.reshape(n_place, share, rows, cols)).reshape(hidden, rows, cols)
    (grad,) = call(
        middle_kernel,
        (shape(hidden, rows, cols),),
        [vmem(hidden, rows, cols, dtype=F32)],
        (product, dxh.reshape(hidden, rows, cols)),
        near=(0, 1),
        outs_near=(0,),
        flops=20 * cells * hidden,
        moved=8 * cells * hidden,
    )
    grad = exchange(grad.reshape(n_place, share, rows, cols))
    grad = grad.reshape(n_line, n_col, share, rows, cols)
    (sent,) = call(
        grad_right_kernel,
        (shape(n_half, n_line, n_col, share, rows, cols),),
        [vmem(n_half, n_line, n_col, share, rows, cols), sems(n_half)],
        (grad, left),
        near=(0, 1),
        flops=2 * share * n_half * (n_line * rows) ** 2 * n_col * cols,
        moved=8 * cells * hidden,
    )
    grad_right = exchange_all(sent).reshape(n_half, n_place, share, rows, cols)
    grad_left = call(
        grad_left_kernel,
        pieces_shape,
        [vmem(n_line, n_col, share, rows, cols)],
        (grad, right),
        near=(0, 1),
        outs_near=range(n_core),
        flops=2 * share * n_half * (n_line * rows) ** 2 * n_col * cols,
        moved=8 * cells * hidden,
    )
    grad_left = exchange_pieces(tuple(grad_left))
    update, dzg, coef, zhat, inv = call(
        update_kernel,
        (
            shape(rows, cols, width),
            shape(rows, width, cols, dtype=F32),
            shape(rows, 4, hidden, cols),
            shape(rows, width, cols, dtype=F32),
            shape(rows, cols, dtype=F32),
        ),
        [wide, block, vector, vector, square, square, block, plane, sems(6), sems(1), sems(3)],
        (
            product, gate, cotangent, norm_gain, norm_bias, out_weight, gate_weight, sent,
            coef, zhat, inv,
        ),
        near=(0,),
        outs_near=range(1, 5),
        flops=2 * cells * width * 3 * hidden,
        moved=24 * cells * hidden,
    )
    (grad_pair,) = call(
        functools.partial(back_kernel, n_chip),
        (shape(rows, cols, width),),
        [vector, proj_v, block, plane, plane, sems(2), sems(2)],
        (grad_right, coef, zhat, inv, dzg, gain_in, proj_weight, *grad_left),
        near=(*range(5), *range(7, 7 + n_pieces)),
        flops=2 * cells * width * 5 * hidden,
        moved=24 * cells * width,
    )
    return (update, grad_pair)


def solution(mesh):
    n_grp, n_row, n_col = (mesh.shape[name] for name in ("grp", "row", "col"))
    n_half = math.gcd(n_row, 2)
    n_core = math.gcd(n_row // n_half, 2)
    split = jax.sharding.Mesh(
        mesh.devices.reshape(n_grp, n_half, n_row // (n_half * n_core), n_core, n_col),
        ("grp", "half", "row", "core", "col"),
    )
    cells = P(("grp", "half", "row", "core"), "col", None)
    return jax.shard_map(
        body,
        mesh=split,
        in_specs=(cells, P("grp"), P(), P(), P(), P(), P(), P(), P(), cells),
        out_specs=(cells, cells),
        check_vma=False,
    )
```

```python
import functools
import math

import jax
import jax.numpy as jnp
from jax import lax
from jax.experimental import pallas as pl
from jax.experimental.pallas import tpu as pltpu
from jax.sharding import PartitionSpec as P

EPS = 1e-05
F32 = jnp.float32
BF16 = jnp.bfloat16
MIB = 1 << 20


def dot(a, b, over=((1,), (0,))):
    return lax.dot_general(a, b, (over, ((), ())), preferred_element_type=F32)


def eye(size):
    down = lax.broadcasted_iota(jnp.int32, (size, size), 0)
    across = lax.broadcasted_iota(jnp.int32, (size, size), 1)
    return (down == across).astype(F32).astype(BF16)


def turned(values):
    return dot(eye(values.shape[1]), values, ((1,), (1,)))


def down_lanes(vector, lanes):
    return jnp.broadcast_to(vector, (lanes, vector.shape[1])).T


def turned_weight(weight):
    c, m = weight.shape
    return jnp.concatenate(
        [turned(weight[:, at : at + c]) for at in range(0, m, c)], axis=0
    ).astype(BF16)


def sigmoid(values):
    return 0.5 + 0.5 * jnp.tanh(0.5 * values)


def normalized(values):
    mean = jnp.mean(values, axis=0, keepdims=True)
    centred = values - mean
    var = jnp.mean(centred * centred, axis=0, keepdims=True)
    inverse = lax.rsqrt(var + EPS)
    return centred * inverse, inverse


def start(sems, copies):
    running = [
        pltpu.make_async_copy(source, target, sems.at[at])
        for at, (source, target) in enumerate(copies)
    ]
    for copy in running:
        copy.start()
    return running


def wait(copies):
    for copy in copies:
        copy.wait()


def groups_of(rows):
    size = math.gcd(rows, 4)
    return [(at, size) for at in range(0, rows, size)]


def side_by_side(ref, at, size):
    return jnp.concatenate([ref[at + r] for r in range(size)], axis=1)


def pair_mask(mask_s, mask_v, at, size, rows, cols):
    here = lax.axis_index("half")
    for name in ("row", "core"):
        here = here * lax.axis_size(name) + lax.axis_index(name)
    first_row = here * rows + at
    first_col = pl.multiple_of(lax.axis_index("col") * cols, cols)
    col_mask = mask_v[:, pl.ds(first_col, cols)].astype(F32)
    return jnp.concatenate(
        [col_mask * mask_s[first_row + r].astype(F32) for r in range(size)], axis=1
    )


def sources(n_chip, n_core):
    n_col = lax.axis_size("col")
    core = lax.axis_index("core")
    chip = lax.axis_index("row") * n_col + lax.axis_index("col")
    found = []
    for n in range(n_chip):
        other = chip ^ n
        for m in range(n_core):
            line = other // n_col * n_core + (core ^ m)
            found.append((m, n, line * n_col + other % n_col))
    return found


def received(refs, n_chip):
    n_core = len(refs) - n_chip + 1
    return [
        (number, refs[m][0] if n == 0 else refs[n_core + n - 1][m])
        for m, n, number in sources(n_chip, n_core)
    ]


def front_kernel(
    part, n_out, pair_h, mask_h, mask_row_h, gain_h, bias_h, proj_h, *refs
):
    outs = refs[:n_out]
    pair, mask_s, mask_v, gain, bias, proj_weight, zbar, plane, sems, *more = refs[n_out:]
    rows, cols, width = pair.shape
    hidden = plane.shape[0] // rows
    groups = groups_of(rows)
    *small, whole = start(
        sems,
        [
            (gain_h, gain), (bias_h, bias),
            (proj_h.at[:, pl.ds(part * hidden, 2 * hidden)], proj_weight),
            (mask_h, mask_s), (mask_row_h, mask_v), (pair_h, pair),
        ],
    )
    wait(small)
    gain_b = jnp.concatenate([down_lanes(gain[...], cols)] * groups[0][1], axis=1)
    bias_b = jnp.concatenate([down_lanes(bias[...], cols)] * groups[0][1], axis=1)
    weight = turned_weight(proj_weight[...])
    whole.wait()
    for at, size in groups:
        zhat, _ = normalized(turned(pair[at : at + size].reshape(size * cols, width)))
        zbar[:, at * cols : (at + size) * cols] = (zhat * gain_b + bias_b).astype(BF16)

    def channels(first, count):
        for at, size in groups:
            z = zbar[:, at * cols : (at + size) * cols]
            p = dot(weight[first : first + count], z)
            q = dot(weight[hidden + first : hidden + first + count], z)
            values = sigmoid(p) * q * pair_mask(mask_s, mask_v, at, size, rows, cols)
            for r in range(size):
                plane[pl.ds(first * rows + at + r, count, stride=rows), :] = values[
                    :, r * cols : (r + 1) * cols
                ]

    if n_out > 1:
        channels(0, hidden)
        give_pieces(plane, outs)
        return
    (out_h,), (ready, out_sems) = outs, more
    n_place, share = ready.shape[:2]
    size = n_place // math.gcd(n_place, 4)
    leaving = []
    for n, at in enumerate(range(0, n_place, size)):
        channels(at * share, size * share)
        values = plane[at * share * rows : (at + size) * share * rows]
        ready[at : at + size] = values.reshape(size, *ready.shape[1:]).astype(BF16)
        for half in range(out_h.shape[0]):
            copy = pltpu.make_async_copy(
                ready.at[pl.ds(at, size)], out_h.at[half, pl.ds(at, size)], out_sems.at[half, n]
            )
            copy.start()
            leaving.append(copy)
    wait(leaving)


def give_pieces(plane, outs):
    n_chip = outs[0].shape[0]
    length = plane.shape[0] // (len(outs) * n_chip)
    for m, n, number in sources(n_chip, len(outs)):
        first = pl.multiple_of(number * length, length)
        values = plane[pl.ds(first, length), :]
        outs[m][n] = values.reshape(outs[m].shape[1:]).astype(BF16)


def side_kernel(
    pair_h, cot_h, gain_h, bias_h, gate_h, norm_gain_h, out_w_h,
    zhat_h, short_h, inv_h, gate_out_h, dxh_out,
    pair, cot, gain, bias, gate_weight, norm_gain, out_weight,
    zhat_out, short_out, inv_out, gate_out, in_sems, out_sems,
):
    rows, cols, width = pair.shape
    hidden = out_weight.shape[0]
    wait(
        start(
            in_sems,
            [
                (pair_h, pair), (cot_h, cot), (gain_h, gain), (bias_h, bias),
                (gate_h, gate_weight), (norm_gain_h, norm_gain), (out_w_h, out_weight),
            ],
        )
    )
    groups = groups_of(rows)
    gain_b = jnp.concatenate([down_lanes(gain[...], cols)] * groups[0][1], axis=1)
    bias_b = jnp.concatenate([down_lanes(bias[...], cols)] * groups[0][1], axis=1)
    norm_gain_b = jnp.concatenate([down_lanes(norm_gain[...], cols)] * groups[0][1], axis=1)
    gate_t = turned_weight(gate_weight[...])
    for at, size in groups:
        zhat, inverse = normalized(turned(pair[at : at + size].reshape(size * cols, width)))
        zbar = (zhat * gain_b + bias_b).astype(BF16)
        gate = sigmoid(dot(gate_t, zbar))
        cot_t = turned(cot[at : at + size].reshape(size * cols, width))
        dxh = dot(out_weight[...], (cot_t * gate).astype(BF16)) * norm_gain_b
        dxh = dxh - jnp.mean(dxh, axis=0, keepdims=True)
        for r in range(size):
            lanes = slice(r * cols, (r + 1) * cols)
            zhat_out[at + r] = zhat[:, lanes]
            short_out[at + r] = zhat[:, lanes].astype(BF16)
            inv_out[at + r : at + r + 1] = inverse[:, lanes]
            gate_out[at + r] = gate[:, lanes]
            dxh_out[pl.ds(at + r, hidden, stride=rows), :] = dxh[:, lanes]
    wait(
        start(
            out_sems,
            [
                (zhat_out, zhat_h), (short_out, short_h), (inv_out, inv_h),
                (gate_out, gate_out_h),
            ],
        )
    )


def factors_kernel(
    zhat_h, mask_h, mask_row_h, gain_h, bias_h, proj_h, coef_h,
    zhat, mask_s, mask_v, gain, bias, proj_weight, coef, in_sems, out_sems,
):
    rows, width, cols = zhat.shape
    hidden = coef.shape[2]
    wait(
        start(
            in_sems,
            [
                (zhat_h, zhat), (mask_h, mask_s), (mask_row_h, mask_v), (gain_h, gain),
                (bias_h, bias), (proj_h, proj_weight),
            ],
        )
    )
    groups = groups_of(rows)
    gain_b = jnp.concatenate([down_lanes(gain[...], cols)] * groups[0][1], axis=1)
    bias_b = jnp.concatenate([down_lanes(bias[...], cols)] * groups[0][1], axis=1)
    weight = turned_weight(proj_weight[...])
    leaving = []
    for n, (at, size) in enumerate(groups):
        zbar = (side_by_side(zhat, at, size) * gain_b + bias_b).astype(BF16)
        pm = pair_mask(mask_s, mask_v, at, size, rows, cols)
        for part in (0, 2):
            s = sigmoid(dot(weight[part * hidden : (part + 1) * hidden], zbar))
            q = dot(weight[(part + 1) * hidden : (part + 2) * hidden], zbar)
            second = pm * s
            first = second * q * (1.0 - s)
            for r in range(size):
                lanes = slice(r * cols, (r + 1) * cols)
                coef[at + r, part] = first[:, lanes].astype(BF16)
                coef[at + r, part + 1] = second[:, lanes].astype(BF16)
        copy = pltpu.make_async_copy(
            coef.at[pl.ds(at, size)], coef_h.at[pl.ds(at, size)], out_sems.at[n]
        )
        copy.start()
        leaving.append(copy)
    wait(leaving)


def channel_matrix(ref, at):
    *_, n_col, _, rows, cols = ref.shape
    lead = (slice(None),) * (len(ref.shape) - 4)
    return jnp.concatenate(
        [ref[(*lead, c, at)].reshape(-1, cols) for c in range(n_col)], axis=1
    )


def put_channel(ref, at, values):
    *shape, n_col, _, rows, cols = ref.shape
    lead = (slice(None),) * len(shape)
    values = values.astype(BF16)
    for c in range(n_col):
        ref[(*lead, c, at)] = values[:, c * cols : (c + 1) * cols].reshape(*shape, rows, cols)


def product_kernel(n_chip, right, after, *refs):
    pieces, (out, left) = refs[:-2], refs[-2:]
    n_col, share = left.shape[1:3]
    for number, piece in received(pieces, n_chip):
        left[number // n_col, number % n_col] = piece
    for h in range(share):
        values = dot(channel_matrix(left, h), channel_matrix(right, h), ((1,), (1,)))
        put_channel(out, h, values)


def middle_kernel(product, dxh, out, xhat):
    hidden = product.shape[0]
    values = product[...].astype(F32)
    mean = jnp.sum(values, axis=0) * (1.0 / hidden)
    centred = values - mean
    var = jnp.sum(centred * centred, axis=0) * (1.0 / hidden)
    inverse = lax.rsqrt(var + EPS)
    xhat[...] = centred * inverse
    m2 = jnp.sum(dxh[...] * xhat[...], axis=0) * (1.0 / hidden)
    out[...] = ((dxh[...] - xhat[...] * m2) * inverse).astype(BF16)


def update_kernel(
    product, gate_h, cot_h, norm_gain_h, norm_bias_h, out_w_h, gate_w_h, after, update_h, dzg_h,
    gate, cot, norm_gain, norm_bias, out_weight, gate_weight, update, dzg, spread,
    in_sems, out_sems,
):
    hidden, rows, cols = product.shape
    width = cot.shape[2]
    copies = start(
        in_sems,
        [
            (gate_h, gate), (cot_h, cot), (norm_gain_h, norm_gain), (norm_bias_h, norm_bias),
            (out_w_h, out_weight), (gate_w_h, gate_weight),
        ],
    )
    spread[...] = product[...].astype(F32).reshape(hidden * rows, cols)
    wait(copies)
    groups = groups_of(rows)
    norm_gain_b = jnp.concatenate([down_lanes(norm_gain[...], cols)] * groups[0][1], axis=1)
    norm_bias_b = jnp.concatenate([down_lanes(norm_bias[...], cols)] * groups[0][1], axis=1)
    out_t = turned_weight(out_weight[...])
    for at, size in groups:
        xhat, _ = normalized(
            jnp.concatenate(
                [spread[pl.ds(at + r, hidden, stride=rows), :] for r in range(size)], axis=1
            )
        )
        ybar = (xhat * norm_gain_b + norm_bias_b).astype(BF16)
        u = dot(out_t, ybar)
        g = side_by_side(gate, at, size)
        done = (g * u).astype(BF16)
        cot_t = turned(cot[at : at + size].reshape(size * cols, width))
        back = dot(gate_weight[...], (cot_t * u * g * (1.0 - g)).astype(BF16))
        for r in range(size):
            lanes = slice(r * cols, (r + 1) * cols)
            update[at + r] = turned(done[:, lanes]).astype(BF16)
            dzg[at + r] = back[:, lanes].astype(BF16)
    wait(start(out_sems, [(update, update_h), (dzg, dzg_h)]))


def grad_right_kernel(grad, left, out_h, ready, sems):
    lead = (slice(None),) * (len(ready.shape) - 3)
    leaving = []
    for h in range(ready.shape[-3]):
        values = dot(channel_matrix(grad, h), channel_matrix(left, h), ((0,), (0,)))
        put_channel(ready, h, values)
        part = (*lead, pl.ds(h, 1))
        copy = pltpu.make_async_copy(ready.at[part], out_h.at[part], sems.at[h])
        copy.start()
        leaving.append(copy)
    wait(leaving)


def grad_left_kernel(grad, right, *refs):
    outs, ready = refs[:-1], refs[-1]
    n_col, share = ready.shape[1:3]
    for h in range(share):
        put_channel(ready, h, dot(channel_matrix(grad, h), channel_matrix(right, h)))
    for m, n, number in sources(outs[0].shape[0], len(outs)):
        outs[m][n] = ready[number // n_col, number % n_col]


def back_kernel(n_chip, grads, coef_h, zhat_h, inv_h, dzg_h, gain_h, proj_h, *refs):
    pieces, out_h = refs[:-15], refs[-15]
    (
        coef, zhat, inv, dzg, gain, proj_weight, out, left, right,
        sems, coef_sems, zhat_sems, dzg_sems, out_sems,
    ) = refs[-14:]
    rows, cols, width = out.shape
    hidden = left.shape[0] // rows
    groups = groups_of(rows)
    small = start(sems, [(gain_h, gain), (proj_h, proj_weight), (inv_h, inv)])
    ahead = rows // math.gcd(rows, 2)
    blocks = [
        [
            pltpu.make_async_copy(
                source.at[pl.ds(at, size)], target.at[pl.ds(at, size)], sem.at[n]
            )
            for source, target, sem in (
                (coef_h, coef, coef_sems), (zhat_h, zhat, zhat_sems), (dzg_h, dzg, dzg_sems)
            )
        ]
        for n, (at, size) in enumerate(groups)
    ]
    for copy in sum(blocks[:2], []):
        copy.start()
    arrived = received(pieces, n_chip)
    length = left.shape[0] // len(arrived)
    for number, piece in arrived:
        first = pl.multiple_of(number * length, length)
        left[pl.ds(first, length), :] = piece.astype(F32).reshape(length, cols)
    total = grads[0].astype(F32)
    for half in range(1, grads.shape[0]):
        total = total + grads[half].astype(F32)
    right[...] = total.reshape(right.shape)
    wait(small)
    gain_b = jnp.concatenate([down_lanes(gain[...], cols)] * groups[0][1], axis=1)
    leaving = []
    for copy in sum(blocks[2:], []):
        copy.start()
    for n, (at, size) in enumerate(groups):
        wait(blocks[n])
        columns = []
        for r in range(size):
            gl = left[pl.ds(at + r, hidden, stride=rows), :].astype(BF16)
            gr = right[pl.ds(at + r, hidden, stride=rows), :].astype(BF16)
            columns.append(
                jnp.concatenate(
                    [g * coef[at + r, part] for part, g in enumerate((gl, gl, gr, gr))], axis=0
                )
            )
        back = dot(proj_weight[...], jnp.concatenate(columns, axis=1))
        dzh = (back + side_by_side(dzg, at, size).astype(F32)) * gain_b
        z = side_by_side(zhat, at, size).astype(F32)
        inverse = jnp.concatenate([inv[at + r : at + r + 1] for r in range(size)], axis=1)
        m1 = jnp.mean(dzh, axis=0, keepdims=True)
        m2 = jnp.mean(dzh * z, axis=0, keepdims=True)
        grad = ((dzh - m1 - z * m2) * inverse).astype(BF16)
        for r in range(size):
            out[at + r] = turned(grad[:, r * cols : (r + 1) * cols]).astype(BF16)
        done = at + size
        if done % ahead == 0:
            part = pl.ds(done - ahead, ahead)
            copy = pltpu.make_async_copy(
                out.at[part], out_h.at[part], out_sems.at[done // ahead - 1]
            )
            copy.start()
            leaving.append(copy)
    wait(leaving)


def call(kernel, outs, scratch, args, near=(), outs_near=(), flops=0, moved=0):
    here, far = (pl.BlockSpec(memory_space=space) for space in (pltpu.VMEM, pltpu.HBM))
    specs = [here if at in near else far for at in range(len(args))]
    return pl.pallas_call(
        kernel,
        out_shape=[
            out if at in outs_near else pltpu.HBM(out.shape, out.dtype)
            for at, out in enumerate(outs)
        ],
        in_specs=specs,
        out_specs=[here if at in outs_near else far for at in range(len(outs))],
        scratch_shapes=scratch,
        compiler_params=pltpu.CompilerParams(vmem_limit_bytes=16 * MIB),
        cost_estimate=pl.CostEstimate(flops=flops, bytes_accessed=moved, transcendentals=0),
    )(
        *[
            pltpu.with_memory_space_constraint(arg, pltpu.HBM) if spec is far else arg
            for arg, spec in zip(args, specs)
        ]
    )


def body(
    pair, mask, gain_in, bias_in, proj_weight, gate_weight,
    product_norm_gain, product_norm_bias, out_weight, cotangent,
):
    rows, cols, width = pair.shape
    hidden = out_weight.shape[0]
    n_half = lax.axis_size("half")
    n_row = lax.axis_size("row")
    n_core = lax.axis_size("core")
    n_col = lax.axis_size("col")
    n_chip = n_row * n_col
    n_line = n_row * n_core
    n_place = n_line * n_col
    within = ("row", "core", "col")
    share = hidden // n_place
    cells = rows * cols
    n_groups = len(groups_of(rows))
    mask_row = mask.reshape(1, -1)
    gain_in, bias_in = gain_in.reshape(1, -1), bias_in.reshape(1, -1)
    norm_gain, norm_bias = product_norm_gain.reshape(1, -1), product_norm_bias.reshape(1, -1)

    def shape(*dims, dtype=BF16):
        return jax.ShapeDtypeStruct(dims, dtype)

    def vmem(*dims, dtype=BF16):
        return pltpu.VMEM(dims, dtype)

    def sems(count):
        return pltpu.SemaphoreType.DMA((count,))

    def exchange(values):
        return lax.all_to_all(values, within, split_axis=0, concat_axis=0, tiled=True)

    def exchange_all(values):
        flat = values.reshape(n_half * n_place, share, rows, cols)
        return lax.all_to_all(
            flat, ("half", *within), split_axis=0, concat_axis=0, tiled=True
        )

    def permute(values, axes, size, distance):
        return lax.ppermute(values, axes, [(at, at ^ distance) for at in range(size)])

    def exchange_pieces(pieces):
        first = [pieces[0]]
        first += [permute(pieces[m], ("core",), n_core, m) for m in range(1, n_core)]
        second = [
            permute(jnp.stack([piece[n] for piece in first]), ("row", "col"), n_chip, n)
            for n in range(n_chip - 1, 0, -1)
        ]
        return tuple(first + second[::-1])

    mask_s = pltpu.SMEM(mask.shape, jnp.int32)
    mask_v = vmem(*mask_row.shape, dtype=jnp.int32)
    vector = vmem(1, width, dtype=F32)
    plane = vmem(hidden * rows, cols, dtype=F32)
    block = vmem(rows, cols, width)
    wide = vmem(rows, width, cols, dtype=F32)
    short = vmem(rows, width, cols)
    square = vmem(width, hidden)
    proj_v = vmem(width, 4 * hidden)
    pieces_shape = (shape(n_chip, share, rows, cols),) * n_core
    n_pieces = n_core + n_chip - 1

    def front(part, outs, scratch, near):
        return call(
            functools.partial(front_kernel, part, len(outs)),
            outs,
            [
                block, mask_s, mask_v, vector, vector, vmem(width, 2 * hidden),
                vmem(width, cells), plane, sems(6), *scratch,
            ],
            (pair, mask, mask_row, gain_in, bias_in, proj_weight),
            outs_near=near,
            flops=2 * cells * width * 3 * hidden,
            moved=5 * cells * width,
        )

    everywhere = vmem(n_place, share, rows, cols)
    (right,) = front(
        2,
        (shape(n_half, n_place, share, rows, cols),),
        [everywhere, pltpu.SemaphoreType.DMA((n_half, math.gcd(n_place, 4)))],
        (),
    )
    right = exchange_all(right).reshape(n_half, n_line, n_col, share, rows, cols)
    left = exchange_pieces(tuple(front(0, pieces_shape, [], range(n_core))))
    zhat, short_zhat, inv, gate, dxh = call(
        side_kernel,
        (
            shape(rows, width, cols, dtype=F32),
            shape(rows, width, cols),
            shape(rows, cols, dtype=F32),
            shape(rows, width, cols, dtype=F32),
            shape(hidden * rows, cols, dtype=F32),
        ),
        [
            block, block, vector, vector, square, vector, square,
            wide, short, vmem(rows, cols, dtype=F32), wide, sems(7), sems(4),
        ],
        (pair, cotangent, gain_in, bias_in, gate_weight, norm_gain, out_weight),
        outs_near=(4,),
        flops=2 * cells * width * 4 * hidden,
        moved=16 * cells * width,
    )
    (coef,) = call(
        factors_kernel,
        (shape(rows, 4, hidden, cols),),
        [
            wide, mask_s, mask_v, vector, vector, proj_v, vmem(rows, 4, hidden, cols),
            sems(6), sems(n_groups),
        ],
        (zhat, mask, mask_row, gain_in, bias_in, proj_weight),
        flops=2 * cells * width * 5 * hidden,
        moved=16 * cells * width,
    )
    product, left = call(
        functools.partial(product_kernel, n_chip),
        (shape(n_line, n_col, share, rows, cols), shape(n_line, n_col, share, rows, cols)),
        [],
        (right, coef, *left),
        near=(0, *range(2, 2 + n_pieces)),
        outs_near=(0, 1),
        flops=2 * share * n_half * (n_line * rows) ** 2 * n_col * cols,
        moved=8 * cells * hidden,
    )
    product = exchange(product.reshape(n_place, share, rows, cols)).reshape(hidden, rows, cols)
    (grad,) = call(
        middle_kernel,
        (shape(hidden, rows, cols),),
        [vmem(hidden, rows, cols, dtype=F32)],
        (product, dxh.reshape(hidden, rows, cols)),
        near=(0, 1),
        outs_near=(0,),
        flops=20 * cells * hidden,
        moved=8 * cells * hidden,
    )
    grad = exchange(grad.reshape(n_place, share, rows, cols))
    grad = grad.reshape(n_line, n_col, share, rows, cols)
    (sent,) = call(
        grad_right_kernel,
        (shape(n_half, n_line, n_col, share, rows, cols),),
        [vmem(n_half, n_line, n_col, share, rows, cols), sems(share)],
        (grad, left),
        near=(0, 1),
        flops=2 * share * n_half * (n_line * rows) ** 2 * n_col * cols,
        moved=8 * cells * hidden,
    )
    grad_right = exchange_all(sent).reshape(n_half, n_place, share, rows, cols)
    grad_left = call(
        grad_left_kernel,
        pieces_shape,
        [vmem(n_line, n_col, share, rows, cols)],
        (grad, right),
        near=(0, 1),
        outs_near=range(n_core),
        flops=2 * share * n_half * (n_line * rows) ** 2 * n_col * cols,
        moved=8 * cells * hidden,
    )
    grad_left = exchange_pieces(tuple(grad_left))
    update, dzg = call(
        update_kernel,
        (shape(rows, cols, width), shape(rows, width, cols)),
        [wide, block, vector, vector, square, square, block, short, plane, sems(6), sems(2)],
        (product, gate, cotangent, norm_gain, norm_bias, out_weight, gate_weight, sent),
        near=(0,),
        flops=2 * cells * width * 3 * hidden,
        moved=14 * cells * hidden,
    )
    (grad_pair,) = call(
        functools.partial(back_kernel, n_chip),
        (shape(rows, cols, width),),
        [
            vmem(rows, 4, hidden, cols), short, vmem(rows, cols, dtype=F32), short,
            vector, proj_v, block, plane, plane,
            sems(3), sems(n_groups), sems(n_groups), sems(n_groups), sems(2),
        ],
        (grad_right, coef, short_zhat, inv, dzg, gain_in, proj_weight, *grad_left),
        near=(0, *range(7, 7 + n_pieces)),
        flops=2 * cells * width * 5 * hidden,
        moved=30 * cells * width,
    )
    return (update, grad_pair)


def solution(mesh):
    n_grp, n_row, n_col = (mesh.shape[name] for name in ("grp", "row", "col"))
    n_half = math.gcd(n_row, 2)
    n_core = math.gcd(n_row // n_half, 2)
    split = jax.sharding.Mesh(
        mesh.devices.reshape(n_grp, n_half, n_row // (n_half * n_core), n_core, n_col),
        ("grp", "half", "row", "core", "col"),
    )
    cells = P(("grp", "half", "row", "core"), "col", None)
    return jax.shard_map(
        body,
        mesh=split,
        in_specs=(cells, P("grp"), P(), P(), P(), P(), P(), P(), P(), cells),
        out_specs=(cells, cells),
        check_vma=False,
    )
```

```python
import functools
import math

import jax
import jax.numpy as jnp
from jax import lax
from jax.experimental import pallas as pl
from jax.experimental.pallas import tpu as pltpu
from jax.sharding import PartitionSpec as P

EPS = 1e-05
F32 = jnp.float32
BF16 = jnp.bfloat16
MIB = 1 << 20


def dot(a, b, over=((1,), (0,))):
    return lax.dot_general(a, b, (over, ((), ())), preferred_element_type=F32)


def eye(size):
    down = lax.broadcasted_iota(jnp.int32, (size, size), 0)
    across = lax.broadcasted_iota(jnp.int32, (size, size), 1)
    return (down == across).astype(F32).astype(BF16)


def turned(values):
    return dot(eye(values.shape[1]), values, ((1,), (1,)))


def down_lanes(vector, lanes):
    return jnp.broadcast_to(vector, (lanes, vector.shape[1])).T


def turned_weight(weight):
    c, m = weight.shape
    return jnp.concatenate(
        [turned(weight[:, at : at + c]) for at in range(0, m, c)], axis=0
    ).astype(BF16)


def sigmoid(values):
    return 0.5 + 0.5 * jnp.tanh(0.5 * values)


def normalized(values):
    mean = jnp.mean(values, axis=0, keepdims=True)
    centred = values - mean
    var = jnp.mean(centred * centred, axis=0, keepdims=True)
    inverse = lax.rsqrt(var + EPS)
    return centred * inverse, inverse


def start(sems, copies):
    running = [
        pltpu.make_async_copy(source, target, sems.at[at])
        for at, (source, target) in enumerate(copies)
    ]
    for copy in running:
        copy.start()
    return running


def wait(copies):
    for copy in copies:
        copy.wait()


def groups_of(rows):
    size = math.gcd(rows, 4)
    return [(at, size) for at in range(0, rows, size)]


def side_by_side(ref, at, size):
    return jnp.concatenate([ref[at + r] for r in range(size)], axis=1)


def pair_mask(mask_s, mask_v, at, size, rows, cols):
    here = lax.axis_index("half")
    for name in ("row", "core"):
        here = here * lax.axis_size(name) + lax.axis_index(name)
    first_row = here * rows + at
    first_col = pl.multiple_of(lax.axis_index("col") * cols, cols)
    col_mask = mask_v[:, pl.ds(first_col, cols)].astype(F32)
    return jnp.concatenate(
        [col_mask * mask_s[first_row + r].astype(F32) for r in range(size)], axis=1
    )


def sources(n_chip, n_core):
    n_col = lax.axis_size("col")
    core = lax.axis_index("core")
    chip = lax.axis_index("row") * n_col + lax.axis_index("col")
    found = []
    for n in range(n_chip):
        other = chip ^ n
        for m in range(n_core):
            line = other // n_col * n_core + (core ^ m)
            found.append((m, n, line * n_col + other % n_col))
    return found


def received(refs, n_chip):
    n_core = len(refs) - n_chip + 1
    return [
        (number, refs[m][0] if n == 0 else refs[n_core + n - 1][m])
        for m, n, number in sources(n_chip, n_core)
    ]


def front_kernel(
    part, n_out, pair_h, mask_h, mask_row_h, gain_h, bias_h, proj_h, *refs
):
    outs = refs[:n_out]
    pair, mask_s, mask_v, gain, bias, proj_weight, zbar, plane, sems, *more = refs[n_out:]
    rows, cols, width = pair.shape
    hidden = plane.shape[0] // rows
    groups = groups_of(rows)
    *small, whole = start(
        sems,
        [
            (gain_h, gain), (bias_h, bias),
            (proj_h.at[:, pl.ds(part * hidden, 2 * hidden)], proj_weight),
            (mask_h, mask_s), (mask_row_h, mask_v), (pair_h, pair),
        ],
    )
    wait(small)
    gain_b = jnp.concatenate([down_lanes(gain[...], cols)] * groups[0][1], axis=1)
    bias_b = jnp.concatenate([down_lanes(bias[...], cols)] * groups[0][1], axis=1)
    weight = turned_weight(proj_weight[...])
    whole.wait()
    for at, size in groups:
        zhat, _ = normalized(turned(pair[at : at + size].reshape(size * cols, width)))
        zbar[:, at * cols : (at + size) * cols] = (zhat * gain_b + bias_b).astype(BF16)

    def channels(first, count):
        block = jnp.concatenate(
            [weight[first : first + count], weight[hidden + first : hidden + first + count]], axis=0
        )
        for at, size in groups:
            proj = dot(block, zbar[:, at * cols : (at + size) * cols])
            pm = pair_mask(mask_s, mask_v, at, size, rows, cols)
            values = sigmoid(proj[:count]) * proj[count:] * pm
            for r in range(size):
                plane[pl.ds(first * rows + at + r, count, stride=rows), :] = values[
                    :, r * cols : (r + 1) * cols
                ]

    if n_out > 1:
        channels(0, hidden)
        give_pieces(plane, outs)
        return
    (out_h,), (ready, out_sems) = outs, more
    n_place, share = ready.shape[:2]
    size = n_place // math.gcd(n_place, 2)
    leaving = []
    for n, at in enumerate(range(0, n_place, size)):
        channels(at * share, size * share)
        values = plane[at * share * rows : (at + size) * share * rows]
        ready[at : at + size] = values.reshape(size, *ready.shape[1:]).astype(BF16)
        for half in range(out_h.shape[0]):
            copy = pltpu.make_async_copy(
                ready.at[pl.ds(at, size)], out_h.at[half, pl.ds(at, size)], out_sems.at[half, n]
            )
            copy.start()
            leaving.append(copy)
    wait(leaving)


def give_pieces(plane, outs):
    n_chip = outs[0].shape[0]
    length = plane.shape[0] // (len(outs) * n_chip)
    for m, n, number in sources(n_chip, len(outs)):
        first = pl.multiple_of(number * length, length)
        values = plane[pl.ds(first, length), :]
        outs[m][n] = values.reshape(outs[m].shape[1:]).astype(BF16)


def side_kernel(
    pair_h, cot_h, gain_h, bias_h, gate_h, norm_gain_h, out_w_h,
    zhat_h, short_h, inv_h, gate_out_h, dxh_out,
    pair, cot, gain, bias, gate_weight, norm_gain, out_weight,
    zhat_out, short_out, inv_out, gate_out, in_sems, out_sems,
):
    rows, cols, width = pair.shape
    hidden = out_weight.shape[0]
    wait(
        start(
            in_sems,
            [
                (pair_h, pair), (cot_h, cot), (gain_h, gain), (bias_h, bias),
                (gate_h, gate_weight), (norm_gain_h, norm_gain), (out_w_h, out_weight),
            ],
        )
    )
    groups = groups_of(rows)
    gain_b = jnp.concatenate([down_lanes(gain[...], cols)] * groups[0][1], axis=1)
    bias_b = jnp.concatenate([down_lanes(bias[...], cols)] * groups[0][1], axis=1)
    norm_gain_b = jnp.concatenate([down_lanes(norm_gain[...], cols)] * groups[0][1], axis=1)
    gate_t = turned_weight(gate_weight[...])
    for at, size in groups:
        zhat, inverse = normalized(turned(pair[at : at + size].reshape(size * cols, width)))
        zbar = (zhat * gain_b + bias_b).astype(BF16)
        gate = sigmoid(dot(gate_t, zbar))
        cot_t = turned(cot[at : at + size].reshape(size * cols, width))
        dxh = dot(out_weight[...], (cot_t * gate).astype(BF16)) * norm_gain_b
        dxh = dxh - jnp.mean(dxh, axis=0, keepdims=True)
        for r in range(size):
            lanes = slice(r * cols, (r + 1) * cols)
            zhat_out[at + r] = zhat[:, lanes]
            short_out[at + r] = zhat[:, lanes].astype(BF16)
            inv_out[at + r : at + r + 1] = inverse[:, lanes]
            gate_out[at + r] = gate[:, lanes]
            dxh_out[pl.ds(at + r, hidden, stride=rows), :] = dxh[:, lanes]
    wait(
        start(
            out_sems,
            [
                (zhat_out, zhat_h), (short_out, short_h), (inv_out, inv_h),
                (gate_out, gate_out_h),
            ],
        )
    )


def factors_kernel(
    zhat_h, mask_h, mask_row_h, gain_h, bias_h, proj_h, coef_h,
    zhat, mask_s, mask_v, gain, bias, proj_weight, coef, in_sems, out_sems,
):
    rows, width, cols = zhat.shape
    hidden = coef.shape[2]
    wait(
        start(
            in_sems,
            [
                (zhat_h, zhat), (mask_h, mask_s), (mask_row_h, mask_v), (gain_h, gain),
                (bias_h, bias), (proj_h, proj_weight),
            ],
        )
    )
    groups = groups_of(rows)
    gain_b = jnp.concatenate([down_lanes(gain[...], cols)] * groups[0][1], axis=1)
    bias_b = jnp.concatenate([down_lanes(bias[...], cols)] * groups[0][1], axis=1)
    weight = turned_weight(proj_weight[...])
    leaving = []
    for n, (at, size) in enumerate(groups):
        zbar = (side_by_side(zhat, at, size) * gain_b + bias_b).astype(BF16)
        pm = pair_mask(mask_s, mask_v, at, size, rows, cols)
        for part in (0, 2):
            s = sigmoid(dot(weight[part * hidden : (part + 1) * hidden], zbar))
            q = dot(weight[(part + 1) * hidden : (part + 2) * hidden], zbar)
            second = pm * s
            first = second * q * (1.0 - s)
            for r in range(size):
                lanes = slice(r * cols, (r + 1) * cols)
                coef[at + r, part] = first[:, lanes].astype(BF16)
                coef[at + r, part + 1] = second[:, lanes].astype(BF16)
        copy = pltpu.make_async_copy(
            coef.at[pl.ds(at, size)], coef_h.at[pl.ds(at, size)], out_sems.at[n]
        )
        copy.start()
        leaving.append(copy)
    wait(leaving)


def channel_matrix(ref, at):
    *_, n_col, _, rows, cols = ref.shape
    lead = (slice(None),) * (len(ref.shape) - 4)
    return jnp.concatenate(
        [ref[(*lead, c, at)].reshape(-1, cols) for c in range(n_col)], axis=1
    )


def put_channel(ref, at, values):
    *shape, n_col, _, rows, cols = ref.shape
    lead = (slice(None),) * len(shape)
    values = values.astype(BF16)
    for c in range(n_col):
        ref[(*lead, c, at)] = values[:, c * cols : (c + 1) * cols].reshape(*shape, rows, cols)


def product_kernel(n_chip, right, after, *refs):
    pieces, (out, left) = refs[:-2], refs[-2:]
    n_col, share = left.shape[1:3]
    for number, piece in received(pieces, n_chip):
        left[number // n_col, number % n_col] = piece
    for h in range(share):
        values = dot(channel_matrix(left, h), channel_matrix(right, h), ((1,), (1,)))
        put_channel(out, h, values)


def middle_kernel(product, dxh, out, xhat):
    hidden = product.shape[0]
    values = product[...].astype(F32)
    mean = jnp.sum(values, axis=0) * (1.0 / hidden)
    centred = values - mean
    var = jnp.sum(centred * centred, axis=0) * (1.0 / hidden)
    inverse = lax.rsqrt(var + EPS)
    xhat[...] = centred * inverse
    m2 = jnp.sum(dxh[...] * xhat[...], axis=0) * (1.0 / hidden)
    out[...] = ((dxh[...] - xhat[...] * m2) * inverse).astype(BF16)


def update_kernel(
    product, gate_h, cot_h, norm_gain_h, norm_bias_h, out_w_h, gate_w_h, after, update_h, dzg_h,
    gate, cot, norm_gain, norm_bias, out_weight, gate_weight, update, dzg, spread,
    in_sems, out_sems,
):
    hidden, rows, cols = product.shape
    width = cot.shape[2]
    copies = start(
        in_sems,
        [
            (gate_h, gate), (cot_h, cot), (norm_gain_h, norm_gain), (norm_bias_h, norm_bias),
            (out_w_h, out_weight), (gate_w_h, gate_weight),
        ],
    )
    spread[...] = product[...].astype(F32).reshape(hidden * rows, cols)
    wait(copies)
    groups = groups_of(rows)
    norm_gain_b = jnp.concatenate([down_lanes(norm_gain[...], cols)] * groups[0][1], axis=1)
    norm_bias_b = jnp.concatenate([down_lanes(norm_bias[...], cols)] * groups[0][1], axis=1)
    out_t = turned_weight(out_weight[...])
    for at, size in groups:
        xhat, _ = normalized(
            jnp.concatenate(
                [spread[pl.ds(at + r, hidden, stride=rows), :] for r in range(size)], axis=1
            )
        )
        ybar = (xhat * norm_gain_b + norm_bias_b).astype(BF16)
        u = dot(out_t, ybar)
        g = side_by_side(gate, at, size)
        done = (g * u).astype(BF16)
        cot_t = turned(cot[at : at + size].reshape(size * cols, width))
        back = dot(gate_weight[...], (cot_t * u * g * (1.0 - g)).astype(BF16))
        for r in range(size):
            lanes = slice(r * cols, (r + 1) * cols)
            update[at + r] = turned(done[:, lanes]).astype(BF16)
            dzg[at + r] = back[:, lanes].astype(BF16)
    wait(start(out_sems, [(update, update_h), (dzg, dzg_h)]))


def grad_right_kernel(grad, left, out_h, ready, sems):
    lead = (slice(None),) * (len(ready.shape) - 3)
    leaving = []
    for h in range(ready.shape[-3]):
        values = dot(channel_matrix(grad, h), channel_matrix(left, h), ((0,), (0,)))
        put_channel(ready, h, values)
        part = (*lead, pl.ds(h, 1))
        copy = pltpu.make_async_copy(ready.at[part], out_h.at[part], sems.at[h])
        copy.start()
        leaving.append(copy)
    wait(leaving)


def grad_left_kernel(grad, right, *refs):
    outs, ready = refs[:-1], refs[-1]
    n_col, share = ready.shape[1:3]
    for h in range(share):
        put_channel(ready, h, dot(channel_matrix(grad, h), channel_matrix(right, h)))
    for m, n, number in sources(outs[0].shape[0], len(outs)):
        outs[m][n] = ready[number // n_col, number % n_col]


def back_kernel(n_chip, grads, coef_h, zhat_h, inv_h, dzg_h, gain_h, proj_h, *refs):
    pieces, out_h = refs[:-15], refs[-15]
    (
        coef, zhat, inv, dzg, gain, proj_weight, out, left, right,
        sems, coef_sems, zhat_sems, dzg_sems, out_sems,
    ) = refs[-14:]
    rows, cols, width = out.shape
    hidden = left.shape[0] // rows
    groups = groups_of(rows)
    ahead = rows // math.gcd(rows, 2)
    blocks = [
        [
            pltpu.make_async_copy(
                source.at[pl.ds(at, size)], target.at[pl.ds(at, size)], sem.at[n]
            )
            for source, target, sem in (
                (coef_h, coef, coef_sems), (zhat_h, zhat, zhat_sems), (dzg_h, dzg, dzg_sems)
            )
        ]
        for n, (at, size) in enumerate(groups)
    ]
    for copy in blocks[0]:
        copy.start()
    small = start(sems, [(gain_h, gain), (proj_h, proj_weight), (inv_h, inv)])
    arrived = received(pieces, n_chip)
    length = left.shape[0] // len(arrived)
    for number, piece in arrived:
        first = pl.multiple_of(number * length, length)
        left[pl.ds(first, length), :] = piece.astype(F32).reshape(length, cols)
    for copy in sum(blocks[1:], []):
        copy.start()
    total = grads[0].astype(F32)
    for half in range(1, grads.shape[0]):
        total = total + grads[half].astype(F32)
    right[...] = total.reshape(right.shape)
    wait(small)
    gain_b = jnp.concatenate([down_lanes(gain[...], cols)] * groups[0][1], axis=1)
    leaving = []
    for n, (at, size) in enumerate(groups):
        both = [
            [plane[pl.ds(at + r, hidden, stride=rows), :].astype(BF16) for plane in (left, right)]
            for r in range(size)
        ]
        wait(blocks[n])
        columns = []
        for r, (gl, gr) in enumerate(both):
            columns.append(
                jnp.concatenate(
                    [g * coef[at + r, part] for part, g in enumerate((gl, gl, gr, gr))], axis=0
                )
            )
        back = dot(proj_weight[...], jnp.concatenate(columns, axis=1))
        dzh = (back + side_by_side(dzg, at, size).astype(F32)) * gain_b
        z = side_by_side(zhat, at, size).astype(F32)
        inverse = jnp.concatenate([inv[at + r : at + r + 1] for r in range(size)], axis=1)
        m1 = jnp.mean(dzh, axis=0, keepdims=True)
        m2 = jnp.mean(dzh * z, axis=0, keepdims=True)
        grad = ((dzh - m1 - z * m2) * inverse).astype(BF16)
        for r in range(size):
            out[at + r] = turned(grad[:, r * cols : (r + 1) * cols]).astype(BF16)
        done = at + size
        if done % ahead == 0:
            part = pl.ds(done - ahead, ahead)
            copy = pltpu.make_async_copy(
                out.at[part], out_h.at[part], out_sems.at[done // ahead - 1]
            )
            copy.start()
            leaving.append(copy)
    wait(leaving)


def call(kernel, outs, scratch, args, near=(), outs_near=(), flops=0, moved=0):
    here, far = (pl.BlockSpec(memory_space=space) for space in (pltpu.VMEM, pltpu.HBM))
    specs = [here if at in near else far for at in range(len(args))]
    return pl.pallas_call(
        kernel,
        out_shape=[
            out if at in outs_near else pltpu.HBM(out.shape, out.dtype)
            for at, out in enumerate(outs)
        ],
        in_specs=specs,
        out_specs=[here if at in outs_near else far for at in range(len(outs))],
        scratch_shapes=scratch,
        compiler_params=pltpu.CompilerParams(vmem_limit_bytes=16 * MIB),
        cost_estimate=pl.CostEstimate(flops=flops, bytes_accessed=moved, transcendentals=0),
    )(
        *[
            pltpu.with_memory_space_constraint(arg, pltpu.HBM) if spec is far else arg
            for arg, spec in zip(args, specs)
        ]
    )


def body(
    pair, mask, gain_in, bias_in, proj_weight, gate_weight,
    product_norm_gain, product_norm_bias, out_weight, cotangent,
):
    rows, cols, width = pair.shape
    hidden = out_weight.shape[0]
    n_half = lax.axis_size("half")
    n_row = lax.axis_size("row")
    n_core = lax.axis_size("core")
    n_col = lax.axis_size("col")
    n_chip = n_row * n_col
    n_line = n_row * n_core
    n_place = n_line * n_col
    within = ("row", "core", "col")
    share = hidden // n_place
    cells = rows * cols
    n_groups = len(groups_of(rows))
    mask_row = mask.reshape(1, -1)
    gain_in, bias_in = gain_in.reshape(1, -1), bias_in.reshape(1, -1)
    norm_gain, norm_bias = product_norm_gain.reshape(1, -1), product_norm_bias.reshape(1, -1)

    def shape(*dims, dtype=BF16):
        return jax.ShapeDtypeStruct(dims, dtype)

    def vmem(*dims, dtype=BF16):
        return pltpu.VMEM(dims, dtype)

    def sems(count):
        return pltpu.SemaphoreType.DMA((count,))

    def exchange(values):
        return lax.all_to_all(values, within, split_axis=0, concat_axis=0, tiled=True)

    def exchange_all(values):
        flat = values.reshape(n_half * n_place, share, rows, cols)
        return lax.all_to_all(
            flat, ("half", *within), split_axis=0, concat_axis=0, tiled=True
        )

    def permute(values, axes, size, distance):
        return lax.ppermute(values, axes, [(at, at ^ distance) for at in range(size)])

    def exchange_pieces(pieces):
        first = [pieces[0]]
        first += [permute(pieces[m], ("core",), n_core, m) for m in range(1, n_core)]
        second = [
            permute(jnp.stack([piece[n] for piece in first]), ("row", "col"), n_chip, n)
            for n in range(n_chip - 1, 0, -1)
        ]
        return tuple(first + second[::-1])

    mask_s = pltpu.SMEM(mask.shape, jnp.int32)
    mask_v = vmem(*mask_row.shape, dtype=jnp.int32)
    vector = vmem(1, width, dtype=F32)
    plane = vmem(hidden * rows, cols, dtype=F32)
    block = vmem(rows, cols, width)
    wide = vmem(rows, width, cols, dtype=F32)
    short = vmem(rows, width, cols)
    square = vmem(width, hidden)
    proj_v = vmem(width, 4 * hidden)
    pieces_shape = (shape(n_chip, share, rows, cols),) * n_core
    n_pieces = n_core + n_chip - 1

    def front(part, outs, scratch, near):
        return call(
            functools.partial(front_kernel, part, len(outs)),
            outs,
            [
                block, mask_s, mask_v, vector, vector, vmem(width, 2 * hidden),
                vmem(width, cells), plane, sems(6), *scratch,
            ],
            (pair, mask, mask_row, gain_in, bias_in, proj_weight),
            outs_near=near,
            flops=2 * cells * width * 3 * hidden,
            moved=5 * cells * width,
        )

    everywhere = vmem(n_place, share, rows, cols)
    (right,) = front(
        2,
        (shape(n_half, n_place, share, rows, cols),),
        [everywhere, pltpu.SemaphoreType.DMA((n_half, math.gcd(n_place, 2)))],
        (),
    )
    right = exchange_all(right).reshape(n_half, n_line, n_col, share, rows, cols)
    left = exchange_pieces(tuple(front(0, pieces_shape, [], range(n_core))))
    zhat, short_zhat, inv, gate, dxh = call(
        side_kernel,
        (
            shape(rows, width, cols, dtype=F32),
            shape(rows, width, cols),
            shape(rows, cols, dtype=F32),
            shape(rows, width, cols, dtype=F32),
            shape(hidden * rows, cols, dtype=F32),
        ),
        [
            block, block, vector, vector, square, vector, square,
            wide, short, vmem(rows, cols, dtype=F32), wide, sems(7), sems(4),
        ],
        (pair, cotangent, gain_in, bias_in, gate_weight, norm_gain, out_weight),
        outs_near=(4,),
        flops=2 * cells * width * 4 * hidden,
        moved=16 * cells * width,
    )
    (coef,) = call(
        factors_kernel,
        (shape(rows, 4, hidden, cols),),
        [
            wide, mask_s, mask_v, vector, vector, proj_v, vmem(rows, 4, hidden, cols),
            sems(6), sems(n_groups),
        ],
        (zhat, mask, mask_row, gain_in, bias_in, proj_weight),
        flops=2 * cells * width * 5 * hidden,
        moved=16 * cells * width,
    )
    product, left = call(
        functools.partial(product_kernel, n_chip),
        (shape(n_line, n_col, share, rows, cols), shape(n_line, n_col, share, rows, cols)),
        [],
        (right, coef, *left),
        near=(0, *range(2, 2 + n_pieces)),
        outs_near=(0, 1),
        flops=2 * share * n_half * (n_line * rows) ** 2 * n_col * cols,
        moved=8 * cells * hidden,
    )
    product = exchange(product.reshape(n_place, share, rows, cols)).reshape(hidden, rows, cols)
    (grad,) = call(
        middle_kernel,
        (shape(hidden, rows, cols),),
        [vmem(hidden, rows, cols, dtype=F32)],
        (product, dxh.reshape(hidden, rows, cols)),
        near=(0, 1),
        outs_near=(0,),
        flops=20 * cells * hidden,
        moved=8 * cells * hidden,
    )
    grad = exchange(grad.reshape(n_place, share, rows, cols))
    grad = grad.reshape(n_line, n_col, share, rows, cols)
    (sent,) = call(
        grad_right_kernel,
        (shape(n_half, n_line, n_col, share, rows, cols),),
        [vmem(n_half, n_line, n_col, share, rows, cols), sems(share)],
        (grad, left),
        near=(0, 1),
        flops=2 * share * n_half * (n_line * rows) ** 2 * n_col * cols,
        moved=8 * cells * hidden,
    )
    grad_right = exchange_all(sent).reshape(n_half, n_place, share, rows, cols)
    grad_left = call(
        grad_left_kernel,
        pieces_shape,
        [vmem(n_line, n_col, share, rows, cols)],
        (grad, right),
        near=(0, 1),
        outs_near=range(n_core),
        flops=2 * share * n_half * (n_line * rows) ** 2 * n_col * cols,
        moved=8 * cells * hidden,
    )
    grad_left = exchange_pieces(tuple(grad_left))
    update, dzg = call(
        update_kernel,
        (shape(rows, cols, width), shape(rows, width, cols)),
        [wide, block, vector, vector, square, square, block, short, plane, sems(6), sems(2)],
        (product, gate, cotangent, norm_gain, norm_bias, out_weight, gate_weight, sent),
        near=(0,),
        flops=2 * cells * width * 3 * hidden,
        moved=14 * cells * hidden,
    )
    (grad_pair,) = call(
        functools.partial(back_kernel, n_chip),
        (shape(rows, cols, width),),
        [
            vmem(rows, 4, hidden, cols), short, vmem(rows, cols, dtype=F32), short,
            vector, proj_v, block, plane, plane,
            sems(3), sems(n_groups), sems(n_groups), sems(n_groups), sems(2),
        ],
        (grad_right, coef, short_zhat, inv, dzg, gain_in, proj_weight, *grad_left),
        near=(0, *range(7, 7 + n_pieces)),
        flops=2 * cells * width * 5 * hidden,
        moved=30 * cells * width,
    )
    return (update, grad_pair)


def solution(mesh):
    n_grp, n_row, n_col = (mesh.shape[name] for name in ("grp", "row", "col"))
    n_half = math.gcd(n_row, 2)
    n_core = math.gcd(n_row // n_half, 2)
    split = jax.sharding.Mesh(
        mesh.devices.reshape(n_grp, n_half, n_row // (n_half * n_core), n_core, n_col),
        ("grp", "half", "row", "core", "col"),
    )
    cells = P(("grp", "half", "row", "core"), "col", None)
    return jax.shard_map(
        body,
        mesh=split,
        in_specs=(cells, P("grp"), P(), P(), P(), P(), P(), P(), P(), cells),
        out_specs=(cells, cells),
        check_vma=False,
    )
```

```python
import functools
import math

import jax
import jax.numpy as jnp
from jax import lax
from jax.experimental import pallas as pl
from jax.experimental.pallas import tpu as pltpu
from jax.sharding import PartitionSpec as P

EPS = 1e-05
F32 = jnp.float32
BF16 = jnp.bfloat16
MIB = 1 << 20


def dot(a, b, over=((1,), (0,))):
    return lax.dot_general(a, b, (over, ((), ())), preferred_element_type=F32)


def eye(size):
    down = lax.broadcasted_iota(jnp.int32, (size, size), 0)
    across = lax.broadcasted_iota(jnp.int32, (size, size), 1)
    return (down == across).astype(F32).astype(BF16)


def turned(values):
    return dot(eye(values.shape[1]), values, ((1,), (1,)))


def down_lanes(vector, lanes):
    return jnp.broadcast_to(vector, (lanes, vector.shape[1])).T


def turned_weight(weight):
    c, m = weight.shape
    return jnp.concatenate(
        [turned(weight[:, at : at + c]) for at in range(0, m, c)], axis=0
    ).astype(BF16)


def sigmoid(values):
    return 0.5 + 0.5 * jnp.tanh(0.5 * values)


def normalized(values):
    mean = jnp.mean(values, axis=0, keepdims=True)
    centred = values - mean
    var = jnp.mean(centred * centred, axis=0, keepdims=True)
    inverse = lax.rsqrt(var + EPS)
    return centred * inverse, inverse


def start(sems, copies):
    running = [
        pltpu.make_async_copy(source, target, sems.at[at])
        for at, (source, target) in enumerate(copies)
    ]
    for copy in running:
        copy.start()
    return running


def wait(copies):
    for copy in copies:
        copy.wait()


def groups_of(rows):
    size = math.gcd(rows, 4)
    return [(at, size) for at in range(0, rows, size)]


def side_by_side(ref, at, size):
    return jnp.concatenate([ref[at + r] for r in range(size)], axis=1)


def pair_mask(mask_s, mask_v, at, size, rows, cols):
    here = lax.axis_index("half")
    for name in ("row", "core"):
        here = here * lax.axis_size(name) + lax.axis_index(name)
    first_row = here * rows + at
    first_col = pl.multiple_of(lax.axis_index("col") * cols, cols)
    col_mask = mask_v[:, pl.ds(first_col, cols)].astype(F32)
    return jnp.concatenate(
        [col_mask * mask_s[first_row + r].astype(F32) for r in range(size)], axis=1
    )


def sources(n_chip, n_core):
    n_col = lax.axis_size("col")
    core = lax.axis_index("core")
    chip = lax.axis_index("row") * n_col + lax.axis_index("col")
    found = []
    for n in range(n_chip):
        other = chip ^ n
        for m in range(n_core):
            line = other // n_col * n_core + (core ^ m)
            found.append((m, n, line * n_col + other % n_col))
    return found


def received(refs, n_chip):
    n_core = len(refs) - n_chip + 1
    return [
        (number, refs[m][0] if n == 0 else refs[n_core + n - 1][m])
        for m, n, number in sources(n_chip, n_core)
    ]


def front_kernel(
    part, n_out, pair_h, mask_h, mask_row_h, gain_h, bias_h, proj_h, *refs
):
    outs = refs[:n_out]
    pair, mask_s, mask_v, gain, bias, proj_weight, zbar, plane, sems, *more = refs[n_out:]
    rows, cols, width = pair.shape
    hidden = plane.shape[0] // rows
    groups = groups_of(rows)
    *small, whole = start(
        sems,
        [
            (gain_h, gain), (bias_h, bias),
            (proj_h.at[:, pl.ds(part * hidden, 2 * hidden)], proj_weight),
            (mask_h, mask_s), (mask_row_h, mask_v), (pair_h, pair),
        ],
    )
    wait(small)
    gain_b = jnp.concatenate([down_lanes(gain[...], cols)] * groups[0][1], axis=1)
    bias_b = jnp.concatenate([down_lanes(bias[...], cols)] * groups[0][1], axis=1)
    weight = turned_weight(proj_weight[...])
    whole.wait()
    for at, size in groups:
        zhat, _ = normalized(turned(pair[at : at + size].reshape(size * cols, width)))
        zbar[:, at * cols : (at + size) * cols] = (zhat * gain_b + bias_b).astype(BF16)

    def channels(first, count):
        block = jnp.concatenate(
            [weight[first : first + count], weight[hidden + first : hidden + first + count]], axis=0
        )
        for at, size in groups:
            proj = dot(block, zbar[:, at * cols : (at + size) * cols])
            pm = pair_mask(mask_s, mask_v, at, size, rows, cols)
            values = sigmoid(proj[:count]) * proj[count:] * pm
            for r in range(size):
                plane[pl.ds(first * rows + at + r, count, stride=rows), :] = values[
                    :, r * cols : (r + 1) * cols
                ]

    if n_out > 1:
        channels(0, hidden)
        give_pieces(plane, outs)
        return
    (out_h,), (ready, out_sems) = outs, more
    n_place, share = ready.shape[:2]
    size = n_place // math.gcd(n_place, 2)
    leaving = []
    for n, at in enumerate(range(0, n_place, size)):
        channels(at * share, size * share)
        values = plane[at * share * rows : (at + size) * share * rows]
        ready[at : at + size] = values.reshape(size, *ready.shape[1:]).astype(BF16)
        for half in range(out_h.shape[0]):
            copy = pltpu.make_async_copy(
                ready.at[pl.ds(at, size)], out_h.at[half, pl.ds(at, size)], out_sems.at[half, n]
            )
            copy.start()
            leaving.append(copy)
    wait(leaving)


def give_pieces(plane, outs):
    n_chip = outs[0].shape[0]
    length = plane.shape[0] // (len(outs) * n_chip)
    for m, n, number in sources(n_chip, len(outs)):
        first = pl.multiple_of(number * length, length)
        values = plane[pl.ds(first, length), :]
        outs[m][n] = values.reshape(outs[m].shape[1:]).astype(BF16)


def side_kernel(
    pair_h, cot_h, gain_h, bias_h, gate_h, norm_gain_h, out_w_h,
    zhat_h, short_h, inv_h, gate_out_h, dxh_out,
    pair, cot, gain, bias, gate_weight, norm_gain, out_weight,
    zhat_out, short_out, inv_out, gate_out, in_sems, out_sems,
):
    rows, cols, width = pair.shape
    hidden = out_weight.shape[0]
    wait(
        start(
            in_sems,
            [
                (pair_h, pair), (cot_h, cot), (gain_h, gain), (bias_h, bias),
                (gate_h, gate_weight), (norm_gain_h, norm_gain), (out_w_h, out_weight),
            ],
        )
    )
    groups = groups_of(rows)
    gain_b = jnp.concatenate([down_lanes(gain[...], cols)] * groups[0][1], axis=1)
    bias_b = jnp.concatenate([down_lanes(bias[...], cols)] * groups[0][1], axis=1)
    norm_gain_b = jnp.concatenate([down_lanes(norm_gain[...], cols)] * groups[0][1], axis=1)
    gate_t = turned_weight(gate_weight[...])
    for at, size in groups:
        zhat, inverse = normalized(turned(pair[at : at + size].reshape(size * cols, width)))
        zbar = (zhat * gain_b + bias_b).astype(BF16)
        gate = sigmoid(dot(gate_t, zbar))
        cot_t = turned(cot[at : at + size].reshape(size * cols, width))
        dxh = dot(out_weight[...], (cot_t * gate).astype(BF16)) * norm_gain_b
        dxh = dxh - jnp.mean(dxh, axis=0, keepdims=True)
        for r in range(size):
            lanes = slice(r * cols, (r + 1) * cols)
            zhat_out[at + r] = zhat[:, lanes]
            short_out[at + r] = zhat[:, lanes].astype(BF16)
            inv_out[at + r : at + r + 1] = inverse[:, lanes]
            gate_out[at + r] = gate[:, lanes]
            dxh_out[pl.ds(at + r, hidden, stride=rows), :] = dxh[:, lanes]
    wait(
        start(
            out_sems,
            [
                (zhat_out, zhat_h), (short_out, short_h), (inv_out, inv_h),
                (gate_out, gate_out_h),
            ],
        )
    )


def factors_kernel(
    zhat_h, mask_h, mask_row_h, gain_h, bias_h, proj_h, coef_h,
    zhat, mask_s, mask_v, gain, bias, proj_weight, coef, in_sems, out_sems,
):
    rows, width, cols = zhat.shape
    hidden = coef.shape[2]
    wait(
        start(
            in_sems,
            [
                (zhat_h, zhat), (mask_h, mask_s), (mask_row_h, mask_v), (gain_h, gain),
                (bias_h, bias), (proj_h, proj_weight),
            ],
        )
    )
    groups = groups_of(rows)
    gain_b = jnp.concatenate([down_lanes(gain[...], cols)] * groups[0][1], axis=1)
    bias_b = jnp.concatenate([down_lanes(bias[...], cols)] * groups[0][1], axis=1)
    weight = turned_weight(proj_weight[...])
    leaving = []
    for n, (at, size) in enumerate(groups):
        zbar = (side_by_side(zhat, at, size) * gain_b + bias_b).astype(BF16)
        pm = pair_mask(mask_s, mask_v, at, size, rows, cols)
        for part in (0, 2):
            s = sigmoid(dot(weight[part * hidden : (part + 1) * hidden], zbar))
            q = dot(weight[(part + 1) * hidden : (part + 2) * hidden], zbar)
            second = pm * s
            first = second * q * (1.0 - s)
            for r in range(size):
                lanes = slice(r * cols, (r + 1) * cols)
                coef[at + r, part] = first[:, lanes].astype(BF16)
                coef[at + r, part + 1] = second[:, lanes].astype(BF16)
        copy = pltpu.make_async_copy(
            coef.at[pl.ds(at, size)], coef_h.at[pl.ds(at, size)], out_sems.at[n]
        )
        copy.start()
        leaving.append(copy)
    wait(leaving)


def channel_matrix(ref, at):
    *_, n_col, _, rows, cols = ref.shape
    lead = (slice(None),) * (len(ref.shape) - 4)
    return jnp.concatenate(
        [ref[(*lead, c, at)].reshape(-1, cols) for c in range(n_col)], axis=1
    )


def put_channel(ref, at, values):
    *shape, n_col, _, rows, cols = ref.shape
    lead = (slice(None),) * len(shape)
    values = values.astype(BF16)
    for c in range(n_col):
        ref[(*lead, c, at)] = values[:, c * cols : (c + 1) * cols].reshape(*shape, rows, cols)


def product_kernel(n_chip, right, after, *refs):
    pieces, (out, left) = refs[:-2], refs[-2:]
    n_col, share = left.shape[1:3]
    for number, piece in received(pieces, n_chip):
        left[number // n_col, number % n_col] = piece
    for h in range(share):
        values = dot(channel_matrix(left, h), channel_matrix(right, h), ((1,), (1,)))
        put_channel(out, h, values)


def middle_kernel(product, dxh, out, xhat):
    hidden = product.shape[0]
    values = product[...].astype(F32)
    mean = jnp.sum(values, axis=0) * (1.0 / hidden)
    centred = values - mean
    var = jnp.sum(centred * centred, axis=0) * (1.0 / hidden)
    inverse = lax.rsqrt(var + EPS)
    xhat[...] = centred * inverse
    m2 = jnp.sum(dxh[...] * xhat[...], axis=0) * (1.0 / hidden)
    out[...] = ((dxh[...] - xhat[...] * m2) * inverse).astype(BF16)


def update_kernel(
    product, gate_h, cot_h, norm_gain_h, norm_bias_h, out_w_h, gate_w_h, after, update_h, dzg_h,
    gate, cot, norm_gain, norm_bias, out_weight, gate_weight, update, dzg, spread,
    in_sems, out_sems,
):
    hidden, rows, cols = product.shape
    width = cot.shape[2]
    copies = start(
        in_sems,
        [
            (gate_h, gate), (cot_h, cot), (norm_gain_h, norm_gain), (norm_bias_h, norm_bias),
            (out_w_h, out_weight), (gate_w_h, gate_weight),
        ],
    )
    spread[...] = product[...].astype(F32).reshape(hidden * rows, cols)
    wait(copies)
    groups = groups_of(rows)
    norm_gain_b = jnp.concatenate([down_lanes(norm_gain[...], cols)] * groups[0][1], axis=1)
    norm_bias_b = jnp.concatenate([down_lanes(norm_bias[...], cols)] * groups[0][1], axis=1)
    out_t = turned_weight(out_weight[...])
    for at, size in groups:
        xhat, _ = normalized(
            jnp.concatenate(
                [spread[pl.ds(at + r, hidden, stride=rows), :] for r in range(size)], axis=1
            )
        )
        ybar = (xhat * norm_gain_b + norm_bias_b).astype(BF16)
        u = dot(out_t, ybar)
        g = side_by_side(gate, at, size)
        done = (g * u).astype(BF16)
        cot_t = turned(cot[at : at + size].reshape(size * cols, width))
        back = dot(gate_weight[...], (cot_t * u * g * (1.0 - g)).astype(BF16))
        for r in range(size):
            lanes = slice(r * cols, (r + 1) * cols)
            update[at + r] = turned(done[:, lanes]).astype(BF16)
            dzg[at + r] = back[:, lanes].astype(BF16)
    wait(start(out_sems, [(update, update_h), (dzg, dzg_h)]))


def grad_right_kernel(grad, left, out_h, ready, sems):
    lead = (slice(None),) * (len(ready.shape) - 3)
    leaving = []
    for h in range(ready.shape[-3]):
        values = dot(channel_matrix(grad, h), channel_matrix(left, h), ((0,), (0,)))
        put_channel(ready, h, values)
        part = (*lead, pl.ds(h, 1))
        copy = pltpu.make_async_copy(ready.at[part], out_h.at[part], sems.at[h])
        copy.start()
        leaving.append(copy)
    wait(leaving)


def grad_left_kernel(grad, right, *refs):
    outs, ready = refs[:-1], refs[-1]
    n_col, share = ready.shape[1:3]
    for h in range(share):
        put_channel(ready, h, dot(channel_matrix(grad, h), channel_matrix(right, h)))
    for m, n, number in sources(outs[0].shape[0], len(outs)):
        outs[m][n] = ready[number // n_col, number % n_col]


def back_kernel(n_chip, grads, coef_h, zhat_h, inv_h, dzg_h, gain_h, proj_h, *refs):
    pieces, out_h = refs[:-14], refs[-14]
    (
        coef, zhat, inv, dzg, gain, proj_weight, out, left, right,
        sems, near_sems, far_sems, out_sems,
    ) = refs[-13:]
    rows, cols, width = out.shape
    hidden = left.shape[0] // rows
    groups = groups_of(rows)
    ahead = rows // math.gcd(rows, 2)
    blocks = {
        at: start(
            sem,
            [
                (source.at[pl.ds(at, ahead)], target.at[pl.ds(at, ahead)])
                for source, target in ((coef_h, coef), (zhat_h, zhat), (dzg_h, dzg))
            ],
        )
        for at, sem in zip(range(0, rows, ahead), (near_sems, far_sems))
    }
    small = start(sems, [(gain_h, gain), (proj_h, proj_weight), (inv_h, inv)])
    arrived = received(pieces, n_chip)
    length = left.shape[0] // len(arrived)
    for number, piece in arrived:
        first = pl.multiple_of(number * length, length)
        left[pl.ds(first, length), :] = piece.astype(F32).reshape(length, cols)
    total = grads[0].astype(F32)
    for half in range(1, grads.shape[0]):
        total = total + grads[half].astype(F32)
    right[...] = total.reshape(right.shape)
    wait(small)
    gain_b = jnp.concatenate([down_lanes(gain[...], cols)] * groups[0][1], axis=1)
    leaving = []
    for at, size in groups:
        both = [
            [plane[pl.ds(at + r, hidden, stride=rows), :].astype(BF16) for plane in (left, right)]
            for r in range(size)
        ]
        wait(blocks.get(at, []))
        columns = []
        for r, (gl, gr) in enumerate(both):
            columns.append(
                jnp.concatenate(
                    [g * coef[at + r, part] for part, g in enumerate((gl, gl, gr, gr))], axis=0
                )
            )
        back = dot(proj_weight[...], jnp.concatenate(columns, axis=1))
        dzh = (back + side_by_side(dzg, at, size).astype(F32)) * gain_b
        z = side_by_side(zhat, at, size).astype(F32)
        inverse = jnp.concatenate([inv[at + r : at + r + 1] for r in range(size)], axis=1)
        m1 = jnp.mean(dzh, axis=0, keepdims=True)
        m2 = jnp.mean(dzh * z, axis=0, keepdims=True)
        grad = ((dzh - m1 - z * m2) * inverse).astype(BF16)
        for r in range(size):
            out[at + r] = turned(grad[:, r * cols : (r + 1) * cols]).astype(BF16)
        done = at + size
        if done % ahead == 0:
            part = pl.ds(done - ahead, ahead)
            copy = pltpu.make_async_copy(
                out.at[part], out_h.at[part], out_sems.at[done // ahead - 1]
            )
            copy.start()
            leaving.append(copy)
    wait(leaving)


def call(kernel, outs, scratch, args, near=(), outs_near=(), flops=0, moved=0):
    here, far = (pl.BlockSpec(memory_space=space) for space in (pltpu.VMEM, pltpu.HBM))
    specs = [here if at in near else far for at in range(len(args))]
    return pl.pallas_call(
        kernel,
        out_shape=[
            out if at in outs_near else pltpu.HBM(out.shape, out.dtype)
            for at, out in enumerate(outs)
        ],
        in_specs=specs,
        out_specs=[here if at in outs_near else far for at in range(len(outs))],
        scratch_shapes=scratch,
        compiler_params=pltpu.CompilerParams(vmem_limit_bytes=16 * MIB),
        cost_estimate=pl.CostEstimate(flops=flops, bytes_accessed=moved, transcendentals=0),
    )(
        *[
            pltpu.with_memory_space_constraint(arg, pltpu.HBM) if spec is far else arg
            for arg, spec in zip(args, specs)
        ]
    )


def body(
    pair, mask, gain_in, bias_in, proj_weight, gate_weight,
    product_norm_gain, product_norm_bias, out_weight, cotangent,
):
    rows, cols, width = pair.shape
    hidden = out_weight.shape[0]
    n_half = lax.axis_size("half")
    n_row = lax.axis_size("row")
    n_core = lax.axis_size("core")
    n_col = lax.axis_size("col")
    n_chip = n_row * n_col
    n_line = n_row * n_core
    n_place = n_line * n_col
    within = ("row", "core", "col")
    share = hidden // n_place
    cells = rows * cols
    n_groups = len(groups_of(rows))
    mask_row = mask.reshape(1, -1)
    gain_in, bias_in = gain_in.reshape(1, -1), bias_in.reshape(1, -1)
    norm_gain, norm_bias = product_norm_gain.reshape(1, -1), product_norm_bias.reshape(1, -1)

    def shape(*dims, dtype=BF16):
        return jax.ShapeDtypeStruct(dims, dtype)

    def vmem(*dims, dtype=BF16):
        return pltpu.VMEM(dims, dtype)

    def sems(count):
        return pltpu.SemaphoreType.DMA((count,))

    def exchange(values):
        return lax.all_to_all(values, within, split_axis=0, concat_axis=0, tiled=True)

    def exchange_all(values):
        flat = values.reshape(n_half * n_place, share, rows, cols)
        return lax.all_to_all(
            flat, ("half", *within), split_axis=0, concat_axis=0, tiled=True
        )

    def permute(values, axes, size, distance):
        return lax.ppermute(values, axes, [(at, at ^ distance) for at in range(size)])

    def exchange_pieces(pieces):
        first = [pieces[0]]
        first += [permute(pieces[m], ("core",), n_core, m) for m in range(1, n_core)]
        second = [
            permute(jnp.stack([piece[n] for piece in first]), ("row", "col"), n_chip, n)
            for n in range(n_chip - 1, 0, -1)
        ]
        return tuple(first + second[::-1])

    mask_s = pltpu.SMEM(mask.shape, jnp.int32)
    mask_v = vmem(*mask_row.shape, dtype=jnp.int32)
    vector = vmem(1, width, dtype=F32)
    plane = vmem(hidden * rows, cols, dtype=F32)
    block = vmem(rows, cols, width)
    wide = vmem(rows, width, cols, dtype=F32)
    short = vmem(rows, width, cols)
    square = vmem(width, hidden)
    proj_v = vmem(width, 4 * hidden)
    pieces_shape = (shape(n_chip, share, rows, cols),) * n_core
    n_pieces = n_core + n_chip - 1

    def front(part, outs, scratch, near):
        return call(
            functools.partial(front_kernel, part, len(outs)),
            outs,
            [
                block, mask_s, mask_v, vector, vector, vmem(width, 2 * hidden),
                vmem(width, cells), plane, sems(6), *scratch,
            ],
            (pair, mask, mask_row, gain_in, bias_in, proj_weight),
            outs_near=near,
            flops=2 * cells * width * 3 * hidden,
            moved=5 * cells * width,
        )

    everywhere = vmem(n_place, share, rows, cols)
    (right,) = front(
        2,
        (shape(n_half, n_place, share, rows, cols),),
        [everywhere, pltpu.SemaphoreType.DMA((n_half, math.gcd(n_place, 2)))],
        (),
    )
    right = exchange_all(right).reshape(n_half, n_line, n_col, share, rows, cols)
    left = exchange_pieces(tuple(front(0, pieces_shape, [], range(n_core))))
    zhat, short_zhat, inv, gate, dxh = call(
        side_kernel,
        (
            shape(rows, width, cols, dtype=F32),
            shape(rows, width, cols),
            shape(rows, cols, dtype=F32),
            shape(rows, width, cols, dtype=F32),
            shape(hidden * rows, cols, dtype=F32),
        ),
        [
            block, block, vector, vector, square, vector, square,
            wide, short, vmem(rows, cols, dtype=F32), wide, sems(7), sems(4),
        ],
        (pair, cotangent, gain_in, bias_in, gate_weight, norm_gain, out_weight),
        outs_near=(4,),
        flops=2 * cells * width * 4 * hidden,
        moved=16 * cells * width,
    )
    (coef,) = call(
        factors_kernel,
        (shape(rows, 4, hidden, cols),),
        [
            wide, mask_s, mask_v, vector, vector, proj_v, vmem(rows, 4, hidden, cols),
            sems(6), sems(n_groups),
        ],
        (zhat, mask, mask_row, gain_in, bias_in, proj_weight),
        flops=2 * cells * width * 5 * hidden,
        moved=16 * cells * width,
    )
    product, left = call(
        functools.partial(product_kernel, n_chip),
        (shape(n_line, n_col, share, rows, cols), shape(n_line, n_col, share, rows, cols)),
        [],
        (right, coef, *left),
        near=(0, *range(2, 2 + n_pieces)),
        outs_near=(0, 1),
        flops=2 * share * n_half * (n_line * rows) ** 2 * n_col * cols,
        moved=8 * cells * hidden,
    )
    product = exchange(product.reshape(n_place, share, rows, cols)).reshape(hidden, rows, cols)
    (grad,) = call(
        middle_kernel,
        (shape(hidden, rows, cols),),
        [vmem(hidden, rows, cols, dtype=F32)],
        (product, dxh.reshape(hidden, rows, cols)),
        near=(0, 1),
        outs_near=(0,),
        flops=20 * cells * hidden,
        moved=8 * cells * hidden,
    )
    grad = exchange(grad.reshape(n_place, share, rows, cols))
    grad = grad.reshape(n_line, n_col, share, rows, cols)
    (sent,) = call(
        grad_right_kernel,
        (shape(n_half, n_line, n_col, share, rows, cols),),
        [vmem(n_half, n_line, n_col, share, rows, cols), sems(share)],
        (grad, left),
        near=(0, 1),
        flops=2 * share * n_half * (n_line * rows) ** 2 * n_col * cols,
        moved=8 * cells * hidden,
    )
    grad_right = exchange_all(sent).reshape(n_half, n_place, share, rows, cols)
    grad_left = call(
        grad_left_kernel,
        pieces_shape,
        [vmem(n_line, n_col, share, rows, cols)],
        (grad, right),
        near=(0, 1),
        outs_near=range(n_core),
        flops=2 * share * n_half * (n_line * rows) ** 2 * n_col * cols,
        moved=8 * cells * hidden,
    )
    grad_left = exchange_pieces(tuple(grad_left))
    update, dzg = call(
        update_kernel,
        (shape(rows, cols, width), shape(rows, width, cols)),
        [wide, block, vector, vector, square, square, block, short, plane, sems(6), sems(2)],
        (product, gate, cotangent, norm_gain, norm_bias, out_weight, gate_weight, sent),
        near=(0,),
        flops=2 * cells * width * 3 * hidden,
        moved=14 * cells * hidden,
    )
    (grad_pair,) = call(
        functools.partial(back_kernel, n_chip),
        (shape(rows, cols, width),),
        [
            vmem(rows, 4, hidden, cols), short, vmem(rows, cols, dtype=F32), short,
            vector, proj_v, block, plane, plane,
            sems(3), sems(3), sems(3), sems(2),
        ],
        (grad_right, coef, short_zhat, inv, dzg, gain_in, proj_weight, *grad_left),
        near=(0, *range(7, 7 + n_pieces)),
        flops=2 * cells * width * 5 * hidden,
        moved=30 * cells * width,
    )
    return (update, grad_pair)


def solution(mesh):
    n_grp, n_row, n_col = (mesh.shape[name] for name in ("grp", "row", "col"))
    n_half = math.gcd(n_row, 2)
    n_core = math.gcd(n_row // n_half, 2)
    split = jax.sharding.Mesh(
        mesh.devices.reshape(n_grp, n_half, n_row // (n_half * n_core), n_core, n_col),
        ("grp", "half", "row", "core", "col"),
    )
    cells = P(("grp", "half", "row", "core"), "col", None)
    return jax.shard_map(
        body,
        mesh=split,
        in_specs=(cells, P("grp"), P(), P(), P(), P(), P(), P(), P(), cells),
        out_specs=(cells, cells),
        check_vma=False,
    )
```

```python
import functools
import math

import jax
import jax.numpy as jnp
from jax import lax
from jax.experimental import pallas as pl
from jax.experimental.pallas import tpu as pltpu
from jax.sharding import PartitionSpec as P

EPS = 1e-05
F32 = jnp.float32
BF16 = jnp.bfloat16
MIB = 1 << 20


def dot(a, b, over=((1,), (0,))):
    return lax.dot_general(a, b, (over, ((), ())), preferred_element_type=F32)


def eye(size):
    down = lax.broadcasted_iota(jnp.int32, (size, size), 0)
    across = lax.broadcasted_iota(jnp.int32, (size, size), 1)
    return (down == across).astype(F32).astype(BF16)


def turned(values):
    return dot(eye(values.shape[1]), values, ((1,), (1,)))


def down_lanes(vector, lanes):
    return jnp.broadcast_to(vector, (lanes, vector.shape[1])).T


def turned_weight(weight):
    c, m = weight.shape
    return jnp.concatenate(
        [turned(weight[:, at : at + c]) for at in range(0, m, c)], axis=0
    ).astype(BF16)


def sigmoid(values):
    return 0.5 + 0.5 * jnp.tanh(0.5 * values)


def normalized(values):
    mean = jnp.mean(values, axis=0, keepdims=True)
    centred = values - mean
    var = jnp.mean(centred * centred, axis=0, keepdims=True)
    inverse = lax.rsqrt(var + EPS)
    return centred * inverse, inverse


def start(sems, copies):
    running = [
        pltpu.make_async_copy(source, target, sems.at[at])
        for at, (source, target) in enumerate(copies)
    ]
    for copy in running:
        copy.start()
    return running


def wait(copies):
    for copy in copies:
        copy.wait()


def groups_of(rows, most=2):
    size = math.gcd(rows, most)
    return [(at, size) for at in range(0, rows, size)]


def side_by_side(ref, at, size):
    return jnp.concatenate([ref[at + r] for r in range(size)], axis=1)


def pair_mask(mask_s, mask_v, at, size, rows, cols):
    here = lax.axis_index("half")
    for name in ("row", "core"):
        here = here * lax.axis_size(name) + lax.axis_index(name)
    first_row = here * rows + at
    first_col = pl.multiple_of(lax.axis_index("col") * cols, cols)
    col_mask = mask_v[:, pl.ds(first_col, cols)].astype(F32)
    return jnp.concatenate(
        [col_mask * mask_s[first_row + r].astype(F32) for r in range(size)], axis=1
    )


def sources(n_chip, n_core):
    n_col = lax.axis_size("col")
    core = lax.axis_index("core")
    chip = lax.axis_index("row") * n_col + lax.axis_index("col")
    found = []
    for n in range(n_chip):
        other = chip ^ n
        for m in range(n_core):
            line = other // n_col * n_core + (core ^ m)
            found.append((m, n, line * n_col + other % n_col))
    return found


def received(refs, n_chip):
    n_core = len(refs) - n_chip + 1
    return [
        (number, refs[m][0] if n == 0 else refs[n_core + n - 1][m])
        for m, n, number in sources(n_chip, n_core)
    ]


def front_kernel(
    part, n_out, pair_h, mask_h, mask_row_h, gain_h, bias_h, proj_h, *refs
):
    outs = refs[:n_out]
    pair, mask_s, mask_v, gain, bias, proj_weight, zbar, plane, sems, *more = refs[n_out:]
    rows, cols, width = pair.shape
    hidden = plane.shape[0] // rows
    groups = groups_of(rows)
    *small, whole = start(
        sems,
        [
            (gain_h, gain), (bias_h, bias),
            (proj_h.at[:, pl.ds(part * hidden, 2 * hidden)], proj_weight),
            (mask_h, mask_s), (mask_row_h, mask_v), (pair_h, pair),
        ],
    )
    wait(small)
    gain_b = jnp.concatenate([down_lanes(gain[...], cols)] * groups[0][1], axis=1)
    bias_b = jnp.concatenate([down_lanes(bias[...], cols)] * groups[0][1], axis=1)
    weight = turned_weight(proj_weight[...])
    whole.wait()
    for at, size in groups:
        zhat, _ = normalized(turned(pair[at : at + size].reshape(size * cols, width)))
        zbar[:, at * cols : (at + size) * cols] = (zhat * gain_b + bias_b).astype(BF16)

    def channels(first, count):
        block = jnp.concatenate(
            [weight[first : first + count], weight[hidden + first : hidden + first + count]], axis=0
        )
        for at, size in groups:
            proj = dot(block, zbar[:, at * cols : (at + size) * cols])
            pm = pair_mask(mask_s, mask_v, at, size, rows, cols)
            values = sigmoid(proj[:count]) * proj[count:] * pm
            for r in range(size):
                plane[pl.ds(first * rows + at + r, count, stride=rows), :] = values[
                    :, r * cols : (r + 1) * cols
                ]

    if n_out > 1:
        channels(0, hidden)
        give_pieces(plane, outs)
        return
    (out_h,), (ready, out_sems) = outs, more
    n_place, share = ready.shape[:2]
    size = n_place // math.gcd(n_place, 2)
    leaving = []
    for n, at in enumerate(range(0, n_place, size)):
        channels(at * share, size * share)
        values = plane[at * share * rows : (at + size) * share * rows]
        ready[at : at + size] = values.reshape(size, *ready.shape[1:]).astype(BF16)
        for half in range(out_h.shape[0]):
            copy = pltpu.make_async_copy(
                ready.at[pl.ds(at, size)], out_h.at[half, pl.ds(at, size)], out_sems.at[half, n]
            )
            copy.start()
            leaving.append(copy)
    wait(leaving)


def give_pieces(plane, outs):
    n_chip = outs[0].shape[0]
    length = plane.shape[0] // (len(outs) * n_chip)
    for m, n, number in sources(n_chip, len(outs)):
        first = pl.multiple_of(number * length, length)
        values = plane[pl.ds(first, length), :]
        outs[m][n] = values.reshape(outs[m].shape[1:]).astype(BF16)


def side_kernel(
    pair_h, cot_h, gain_h, bias_h, gate_h, norm_gain_h, out_w_h,
    zhat_h, short_h, inv_h, gate_out_h, dxh_out,
    pair, cot, gain, bias, gate_weight, norm_gain, out_weight,
    zhat_out, short_out, inv_out, gate_out, in_sems, out_sems,
):
    rows, cols, width = pair.shape
    hidden = out_weight.shape[0]
    wait(
        start(
            in_sems,
            [
                (pair_h, pair), (cot_h, cot), (gain_h, gain), (bias_h, bias),
                (gate_h, gate_weight), (norm_gain_h, norm_gain), (out_w_h, out_weight),
            ],
        )
    )
    groups = groups_of(rows)
    gain_b = jnp.concatenate([down_lanes(gain[...], cols)] * groups[0][1], axis=1)
    bias_b = jnp.concatenate([down_lanes(bias[...], cols)] * groups[0][1], axis=1)
    norm_gain_b = jnp.concatenate([down_lanes(norm_gain[...], cols)] * groups[0][1], axis=1)
    gate_t = turned_weight(gate_weight[...])
    for at, size in groups:
        zhat, inverse = normalized(turned(pair[at : at + size].reshape(size * cols, width)))
        zbar = (zhat * gain_b + bias_b).astype(BF16)
        gate = sigmoid(dot(gate_t, zbar))
        cot_t = turned(cot[at : at + size].reshape(size * cols, width))
        dxh = dot(out_weight[...], (cot_t * gate).astype(BF16)) * norm_gain_b
        dxh = dxh - jnp.mean(dxh, axis=0, keepdims=True)
        for r in range(size):
            lanes = slice(r * cols, (r + 1) * cols)
            zhat_out[at + r] = zhat[:, lanes]
            short_out[at + r] = zhat[:, lanes].astype(BF16)
            inv_out[at + r : at + r + 1] = inverse[:, lanes]
            gate_out[at + r] = gate[:, lanes]
            dxh_out[pl.ds(at + r, hidden, stride=rows), :] = dxh[:, lanes]
    wait(
        start(
            out_sems,
            [
                (zhat_out, zhat_h), (short_out, short_h), (inv_out, inv_h),
                (gate_out, gate_out_h),
            ],
        )
    )


def factors_kernel(
    zhat_h, mask_h, mask_row_h, gain_h, bias_h, proj_h, coef_h,
    zhat, mask_s, mask_v, gain, bias, proj_weight, coef, in_sems, out_sems,
):
    rows, width, cols = zhat.shape
    hidden = coef.shape[2]
    wait(
        start(
            in_sems,
            [
                (zhat_h, zhat), (mask_h, mask_s), (mask_row_h, mask_v), (gain_h, gain),
                (bias_h, bias), (proj_h, proj_weight),
            ],
        )
    )
    groups = groups_of(rows)
    gain_b = jnp.concatenate([down_lanes(gain[...], cols)] * groups[0][1], axis=1)
    bias_b = jnp.concatenate([down_lanes(bias[...], cols)] * groups[0][1], axis=1)
    weight = turned_weight(proj_weight[...])
    leaving = []
    for n, (at, size) in enumerate(groups):
        zbar = (side_by_side(zhat, at, size) * gain_b + bias_b).astype(BF16)
        pm = pair_mask(mask_s, mask_v, at, size, rows, cols)
        for part in (0, 2):
            s = sigmoid(dot(weight[part * hidden : (part + 1) * hidden], zbar))
            q = dot(weight[(part + 1) * hidden : (part + 2) * hidden], zbar)
            second = pm * s
            first = second * q * (1.0 - s)
            for r in range(size):
                lanes = slice(r * cols, (r + 1) * cols)
                coef[at + r, part] = first[:, lanes].astype(BF16)
                coef[at + r, part + 1] = second[:, lanes].astype(BF16)
        copy = pltpu.make_async_copy(
            coef.at[pl.ds(at, size)], coef_h.at[pl.ds(at, size)], out_sems.at[n]
        )
        copy.start()
        leaving.append(copy)
    wait(leaving)


def channel_matrix(ref, at):
    *_, n_col, _, rows, cols = ref.shape
    lead = (slice(None),) * (len(ref.shape) - 4)
    return jnp.concatenate(
        [ref[(*lead, c, at)].reshape(-1, cols) for c in range(n_col)], axis=1
    )


def put_channel(ref, at, values):
    *shape, n_col, _, rows, cols = ref.shape
    lead = (slice(None),) * len(shape)
    values = values.astype(BF16)
    for c in range(n_col):
        ref[(*lead, c, at)] = values[:, c * cols : (c + 1) * cols].reshape(*shape, rows, cols)


def product_kernel(n_chip, right, after, *refs):
    pieces, (out, left) = refs[:-2], refs[-2:]
    n_col, share = left.shape[1:3]
    for number, piece in received(pieces, n_chip):
        left[number // n_col, number % n_col] = piece
    for h in range(share):
        values = dot(channel_matrix(left, h), channel_matrix(right, h), ((1,), (1,)))
        put_channel(out, h, values)


def middle_kernel(product, dxh, out, xhat):
    hidden = product.shape[0]
    values = product[...].astype(F32)
    mean = jnp.sum(values, axis=0) * (1.0 / hidden)
    centred = values - mean
    var = jnp.sum(centred * centred, axis=0) * (1.0 / hidden)
    inverse = lax.rsqrt(var + EPS)
    xhat[...] = centred * inverse
    m2 = jnp.sum(dxh[...] * xhat[...], axis=0) * (1.0 / hidden)
    out[...] = ((dxh[...] - xhat[...] * m2) * inverse).astype(BF16)


def update_kernel(
    product, gate_h, cot_h, norm_gain_h, norm_bias_h, out_w_h, gate_w_h, after, update_h, dzg_h,
    gate, cot, norm_gain, norm_bias, out_weight, gate_weight, update, dzg, spread,
    in_sems, out_sems,
):
    hidden, rows, cols = product.shape
    width = cot.shape[2]
    copies = start(
        in_sems,
        [
            (gate_h, gate), (cot_h, cot), (norm_gain_h, norm_gain), (norm_bias_h, norm_bias),
            (out_w_h, out_weight), (gate_w_h, gate_weight),
        ],
    )
    spread[...] = product[...].astype(F32).reshape(hidden * rows, cols)
    wait(copies)
    groups = groups_of(rows)
    norm_gain_b = jnp.concatenate([down_lanes(norm_gain[...], cols)] * groups[0][1], axis=1)
    norm_bias_b = jnp.concatenate([down_lanes(norm_bias[...], cols)] * groups[0][1], axis=1)
    out_t = turned_weight(out_weight[...])
    for at, size in groups:
        xhat, _ = normalized(
            jnp.concatenate(
                [spread[pl.ds(at + r, hidden, stride=rows), :] for r in range(size)], axis=1
            )
        )
        ybar = (xhat * norm_gain_b + norm_bias_b).astype(BF16)
        u = dot(out_t, ybar)
        g = side_by_side(gate, at, size)
        done = (g * u).astype(BF16)
        cot_t = turned(cot[at : at + size].reshape(size * cols, width))
        back = dot(gate_weight[...], (cot_t * u * g * (1.0 - g)).astype(BF16))
        for r in range(size):
            lanes = slice(r * cols, (r + 1) * cols)
            update[at + r] = turned(done[:, lanes]).astype(BF16)
            dzg[at + r] = back[:, lanes].astype(BF16)
    wait(start(out_sems, [(update, update_h), (dzg, dzg_h)]))


def grad_right_kernel(grad, left, out_h, ready, sems):
    lead = (slice(None),) * (len(ready.shape) - 3)
    leaving = []
    for h in range(ready.shape[-3]):
        values = dot(channel_matrix(grad, h), channel_matrix(left, h), ((0,), (0,)))
        put_channel(ready, h, values)
        part = (*lead, pl.ds(h, 1))
        copy = pltpu.make_async_copy(ready.at[part], out_h.at[part], sems.at[h])
        copy.start()
        leaving.append(copy)
    wait(leaving)


def grad_left_kernel(grad, right, *refs):
    outs, ready = refs[:-1], refs[-1]
    n_col, share = ready.shape[1:3]
    for h in range(share):
        put_channel(ready, h, dot(channel_matrix(grad, h), channel_matrix(right, h)))
    for m, n, number in sources(outs[0].shape[0], len(outs)):
        outs[m][n] = ready[number // n_col, number % n_col]


def back_kernel(n_chip, grads, coef_h, zhat_h, inv_h, dzg_h, gain_h, proj_h, *refs):
    pieces, out_h = refs[:-15], refs[-15]
    (
        coef, zhat, inv, dzg, gain, proj_weight, out, left, right,
        sems, coef_sems, zhat_sems, dzg_sems, out_sems,
    ) = refs[-14:]
    rows, cols, width = out.shape
    hidden = left.shape[0] // rows
    groups, parts = groups_of(rows), groups_of(rows, 4)
    small = start(sems, [(gain_h, gain), (proj_h, proj_weight), (inv_h, inv)])
    ahead = rows // math.gcd(rows, 2)
    blocks = [
        [
            pltpu.make_async_copy(
                source.at[pl.ds(at, size)], target.at[pl.ds(at, size)], sem.at[n]
            )
            for source, target, sem in (
                (coef_h, coef, coef_sems), (zhat_h, zhat, zhat_sems), (dzg_h, dzg, dzg_sems)
            )
        ]
        for n, (at, size) in enumerate(parts)
    ]
    for copy in sum(blocks[:2], []):
        copy.start()
    arrived = received(pieces, n_chip)
    length = left.shape[0] // len(arrived)
    for number, piece in arrived:
        first = pl.multiple_of(number * length, length)
        left[pl.ds(first, length), :] = piece.astype(F32).reshape(length, cols)
    total = grads[0].astype(F32)
    for half in range(1, grads.shape[0]):
        total = total + grads[half].astype(F32)
    right[...] = total.reshape(right.shape)
    wait(small)
    gain_b = jnp.concatenate([down_lanes(gain[...], cols)] * groups[0][1], axis=1)
    leaving = []
    for copy in sum(blocks[2:], []):
        copy.start()
    arriving = {at: copies for (at, _), copies in zip(parts, blocks)}
    for at, size in groups:
        wait(arriving.get(at, []))
        columns = []
        for r in range(size):
            gl = left[pl.ds(at + r, hidden, stride=rows), :].astype(BF16)
            gr = right[pl.ds(at + r, hidden, stride=rows), :].astype(BF16)
            columns.append(
                jnp.concatenate(
                    [g * coef[at + r, part] for part, g in enumerate((gl, gl, gr, gr))], axis=0
                )
            )
        back = dot(proj_weight[...], jnp.concatenate(columns, axis=1))
        dzh = (back + side_by_side(dzg, at, size).astype(F32)) * gain_b
        z = side_by_side(zhat, at, size).astype(F32)
        inverse = jnp.concatenate([inv[at + r : at + r + 1] for r in range(size)], axis=1)
        m1 = jnp.mean(dzh, axis=0, keepdims=True)
        m2 = jnp.mean(dzh * z, axis=0, keepdims=True)
        grad = ((dzh - m1 - z * m2) * inverse).astype(BF16)
        for r in range(size):
            out[at + r] = turned(grad[:, r * cols : (r + 1) * cols]).astype(BF16)
        done = at + size
        if done % ahead == 0:
            part = pl.ds(done - ahead, ahead)
            copy = pltpu.make_async_copy(
                out.at[part], out_h.at[part], out_sems.at[done // ahead - 1]
            )
            copy.start()
            leaving.append(copy)
    wait(leaving)


def call(kernel, outs, scratch, args, near=(), outs_near=(), flops=0, moved=0):
    here, far = (pl.BlockSpec(memory_space=space) for space in (pltpu.VMEM, pltpu.HBM))
    specs = [here if at in near else far for at in range(len(args))]
    return pl.pallas_call(
        kernel,
        out_shape=[
            out if at in outs_near else pltpu.HBM(out.shape, out.dtype)
            for at, out in enumerate(outs)
        ],
        in_specs=specs,
        out_specs=[here if at in outs_near else far for at in range(len(outs))],
        scratch_shapes=scratch,
        compiler_params=pltpu.CompilerParams(vmem_limit_bytes=16 * MIB),
        cost_estimate=pl.CostEstimate(flops=flops, bytes_accessed=moved, transcendentals=0),
    )(
        *[
            pltpu.with_memory_space_constraint(arg, pltpu.HBM) if spec is far else arg
            for arg, spec in zip(args, specs)
        ]
    )


def body(
    pair, mask, gain_in, bias_in, proj_weight, gate_weight,
    product_norm_gain, product_norm_bias, out_weight, cotangent,
):
    rows, cols, width = pair.shape
    hidden = out_weight.shape[0]
    n_half = lax.axis_size("half")
    n_row = lax.axis_size("row")
    n_core = lax.axis_size("core")
    n_col = lax.axis_size("col")
    n_chip = n_row * n_col
    n_line = n_row * n_core
    n_place = n_line * n_col
    within = ("row", "core", "col")
    share = hidden // n_place
    cells = rows * cols
    n_groups = len(groups_of(rows))
    n_parts = len(groups_of(rows, 4))
    mask_row = mask.reshape(1, -1)
    gain_in, bias_in = gain_in.reshape(1, -1), bias_in.reshape(1, -1)
    norm_gain, norm_bias = product_norm_gain.reshape(1, -1), product_norm_bias.reshape(1, -1)

    def shape(*dims, dtype=BF16):
        return jax.ShapeDtypeStruct(dims, dtype)

    def vmem(*dims, dtype=BF16):
        return pltpu.VMEM(dims, dtype)

    def sems(count):
        return pltpu.SemaphoreType.DMA((count,))

    def exchange(values):
        return lax.all_to_all(values, within, split_axis=0, concat_axis=0, tiled=True)

    def exchange_all(values):
        flat = values.reshape(n_half * n_place, share, rows, cols)
        return lax.all_to_all(
            flat, ("half", *within), split_axis=0, concat_axis=0, tiled=True
        )

    def permute(values, axes, size, distance):
        return lax.ppermute(values, axes, [(at, at ^ distance) for at in range(size)])

    def exchange_pieces(pieces):
        first = [pieces[0]]
        first += [permute(pieces[m], ("core",), n_core, m) for m in range(1, n_core)]
        second = [
            permute(jnp.stack([piece[n] for piece in first]), ("row", "col"), n_chip, n)
            for n in range(n_chip - 1, 0, -1)
        ]
        return tuple(first + second[::-1])

    mask_s = pltpu.SMEM(mask.shape, jnp.int32)
    mask_v = vmem(*mask_row.shape, dtype=jnp.int32)
    vector = vmem(1, width, dtype=F32)
    plane = vmem(hidden * rows, cols, dtype=F32)
    block = vmem(rows, cols, width)
    wide = vmem(rows, width, cols, dtype=F32)
    short = vmem(rows, width, cols)
    square = vmem(width, hidden)
    proj_v = vmem(width, 4 * hidden)
    pieces_shape = (shape(n_chip, share, rows, cols),) * n_core
    n_pieces = n_core + n_chip - 1

    def front(part, outs, scratch, near):
        return call(
            functools.partial(front_kernel, part, len(outs)),
            outs,
            [
                block, mask_s, mask_v, vector, vector, vmem(width, 2 * hidden),
                vmem(width, cells), plane, sems(6), *scratch,
            ],
            (pair, mask, mask_row, gain_in, bias_in, proj_weight),
            outs_near=near,
            flops=2 * cells * width * 3 * hidden,
            moved=5 * cells * width,
        )

    everywhere = vmem(n_place, share, rows, cols)
    (right,) = front(
        2,
        (shape(n_half, n_place, share, rows, cols),),
        [everywhere, pltpu.SemaphoreType.DMA((n_half, math.gcd(n_place, 2)))],
        (),
    )
    right = exchange_all(right).reshape(n_half, n_line, n_col, share, rows, cols)
    left = exchange_pieces(tuple(front(0, pieces_shape, [], range(n_core))))
    zhat, short_zhat, inv, gate, dxh = call(
        side_kernel,
        (
            shape(rows, width, cols, dtype=F32),
            shape(rows, width, cols),
            shape(rows, cols, dtype=F32),
            shape(rows, width, cols, dtype=F32),
            shape(hidden * rows, cols, dtype=F32),
        ),
        [
            block, block, vector, vector, square, vector, square,
            wide, short, vmem(rows, cols, dtype=F32), wide, sems(7), sems(4),
        ],
        (pair, cotangent, gain_in, bias_in, gate_weight, norm_gain, out_weight),
        outs_near=(4,),
        flops=2 * cells * width * 4 * hidden,
        moved=16 * cells * width,
    )
    (coef,) = call(
        factors_kernel,
        (shape(rows, 4, hidden, cols),),
        [
            wide, mask_s, mask_v, vector, vector, proj_v, vmem(rows, 4, hidden, cols),
            sems(6), sems(n_groups),
        ],
        (zhat, mask, mask_row, gain_in, bias_in, proj_weight),
        flops=2 * cells * width * 5 * hidden,
        moved=16 * cells * width,
    )
    product, left = call(
        functools.partial(product_kernel, n_chip),
        (shape(n_line, n_col, share, rows, cols), shape(n_line, n_col, share, rows, cols)),
        [],
        (right, coef, *left),
        near=(0, *range(2, 2 + n_pieces)),
        outs_near=(0, 1),
        flops=2 * share * n_half * (n_line * rows) ** 2 * n_col * cols,
        moved=8 * cells * hidden,
    )
    product = exchange(product.reshape(n_place, share, rows, cols)).reshape(hidden, rows, cols)
    (grad,) = call(
        middle_kernel,
        (shape(hidden, rows, cols),),
        [vmem(hidden, rows, cols, dtype=F32)],
        (product, dxh.reshape(hidden, rows, cols)),
        near=(0, 1),
        outs_near=(0,),
        flops=20 * cells * hidden,
        moved=8 * cells * hidden,
    )
    grad = exchange(grad.reshape(n_place, share, rows, cols))
    grad = grad.reshape(n_line, n_col, share, rows, cols)
    (sent,) = call(
        grad_right_kernel,
        (shape(n_half, n_line, n_col, share, rows, cols),),
        [vmem(n_half, n_line, n_col, share, rows, cols), sems(share)],
        (grad, left),
        near=(0, 1),
        flops=2 * share * n_half * (n_line * rows) ** 2 * n_col * cols,
        moved=8 * cells * hidden,
    )
    grad_right = exchange_all(sent).reshape(n_half, n_place, share, rows, cols)
    grad_left = call(
        grad_left_kernel,
        pieces_shape,
        [vmem(n_line, n_col, share, rows, cols)],
        (grad, right),
        near=(0, 1),
        outs_near=range(n_core),
        flops=2 * share * n_half * (n_line * rows) ** 2 * n_col * cols,
        moved=8 * cells * hidden,
    )
    grad_left = exchange_pieces(tuple(grad_left))
    update, dzg = call(
        update_kernel,
        (shape(rows, cols, width), shape(rows, width, cols)),
        [wide, block, vector, vector, square, square, block, short, plane, sems(6), sems(2)],
        (product, gate, cotangent, norm_gain, norm_bias, out_weight, gate_weight, sent),
        near=(0,),
        flops=2 * cells * width * 3 * hidden,
        moved=14 * cells * hidden,
    )
    (grad_pair,) = call(
        functools.partial(back_kernel, n_chip),
        (shape(rows, cols, width),),
        [
            vmem(rows, 4, hidden, cols), short, vmem(rows, cols, dtype=F32), short,
            vector, proj_v, block, plane, plane,
            sems(3), sems(n_parts), sems(n_parts), sems(n_parts), sems(2),
        ],
        (grad_right, coef, short_zhat, inv, dzg, gain_in, proj_weight, *grad_left),
        near=(0, *range(7, 7 + n_pieces)),
        flops=2 * cells * width * 5 * hidden,
        moved=30 * cells * width,
    )
    return (update, grad_pair)


def solution(mesh):
    n_grp, n_row, n_col = (mesh.shape[name] for name in ("grp", "row", "col"))
    n_half = math.gcd(n_row, 2)
    n_core = math.gcd(n_row // n_half, 2)
    split = jax.sharding.Mesh(
        mesh.devices.reshape(n_grp, n_half, n_row // (n_half * n_core), n_core, n_col),
        ("grp", "half", "row", "core", "col"),
    )
    cells = P(("grp", "half", "row", "core"), "col", None)
    return jax.shard_map(
        body,
        mesh=split,
        in_specs=(cells, P("grp"), P(), P(), P(), P(), P(), P(), P(), cells),
        out_specs=(cells, cells),
        check_vma=False,
    )
```

```python
import functools
import math

import jax
import jax.numpy as jnp
from jax import lax
from jax.experimental import pallas as pl
from jax.experimental.pallas import tpu as pltpu
from jax.sharding import PartitionSpec as P

EPS = 1e-05
F32 = jnp.float32
BF16 = jnp.bfloat16
MIB = 1 << 20


def dot(a, b, over=((1,), (0,))):
    return lax.dot_general(a, b, (over, ((), ())), preferred_element_type=F32)


def eye(size):
    down = lax.broadcasted_iota(jnp.int32, (size, size), 0)
    across = lax.broadcasted_iota(jnp.int32, (size, size), 1)
    return (down == across).astype(F32).astype(BF16)


def turned(values):
    return dot(eye(values.shape[1]), values, ((1,), (1,)))


def down_lanes(vector, lanes):
    return jnp.broadcast_to(vector, (lanes, vector.shape[1])).T


def turned_weight(weight):
    c, m = weight.shape
    return jnp.concatenate(
        [turned(weight[:, at : at + c]) for at in range(0, m, c)], axis=0
    ).astype(BF16)


def sigmoid(values):
    return 0.5 + 0.5 * jnp.tanh(0.5 * values)


def normalized(values):
    mean = jnp.mean(values, axis=0, keepdims=True)
    centred = values - mean
    var = jnp.mean(centred * centred, axis=0, keepdims=True)
    inverse = lax.rsqrt(var + EPS)
    return centred * inverse, inverse


def start(sems, copies):
    running = [
        pltpu.make_async_copy(source, target, sems.at[at])
        for at, (source, target) in enumerate(copies)
    ]
    for copy in running:
        copy.start()
    return running


def wait(copies):
    for copy in copies:
        copy.wait()


def groups_of(rows, most=2):
    size = math.gcd(rows, most)
    return [(at, size) for at in range(0, rows, size)]


def side_by_side(ref, at, size):
    return jnp.concatenate([ref[at + r] for r in range(size)], axis=1)


def pair_mask(mask_s, mask_v, at, size, rows, cols):
    here = lax.axis_index("half")
    for name in ("row", "core"):
        here = here * lax.axis_size(name) + lax.axis_index(name)
    first_row = here * rows + at
    first_col = pl.multiple_of(lax.axis_index("col") * cols, cols)
    col_mask = mask_v[:, pl.ds(first_col, cols)].astype(F32)
    return jnp.concatenate(
        [col_mask * mask_s[first_row + r].astype(F32) for r in range(size)], axis=1
    )


def sources(n_chip, n_core):
    n_col = lax.axis_size("col")
    core = lax.axis_index("core")
    chip = lax.axis_index("row") * n_col + lax.axis_index("col")
    found = []
    for n in range(n_chip):
        other = chip ^ n
        for m in range(n_core):
            line = other // n_col * n_core + (core ^ m)
            found.append((m, n, line * n_col + other % n_col))
    return found


def received(refs, n_chip):
    n_core = len(refs) - n_chip + 1
    return [
        (number, refs[m][0] if n == 0 else refs[n_core + n - 1][m])
        for m, n, number in sources(n_chip, n_core)
    ]


def front_kernel(
    part, n_out, pair_h, mask_h, mask_row_h, gain_h, bias_h, proj_h, *refs
):
    outs = refs[:n_out]
    pair, mask_s, mask_v, gain, bias, proj_weight, zbar, plane, sems, *more = refs[n_out:]
    rows, cols, width = pair.shape
    hidden = plane.shape[0] // rows
    groups = groups_of(rows)
    *small, whole = start(
        sems,
        [
            (gain_h, gain), (bias_h, bias),
            (proj_h.at[:, pl.ds(part * hidden, 2 * hidden)], proj_weight),
            (mask_h, mask_s), (mask_row_h, mask_v), (pair_h, pair),
        ],
    )
    wait(small)
    gain_b = jnp.concatenate([down_lanes(gain[...], cols)] * groups[0][1], axis=1)
    bias_b = jnp.concatenate([down_lanes(bias[...], cols)] * groups[0][1], axis=1)
    weight = turned_weight(proj_weight[...])
    whole.wait()
    for at, size in groups:
        zhat, _ = normalized(turned(pair[at : at + size].reshape(size * cols, width)))
        zbar[:, at * cols : (at + size) * cols] = (zhat * gain_b + bias_b).astype(BF16)

    def channels(first, count):
        block = jnp.concatenate(
            [weight[first : first + count], weight[hidden + first : hidden + first + count]], axis=0
        )
        for at, size in groups:
            proj = dot(block, zbar[:, at * cols : (at + size) * cols])
            pm = pair_mask(mask_s, mask_v, at, size, rows, cols)
            values = sigmoid(proj[:count]) * proj[count:] * pm
            for r in range(size):
                plane[pl.ds(first * rows + at + r, count, stride=rows), :] = values[
                    :, r * cols : (r + 1) * cols
                ]

    if n_out > 1:
        channels(0, hidden)
        give_pieces(plane, outs)
        return
    (out_h,), (ready, out_sems) = outs, more
    n_place, share = ready.shape[:2]
    size = n_place // math.gcd(n_place, 2)
    leaving = []
    for n, at in enumerate(range(0, n_place, size)):
        channels(at * share, size * share)
        values = plane[at * share * rows : (at + size) * share * rows]
        ready[at : at + size] = values.reshape(size, *ready.shape[1:]).astype(BF16)
        for half in range(out_h.shape[0]):
            copy = pltpu.make_async_copy(
                ready.at[pl.ds(at, size)], out_h.at[half, pl.ds(at, size)], out_sems.at[half, n]
            )
            copy.start()
            leaving.append(copy)
    wait(leaving)


def give_pieces(plane, outs):
    n_chip = outs[0].shape[0]
    length = plane.shape[0] // (len(outs) * n_chip)
    for m, n, number in sources(n_chip, len(outs)):
        first = pl.multiple_of(number * length, length)
        values = plane[pl.ds(first, length), :]
        outs[m][n] = values.reshape(outs[m].shape[1:]).astype(BF16)


def side_kernel(
    pair_h, cot_h, gain_h, bias_h, gate_h, norm_gain_h, out_w_h,
    zhat_h, short_h, inv_h, gate_out_h, dxh_out,
    pair, cot, gain, bias, gate_weight, norm_gain, out_weight,
    zhat_out, short_out, inv_out, gate_out, in_sems, out_sems,
):
    rows, cols, width = pair.shape
    hidden = out_weight.shape[0]
    wait(
        start(
            in_sems,
            [
                (pair_h, pair), (cot_h, cot), (gain_h, gain), (bias_h, bias),
                (gate_h, gate_weight), (norm_gain_h, norm_gain), (out_w_h, out_weight),
            ],
        )
    )
    groups = groups_of(rows)
    gain_b = jnp.concatenate([down_lanes(gain[...], cols)] * groups[0][1], axis=1)
    bias_b = jnp.concatenate([down_lanes(bias[...], cols)] * groups[0][1], axis=1)
    norm_gain_b = jnp.concatenate([down_lanes(norm_gain[...], cols)] * groups[0][1], axis=1)
    gate_t = turned_weight(gate_weight[...])
    for at, size in groups:
        zhat, inverse = normalized(turned(pair[at : at + size].reshape(size * cols, width)))
        zbar = (zhat * gain_b + bias_b).astype(BF16)
        gate = sigmoid(dot(gate_t, zbar))
        cot_t = turned(cot[at : at + size].reshape(size * cols, width))
        dxh = dot(out_weight[...], (cot_t * gate).astype(BF16)) * norm_gain_b
        dxh = dxh - jnp.mean(dxh, axis=0, keepdims=True)
        for r in range(size):
            lanes = slice(r * cols, (r + 1) * cols)
            zhat_out[at + r] = zhat[:, lanes]
            short_out[at + r] = zhat[:, lanes].astype(BF16)
            inv_out[at + r : at + r + 1] = inverse[:, lanes]
            gate_out[at + r] = gate[:, lanes]
            dxh_out[pl.ds(at + r, hidden, stride=rows), :] = dxh[:, lanes]
    wait(
        start(
            out_sems,
            [
                (zhat_out, zhat_h), (short_out, short_h), (inv_out, inv_h),
                (gate_out, gate_out_h),
            ],
        )
    )


def factors_kernel(
    zhat_h, mask_h, mask_row_h, gain_h, bias_h, proj_h, coef_h,
    zhat, mask_s, mask_v, gain, bias, proj_weight, coef, in_sems, out_sems,
):
    rows, width, cols = zhat.shape
    hidden = coef.shape[2]
    wait(
        start(
            in_sems,
            [
                (zhat_h, zhat), (mask_h, mask_s), (mask_row_h, mask_v), (gain_h, gain),
                (bias_h, bias), (proj_h, proj_weight),
            ],
        )
    )
    groups = groups_of(rows)
    gain_b = jnp.concatenate([down_lanes(gain[...], cols)] * groups[0][1], axis=1)
    bias_b = jnp.concatenate([down_lanes(bias[...], cols)] * groups[0][1], axis=1)
    weight = turned_weight(proj_weight[...])
    leaving = []
    for n, (at, size) in enumerate(groups):
        zbar = (side_by_side(zhat, at, size) * gain_b + bias_b).astype(BF16)
        pm = pair_mask(mask_s, mask_v, at, size, rows, cols)
        for part in (0, 2):
            s = sigmoid(dot(weight[part * hidden : (part + 1) * hidden], zbar))
            q = dot(weight[(part + 1) * hidden : (part + 2) * hidden], zbar)
            second = pm * s
            first = second * q * (1.0 - s)
            for r in range(size):
                lanes = slice(r * cols, (r + 1) * cols)
                coef[at + r, part] = first[:, lanes].astype(BF16)
                coef[at + r, part + 1] = second[:, lanes].astype(BF16)
        copy = pltpu.make_async_copy(
            coef.at[pl.ds(at, size)], coef_h.at[pl.ds(at, size)], out_sems.at[n]
        )
        copy.start()
        leaving.append(copy)
    wait(leaving)


def channel_matrix(ref, at):
    *_, n_col, _, rows, cols = ref.shape
    lead = (slice(None),) * (len(ref.shape) - 4)
    return jnp.concatenate(
        [ref[(*lead, c, at)].reshape(-1, cols) for c in range(n_col)], axis=1
    )


def put_channel(ref, at, values):
    *shape, n_col, _, rows, cols = ref.shape
    lead = (slice(None),) * len(shape)
    values = values.astype(BF16)
    for c in range(n_col):
        ref[(*lead, c, at)] = values[:, c * cols : (c + 1) * cols].reshape(*shape, rows, cols)


def product_kernel(n_chip, right, after, *refs):
    pieces, (out, left) = refs[:-2], refs[-2:]
    n_col, share = left.shape[1:3]
    for number, piece in received(pieces, n_chip):
        left[number // n_col, number % n_col] = piece
    for h in range(share):
        values = dot(channel_matrix(left, h), channel_matrix(right, h), ((1,), (1,)))
        put_channel(out, h, values)


def middle_kernel(product, dxh, out, xhat):
    hidden = product.shape[0]
    values = product[...].astype(F32)
    mean = jnp.sum(values, axis=0) * (1.0 / hidden)
    centred = values - mean
    var = jnp.sum(centred * centred, axis=0) * (1.0 / hidden)
    inverse = lax.rsqrt(var + EPS)
    xhat[...] = centred * inverse
    m2 = jnp.sum(dxh[...] * xhat[...], axis=0) * (1.0 / hidden)
    out[...] = ((dxh[...] - xhat[...] * m2) * inverse).astype(BF16)


def update_kernel(
    product, gate_h, cot_h, norm_gain_h, norm_bias_h, out_w_h, gate_w_h, after, update_h, dzg_h,
    gate, cot, norm_gain, norm_bias, out_weight, gate_weight, update, dzg, spread,
    in_sems, out_sems,
):
    hidden, rows, cols = product.shape
    width = cot.shape[2]
    copies = start(
        in_sems,
        [
            (gate_h, gate), (cot_h, cot), (norm_gain_h, norm_gain), (norm_bias_h, norm_bias),
            (out_w_h, out_weight), (gate_w_h, gate_weight),
        ],
    )
    spread[...] = product[...].astype(F32).reshape(hidden * rows, cols)
    wait(copies)
    groups = groups_of(rows)
    norm_gain_b = jnp.concatenate([down_lanes(norm_gain[...], cols)] * groups[0][1], axis=1)
    norm_bias_b = jnp.concatenate([down_lanes(norm_bias[...], cols)] * groups[0][1], axis=1)
    out_t = turned_weight(out_weight[...])
    for at, size in groups:
        xhat, _ = normalized(
            jnp.concatenate(
                [spread[pl.ds(at + r, hidden, stride=rows), :] for r in range(size)], axis=1
            )
        )
        ybar = (xhat * norm_gain_b + norm_bias_b).astype(BF16)
        u = dot(out_t, ybar)
        g = side_by_side(gate, at, size)
        done = (g * u).astype(BF16)
        cot_t = turned(cot[at : at + size].reshape(size * cols, width))
        back = dot(gate_weight[...], (cot_t * u * g * (1.0 - g)).astype(BF16))
        for r in range(size):
            lanes = slice(r * cols, (r + 1) * cols)
            update[at + r] = turned(done[:, lanes]).astype(BF16)
            dzg[at + r] = back[:, lanes].astype(BF16)
    wait(start(out_sems, [(update, update_h), (dzg, dzg_h)]))


def grad_right_kernel(grad, left, out_h, ready, sems):
    lead = (slice(None),) * (len(ready.shape) - 3)
    leaving = []
    for h in range(ready.shape[-3]):
        values = dot(channel_matrix(grad, h), channel_matrix(left, h), ((0,), (0,)))
        put_channel(ready, h, values)
        part = (*lead, pl.ds(h, 1))
        copy = pltpu.make_async_copy(ready.at[part], out_h.at[part], sems.at[h])
        copy.start()
        leaving.append(copy)
    wait(leaving)


def grad_left_kernel(grad, right, *refs):
    outs, ready = refs[:-1], refs[-1]
    n_col, share = ready.shape[1:3]
    for h in range(share):
        put_channel(ready, h, dot(channel_matrix(grad, h), channel_matrix(right, h)))
    for m, n, number in sources(outs[0].shape[0], len(outs)):
        outs[m][n] = ready[number // n_col, number % n_col]


def back_kernel(n_chip, grads, coef_h, zhat_h, inv_h, dzg_h, gain_h, proj_h, *refs):
    pieces, out_h = refs[:-15], refs[-15]
    (
        coef, zhat, inv, dzg, gain, proj_weight, out, left, right,
        sems, coef_sems, zhat_sems, dzg_sems, out_sems,
    ) = refs[-14:]
    rows, cols, width = out.shape
    hidden = left.shape[0] // rows
    groups, parts = groups_of(rows), groups_of(rows, 4)
    ahead = rows // math.gcd(rows, 2)
    blocks = [
        [
            pltpu.make_async_copy(
                source.at[pl.ds(at, size)], target.at[pl.ds(at, size)], sem.at[n]
            )
            for source, target, sem in (
                (coef_h, coef, coef_sems), (zhat_h, zhat, zhat_sems), (dzg_h, dzg, dzg_sems)
            )
        ]
        for n, (at, size) in enumerate(parts)
    ]
    for copy in sum(blocks, []):
        copy.start()
    small = start(sems, [(gain_h, gain), (proj_h, proj_weight), (inv_h, inv)])
    arrived = received(pieces, n_chip)
    length = left.shape[0] // len(arrived)
    for number, piece in arrived:
        first = pl.multiple_of(number * length, length)
        left[pl.ds(first, length), :] = piece.astype(F32).reshape(length, cols)
    total = grads[0].astype(F32)
    for half in range(1, grads.shape[0]):
        total = total + grads[half].astype(F32)
    right[...] = total.reshape(right.shape)
    wait(small)
    gain_b = jnp.concatenate([down_lanes(gain[...], cols)] * groups[0][1], axis=1)
    leaving = []
    arriving = {at: copies for (at, _), copies in zip(parts, blocks)}
    for at, size in groups:
        wait(arriving.get(at, []))
        columns = []
        for r in range(size):
            gl = left[pl.ds(at + r, hidden, stride=rows), :].astype(BF16)
            gr = right[pl.ds(at + r, hidden, stride=rows), :].astype(BF16)
            columns.append(
                jnp.concatenate(
                    [g * coef[at + r, part] for part, g in enumerate((gl, gl, gr, gr))], axis=0
                )
            )
        back = dot(proj_weight[...], jnp.concatenate(columns, axis=1))
        dzh = (back + side_by_side(dzg, at, size).astype(F32)) * gain_b
        z = side_by_side(zhat, at, size).astype(F32)
        inverse = jnp.concatenate([inv[at + r : at + r + 1] for r in range(size)], axis=1)
        m1 = jnp.mean(dzh, axis=0, keepdims=True)
        m2 = jnp.mean(dzh * z, axis=0, keepdims=True)
        grad = ((dzh - m1 - z * m2) * inverse).astype(BF16)
        for r in range(size):
            out[at + r] = turned(grad[:, r * cols : (r + 1) * cols]).astype(BF16)
        done = at + size
        if done % ahead == 0:
            part = pl.ds(done - ahead, ahead)
            copy = pltpu.make_async_copy(
                out.at[part], out_h.at[part], out_sems.at[done // ahead - 1]
            )
            copy.start()
            leaving.append(copy)
    wait(leaving)


def call(kernel, outs, scratch, args, near=(), outs_near=(), flops=0, moved=0):
    here, far = (pl.BlockSpec(memory_space=space) for space in (pltpu.VMEM, pltpu.HBM))
    specs = [here if at in near else far for at in range(len(args))]
    return pl.pallas_call(
        kernel,
        out_shape=[
            out if at in outs_near else pltpu.HBM(out.shape, out.dtype)
            for at, out in enumerate(outs)
        ],
        in_specs=specs,
        out_specs=[here if at in outs_near else far for at in range(len(outs))],
        scratch_shapes=scratch,
        compiler_params=pltpu.CompilerParams(vmem_limit_bytes=16 * MIB),
        cost_estimate=pl.CostEstimate(flops=flops, bytes_accessed=moved, transcendentals=0),
    )(
        *[
            pltpu.with_memory_space_constraint(arg, pltpu.HBM) if spec is far else arg
            for arg, spec in zip(args, specs)
        ]
    )


def body(
    pair, mask, gain_in, bias_in, proj_weight, gate_weight,
    product_norm_gain, product_norm_bias, out_weight, cotangent,
):
    rows, cols, width = pair.shape
    hidden = out_weight.shape[0]
    n_half = lax.axis_size("half")
    n_row = lax.axis_size("row")
    n_core = lax.axis_size("core")
    n_col = lax.axis_size("col")
    n_chip = n_row * n_col
    n_line = n_row * n_core
    n_place = n_line * n_col
    within = ("row", "core", "col")
    share = hidden // n_place
    cells = rows * cols
    n_groups = len(groups_of(rows))
    n_parts = len(groups_of(rows, 4))
    mask_row = mask.reshape(1, -1)
    gain_in, bias_in = gain_in.reshape(1, -1), bias_in.reshape(1, -1)
    norm_gain, norm_bias = product_norm_gain.reshape(1, -1), product_norm_bias.reshape(1, -1)

    def shape(*dims, dtype=BF16):
        return jax.ShapeDtypeStruct(dims, dtype)

    def vmem(*dims, dtype=BF16):
        return pltpu.VMEM(dims, dtype)

    def sems(count):
        return pltpu.SemaphoreType.DMA((count,))

    def exchange(values):
        return lax.all_to_all(values, within, split_axis=0, concat_axis=0, tiled=True)

    def exchange_all(values):
        flat = values.reshape(n_half * n_place, share, rows, cols)
        return lax.all_to_all(
            flat, ("half", *within), split_axis=0, concat_axis=0, tiled=True
        )

    def permute(values, axes, size, distance):
        return lax.ppermute(values, axes, [(at, at ^ distance) for at in range(size)])

    def exchange_pieces(pieces):
        first = [pieces[0]]
        first += [permute(pieces[m], ("core",), n_core, m) for m in range(1, n_core)]
        second = [
            permute(jnp.stack([piece[n] for piece in first]), ("row", "col"), n_chip, n)
            for n in range(n_chip - 1, 0, -1)
        ]
        return tuple(first + second[::-1])

    mask_s = pltpu.SMEM(mask.shape, jnp.int32)
    mask_v = vmem(*mask_row.shape, dtype=jnp.int32)
    vector = vmem(1, width, dtype=F32)
    plane = vmem(hidden * rows, cols, dtype=F32)
    block = vmem(rows, cols, width)
    wide = vmem(rows, width, cols, dtype=F32)
    short = vmem(rows, width, cols)
    square = vmem(width, hidden)
    proj_v = vmem(width, 4 * hidden)
    pieces_shape = (shape(n_chip, share, rows, cols),) * n_core
    n_pieces = n_core + n_chip - 1

    def front(part, outs, scratch, near):
        return call(
            functools.partial(front_kernel, part, len(outs)),
            outs,
            [
                block, mask_s, mask_v, vector, vector, vmem(width, 2 * hidden),
                vmem(width, cells), plane, sems(6), *scratch,
            ],
            (pair, mask, mask_row, gain_in, bias_in, proj_weight),
            outs_near=near,
            flops=2 * cells * width * 3 * hidden,
            moved=5 * cells * width,
        )

    everywhere = vmem(n_place, share, rows, cols)
    (right,) = front(
        2,
        (shape(n_half, n_place, share, rows, cols),),
        [everywhere, pltpu.SemaphoreType.DMA((n_half, math.gcd(n_place, 2)))],
        (),
    )
    right = exchange_all(right).reshape(n_half, n_line, n_col, share, rows, cols)
    left = exchange_pieces(tuple(front(0, pieces_shape, [], range(n_core))))
    zhat, short_zhat, inv, gate, dxh = call(
        side_kernel,
        (
            shape(rows, width, cols, dtype=F32),
            shape(rows, width, cols),
            shape(rows, cols, dtype=F32),
            shape(rows, width, cols, dtype=F32),
            shape(hidden * rows, cols, dtype=F32),
        ),
        [
            block, block, vector, vector, square, vector, square,
            wide, short, vmem(rows, cols, dtype=F32), wide, sems(7), sems(4),
        ],
        (pair, cotangent, gain_in, bias_in, gate_weight, norm_gain, out_weight),
        outs_near=(4,),
        flops=2 * cells * width * 4 * hidden,
        moved=16 * cells * width,
    )
    (coef,) = call(
        factors_kernel,
        (shape(rows, 4, hidden, cols),),
        [
            wide, mask_s, mask_v, vector, vector, proj_v, vmem(rows, 4, hidden, cols),
            sems(6), sems(n_groups),
        ],
        (zhat, mask, mask_row, gain_in, bias_in, proj_weight),
        flops=2 * cells * width * 5 * hidden,
        moved=16 * cells * width,
    )
    product, left = call(
        functools.partial(product_kernel, n_chip),
        (shape(n_line, n_col, share, rows, cols), shape(n_line, n_col, share, rows, cols)),
        [],
        (right, coef, *left),
        near=(0, *range(2, 2 + n_pieces)),
        outs_near=(0, 1),
        flops=2 * share * n_half * (n_line * rows) ** 2 * n_col * cols,
        moved=8 * cells * hidden,
    )
    product = exchange(product.reshape(n_place, share, rows, cols)).reshape(hidden, rows, cols)
    (grad,) = call(
        middle_kernel,
        (shape(hidden, rows, cols),),
        [vmem(hidden, rows, cols, dtype=F32)],
        (product, dxh.reshape(hidden, rows, cols)),
        near=(0, 1),
        outs_near=(0,),
        flops=20 * cells * hidden,
        moved=8 * cells * hidden,
    )
    grad = exchange(grad.reshape(n_place, share, rows, cols))
    grad = grad.reshape(n_line, n_col, share, rows, cols)
    (sent,) = call(
        grad_right_kernel,
        (shape(n_half, n_line, n_col, share, rows, cols),),
        [vmem(n_half, n_line, n_col, share, rows, cols), sems(share)],
        (grad, left),
        near=(0, 1),
        flops=2 * share * n_half * (n_line * rows) ** 2 * n_col * cols,
        moved=8 * cells * hidden,
    )
    grad_right = exchange_all(sent).reshape(n_half, n_place, share, rows, cols)
    grad_left = call(
        grad_left_kernel,
        pieces_shape,
        [vmem(n_line, n_col, share, rows, cols)],
        (grad, right),
        near=(0, 1),
        outs_near=range(n_core),
        flops=2 * share * n_half * (n_line * rows) ** 2 * n_col * cols,
        moved=8 * cells * hidden,
    )
    grad_left = exchange_pieces(tuple(grad_left))
    update, dzg = call(
        update_kernel,
        (shape(rows, cols, width), shape(rows, width, cols)),
        [wide, block, vector, vector, square, square, block, short, plane, sems(6), sems(2)],
        (product, gate, cotangent, norm_gain, norm_bias, out_weight, gate_weight, sent),
        near=(0,),
        flops=2 * cells * width * 3 * hidden,
        moved=14 * cells * hidden,
    )
    (grad_pair,) = call(
        functools.partial(back_kernel, n_chip),
        (shape(rows, cols, width),),
        [
            vmem(rows, 4, hidden, cols), short, vmem(rows, cols, dtype=F32), short,
            vector, proj_v, block, plane, plane,
            sems(3), sems(n_parts), sems(n_parts), sems(n_parts), sems(2),
        ],
        (grad_right, coef, short_zhat, inv, dzg, gain_in, proj_weight, *grad_left),
        near=(0, *range(7, 7 + n_pieces)),
        flops=2 * cells * width * 5 * hidden,
        moved=30 * cells * width,
    )
    return (update, grad_pair)


def solution(mesh):
    n_grp, n_row, n_col = (mesh.shape[name] for name in ("grp", "row", "col"))
    n_half = math.gcd(n_row, 2)
    n_core = math.gcd(n_row // n_half, 2)
    split = jax.sharding.Mesh(
        mesh.devices.reshape(n_grp, n_half, n_row // (n_half * n_core), n_core, n_col),
        ("grp", "half", "row", "core", "col"),
    )
    cells = P(("grp", "half", "row", "core"), "col", None)
    return jax.shard_map(
        body,
        mesh=split,
        in_specs=(cells, P("grp"), P(), P(), P(), P(), P(), P(), P(), cells),
        out_specs=(cells, cells),
        check_vma=False,
    )
```

```python
import functools
import math

import jax
import jax.numpy as jnp
from jax import lax
from jax.experimental import pallas as pl
from jax.experimental.pallas import tpu as pltpu
from jax.sharding import PartitionSpec as P

EPS = 1e-05
F32 = jnp.float32
BF16 = jnp.bfloat16
MIB = 1 << 20


def dot(a, b, over=((1,), (0,))):
    return lax.dot_general(a, b, (over, ((), ())), preferred_element_type=F32)


def eye(size):
    down = lax.broadcasted_iota(jnp.int32, (size, size), 0)
    across = lax.broadcasted_iota(jnp.int32, (size, size), 1)
    return (down == across).astype(F32).astype(BF16)


def turned(values):
    return dot(eye(values.shape[1]), values, ((1,), (1,)))


def down_lanes(vector, lanes):
    return jnp.broadcast_to(vector, (lanes, vector.shape[1])).T


def turned_weight(weight):
    c, m = weight.shape
    return jnp.concatenate(
        [turned(weight[:, at : at + c]) for at in range(0, m, c)], axis=0
    ).astype(BF16)


def sigmoid(values):
    return 0.5 + 0.5 * jnp.tanh(0.5 * values)


def normalized(values):
    mean = jnp.mean(values, axis=0, keepdims=True)
    centred = values - mean
    var = jnp.mean(centred * centred, axis=0, keepdims=True)
    inverse = lax.rsqrt(var + EPS)
    return centred * inverse, inverse


def start(sems, copies):
    running = [
        pltpu.make_async_copy(source, target, sems.at[at])
        for at, (source, target) in enumerate(copies)
    ]
    for copy in running:
        copy.start()
    return running


def wait(copies):
    for copy in copies:
        copy.wait()


def groups_of(rows, most=2):
    size = math.gcd(rows, most)
    return [(at, size) for at in range(0, rows, size)]


def side_by_side(ref, at, size):
    return jnp.concatenate([ref[at + r] for r in range(size)], axis=1)


def pair_mask(mask_s, mask_v, at, size, rows, cols):
    here = lax.axis_index("half")
    for name in ("row", "core"):
        here = here * lax.axis_size(name) + lax.axis_index(name)
    first_row = here * rows + at
    first_col = pl.multiple_of(lax.axis_index("col") * cols, cols)
    col_mask = mask_v[:, pl.ds(first_col, cols)].astype(F32)
    return jnp.concatenate(
        [col_mask * mask_s[first_row + r].astype(F32) for r in range(size)], axis=1
    )


def sources(n_chip, n_core):
    n_col = lax.axis_size("col")
    core = lax.axis_index("core")
    chip = lax.axis_index("row") * n_col + lax.axis_index("col")
    found = []
    for n in range(n_chip):
        other = chip ^ n
        for m in range(n_core):
            line = other // n_col * n_core + (core ^ m)
            found.append((m, n, line * n_col + other % n_col))
    return found


def received(refs, n_chip):
    n_core = len(refs) - n_chip + 1
    return [
        (number, refs[m][0] if n == 0 else refs[n_core + n - 1][m])
        for m, n, number in sources(n_chip, n_core)
    ]


def front_kernel(
    part, n_out, pair_h, mask_h, mask_row_h, gain_h, bias_h, proj_h, *refs
):
    outs = refs[:n_out]
    pair, mask_s, mask_v, gain, bias, proj_weight, zbar, plane, sems, *more = refs[n_out:]
    rows, cols, width = pair.shape
    hidden = plane.shape[0] // rows
    groups = groups_of(rows)
    *small, whole = start(
        sems,
        [
            (gain_h, gain), (bias_h, bias),
            (proj_h.at[:, pl.ds(part * hidden, 2 * hidden)], proj_weight),
            (mask_h, mask_s), (mask_row_h, mask_v), (pair_h, pair),
        ],
    )
    wait(small)
    gain_b = jnp.concatenate([down_lanes(gain[...], cols)] * groups[0][1], axis=1)
    bias_b = jnp.concatenate([down_lanes(bias[...], cols)] * groups[0][1], axis=1)
    weight = turned_weight(proj_weight[...])
    whole.wait()
    for at, size in groups:
        zhat, _ = normalized(turned(pair[at : at + size].reshape(size * cols, width)))
        zbar[:, at * cols : (at + size) * cols] = (zhat * gain_b + bias_b).astype(BF16)

    def channels(first, count):
        block = jnp.concatenate(
            [weight[first : first + count], weight[hidden + first : hidden + first + count]], axis=0
        )
        for at, size in groups:
            proj = dot(block, zbar[:, at * cols : (at + size) * cols])
            pm = pair_mask(mask_s, mask_v, at, size, rows, cols)
            values = sigmoid(proj[:count]) * proj[count:] * pm
            for r in range(size):
                plane[pl.ds(first * rows + at + r, count, stride=rows), :] = values[
                    :, r * cols : (r + 1) * cols
                ]

    if n_out > 1:
        channels(0, hidden)
        give_pieces(plane, outs)
        return
    (out_h,), (ready, out_sems) = outs, more
    n_place, share = ready.shape[:2]
    size = n_place // math.gcd(n_place, 2)
    leaving = []
    for n, at in enumerate(range(0, n_place, size)):
        channels(at * share, size * share)
        values = plane[at * share * rows : (at + size) * share * rows]
        ready[at : at + size] = values.reshape(size, *ready.shape[1:]).astype(BF16)
        for half in range(out_h.shape[0]):
            copy = pltpu.make_async_copy(
                ready.at[pl.ds(at, size)], out_h.at[half, pl.ds(at, size)], out_sems.at[half, n]
            )
            copy.start()
            leaving.append(copy)
    wait(leaving)


def give_pieces(plane, outs):
    n_chip = outs[0].shape[0]
    length = plane.shape[0] // (len(outs) * n_chip)
    for m, n, number in sources(n_chip, len(outs)):
        first = pl.multiple_of(number * length, length)
        values = plane[pl.ds(first, length), :]
        outs[m][n] = values.reshape(outs[m].shape[1:]).astype(BF16)


def side_kernel(
    pair_h, cot_h, gain_h, bias_h, gate_h, norm_gain_h, out_w_h,
    zhat_h, short_h, inv_h, gate_out_h, dxh_out,
    pair, cot, gain, bias, gate_weight, norm_gain, out_weight,
    zhat_out, short_out, inv_out, gate_out, in_sems, out_sems,
):
    rows, cols, width = pair.shape
    hidden = out_weight.shape[0]
    wait(
        start(
            in_sems,
            [
                (pair_h, pair), (cot_h, cot), (gain_h, gain), (bias_h, bias),
                (gate_h, gate_weight), (norm_gain_h, norm_gain), (out_w_h, out_weight),
            ],
        )
    )
    groups = groups_of(rows)
    gain_b = jnp.concatenate([down_lanes(gain[...], cols)] * groups[0][1], axis=1)
    bias_b = jnp.concatenate([down_lanes(bias[...], cols)] * groups[0][1], axis=1)
    norm_gain_b = jnp.concatenate([down_lanes(norm_gain[...], cols)] * groups[0][1], axis=1)
    gate_t = turned_weight(gate_weight[...])
    for at, size in groups:
        zhat, inverse = normalized(turned(pair[at : at + size].reshape(size * cols, width)))
        zbar = (zhat * gain_b + bias_b).astype(BF16)
        gate = sigmoid(dot(gate_t, zbar))
        cot_t = turned(cot[at : at + size].reshape(size * cols, width))
        dxh = dot(out_weight[...], (cot_t * gate).astype(BF16)) * norm_gain_b
        dxh = dxh - jnp.mean(dxh, axis=0, keepdims=True)
        for r in range(size):
            lanes = slice(r * cols, (r + 1) * cols)
            zhat_out[at + r] = zhat[:, lanes]
            short_out[at + r] = zhat[:, lanes].astype(BF16)
            inv_out[at + r : at + r + 1] = inverse[:, lanes]
            gate_out[at + r] = gate[:, lanes]
            dxh_out[pl.ds(at + r, hidden, stride=rows), :] = dxh[:, lanes]
    wait(
        start(
            out_sems,
            [
                (zhat_out, zhat_h), (short_out, short_h), (inv_out, inv_h),
                (gate_out, gate_out_h),
            ],
        )
    )


def factors_kernel(
    zhat_h, mask_h, mask_row_h, gain_h, bias_h, proj_h, coef_h,
    zhat, mask_s, mask_v, gain, bias, proj_weight, coef, in_sems, out_sems,
):
    rows, width, cols = zhat.shape
    hidden = coef.shape[2]
    wait(
        start(
            in_sems,
            [
                (zhat_h, zhat), (mask_h, mask_s), (mask_row_h, mask_v), (gain_h, gain),
                (bias_h, bias), (proj_h, proj_weight),
            ],
        )
    )
    groups = groups_of(rows)
    gain_b = jnp.concatenate([down_lanes(gain[...], cols)] * groups[0][1], axis=1)
    bias_b = jnp.concatenate([down_lanes(bias[...], cols)] * groups[0][1], axis=1)
    weight = turned_weight(proj_weight[...])
    leaving = []
    for n, (at, size) in enumerate(groups):
        zbar = (side_by_side(zhat, at, size) * gain_b + bias_b).astype(BF16)
        pm = pair_mask(mask_s, mask_v, at, size, rows, cols)
        for part in (0, 2):
            s = sigmoid(dot(weight[part * hidden : (part + 1) * hidden], zbar))
            q = dot(weight[(part + 1) * hidden : (part + 2) * hidden], zbar)
            second = pm * s
            first = second * q * (1.0 - s)
            for r in range(size):
                lanes = slice(r * cols, (r + 1) * cols)
                coef[at + r, part] = first[:, lanes].astype(BF16)
                coef[at + r, part + 1] = second[:, lanes].astype(BF16)
        copy = pltpu.make_async_copy(
            coef.at[pl.ds(at, size)], coef_h.at[pl.ds(at, size)], out_sems.at[n]
        )
        copy.start()
        leaving.append(copy)
    wait(leaving)


def channel_matrix(ref, at):
    *_, n_col, _, rows, cols = ref.shape
    lead = (slice(None),) * (len(ref.shape) - 4)
    return jnp.concatenate(
        [ref[(*lead, c, at)].reshape(-1, cols) for c in range(n_col)], axis=1
    )


def put_channel(ref, at, values):
    *shape, n_col, _, rows, cols = ref.shape
    lead = (slice(None),) * len(shape)
    values = values.astype(BF16)
    for c in range(n_col):
        ref[(*lead, c, at)] = values[:, c * cols : (c + 1) * cols].reshape(*shape, rows, cols)


def product_kernel(n_chip, right, after, *refs):
    pieces, (out, left) = refs[:-2], refs[-2:]
    n_col, share = left.shape[1:3]
    for number, piece in received(pieces, n_chip):
        left[number // n_col, number % n_col] = piece
    for h in range(share):
        values = dot(channel_matrix(left, h), channel_matrix(right, h), ((1,), (1,)))
        put_channel(out, h, values)


def middle_kernel(product, dxh, out, xhat):
    hidden = product.shape[0]
    values = product[...].astype(F32)
    mean = jnp.sum(values, axis=0) * (1.0 / hidden)
    centred = values - mean
    var = jnp.sum(centred * centred, axis=0) * (1.0 / hidden)
    inverse = lax.rsqrt(var + EPS)
    xhat[...] = centred * inverse
    m2 = jnp.sum(dxh[...] * xhat[...], axis=0) * (1.0 / hidden)
    out[...] = ((dxh[...] - xhat[...] * m2) * inverse).astype(BF16)


def update_kernel(
    product, gate_h, cot_h, norm_gain_h, norm_bias_h, out_w_h, gate_w_h, after, update_h, dzg_h,
    gate, cot, norm_gain, norm_bias, out_weight, gate_weight, update, dzg, spread,
    in_sems, out_sems,
):
    hidden, rows, cols = product.shape
    width = cot.shape[2]
    copies = start(
        in_sems,
        [
            (gate_h, gate), (cot_h, cot), (norm_gain_h, norm_gain), (norm_bias_h, norm_bias),
            (out_w_h, out_weight), (gate_w_h, gate_weight),
        ],
    )
    spread[...] = product[...].astype(F32).reshape(hidden * rows, cols)
    wait(copies)
    groups = groups_of(rows)
    norm_gain_b = jnp.concatenate([down_lanes(norm_gain[...], cols)] * groups[0][1], axis=1)
    norm_bias_b = jnp.concatenate([down_lanes(norm_bias[...], cols)] * groups[0][1], axis=1)
    out_t = turned_weight(out_weight[...])
    for at, size in groups:
        xhat, _ = normalized(
            jnp.concatenate(
                [spread[pl.ds(at + r, hidden, stride=rows), :] for r in range(size)], axis=1
            )
        )
        ybar = (xhat * norm_gain_b + norm_bias_b).astype(BF16)
        u = dot(out_t, ybar)
        g = side_by_side(gate, at, size)
        done = (g * u).astype(BF16)
        cot_t = turned(cot[at : at + size].reshape(size * cols, width))
        back = dot(gate_weight[...], (cot_t * u * g * (1.0 - g)).astype(BF16))
        for r in range(size):
            lanes = slice(r * cols, (r + 1) * cols)
            update[at + r] = turned(done[:, lanes]).astype(BF16)
            dzg[at + r] = back[:, lanes].astype(BF16)
    wait(start(out_sems, [(update, update_h), (dzg, dzg_h)]))


def grad_right_kernel(grad, left, out_h, ready, sems):
    lead = (slice(None),) * (len(ready.shape) - 3)
    leaving = []
    for h in range(ready.shape[-3]):
        values = dot(channel_matrix(grad, h), channel_matrix(left, h), ((0,), (0,)))
        put_channel(ready, h, values)
        part = (*lead, pl.ds(h, 1))
        copy = pltpu.make_async_copy(ready.at[part], out_h.at[part], sems.at[h])
        copy.start()
        leaving.append(copy)
    wait(leaving)


def grad_left_kernel(grad, right, *refs):
    outs, ready = refs[:-1], refs[-1]
    n_col, share = ready.shape[1:3]
    for h in range(share):
        put_channel(ready, h, dot(channel_matrix(grad, h), channel_matrix(right, h)))
    for m, n, number in sources(outs[0].shape[0], len(outs)):
        outs[m][n] = ready[number // n_col, number % n_col]


def back_kernel(n_chip, grads, coef_h, zhat_h, inv_h, dzg_h, gain_h, proj_h, *refs):
    pieces, out_h = refs[:-15], refs[-15]
    (
        coef, zhat, inv, dzg, gain, proj_weight, out, left, right,
        sems, coef_sems, zhat_sems, dzg_sems, out_sems,
    ) = refs[-14:]
    rows, cols, width = out.shape
    hidden = left.shape[0] // rows
    groups, parts = groups_of(rows), groups_of(rows, 4)
    small = start(sems, [(gain_h, gain), (proj_h, proj_weight), (inv_h, inv)])
    ahead = rows // math.gcd(rows, 4)
    blocks = [
        [
            pltpu.make_async_copy(
                source.at[pl.ds(at, size)], target.at[pl.ds(at, size)], sem.at[n]
            )
            for source, target, sem in (
                (coef_h, coef, coef_sems), (zhat_h, zhat, zhat_sems), (dzg_h, dzg, dzg_sems)
            )
        ]
        for n, (at, size) in enumerate(parts)
    ]
    for copy in sum(blocks[:2], []):
        copy.start()
    arrived = received(pieces, n_chip)
    length = left.shape[0] // len(arrived)
    for number, piece in arrived:
        first = pl.multiple_of(number * length, length)
        left[pl.ds(first, length), :] = piece.astype(F32).reshape(length, cols)
    total = grads[0].astype(F32)
    for half in range(1, grads.shape[0]):
        total = total + grads[half].astype(F32)
    right[...] = total.reshape(right.shape)
    wait(small)
    gain_b = jnp.concatenate([down_lanes(gain[...], cols)] * groups[0][1], axis=1)
    leaving = []
    for copy in sum(blocks[2:], []):
        copy.start()
    arriving = {at: copies for (at, _), copies in zip(parts, blocks)}
    for at, size in groups:
        wait(arriving.get(at, []))
        columns = []
        for r in range(size):
            gl = left[pl.ds(at + r, hidden, stride=rows), :].astype(BF16)
            gr = right[pl.ds(at + r, hidden, stride=rows), :].astype(BF16)
            columns.append(
                jnp.concatenate(
                    [g * coef[at + r, part] for part, g in enumerate((gl, gl, gr, gr))], axis=0
                )
            )
        back = dot(proj_weight[...], jnp.concatenate(columns, axis=1))
        dzh = (back + side_by_side(dzg, at, size).astype(F32)) * gain_b
        z = side_by_side(zhat, at, size).astype(F32)
        inverse = jnp.concatenate([inv[at + r : at + r + 1] for r in range(size)], axis=1)
        m1 = jnp.mean(dzh, axis=0, keepdims=True)
        m2 = jnp.mean(dzh * z, axis=0, keepdims=True)
        grad = ((dzh - m1 - z * m2) * inverse).astype(BF16)
        for r in range(size):
            out[at + r] = turned(grad[:, r * cols : (r + 1) * cols]).astype(BF16)
        done = at + size
        if done % ahead == 0:
            part = pl.ds(done - ahead, ahead)
            copy = pltpu.make_async_copy(
                out.at[part], out_h.at[part], out_sems.at[done // ahead - 1]
            )
            copy.start()
            leaving.append(copy)
    wait(leaving)


def call(kernel, outs, scratch, args, near=(), outs_near=(), flops=0, moved=0):
    here, far = (pl.BlockSpec(memory_space=space) for space in (pltpu.VMEM, pltpu.HBM))
    specs = [here if at in near else far for at in range(len(args))]
    return pl.pallas_call(
        kernel,
        out_shape=[
            out if at in outs_near else pltpu.HBM(out.shape, out.dtype)
            for at, out in enumerate(outs)
        ],
        in_specs=specs,
        out_specs=[here if at in outs_near else far for at in range(len(outs))],
        scratch_shapes=scratch,
        compiler_params=pltpu.CompilerParams(vmem_limit_bytes=16 * MIB),
        cost_estimate=pl.CostEstimate(flops=flops, bytes_accessed=moved, transcendentals=0),
    )(
        *[
            pltpu.with_memory_space_constraint(arg, pltpu.HBM) if spec is far else arg
            for arg, spec in zip(args, specs)
        ]
    )


def body(
    pair, mask, gain_in, bias_in, proj_weight, gate_weight,
    product_norm_gain, product_norm_bias, out_weight, cotangent,
):
    rows, cols, width = pair.shape
    hidden = out_weight.shape[0]
    n_half = lax.axis_size("half")
    n_row = lax.axis_size("row")
    n_core = lax.axis_size("core")
    n_col = lax.axis_size("col")
    n_chip = n_row * n_col
    n_line = n_row * n_core
    n_place = n_line * n_col
    within = ("row", "core", "col")
    share = hidden // n_place
    cells = rows * cols
    n_groups = len(groups_of(rows))
    n_parts = len(groups_of(rows, 4))
    mask_row = mask.reshape(1, -1)
    gain_in, bias_in = gain_in.reshape(1, -1), bias_in.reshape(1, -1)
    norm_gain, norm_bias = product_norm_gain.reshape(1, -1), product_norm_bias.reshape(1, -1)

    def shape(*dims, dtype=BF16):
        return jax.ShapeDtypeStruct(dims, dtype)

    def vmem(*dims, dtype=BF16):
        return pltpu.VMEM(dims, dtype)

    def sems(count):
        return pltpu.SemaphoreType.DMA((count,))

    def exchange(values):
        return lax.all_to_all(values, within, split_axis=0, concat_axis=0, tiled=True)

    def exchange_all(values):
        flat = values.reshape(n_half * n_place, share, rows, cols)
        return lax.all_to_all(
            flat, ("half", *within), split_axis=0, concat_axis=0, tiled=True
        )

    def permute(values, axes, size, distance):
        return lax.ppermute(values, axes, [(at, at ^ distance) for at in range(size)])

    def exchange_pieces(pieces):
        first = [pieces[0]]
        first += [permute(pieces[m], ("core",), n_core, m) for m in range(1, n_core)]
        second = [
            permute(jnp.stack([piece[n] for piece in first]), ("row", "col"), n_chip, n)
            for n in range(n_chip - 1, 0, -1)
        ]
        return tuple(first + second[::-1])

    mask_s = pltpu.SMEM(mask.shape, jnp.int32)
    mask_v = vmem(*mask_row.shape, dtype=jnp.int32)
    vector = vmem(1, width, dtype=F32)
    plane = vmem(hidden * rows, cols, dtype=F32)
    block = vmem(rows, cols, width)
    wide = vmem(rows, width, cols, dtype=F32)
    short = vmem(rows, width, cols)
    square = vmem(width, hidden)
    proj_v = vmem(width, 4 * hidden)
    pieces_shape = (shape(n_chip, share, rows, cols),) * n_core
    n_pieces = n_core + n_chip - 1

    def front(part, outs, scratch, near):
        return call(
            functools.partial(front_kernel, part, len(outs)),
            outs,
            [
                block, mask_s, mask_v, vector, vector, vmem(width, 2 * hidden),
                vmem(width, cells), plane, sems(6), *scratch,
            ],
            (pair, mask, mask_row, gain_in, bias_in, proj_weight),
            outs_near=near,
            flops=2 * cells * width * 3 * hidden,
            moved=5 * cells * width,
        )

    everywhere = vmem(n_place, share, rows, cols)
    (right,) = front(
        2,
        (shape(n_half, n_place, share, rows, cols),),
        [everywhere, pltpu.SemaphoreType.DMA((n_half, math.gcd(n_place, 2)))],
        (),
    )
    right = exchange_all(right).reshape(n_half, n_line, n_col, share, rows, cols)
    left = exchange_pieces(tuple(front(0, pieces_shape, [], range(n_core))))
    zhat, short_zhat, inv, gate, dxh = call(
        side_kernel,
        (
            shape(rows, width, cols, dtype=F32),
            shape(rows, width, cols),
            shape(rows, cols, dtype=F32),
            shape(rows, width, cols, dtype=F32),
            shape(hidden * rows, cols, dtype=F32),
        ),
        [
            block, block, vector, vector, square, vector, square,
            wide, short, vmem(rows, cols, dtype=F32), wide, sems(7), sems(4),
        ],
        (pair, cotangent, gain_in, bias_in, gate_weight, norm_gain, out_weight),
        outs_near=(4,),
        flops=2 * cells * width * 4 * hidden,
        moved=16 * cells * width,
    )
    (coef,) = call(
        factors_kernel,
        (shape(rows, 4, hidden, cols),),
        [
            wide, mask_s, mask_v, vector, vector, proj_v, vmem(rows, 4, hidden, cols),
            sems(6), sems(n_groups),
        ],
        (zhat, mask, mask_row, gain_in, bias_in, proj_weight),
        flops=2 * cells * width * 5 * hidden,
        moved=16 * cells * width,
    )
    product, left = call(
        functools.partial(product_kernel, n_chip),
        (shape(n_line, n_col, share, rows, cols), shape(n_line, n_col, share, rows, cols)),
        [],
        (right, coef, *left),
        near=(0, *range(2, 2 + n_pieces)),
        outs_near=(0, 1),
        flops=2 * share * n_half * (n_line * rows) ** 2 * n_col * cols,
        moved=8 * cells * hidden,
    )
    product = exchange(product.reshape(n_place, share, rows, cols)).reshape(hidden, rows, cols)
    (grad,) = call(
        middle_kernel,
        (shape(hidden, rows, cols),),
        [vmem(hidden, rows, cols, dtype=F32)],
        (product, dxh.reshape(hidden, rows, cols)),
        near=(0, 1),
        outs_near=(0,),
        flops=20 * cells * hidden,
        moved=8 * cells * hidden,
    )
    grad = exchange(grad.reshape(n_place, share, rows, cols))
    grad = grad.reshape(n_line, n_col, share, rows, cols)
    (sent,) = call(
        grad_right_kernel,
        (shape(n_half, n_line, n_col, share, rows, cols),),
        [vmem(n_half, n_line, n_col, share, rows, cols), sems(share)],
        (grad, left),
        near=(0, 1),
        flops=2 * share * n_half * (n_line * rows) ** 2 * n_col * cols,
        moved=8 * cells * hidden,
    )
    grad_right = exchange_all(sent).reshape(n_half, n_place, share, rows, cols)
    grad_left = call(
        grad_left_kernel,
        pieces_shape,
        [vmem(n_line, n_col, share, rows, cols)],
        (grad, right),
        near=(0, 1),
        outs_near=range(n_core),
        flops=2 * share * n_half * (n_line * rows) ** 2 * n_col * cols,
        moved=8 * cells * hidden,
    )
    grad_left = exchange_pieces(tuple(grad_left))
    update, dzg = call(
        update_kernel,
        (shape(rows, cols, width), shape(rows, width, cols)),
        [wide, block, vector, vector, square, square, block, short, plane, sems(6), sems(2)],
        (product, gate, cotangent, norm_gain, norm_bias, out_weight, gate_weight, sent),
        near=(0,),
        flops=2 * cells * width * 3 * hidden,
        moved=14 * cells * hidden,
    )
    (grad_pair,) = call(
        functools.partial(back_kernel, n_chip),
        (shape(rows, cols, width),),
        [
            vmem(rows, 4, hidden, cols), short, vmem(rows, cols, dtype=F32), short,
            vector, proj_v, block, plane, plane,
            sems(3), sems(n_parts), sems(n_parts), sems(n_parts), sems(n_parts),
        ],
        (grad_right, coef, short_zhat, inv, dzg, gain_in, proj_weight, *grad_left),
        near=(0, *range(7, 7 + n_pieces)),
        flops=2 * cells * width * 5 * hidden,
        moved=30 * cells * width,
    )
    return (update, grad_pair)


def solution(mesh):
    n_grp, n_row, n_col = (mesh.shape[name] for name in ("grp", "row", "col"))
    n_half = math.gcd(n_row, 2)
    n_core = math.gcd(n_row // n_half, 2)
    split = jax.sharding.Mesh(
        mesh.devices.reshape(n_grp, n_half, n_row // (n_half * n_core), n_core, n_col),
        ("grp", "half", "row", "core", "col"),
    )
    cells = P(("grp", "half", "row", "core"), "col", None)
    return jax.shard_map(
        body,
        mesh=split,
        in_specs=(cells, P("grp"), P(), P(), P(), P(), P(), P(), P(), cells),
        out_specs=(cells, cells),
        check_vma=False,
    )
```
